32 devices in a mesh: seq: 4 (over z), dp: 8 (over y, x, core).
Axes of the slice: x: 2, y: 2, z: 4, core: 2. Of those that a mesh axis runs over, the one named last changes fastest.
Arguments:
- hidden_in: bfloat16 [8, 512, 2048], P('dp', 'seq'), may hold values from -6 to 6
- routes: int32 [8, 512, 8], P('dp', 'seq'), may hold values from 0 to 31, all different within a row; in each aligned block of 128 rows (0 to 127, 128 to 255, ..., all dimensions but the last counted through in order) at most 36 rows name the same one
- norm1_gain: bfloat16 [2048], P(('seq', 'dp')), may hold values from 0.5 to 1.5
- query_gain: bfloat16 [128], P(('seq', 'dp')), may hold values from 0.5 to 1.5
- key_gain: bfloat16 [128], P(('seq', 'dp')), may hold values from 0.5 to 1.5
- qkv_weight: bfloat16 [2048, 5120], P(('seq', 'dp')), may hold values from -0.125 to 0.125
- out_weight: bfloat16 [4096, 2048], P(('seq', 'dp')), may hold values from -1.5 to 1.5
- norm2_gain: bfloat16 [2048], P(('seq', 'dp')), may hold values from 0.5 to 1.5
- router: bfloat16 [2048, 32], P(('seq', 'dp')), may hold values from -0.06982422 to 0.06982422
- gate_up_weight: bfloat16 [32, 2048, 1536], P(('seq', 'dp')), may hold values from -0.125 to 0.125
- down_weight: bfloat16 [32, 768, 2048], P(('seq', 'dp')), may hold values from -0.875 to 0.875
- cotangent: bfloat16 [8, 512, 2048], P('dp', 'seq'), may hold values from -6 to 6
Outputs:
- output: bfloat16 [8, 512, 2048], P('dp', 'seq')
- grad_input: float32 [8, 512, 2048], P('dp', 'seq')
- grad_norm1: float32 [2048], P(('seq', 'dp'))
- grad_query_gain: float32 [128], P(('seq', 'dp'))
- grad_key_gain: float32 [128], P(('seq', 'dp'))
- grad_qkv: float32 [2048, 5120], P(('seq', 'dp'))
- grad_out: float32 [4096, 2048], P(('seq', 'dp'))
- grad_norm2: float32 [2048], P(('seq', 'dp'))
- grad_router: float32 [2048, 32], P(('seq', 'dp'))
- grad_gate_up: float32 [32, 2048, 1536], P(('seq', 'dp'))
- grad_down: float32 [32, 768, 2048], P(('seq', 'dp'))
The draws below stay inside these ranges and needn't reach their ends.
Inputs may be any that keep to these rules, and one draw needn't show every extreme that they name: Each token names 8 different experts; in the rows of one device no expert is named by more than 36 routes, and in some device's rows one is named by exactly 36; every expert is named somewhere.
All inputs are finite; a program needn't handle non-finite values.
Results may differ from the reference program's by a relative error of at most 0.025.
Values may be sent and summed in bfloat16 or wider, within the bound.
A program may use at most 320 MiB of HBM per device.

```python
import math
import jax
import jax.numpy as jnp
import numpy as np
from jax import lax

MODEL_WIDTH = 2048
QUERY_HEADS = 32
KEY_VALUE_HEADS = 4
HEAD_SIZE = 128
FF = 768
TOP = 8
TOK_DEV = 128
EXPERTS = 32
LENGTH = 512
BATCH = 8
QD = 8
QKV = 5120
CAP = 36
N_SEQ = 4


def levels(stream_key, extent, shards, smallest, high):
    level = 1.0
    for axis_at, parts in shards:
        steps = jax.random.uniform(jax.random.fold_in(jax.random.fold_in(stream_key, 6), axis_at), (parts,), jnp.float32, smallest / len(shards), high / len(shards))
        level = level * jnp.repeat(jnp.exp(steps), extent[axis_at] // parts).reshape((-1,) + (1,) * (len(extent) - 1 - axis_at))
    return level


def assign_block(stream_key, own, number, rows, amount, top, bound, slope):
    order = jax.random.permutation(stream_key, amount)
    heavy_load, usual = shares(amount, rows * top, bound, slope, True), shares(amount, rows * top, bound, slope, False)
    places = jnp.arange(amount)

    def named(tallies, offset_by):
        used = int((tallies > 0).sum())
        fixed = max(1, used // 4)
        passed = fixed + (places - fixed + offset_by * (used - fixed)) % max(1, amount - fixed)
        return jnp.zeros((amount,), jnp.int32).at[order[jnp.where(places < fixed, places, passed)]].set(jnp.asarray(tallies, jnp.int32))

    tallies = jnp.where(number % 4 == 0, named(heavy_load, number // 4), named(usual, number - number // 4 - 1))
    mixed = jax.random.permutation(jax.random.fold_in(own, 3), amount)
    source_of, sink = mixed[0:amount // 2 * 2:2], mixed[1:amount // 2 * 2:2]
    margin = jnp.minimum(tallies[source_of] - 1, bound - tallies[sink]) // 2
    margin = jnp.where((source_of == order[0]) | (sink == order[0]) | (tallies[sink] == 0), 0, jnp.maximum(margin, 0))
    passed = jax.random.randint(jax.random.fold_in(own, 4), (amount // 2,), 0, 1 << 20) % (margin + 1)
    tallies = tallies.at[source_of].add(-passed).at[sink].add(passed)
    items = jnp.searchsorted(jnp.cumsum(tallies), jnp.arange(rows * top), side="right").astype(jnp.int32)
    table = items.reshape(top, rows).T
    table = table[jax.random.permutation(jax.random.fold_in(own, 1), rows)]
    offset_by = jax.random.randint(jax.random.fold_in(own, 2), (rows, 1), 0, top)
    return jnp.take_along_axis(table, (jnp.arange(top)[None, :] + offset_by) % top, axis=1)


def shares(number_of, total, most, skew, full):
    loads = [(1 << 20) // math.isqrt(grade ** skew) + 1 for grade in range(1, number_of + 1)]
    largest = most if full else min(most, max(-(-total // number_of), total * loads[0] // sum(loads)))
    least = 1 if total - largest >= number_of - 1 else 0
    counts, spare = [largest] + [least] * (number_of - 1), total - largest - least * (number_of - 1)
    while spare > 0:
        candidates = [i for i in range(1, number_of) if counts[i] < largest] or [i for i in range(1, number_of) if counts[i] < most]
        pool, remaining = sum([loads[i] for i in candidates]), spare
        for i in candidates:
            extra = min(most - counts[i], max(1, remaining * loads[i] // pool), spare)
            counts[i] = counts[i] + extra
            spare = spare - extra
    return np.array(counts)


def normal_values(own_key, shape, deviation, limit, pieces=(), kind=jnp.bfloat16):
    entries = deviation * jax.random.normal(own_key, shape, jnp.float32)
    if pieces:
        entries = entries * levels(own_key, shape, pieces, -0.22, 0.18)
    return jnp.clip(entries, -limit, limit).astype(kind)


def setup_inputs(seed: int = 0) -> dict:
    key_of = jax.random.split(jax.random.key(seed), 13)
    hidden_in = normal_values(key_of[0], (BATCH, LENGTH, MODEL_WIDTH), 1.0, 6.0, ((0, 8), (1, 4)))
    routes_keys = jax.random.split(jax.random.fold_in(key_of[1], 1), BATCH * LENGTH // TOK_DEV)
    routes_turns = jax.random.permutation(jax.random.fold_in(key_of[1], 3), BATCH * LENGTH // TOK_DEV)
    routes = jax.vmap(lambda own, number: assign_block(jax.random.fold_in(key_of[1], 2), own, number, TOK_DEV, EXPERTS, TOP, CAP, 2))(routes_keys, routes_turns).reshape((BATCH, LENGTH, TOP))
    norm1_gain = jnp.clip(1.0 + 0.1 * jax.random.normal(key_of[2], (MODEL_WIDTH,), jnp.float32), 0.5, 1.5).astype(jnp.bfloat16)
    query_gain = jnp.clip(1.0 + 0.1 * jax.random.normal(key_of[3], (HEAD_SIZE,), jnp.float32), 0.5, 1.5).astype(jnp.bfloat16)
    key_gain = jnp.clip(1.0 + 0.1 * jax.random.normal(key_of[4], (HEAD_SIZE,), jnp.float32), 0.5, 1.5).astype(jnp.bfloat16)
    qkv_weight = normal_values(key_of[5], (MODEL_WIDTH, QKV), MODEL_WIDTH ** -0.5, 0.125, ((0, 32),))
    out_weight = normal_values(key_of[6], (QUERY_HEADS * HEAD_SIZE, MODEL_WIDTH), (QUERY_HEADS * HEAD_SIZE // 256) ** -0.5, 1.5, ((0, 32),))
    norm2_gain = jnp.clip(1.0 + 0.1 * jax.random.normal(key_of[7], (MODEL_WIDTH,), jnp.float32), 0.5, 1.5).astype(jnp.bfloat16)
    router = normal_values(key_of[8], (MODEL_WIDTH, EXPERTS), 0.011, 0.06982422, ((0, 32),))
    gate_up_weight = normal_values(key_of[9], (EXPERTS, MODEL_WIDTH, 2 * FF), MODEL_WIDTH ** -0.5, 0.125, ((0, 32),))
    down_weight = normal_values(key_of[10], (EXPERTS, FF, MODEL_WIDTH), (FF // 16) ** -0.5, 0.875, ((0, 32),))
    cotangent = normal_values(key_of[11], (BATCH, LENGTH, MODEL_WIDTH), 1.0, 6.0, ((0, 8), (1, 4)))
    return dict(hidden_in=hidden_in, routes=routes, norm1_gain=norm1_gain, query_gain=query_gain, key_gain=key_gain, qkv_weight=qkv_weight, out_weight=out_weight, norm2_gain=norm2_gain, router=router, gate_up_weight=gate_up_weight, down_weight=down_weight, cotangent=cotangent)


@jax.custom_vjp
def low(v):
    return lax.optimization_barrier(v.astype(jnp.bfloat16)).astype(jnp.float32)

@jax.custom_vjp
def low_back(v):
    return v

def low_keep(v):
    return (low(v), None)

def low_pass(kept, grad):
    return (grad,)

def back_keep(v):
    return (v, None)

def back_low(kept, grad):
    return (low(grad),)
low.defvjp(low_keep, low_pass)
low_back.defvjp(back_keep, back_low)
EPSILON = 1e-06
ROPE_BASE = 1000000.0
PRECISE = lax.Precision.HIGHEST
FILLER = -1e+30

def rms_norm(values, gain):
    return values * lax.rsqrt(lax.optimization_barrier(jnp.mean(values * values, axis=-1, keepdims=True)) + EPSILON) * gain

def rope_tables(positions, width):
    half_width = width // 2
    freqs = ROPE_BASE ** (-(jnp.arange(half_width, dtype=jnp.float32) * (2.0 / width)))
    angles = positions[:, None] * freqs[None, :]
    return (jnp.cos(angles), jnp.sin(angles))

def rotate(values, cosine, sine_table):
    half_width = values.shape[-1] // 2
    first = values[..., :half_width]
    second = values[..., half_width:]
    cosine = cosine[:, None, :]
    sine_table = sine_table[:, None, :]
    return jnp.concatenate([first * cosine - second * sine_table, second * cosine + first * sine_table], axis=-1)

def attend_sequence(item):
    queries, key_copies, value_copies = item
    sequence_length = queries.shape[0]
    grouped = queries.reshape(sequence_length, N_SEQ, QD, HEAD_SIZE)
    scores = jnp.einsum('lgqd,mgd->gqlm', grouped, key_copies, precision=PRECISE) * HEAD_SIZE ** (-0.5)
    scores = low_back(scores)
    places = jnp.arange(sequence_length)
    visible = places[:, None] >= places[None, :]
    scores = jnp.where(visible, scores, FILLER)
    log_totals = jax.nn.logsumexp(scores, axis=-1, keepdims=True)
    weights_low = low(jnp.exp(scores - log_totals))
    mixed = jnp.einsum('gqlm,mgd->lgqd', weights_low, value_copies, precision=PRECISE)
    return mixed.reshape(sequence_length, QUERY_HEADS * HEAD_SIZE)

def expert_rows(item):
    rows_in, weight_in, weight_back = item
    gate_up = low_back(jnp.dot(rows_in, weight_in, precision=PRECISE))
    hidden = low(jax.nn.silu(gate_up[:, :FF]) * gate_up[:, FF:])
    return low(low_back(jnp.dot(hidden, weight_back, precision=PRECISE)))

def mixture(normed_low, gate_weights, routes, gate_up_w, down_w):
    flat_rows = normed_low.reshape(-1, MODEL_WIDTH)
    blocks = routes.reshape(-1, TOK_DEV * TOP)
    block_count = blocks.shape[0]
    onehot = (blocks[:, :, None] == jnp.arange(EXPERTS, dtype=jnp.int32)[None, None, :]).astype(jnp.int32)
    slot_index = lax.optimization_barrier(jnp.sum(jnp.cumsum(onehot, axis=1) * onehot, axis=-1)) - 1
    block_ids = jnp.arange(block_count, dtype=jnp.int32)[:, None]
    target = ((blocks * block_count + block_ids) * CAP + slot_index).reshape(-1).astype(jnp.int32)
    owner_row = (jnp.arange(block_count * TOK_DEV * TOP, dtype=jnp.int32) // TOP).astype(jnp.int32)
    slots_all = EXPERTS * block_count * CAP
    source = jnp.zeros((slots_all,), jnp.int32).at[target].set(owner_row)
    filled = jnp.zeros((slots_all,), jnp.float32).at[target].set(1.0)
    buffer = low_back(flat_rows[source] * filled[:, None]).reshape(EXPERTS, block_count * CAP, MODEL_WIDTH)
    results = lax.map(jax.checkpoint(expert_rows), (buffer, gate_up_w, down_w)).reshape(slots_all, MODEL_WIDTH)
    picked = results[target].reshape(-1, TOP, MODEL_WIDTH)
    combined = lax.optimization_barrier(jnp.sum(gate_weights.reshape(-1, TOP, 1) * picked, axis=1))
    return combined.reshape(normed_low.shape)

def layer_forward(hidden_in, gain_one, gain_query, gain_key, qkv_w, out_w, gain_two, router_w, gate_up_w, down_w, routes):
    batch_number, sequence_length = (hidden_in.shape[0], hidden_in.shape[1])
    head_replicas = N_SEQ // KEY_VALUE_HEADS
    cosine, sine_table = rope_tables(jnp.arange(sequence_length, dtype=jnp.float32), HEAD_SIZE)
    normed1 = low(rms_norm(hidden_in, gain_one))
    projected_rows = jnp.einsum('bld,de->ble', normed1, qkv_w, precision=PRECISE)
    query_raw = low_back(projected_rows[..., :QUERY_HEADS * HEAD_SIZE]).reshape(batch_number, sequence_length, QUERY_HEADS, HEAD_SIZE)
    paired_unprocessed = projected_rows[..., QUERY_HEADS * HEAD_SIZE:].reshape(batch_number, sequence_length, 2, KEY_VALUE_HEADS, HEAD_SIZE)
    pair_copies = low_back(jnp.repeat(paired_unprocessed, head_replicas, axis=3))
    queries = low(rotate(rms_norm(query_raw, gain_query), cosine, sine_table))
    keys_all = low(rotate(rms_norm(pair_copies[:, :, 0], gain_key), cosine, sine_table))
    values_all = low(pair_copies[:, :, 1])
    heads_out = lax.map(jax.checkpoint(attend_sequence), (queries, keys_all, values_all))
    heads_out = low(low_back(heads_out))
    branch = low_back(jnp.einsum('blf,fd->bld', heads_out, out_w, precision=PRECISE))
    hidden1 = hidden_in + branch
    normed2 = low(rms_norm(hidden1, gain_two))
    logits = low_back(jnp.einsum('bld,de->ble', normed2, router_w, precision=PRECISE))
    chosen = jnp.take_along_axis(logits, routes, axis=-1)
    gate_weights = jax.nn.softmax(chosen, axis=-1)
    return hidden1 + mixture(normed2, gate_weights, routes, gate_up_w, down_w)

def reference(hidden_in, routes, norm1_gain, query_gain, key_gain, qkv_weight, out_weight, norm2_gain, router, gate_up_weight, down_weight, cotangent):
    inputs = tuple((array.astype(jnp.float32) for array in (hidden_in, norm1_gain, query_gain, key_gain, qkv_weight, out_weight, norm2_gain, router, gate_up_weight, down_weight)))

    def forward(*params):
        return layer_forward(*params, routes)
    result, pull_back = jax.vjp(forward, *inputs)
    grads = pull_back(cotangent.astype(jnp.float32))
    return (result.astype(jnp.bfloat16), grads[0], grads[1], grads[2], grads[3], grads[4], grads[5], grads[6], grads[7], grads[8], grads[9])
```

```python
import jax
import jax.numpy as jnp
from jax import lax
from jax.sharding import PartitionSpec as P

MODEL_WIDTH = 2048
QUERY_HEADS = 32
KEY_VALUE_HEADS = 4
HEAD_SIZE = 128
FF = 768
TOP = 8


EPSILON = 1e-06
ROPE_BASE = 1000000.0
FILLER = -1e30
QUERY_BLOCK = 512


def rms_norm(values, gain):
    return values * lax.rsqrt(jnp.mean(values * values, axis=-1, keepdims=True) + EPSILON) * gain


def rope_tables(positions, width):
    half_width = width // 2
    freqs = ROPE_BASE ** (-(jnp.arange(half_width, dtype=jnp.float32) * (2.0 / width)))
    angles = positions[:, None] * freqs[None, :]
    return (jnp.cos(angles), jnp.sin(angles))


def rotate(values, cosine, sine_table):
    half_width = values.shape[-1] // 2
    first = values[..., :half_width]
    second = values[..., half_width:]
    cosine = cosine[:, None, :]
    sine_table = sine_table[:, None, :]
    return jnp.concatenate(
        [first * cosine - second * sine_table, second * cosine + first * sine_table], axis=-1
    )


def prepare_heads(projected_rows, gain_query, gain_key, cosine, sine_table):
    row_count = projected_rows.shape[0]
    query_columns = projected_rows.shape[1] - 2 * HEAD_SIZE
    queries = projected_rows[:, :query_columns].reshape(
        row_count, query_columns // HEAD_SIZE, HEAD_SIZE
    )
    key_head = projected_rows[:, query_columns : query_columns + HEAD_SIZE].reshape(
        row_count, 1, HEAD_SIZE
    )
    value_head = projected_rows[:, query_columns + HEAD_SIZE :]
    queries = rotate(rms_norm(queries, gain_query), cosine, sine_table)
    key_head = rotate(rms_norm(key_head, gain_key), cosine, sine_table).reshape(
        row_count, HEAD_SIZE
    )
    return (queries, key_head, value_head)


def inner_rows(left, right):
    return lax.dot_general(
        left, right, (((0,), (0,)), ((), ())), preferred_element_type=jnp.float32
    )


def outer_cols(left, right):
    return lax.dot_general(
        left, right, (((1,), (1,)), ((), ())), preferred_element_type=jnp.float32
    )


def block_slice(array, index, block_rows):
    return lax.dynamic_slice_in_dim(array, index * block_rows, block_rows, 0)


def block_scores(query_block, key_block, i, j, block_rows):
    scores = jnp.einsum(
        "qhd,kd->hqk", query_block, key_block, preferred_element_type=jnp.float32
    ) * HEAD_SIZE ** (-0.5)
    row_ids = i * block_rows + jnp.arange(block_rows)
    col_ids = j * block_rows + jnp.arange(block_rows)
    return jnp.where((row_ids[:, None] >= col_ids[None, :])[None], scores, FILLER)


def attend_forward(queries, keys_in, values_in):
    sequence_length, head_count = (queries.shape[0], queries.shape[1])
    block_rows = min(QUERY_BLOCK, sequence_length)
    block_count = sequence_length // block_rows

    def one_block(i):
        query_block = block_slice(queries, i, block_rows)

        def max_step(j, carry):
            row_top, row_total = carry
            scores = block_scores(
                query_block, block_slice(keys_in, j, block_rows), i, j, block_rows
            )
            new_top = jnp.maximum(row_top, jnp.max(scores, axis=-1))
            row_total = row_total * jnp.exp(row_top - new_top) + jnp.sum(
                jnp.exp(scores - new_top[..., None]), axis=-1
            )
            return (new_top, row_total)

        start = (
            jnp.full((head_count, block_rows), FILLER, jnp.float32),
            jnp.zeros((head_count, block_rows), jnp.float32),
        )
        row_top, row_total = lax.fori_loop(0, i + 1, max_step, start)
        log_totals = row_top + jnp.log(row_total)

        def out_step(j, accum_out):
            scores = block_scores(
                query_block, block_slice(keys_in, j, block_rows), i, j, block_rows
            )
            probabilities = jnp.exp(scores - log_totals[..., None]).astype(jnp.bfloat16)
            return accum_out + jnp.einsum(
                "hqk,kd->qhd",
                probabilities,
                block_slice(values_in, j, block_rows),
                preferred_element_type=jnp.float32,
            )

        accum_out = lax.fori_loop(
            0, i + 1, out_step, jnp.zeros((block_rows, head_count, HEAD_SIZE), jnp.float32)
        )
        return (accum_out, log_totals)

    outputs, log_totals = lax.map(one_block, jnp.arange(block_count))
    return (outputs.reshape(sequence_length, head_count, HEAD_SIZE), log_totals)


def attend_backward(queries, keys_in, values_in, out_full, log_totals, grad_heads):
    sequence_length, head_count = (queries.shape[0], queries.shape[1])
    block_rows = min(QUERY_BLOCK, sequence_length)
    block_count = sequence_length // block_rows
    row_dots = jnp.sum(grad_heads.astype(jnp.float32) * out_full, axis=-1)

    def one_block(carry, i):
        query_block = block_slice(queries, i, block_rows)
        grad_block = block_slice(grad_heads, i, block_rows)
        dot_block = block_slice(row_dots, i, block_rows).T
        block_totals = log_totals[i]

        def step(j, inner):
            grad_query, grad_keys, grad_values = inner
            key_block = block_slice(keys_in, j, block_rows)
            value_block = block_slice(values_in, j, block_rows)
            scores = block_scores(query_block, key_block, i, j, block_rows)
            probabilities = jnp.exp(scores - block_totals[..., None])
            grad_probs = jnp.einsum(
                "qhd,kd->hqk", grad_block, value_block, preferred_element_type=jnp.float32
            )
            grad_scores = (probabilities * (grad_probs - dot_block[..., None])).astype(jnp.bfloat16)
            grad_query = grad_query + jnp.einsum(
                "hqk,kd->qhd", grad_scores, key_block, preferred_element_type=jnp.float32
            ) * HEAD_SIZE ** (-0.5)
            key_part = jnp.einsum(
                "hqk,qhd->kd", grad_scores, query_block, preferred_element_type=jnp.float32
            ) * HEAD_SIZE ** (-0.5)
            value_part = jnp.einsum(
                "hqk,qhd->kd",
                probabilities.astype(jnp.bfloat16),
                grad_block,
                preferred_element_type=jnp.float32,
            )
            grad_keys = lax.dynamic_update_slice_in_dim(
                grad_keys, block_slice(grad_keys, j, block_rows) + key_part, j * block_rows, 0
            )
            grad_values = lax.dynamic_update_slice_in_dim(
                grad_values, block_slice(grad_values, j, block_rows) + value_part, j * block_rows, 0
            )
            return (grad_query, grad_keys, grad_values)

        start = (jnp.zeros((block_rows, head_count, HEAD_SIZE), jnp.float32), carry[0], carry[1])
        grad_query, grad_keys, grad_values = lax.fori_loop(0, i + 1, step, start)
        return ((grad_keys, grad_values), grad_query)

    empty = jnp.zeros((sequence_length, HEAD_SIZE), jnp.float32)
    (grad_keys, grad_values), grad_query = lax.scan(
        one_block, (empty, empty), jnp.arange(block_count)
    )
    return (grad_query.reshape(sequence_length, head_count, HEAD_SIZE), grad_keys, grad_values)


def masked_softmax(logits, mask):
    shifted = jnp.where(mask > 0, logits, FILLER)
    top = jnp.max(shifted, axis=-1, keepdims=True)
    powers = jnp.where(mask > 0, jnp.exp(shifted - top), 0.0)
    total = jnp.sum(powers, axis=-1, keepdims=True)
    return powers / jnp.where(total > 0, total, 1.0)


def body(
    hidden_in,
    routes,
    norm1_gain,
    query_gain,
    key_gain,
    qkv_weight,
    out_weight,
    norm2_gain,
    router,
    gate_up_weight,
    down_weight,
    cotangent,
):
    tokens = hidden_in.shape[1]
    sequence_number = lax.axis_size("seq")
    planes = lax.axis_size("dp")
    devices = sequence_number * planes
    group = lax.axis_index("seq")
    member = lax.axis_index("dp")
    per_device = QUERY_HEADS // sequence_number
    query_columns = per_device * HEAD_SIZE
    own_width = query_columns + 2 * HEAD_SIZE
    head_replicas = sequence_number // KEY_VALUE_HEADS
    capacity = (tokens * TOP * 9 + 8 * devices - 1) // (8 * devices)
    slots = sequence_number * capacity
    sequence_length = sequence_number * tokens
    extra = -(-2 * devices // 128) * 128

    shard = norm1_gain.shape[0]
    small_shard = query_gain.shape[0]
    small_width = 2 * shard + 2 * small_shard + shard * devices
    small_rows = -(-small_width // 2048) * 16
    packed = jnp.concatenate(
        [norm1_gain, norm2_gain, query_gain, key_gain, router.reshape(-1)]
    )
    packed = jnp.pad(packed, (0, small_rows * 128 - small_width)).reshape(small_rows, 128)
    packed = lax.all_gather(packed, ("seq", "dp"), axis=0, tiled=True)
    packed = packed.reshape(devices, small_rows * 128)
    cut = 0
    pieces = []
    for width in (shard, shard, small_shard, small_shard, shard * devices):
        pieces.append(packed[:, cut : cut + width])
        cut += width
    gain_one = pieces[0].reshape(-1).astype(jnp.float32)
    gain_two = pieces[1].reshape(-1).astype(jnp.float32)
    gain_query = pieces[2].reshape(-1).astype(jnp.float32)
    gain_key = pieces[3].reshape(-1).astype(jnp.float32)
    full_router = pieces[4].reshape(MODEL_WIDTH, devices)

    query_part = qkv_weight[:, : QUERY_HEADS * HEAD_SIZE].reshape(
        shard, sequence_number, query_columns
    )
    paired_portion = jnp.repeat(
        qkv_weight[:, QUERY_HEADS * HEAD_SIZE :].reshape(shard, 2, KEY_VALUE_HEADS, HEAD_SIZE),
        head_replicas,
        axis=2,
    )
    paired_portion = jnp.transpose(paired_portion, (0, 2, 1, 3)).reshape(
        shard, sequence_number, 2 * HEAD_SIZE
    )
    column_send = jnp.transpose(
        jnp.concatenate([query_part, paired_portion], axis=-1), (1, 0, 2)
    )
    own_part = lax.all_to_all(column_send, "seq", split_axis=0, concat_axis=0, tiled=True)
    own_cols = lax.all_gather(own_part, "dp", axis=1, tiled=True).reshape(MODEL_WIDTH, own_width)
    out_rows = lax.all_gather(out_weight, "dp", axis=0, tiled=True)

    full_routes = lax.all_gather(routes[0], "seq", axis=0, tiled=True)
    expert_ids = jnp.arange(devices, dtype=jnp.int32)
    route_mask = jnp.sum(
        (full_routes[:, :, None] == expert_ids[None, None, :]).astype(jnp.float32), axis=1
    )
    before = (
        jnp.arange(tokens)[:, None] > jnp.arange(tokens)[None, :]
    ).astype(jnp.bfloat16)
    places = jnp.einsum(
        "tu,sue->ste",
        before,
        route_mask.astype(jnp.bfloat16).reshape(sequence_number, tokens, devices),
        preferred_element_type=jnp.float32,
    ).astype(jnp.int32)
    places = places + (jnp.arange(sequence_number, dtype=jnp.int32) * capacity)[:, None, None]
    places = jnp.where(route_mask > 0, places.reshape(sequence_length, devices), -1)
    plane_places = lax.dynamic_slice_in_dim(places, group * planes, planes, 1)
    picker = (
        plane_places.T[:, None, :] == jnp.arange(slots, dtype=jnp.int32)[None, :, None]
    ).astype(jnp.bfloat16).reshape(planes * slots, sequence_length)

    def dispatch(rows):
        sent = jnp.dot(picker, rows, preferred_element_type=jnp.float32).astype(jnp.bfloat16)
        return lax.all_to_all(
            sent.reshape(planes, slots, rows.shape[-1]), "dp", split_axis=0, concat_axis=0, tiled=True
        ).reshape(planes * slots, rows.shape[-1])

    def combine(rows):
        width = rows.shape[-1]
        back = lax.all_to_all(
            rows.reshape(planes, slots, width), "dp", split_axis=0, concat_axis=0, tiled=True
        ).reshape(planes * slots, width)
        sums = inner_rows(picker, back).astype(jnp.bfloat16)
        return lax.psum_scatter(sums, "seq", scatter_dimension=0, tiled=True).astype(jnp.float32)

    mask_columns = jnp.pad(route_mask.astype(jnp.bfloat16), ((0, 0), (0, extra - devices)))
    cotangent_full = lax.all_gather(cotangent[0], "seq", axis=0, tiled=True)
    grad_arrived = dispatch(jnp.concatenate([cotangent_full, mask_columns], axis=1))

    hidden_full = lax.all_gather(hidden_in[0], "seq", axis=0, tiled=True)
    residual = hidden_in[0].astype(jnp.float32)
    normed_full = rms_norm(hidden_full.astype(jnp.float32), gain_one).astype(jnp.bfloat16)
    cosine, sine_table = rope_tables(jnp.arange(sequence_length).astype(jnp.float32), HEAD_SIZE)
    projected_rows = jnp.dot(normed_full, own_cols, preferred_element_type=jnp.float32)
    queries, key_head, value_head = prepare_heads(
        projected_rows, gain_query, gain_key, cosine, sine_table
    )
    query_heads = queries.astype(jnp.bfloat16)
    key_heads = key_head.astype(jnp.bfloat16)
    value_heads = value_head.astype(jnp.bfloat16)
    out_full, log_totals = attend_forward(query_heads, key_heads, value_heads)
    heads_low = out_full.astype(jnp.bfloat16).reshape(sequence_length, query_columns)
    branch_part = jnp.dot(heads_low, out_rows, preferred_element_type=jnp.float32)
    hidden1 = residual + lax.psum_scatter(
        branch_part.astype(jnp.bfloat16), "seq", scatter_dimension=0, tiled=True
    ).astype(jnp.float32)
    mixed_low = rms_norm(hidden1, gain_two).astype(jnp.bfloat16)
    mixed_full = lax.all_gather(mixed_low, "seq", axis=0, tiled=True)
    arrived = dispatch(mixed_full)

    weight_in = gate_up_weight[0]
    weight_back = down_weight[0]
    own_expert = group * planes + member
    row_mask = grad_arrived[:, MODEL_WIDTH : MODEL_WIDTH + devices].astype(jnp.float32)
    grad_rows = grad_arrived[:, :MODEL_WIDTH].astype(jnp.float32)
    row_gates = masked_softmax(
        jnp.dot(arrived, full_router, preferred_element_type=jnp.float32), row_mask
    )
    gate = jnp.sum(jnp.where(expert_ids[None, :] == own_expert, row_gates, 0.0), axis=1)[:, None]
    gate_up = jnp.dot(arrived, weight_in, preferred_element_type=jnp.float32)
    hidden = (jax.nn.silu(gate_up[:, :FF]) * gate_up[:, FF:]).astype(jnp.bfloat16)
    expert_out = (
        jnp.dot(hidden, weight_back, preferred_element_type=jnp.float32)
        .astype(jnp.bfloat16)
        .astype(jnp.float32)
    )
    grad_gate = jnp.sum(expert_out * grad_rows, axis=1, keepdims=True)
    combined_rows = (gate * expert_out).astype(jnp.bfloat16)
    back_rows = (gate * grad_rows).astype(jnp.bfloat16)
    grad_weight_back = inner_rows(hidden, back_rows)
    grad_hidden = outer_cols(back_rows, weight_back)
    _, pull_act = jax.vjp(
        lambda gate_in, up_in: jax.nn.silu(gate_in) * up_in, gate_up[:, :FF], gate_up[:, FF:]
    )
    grad_gate_in, grad_up_in = pull_act(grad_hidden)
    grad_gate_up = jnp.concatenate([grad_gate_in, grad_up_in], axis=1).astype(jnp.bfloat16)
    grad_weight_in = inner_rows(arrived, grad_gate_up)
    grad_back = outer_cols(grad_gate_up, weight_in).astype(jnp.bfloat16)
    high = grad_gate.astype(jnp.bfloat16)
    rest = (grad_gate - high.astype(jnp.float32)).astype(jnp.bfloat16)
    extra_ids = jnp.arange(extra, dtype=jnp.int32)[None, :]
    gate_columns = jnp.where(
        extra_ids == own_expert,
        high,
        jnp.where(extra_ids == own_expert + devices, rest, jnp.zeros((), jnp.bfloat16)),
    )
    grad_sent = combine(jnp.concatenate([grad_back, gate_columns], axis=1))
    output = (hidden1 + combine(combined_rows)).astype(jnp.bfloat16)

    grad_result = cotangent[0].astype(jnp.float32)
    own_mask = lax.dynamic_slice_in_dim(route_mask, group * tokens, tokens, 0)
    logits = jnp.dot(mixed_low, full_router, preferred_element_type=jnp.float32)
    gates = masked_softmax(logits, own_mask)
    grad_gates = (
        grad_sent[:, MODEL_WIDTH : MODEL_WIDTH + devices]
        + grad_sent[:, MODEL_WIDTH + devices : MODEL_WIDTH + 2 * devices]
    )
    grad_logits = (
        gates * (grad_gates - jnp.sum(gates * grad_gates, axis=-1, keepdims=True))
    ).astype(jnp.bfloat16)
    grad_mixed = grad_sent[:, :MODEL_WIDTH] + outer_cols(grad_logits, full_router)
    grad_router_w = inner_rows(mixed_low, grad_logits)
    _, pull_two = jax.vjp(rms_norm, hidden1, gain_two)
    grad_hidden_norm, grad_gain_two = pull_two(grad_mixed)
    grad_hidden1 = grad_result + grad_hidden_norm
    grad_branch = grad_hidden1.astype(jnp.bfloat16)
    branch_full = lax.all_gather(grad_branch, "seq", axis=0, tiled=True)
    grad_out_rows = inner_rows(heads_low, branch_full)
    shard_out = lax.psum_scatter(
        grad_out_rows.astype(jnp.bfloat16), "dp", scatter_dimension=0, tiled=True
    ).astype(jnp.float32)
    grad_heads = (
        outer_cols(branch_full, out_rows)
        .astype(jnp.bfloat16)
        .reshape(sequence_length, per_device, HEAD_SIZE)
    )
    grad_query, grad_keys, grad_values = attend_backward(
        query_heads, key_heads, value_heads, out_full, log_totals, grad_heads
    )
    _, pull_prep = jax.vjp(
        lambda proj_in, query_in, key_in: prepare_heads(
            proj_in, query_in, key_in, cosine, sine_table
        ),
        projected_rows,
        gain_query,
        gain_key,
    )
    grad_projected, grad_gain_query, grad_gain_key = pull_prep((grad_query, grad_keys, grad_values))
    grad_proj_low = grad_projected.astype(jnp.bfloat16)
    grad_normed = lax.psum_scatter(
        outer_cols(grad_proj_low, own_cols).astype(jnp.bfloat16),
        "seq",
        scatter_dimension=0,
        tiled=True,
    ).astype(jnp.float32)
    gradient_columns = inner_rows(normed_full, grad_proj_low).astype(jnp.bfloat16)
    gradient_columns = jnp.transpose(
        gradient_columns.reshape(sequence_number, planes, shard, own_width), (1, 0, 2, 3)
    ).reshape(MODEL_WIDTH, own_width)
    column_sums = lax.psum_scatter(gradient_columns, "dp", scatter_dimension=0, tiled=True)
    column_sums = lax.all_to_all(
        column_sums.reshape(sequence_number, shard, own_width),
        "seq",
        split_axis=0,
        concat_axis=0,
        tiled=True,
    ).astype(jnp.float32)
    shard_query = jnp.transpose(column_sums[:, :, :query_columns], (1, 0, 2)).reshape(
        shard, QUERY_HEADS * HEAD_SIZE
    )
    shard_paired = jnp.sum(
        column_sums[:, :, query_columns:].reshape(
            KEY_VALUE_HEADS, head_replicas, shard, 2, HEAD_SIZE
        ),
        axis=1,
    )
    shard_paired = jnp.transpose(shard_paired, (1, 2, 0, 3)).reshape(
        shard, 2 * KEY_VALUE_HEADS * HEAD_SIZE
    )
    shard_qkv = jnp.concatenate([shard_query, shard_paired], axis=1)
    _, pull_one = jax.vjp(rms_norm, residual, gain_one)
    grad_residual_norm, grad_gain_one = pull_one(grad_normed)
    grad_input = grad_hidden1 + grad_residual_norm

    small = jnp.concatenate(
        [
            grad_gain_one.reshape(devices, shard),
            grad_gain_two.reshape(devices, shard),
            grad_gain_query.reshape(devices, small_shard),
            grad_gain_key.reshape(devices, small_shard),
            grad_router_w.reshape(devices, shard * devices),
        ],
        axis=1,
    )
    small = jnp.pad(small, ((0, 0), (0, small_rows * 128 - small_width)))
    small = lax.psum_scatter(
        small.reshape(devices * small_rows, 128), ("seq", "dp"), scatter_dimension=0, tiled=True
    ).reshape(-1)
    cut = 0
    pieces = []
    for width in (shard, shard, small_shard, small_shard, shard * devices):
        pieces.append(small[cut : cut + width])
        cut += width
    return (
        output[None],
        grad_input[None],
        pieces[0],
        pieces[2],
        pieces[3],
        shard_qkv,
        shard_out,
        pieces[1],
        pieces[4].reshape(shard, devices),
        grad_weight_in[None],
        grad_weight_back[None],
    )


def solution(mesh):
    in_specs = (
        P("dp", "seq", None),
        P("dp", "seq", None),
        P(("seq", "dp")),
        P(("seq", "dp")),
        P(("seq", "dp")),
        P(("seq", "dp"), None),
        P(("seq", "dp"), None),
        P(("seq", "dp")),
        P(("seq", "dp"), None),
        P(("seq", "dp"), None, None),
        P(("seq", "dp"), None, None),
        P("dp", "seq", None),
    )
    out_specs = (
        P("dp", "seq", None),
        P("dp", "seq", None),
        P(("seq", "dp")),
        P(("seq", "dp")),
        P(("seq", "dp")),
        P(("seq", "dp"), None),
        P(("seq", "dp"), None),
        P(("seq", "dp")),
        P(("seq", "dp"), None),
        P(("seq", "dp"), None, None),
        P(("seq", "dp"), None, None),
    )
    return jax.shard_map(body, mesh=mesh, in_specs=in_specs, out_specs=out_specs, check_vma=False)
```

```python
import functools
import jax
import jax.numpy as jnp
from jax import lax
from jax.experimental import pallas as pl
from jax.experimental.pallas import tpu as pltpu
from jax.sharding import PartitionSpec as P


MODEL_WIDTH = 2048
QUERY_HEADS = 32
KEY_VALUE_HEADS = 4
HEAD_SIZE = 128
FF = 768
TOP = 8


EPSILON = 1e-06
ROPE_BASE = 1000000.0
FILLER = -1e30
QUERY_BLOCK = 512


MESH = pl.DeviceIdType.MESH
VMEM_BYTES = 62 * 1024 * 1024


def dot_nn(left, right):
    return jnp.dot(left, right, preferred_element_type=jnp.float32)


def dot_nt(left, right):
    return lax.dot_general(
        left, right, (((1,), (1,)), ((), ())), preferred_element_type=jnp.float32
    )


def dot_tn(left, right):
    return lax.dot_general(
        left, right, (((0,), (0,)), ((), ())), preferred_element_type=jnp.float32
    )


def greet(peers):
    barrier = pltpu.get_barrier_semaphore()
    for peer in peers:
        pl.semaphore_signal(barrier, inc=1, device_id=peer, device_id_type=MESH)
    pl.semaphore_wait(barrier, len(peers))


def remote(source, target, send_sem, recv_sem, device):
    return pltpu.make_async_remote_copy(
        src_ref=source,
        dst_ref=target,
        send_sem=send_sem,
        recv_sem=recv_sem,
        device_id=device,
        device_id_type=MESH,
    )


def line_gather_step(step, count, place, column, blocks, send_sems, recv_sems):
    right, left = place + 1, place - 1
    if step > 0:

        @pl.when(place - step >= 0)
        def _():
            block = blocks.at[place - step]
            remote(block, block, send_sems.at[0, step], recv_sems.at[0, step], (right, column)).wait_recv()

        @pl.when(place + step < count)
        def _():
            block = blocks.at[place + step]
            remote(block, block, send_sems.at[1, step], recv_sems.at[1, step], (left, column)).wait_recv()

    if step < count - 1:

        @pl.when((place - step >= 0) & (place + 1 < count))
        def _():
            block = blocks.at[place - step]
            remote(block, block, send_sems.at[0, step], recv_sems.at[0, step + 1], (right, column)).start()

        @pl.when((place + step < count) & (place - 1 >= 0))
        def _():
            block = blocks.at[place + step]
            remote(block, block, send_sems.at[1, step], recv_sems.at[1, step + 1], (left, column)).start()


def line_gather_end(count, place, column, blocks, send_sems, recv_sems):
    for step in range(count - 1):

        @pl.when((place - step >= 0) & (place + 1 < count))
        def _():
            block = blocks.at[place - step]
            remote(block, block, send_sems.at[0, step], recv_sems.at[0, step], (place + 1, column)).wait_send()

        @pl.when((place + step < count) & (place - 1 >= 0))
        def _():
            block = blocks.at[place + step]
            remote(block, block, send_sems.at[1, step], recv_sems.at[1, step], (place - 1, column)).wait_send()


def line_sum_step(step, count, place, column, own, sums, send_sems, recv_sems):
    turn = step - place
    last = count - 1 - turn

    @pl.when((turn >= 0) & (last > place))
    def _():
        block = sums.at[0, last]

        @pl.when(place > 0)
        def _():
            remote(block, block, send_sems.at[0, last], recv_sems.at[0, last], (place, column)).wait_recv()
            sums[0, last] = (
                sums[0, last].astype(jnp.float32) + own[last].astype(jnp.float32)
            ).astype(jnp.bfloat16)

        @pl.when(place == 0)
        def _():
            sums[0, last] = own[last]

        remote(block, block, send_sems.at[0, last], recv_sems.at[0, last], (place + 1, column)).start()

    first = step - (count - 1 - place)

    @pl.when((first >= 0) & (first < place))
    def _():
        block = sums.at[1, first]

        @pl.when(place < count - 1)
        def _():
            remote(block, block, send_sems.at[1, first], recv_sems.at[1, first], (place, column)).wait_recv()
            sums[1, first] = (
                sums[1, first].astype(jnp.float32) + own[first].astype(jnp.float32)
            ).astype(jnp.bfloat16)

        @pl.when(place == count - 1)
        def _():
            sums[1, first] = own[first]

        remote(block, block, send_sems.at[1, first], recv_sems.at[1, first], (place - 1, column)).start()


def line_sum_end(count, place, column, own, sums, send_sems, recv_sems, total):
    total[...] = own[place].astype(jnp.float32)

    @pl.when(place > 0)
    def _():
        block = sums.at[0, place]
        remote(block, block, send_sems.at[0, place], recv_sems.at[0, place], (place, column)).wait_recv()
        total[...] += sums[0, place].astype(jnp.float32)

    @pl.when(place < count - 1)
    def _():
        block = sums.at[1, place]
        remote(block, block, send_sems.at[1, place], recv_sems.at[1, place], (place, column)).wait_recv()
        total[...] += sums[1, place].astype(jnp.float32)

    for step in range(count - 1):
        last = count - 1 - step

        @pl.when(last > place)
        def _():
            block = sums.at[0, last]
            remote(block, block, send_sems.at[0, last], recv_sems.at[0, last], (place + 1, column)).wait_send()

        @pl.when(step < place)
        def _():
            block = sums.at[1, step]
            remote(block, block, send_sems.at[1, step], recv_sems.at[1, step], (place - 1, column)).wait_send()


def backward_kernel(
    count, planes, tokens, heads, shard,
    branch_ref, out_rows_hbm, own_cols_hbm, normed_hbm, heads_hbm, query_hbm, pair_hbm,
    proj_hbm, lse_ref, turn_cos_ref, turn_sin_ref, gain_ref,
    normed_total, out_total, columns_out, gain_total,
    out_rows, own_cols, normed, heads_low, queries, pair, proj, local_sems,
    branch_full, ag_send, ag_recv,
    grad_heads, grad_proj, grad_pair,
    grad_out, out_pair, out_far, out_sems,
    grad_cols, col_pair, col_far, col_sums, col_sems,
    normed_part, normed_sums, rs_send, rs_recv, z_sems,
):
    place = lax.axis_index("seq")
    member = lax.axis_index("dp")
    core = lax.rem(member, 2)
    chip = member // 2
    chips = planes // 2
    partner = member + 1 - 2 * core
    length = count * tokens
    query_columns = heads * HEAD_SIZE
    out_block = query_columns // planes
    scale = HEAD_SIZE ** (-0.5)

    loads = [
        pltpu.make_async_copy(source, target, local_sems.at[index])
        for index, (source, target) in enumerate(
            [
                (out_rows_hbm, out_rows),
                (query_hbm, queries),
                (pair_hbm, pair),
                (heads_hbm, heads_low),
                (proj_hbm, proj),
                (own_cols_hbm, own_cols),
                (normed_hbm, normed),
            ]
        )
    ]
    for load in loads:
        load.start()
    branch_full[place] = branch_ref[...]

    far_chips = [lax.rem(chip + k, chips) for k in range(1, chips)]
    far_places = [lax.rem(place + k, count) for k in range(1, count)]
    greet(
        [(place, partner)]
        + [(place, 2 * other + core) for other in far_chips]
        + [(other, member) for other in far_places]
    )

    line = (count, place, member, branch_full, ag_send, ag_recv)
    line_gather_step(0, *line)
    for load in loads:
        load.wait()

    def head_gradients(block):
        partial_heads = dot_nt(branch_full[block], out_rows[...]).astype(jnp.bfloat16)
        for head in range(heads):
            grad_heads[head, pl.ds(pl.multiple_of(block * tokens, tokens), tokens), :] = (
                partial_heads[:, head * HEAD_SIZE : (head + 1) * HEAD_SIZE]
            )

    head_gradients(place)
    for step in range(1, count):
        line_gather_step(step, *line)

        @pl.when(place - step >= 0)
        def _():
            head_gradients(place - step)

        @pl.when(place + step < count)
        def _():
            head_gradients(place + step)

    def out_copy(target, k):
        rows = grad_out.at[2 * k + 1 - core]
        return remote(rows, out_pair.at[k], out_sems.at[0, k], out_sems.at[1, k], (place, partner))

    def out_gradient(block):
        all_branch = branch_full[...].reshape(length, MODEL_WIDTH)
        columns = heads_low[block]
        grad_out[block] = dot_tn(columns, all_branch).astype(jnp.bfloat16)

    for k in range(chips):
        out_gradient(2 * k + 1 - core)
        out_copy(None, k).start()
    for k in range(chips):
        out_gradient(2 * k + core)

    def out_far_copy(k):
        other = lax.rem(chip + k, chips)
        return remote(
            out_pair.at[other], out_far.at[k - 1], out_sems.at[2, k], out_sems.at[3, k],
            (place, 2 * other + core),
        )

    for k in range(chips):
        out_copy(None, k).wait_recv()
        out_pair[k] = (
            out_pair[k].astype(jnp.float32) + grad_out[2 * k + core].astype(jnp.float32)
        ).astype(jnp.bfloat16)
    for k in range(1, chips):
        out_far_copy(k).start()

    grad_pair[...] = jnp.zeros_like(grad_pair)
    gain_total[...] = jnp.zeros_like(gain_total)
    block_rows = min(256, length)

    def unprepare(grad, raw, gain):
        turned = grad * turn_cos_ref[...] + pltpu.roll(grad, HEAD_SIZE // 2, 1) * turn_sin_ref[...]
        inverse = lax.rsqrt(jnp.mean(raw * raw, axis=-1, keepdims=True) + EPSILON)
        unit = raw * inverse
        gain_part = jnp.sum(turned * unit, axis=0, keepdims=True)
        turned = turned * gain
        middle = jnp.mean(turned * unit, axis=-1, keepdims=True)
        return inverse * (turned - unit * middle), gain_part

    def one_head(head, carry):
        lse = lse_ref[head]
        grads = []
        for block in range(length // block_rows):
            low, high = block * block_rows, (block + 1) * block_rows
            query = queries[head, low:high, :]
            grad = grad_heads[head, low:high, :]
            key = pair[0, :high, :]
            scores = dot_nt(key, query) * scale
            row_ids = lax.broadcasted_iota(jnp.int32, (high, block_rows), 0)
            col_ids = lax.broadcasted_iota(jnp.int32, (high, block_rows), 1) + low
            scores = jnp.where(row_ids <= col_ids, scores, FILLER)
            probs = jnp.exp(scores - lse[:, low:high])
            grad_probs = dot_nt(pair[1, :high, :], grad)
            delta = jnp.sum(probs * grad_probs, axis=0, keepdims=True)
            grad_scores = (probs * (grad_probs - delta)).astype(jnp.bfloat16)
            grad_pair[0, :high, :] += dot_nn(grad_scores, query) * scale
            grad_pair[1, :high, :] += dot_nn(probs.astype(jnp.bfloat16), grad)
            grads.append(dot_tn(grad_scores, key) * scale)
        grad_query = jnp.concatenate(grads, axis=0)
        grad_raw, gain_part = unprepare(grad_query, proj[head], gain_ref[0:1, :])
        gain_total[0:1, :] += gain_part
        grad_proj[head] = grad_raw.astype(jnp.bfloat16)
        return carry

    lax.fori_loop(0, heads, one_head, 0)
    grad_raw, gain_part = unprepare(grad_pair[0], proj[heads], gain_ref[1:2, :])
    gain_total[1:2, :] += gain_part
    grad_proj[heads] = grad_raw.astype(jnp.bfloat16)
    grad_proj[heads + 1] = grad_pair[1].astype(jnp.bfloat16)
    grad_rows = jnp.concatenate([grad_proj[head] for head in range(heads + 2)], axis=1)

    for block in range(count):
        normed_part[block] = dot_nt(
            grad_rows[block * tokens : (block + 1) * tokens, :], own_cols[...]
        ).astype(jnp.bfloat16)
    sums = (count, place, member, normed_part, normed_sums, rs_send, rs_recv)
    line_sum_step(0, *sums)

    for block in range(count):
        width = planes * shard
        part = dot_tn(normed[:, block * width : (block + 1) * width], grad_rows).astype(jnp.bfloat16)
        grad_cols[block] = part.reshape(planes, shard, part.shape[-1])

    def col_copy(k):
        rows = grad_cols.at[:, 2 * k + 1 - core]
        return remote(rows, col_pair.at[k], col_sems.at[0, k], col_sems.at[1, k], (place, partner))

    def col_far_copy(k):
        other = lax.rem(chip + k, chips)
        return remote(
            col_pair.at[other], col_far.at[k - 1], col_sems.at[2, k], col_sems.at[3, k],
            (place, 2 * other + core),
        )

    for k in range(chips):
        col_copy(k).start()
    for k in range(chips):
        col_copy(k).wait_recv()
        col_pair[k] = (
            col_pair[k].astype(jnp.float32) + grad_cols[:, 2 * k + core].astype(jnp.float32)
        ).astype(jnp.bfloat16)
    for k in range(1, chips):
        col_far_copy(k).start()

    if count > 2:
        line_sum_step(1, *sums)

    total = out_pair[chip].astype(jnp.float32)
    for k in range(1, chips):
        out_far_copy(k).wait_recv()
        total += out_far[k - 1].astype(jnp.float32)
    out_total[...] = total

    for step in range(2, count - 1):
        line_sum_step(step, *sums)

    columns = col_pair[chip].astype(jnp.float32)
    for k in range(1, chips):
        col_far_copy(k).wait_recv()
        columns += col_far[k - 1].astype(jnp.float32)
    col_sums[...] = columns.astype(jnp.bfloat16)

    def z_copy(k):
        other = lax.rem(place + k, count)
        return remote(
            col_sums.at[other], columns_out.at[place], z_sems.at[0, k], z_sems.at[1, k], (other, member)
        )

    for k in range(1, count):
        z_copy(k).start()
    columns_out[place] = col_sums[place]

    line_sum_end(*sums, normed_total)
    for k in range(1, count):
        z_copy(k).wait_recv()
    for k in range(1, count):
        z_copy(k).wait_send()
    for k in range(chips):
        out_copy(None, k).wait_send()
        col_copy(k).wait_send()
    for k in range(1, chips):
        out_far_copy(k).wait_send()
        col_far_copy(k).wait_send()
    line_gather_end(*line)


def attention_backward(
    count, planes, heads, shard, branch, out_rows, own_cols, normed, heads_low, queries, pair, proj,
    lse, turn_cos, turn_sin, gains,
):
    tokens = branch.shape[0]
    length = count * tokens
    width = (heads + 2) * HEAD_SIZE
    chips = planes // 2
    out_block = heads * HEAD_SIZE // planes
    low = jnp.bfloat16
    vmem = pl.BlockSpec(memory_space=pltpu.VMEM)
    anywhere = pl.BlockSpec(memory_space=pl.ANY)
    dma = pltpu.SemaphoreType.DMA
    return pl.pallas_call(
        functools.partial(backward_kernel, count, planes, tokens, heads, shard),
        out_shape=(
            jax.ShapeDtypeStruct((tokens, MODEL_WIDTH), jnp.float32),
            jax.ShapeDtypeStruct((out_block, MODEL_WIDTH), jnp.float32),
            jax.ShapeDtypeStruct((count, shard, width), low),
            jax.ShapeDtypeStruct((8, HEAD_SIZE), jnp.float32),
        ),
        in_specs=[vmem] + [anywhere] * 7 + [vmem] * 4,
        out_specs=(vmem,) * 4,
        scratch_shapes=[
            pltpu.VMEM(out_rows.shape, low),
            pltpu.VMEM(own_cols.shape, low),
            pltpu.VMEM(normed.shape, low),
            pltpu.VMEM(heads_low.shape, low),
            pltpu.VMEM(queries.shape, low),
            pltpu.VMEM(pair.shape, low),
            pltpu.VMEM(proj.shape, jnp.float32),
            dma((7,)),
            pltpu.VMEM((count, tokens, MODEL_WIDTH), low),
            dma((2, count)),
            dma((2, count)),
            pltpu.VMEM((heads, length, HEAD_SIZE), low),
            pltpu.VMEM((heads + 2, length, HEAD_SIZE), low),
            pltpu.VMEM((2, length, HEAD_SIZE), jnp.float32),
            pltpu.VMEM((planes, out_block, MODEL_WIDTH), low),
            pltpu.VMEM((chips, out_block, MODEL_WIDTH), low),
            pltpu.VMEM((chips - 1, out_block, MODEL_WIDTH), low),
            dma((4, chips)),
            pltpu.VMEM((count, planes, shard, width), low),
            pltpu.VMEM((chips, count, shard, width), low),
            pltpu.VMEM((chips - 1, count, shard, width), low),
            pltpu.VMEM((count, shard, width), low),
            dma((4, chips)),
            pltpu.VMEM((count, tokens, MODEL_WIDTH), low),
            pltpu.VMEM((2, count, tokens, MODEL_WIDTH), low),
            dma((2, count)),
            dma((2, count)),
            dma((2, count)),
        ],
        compiler_params=pltpu.CompilerParams(
            collective_id=3, has_side_effects=True, vmem_limit_bytes=VMEM_BYTES
        ),
        name="attention_backward",
    )(branch, out_rows, own_cols, normed, heads_low, queries, pair, proj, lse, turn_cos, turn_sin, gains)


def rms_norm(values, gain):
    return values * lax.rsqrt(jnp.mean(values * values, axis=-1, keepdims=True) + EPSILON) * gain


def rope_tables(positions, width):
    half_width = width // 2
    freqs = ROPE_BASE ** (-(jnp.arange(half_width, dtype=jnp.float32) * (2.0 / width)))
    angles = positions[:, None] * freqs[None, :]
    return (jnp.cos(angles), jnp.sin(angles))


def rotate(values, cosine, sine_table):
    half_width = values.shape[-1] // 2
    first = values[..., :half_width]
    second = values[..., half_width:]
    cosine = cosine[:, None, :]
    sine_table = sine_table[:, None, :]
    return jnp.concatenate(
        [first * cosine - second * sine_table, second * cosine + first * sine_table], axis=-1
    )


def prepare_heads(projected_rows, gain_query, gain_key, cosine, sine_table):
    row_count = projected_rows.shape[0]
    query_columns = projected_rows.shape[1] - 2 * HEAD_SIZE
    queries = projected_rows[:, :query_columns].reshape(
        row_count, query_columns // HEAD_SIZE, HEAD_SIZE
    )
    key_head = projected_rows[:, query_columns : query_columns + HEAD_SIZE].reshape(
        row_count, 1, HEAD_SIZE
    )
    value_head = projected_rows[:, query_columns + HEAD_SIZE :]
    queries = rotate(rms_norm(queries, gain_query), cosine, sine_table)
    key_head = rotate(rms_norm(key_head, gain_key), cosine, sine_table).reshape(
        row_count, HEAD_SIZE
    )
    return (queries, key_head, value_head)


def inner_rows(left, right):
    return lax.dot_general(
        left, right, (((0,), (0,)), ((), ())), preferred_element_type=jnp.float32
    )


def outer_cols(left, right):
    return lax.dot_general(
        left, right, (((1,), (1,)), ((), ())), preferred_element_type=jnp.float32
    )


def block_slice(array, index, block_rows):
    return lax.dynamic_slice_in_dim(array, index * block_rows, block_rows, 0)


def block_scores(query_block, key_block, i, j, block_rows):
    scores = jnp.einsum(
        "qhd,kd->hqk", query_block, key_block, preferred_element_type=jnp.float32
    ) * HEAD_SIZE ** (-0.5)
    row_ids = i * block_rows + jnp.arange(block_rows)
    col_ids = j * block_rows + jnp.arange(block_rows)
    return jnp.where((row_ids[:, None] >= col_ids[None, :])[None], scores, FILLER)


def attend_forward(queries, keys_in, values_in):
    sequence_length, head_count = (queries.shape[0], queries.shape[1])
    block_rows = min(QUERY_BLOCK, sequence_length)
    block_count = sequence_length // block_rows

    def one_block(i):
        query_block = block_slice(queries, i, block_rows)

        def max_step(j, carry):
            row_top, row_total = carry
            scores = block_scores(
                query_block, block_slice(keys_in, j, block_rows), i, j, block_rows
            )
            new_top = jnp.maximum(row_top, jnp.max(scores, axis=-1))
            row_total = row_total * jnp.exp(row_top - new_top) + jnp.sum(
                jnp.exp(scores - new_top[..., None]), axis=-1
            )
            return (new_top, row_total)

        start = (
            jnp.full((head_count, block_rows), FILLER, jnp.float32),
            jnp.zeros((head_count, block_rows), jnp.float32),
        )
        row_top, row_total = lax.fori_loop(0, i + 1, max_step, start)
        log_totals = row_top + jnp.log(row_total)

        def out_step(j, accum_out):
            scores = block_scores(
                query_block, block_slice(keys_in, j, block_rows), i, j, block_rows
            )
            probabilities = jnp.exp(scores - log_totals[..., None]).astype(jnp.bfloat16)
            return accum_out + jnp.einsum(
                "hqk,kd->qhd",
                probabilities,
                block_slice(values_in, j, block_rows),
                preferred_element_type=jnp.float32,
            )

        accum_out = lax.fori_loop(
            0, i + 1, out_step, jnp.zeros((block_rows, head_count, HEAD_SIZE), jnp.float32)
        )
        return (accum_out, log_totals)

    outputs, log_totals = lax.map(one_block, jnp.arange(block_count))
    return (outputs.reshape(sequence_length, head_count, HEAD_SIZE), log_totals)


def masked_softmax(logits, mask):
    shifted = jnp.where(mask > 0, logits, FILLER)
    top = jnp.max(shifted, axis=-1, keepdims=True)
    powers = jnp.where(mask > 0, jnp.exp(shifted - top), 0.0)
    total = jnp.sum(powers, axis=-1, keepdims=True)
    return powers / jnp.where(total > 0, total, 1.0)


def body(
    hidden_in,
    routes,
    norm1_gain,
    query_gain,
    key_gain,
    qkv_weight,
    out_weight,
    norm2_gain,
    router,
    gate_up_weight,
    down_weight,
    cotangent,
):
    tokens = hidden_in.shape[1]
    sequence_number = lax.axis_size("seq")
    planes = lax.axis_size("dp")
    devices = sequence_number * planes
    group = lax.axis_index("seq")
    member = lax.axis_index("dp")
    per_device = QUERY_HEADS // sequence_number
    query_columns = per_device * HEAD_SIZE
    own_width = query_columns + 2 * HEAD_SIZE
    head_replicas = sequence_number // KEY_VALUE_HEADS
    capacity = (tokens * TOP * 9 + 8 * devices - 1) // (8 * devices)
    slots = sequence_number * capacity
    sequence_length = sequence_number * tokens
    extra = -(-2 * devices // 128) * 128

    shard = norm1_gain.shape[0]
    small_shard = query_gain.shape[0]
    small_width = 2 * shard + 2 * small_shard + shard * devices
    small_rows = -(-small_width // 2048) * 16
    packed = jnp.concatenate(
        [norm1_gain, norm2_gain, query_gain, key_gain, router.reshape(-1)]
    )
    packed = jnp.pad(packed, (0, small_rows * 128 - small_width)).reshape(small_rows, 128)
    packed = lax.all_gather(packed, ("seq", "dp"), axis=0, tiled=True)
    packed = packed.reshape(devices, small_rows * 128)
    cut = 0
    pieces = []
    for width in (shard, shard, small_shard, small_shard, shard * devices):
        pieces.append(packed[:, cut : cut + width])
        cut += width
    gain_one = pieces[0].reshape(-1).astype(jnp.float32)
    gain_two = pieces[1].reshape(-1).astype(jnp.float32)
    gain_query = pieces[2].reshape(-1).astype(jnp.float32)
    gain_key = pieces[3].reshape(-1).astype(jnp.float32)
    full_router = pieces[4].reshape(MODEL_WIDTH, devices)

    query_part = qkv_weight[:, : QUERY_HEADS * HEAD_SIZE].reshape(
        shard, sequence_number, query_columns
    )
    paired_portion = jnp.repeat(
        qkv_weight[:, QUERY_HEADS * HEAD_SIZE :].reshape(shard, 2, KEY_VALUE_HEADS, HEAD_SIZE),
        head_replicas,
        axis=2,
    )
    paired_portion = jnp.transpose(paired_portion, (0, 2, 1, 3)).reshape(
        shard, sequence_number, 2 * HEAD_SIZE
    )
    column_send = jnp.transpose(
        jnp.concatenate([query_part, paired_portion], axis=-1), (1, 0, 2)
    )
    own_part = lax.all_to_all(column_send, "seq", split_axis=0, concat_axis=0, tiled=True)
    own_cols = lax.all_gather(own_part, "dp", axis=1, tiled=True).reshape(MODEL_WIDTH, own_width)
    out_rows = lax.all_gather(out_weight, "dp", axis=0, tiled=True)

    full_routes = lax.all_gather(routes[0], "seq", axis=0, tiled=True)
    expert_ids = jnp.arange(devices, dtype=jnp.int32)
    route_mask = jnp.sum(
        (full_routes[:, :, None] == expert_ids[None, None, :]).astype(jnp.float32), axis=1
    )
    before = (
        jnp.arange(tokens)[:, None] > jnp.arange(tokens)[None, :]
    ).astype(jnp.bfloat16)
    places = jnp.einsum(
        "tu,sue->ste",
        before,
        route_mask.astype(jnp.bfloat16).reshape(sequence_number, tokens, devices),
        preferred_element_type=jnp.float32,
    ).astype(jnp.int32)
    places = places + (jnp.arange(sequence_number, dtype=jnp.int32) * capacity)[:, None, None]
    places = jnp.where(route_mask > 0, places.reshape(sequence_length, devices), -1)
    plane_places = lax.dynamic_slice_in_dim(places, group * planes, planes, 1)
    picker = (
        plane_places.T[:, None, :] == jnp.arange(slots, dtype=jnp.int32)[None, :, None]
    ).astype(jnp.bfloat16).reshape(planes * slots, sequence_length)

    def dispatch(rows):
        sent = jnp.dot(picker, rows, preferred_element_type=jnp.float32).astype(jnp.bfloat16)
        return lax.all_to_all(
            sent.reshape(planes, slots, rows.shape[-1]), "dp", split_axis=0, concat_axis=0, tiled=True
        ).reshape(planes * slots, rows.shape[-1])

    def combine(rows):
        width = rows.shape[-1]
        back = lax.all_to_all(
            rows.reshape(planes, slots, width), "dp", split_axis=0, concat_axis=0, tiled=True
        ).reshape(planes * slots, width)
        sums = inner_rows(picker, back).astype(jnp.bfloat16)
        return lax.psum_scatter(sums, "seq", scatter_dimension=0, tiled=True).astype(jnp.float32)

    mask_columns = jnp.pad(route_mask.astype(jnp.bfloat16), ((0, 0), (0, extra - devices)))
    cotangent_full = lax.all_gather(cotangent[0], "seq", axis=0, tiled=True)
    grad_arrived = dispatch(jnp.concatenate([cotangent_full, mask_columns], axis=1))

    hidden_full = lax.all_gather(hidden_in[0], "seq", axis=0, tiled=True)
    residual = hidden_in[0].astype(jnp.float32)
    normed_full = rms_norm(hidden_full.astype(jnp.float32), gain_one).astype(jnp.bfloat16)
    cosine, sine_table = rope_tables(jnp.arange(sequence_length).astype(jnp.float32), HEAD_SIZE)
    projected_rows = jnp.dot(normed_full, own_cols, preferred_element_type=jnp.float32)
    queries, key_head, value_head = prepare_heads(
        projected_rows, gain_query, gain_key, cosine, sine_table
    )
    query_heads = queries.astype(jnp.bfloat16)
    key_heads = key_head.astype(jnp.bfloat16)
    value_heads = value_head.astype(jnp.bfloat16)
    out_full, log_totals = attend_forward(query_heads, key_heads, value_heads)
    heads_low = out_full.astype(jnp.bfloat16).reshape(sequence_length, query_columns)
    branch_part = jnp.dot(heads_low, out_rows, preferred_element_type=jnp.float32)
    hidden1 = residual + lax.psum_scatter(
        branch_part.astype(jnp.bfloat16), "seq", scatter_dimension=0, tiled=True
    ).astype(jnp.float32)
    mixed_low = rms_norm(hidden1, gain_two).astype(jnp.bfloat16)
    mixed_full = lax.all_gather(mixed_low, "seq", axis=0, tiled=True)
    arrived = dispatch(mixed_full)

    weight_in = gate_up_weight[0]
    weight_back = down_weight[0]
    own_expert = group * planes + member
    row_mask = grad_arrived[:, MODEL_WIDTH : MODEL_WIDTH + devices].astype(jnp.float32)
    grad_rows = grad_arrived[:, :MODEL_WIDTH].astype(jnp.float32)
    row_gates = masked_softmax(
        jnp.dot(arrived, full_router, preferred_element_type=jnp.float32), row_mask
    )
    gate = jnp.sum(jnp.where(expert_ids[None, :] == own_expert, row_gates, 0.0), axis=1)[:, None]
    gate_up = jnp.dot(arrived, weight_in, preferred_element_type=jnp.float32)
    hidden = (jax.nn.silu(gate_up[:, :FF]) * gate_up[:, FF:]).astype(jnp.bfloat16)
    expert_out = (
        jnp.dot(hidden, weight_back, preferred_element_type=jnp.float32)
        .astype(jnp.bfloat16)
        .astype(jnp.float32)
    )
    grad_gate = jnp.sum(expert_out * grad_rows, axis=1, keepdims=True)
    combined_rows = (gate * expert_out).astype(jnp.bfloat16)
    back_rows = (gate * grad_rows).astype(jnp.bfloat16)
    grad_weight_back = inner_rows(hidden, back_rows)
    grad_hidden = outer_cols(back_rows, weight_back)
    _, pull_act = jax.vjp(
        lambda gate_in, up_in: jax.nn.silu(gate_in) * up_in, gate_up[:, :FF], gate_up[:, FF:]
    )
    grad_gate_in, grad_up_in = pull_act(grad_hidden)
    grad_gate_up = jnp.concatenate([grad_gate_in, grad_up_in], axis=1).astype(jnp.bfloat16)
    grad_weight_in = inner_rows(arrived, grad_gate_up)
    grad_back = outer_cols(grad_gate_up, weight_in).astype(jnp.bfloat16)
    high = grad_gate.astype(jnp.bfloat16)
    rest = (grad_gate - high.astype(jnp.float32)).astype(jnp.bfloat16)
    extra_ids = jnp.arange(extra, dtype=jnp.int32)[None, :]
    gate_columns = jnp.where(
        extra_ids == own_expert,
        high,
        jnp.where(extra_ids == own_expert + devices, rest, jnp.zeros((), jnp.bfloat16)),
    )
    grad_sent = combine(jnp.concatenate([grad_back, gate_columns], axis=1))
    output = (hidden1 + combine(combined_rows)).astype(jnp.bfloat16)

    grad_result = cotangent[0].astype(jnp.float32)
    own_mask = lax.dynamic_slice_in_dim(route_mask, group * tokens, tokens, 0)
    logits = jnp.dot(mixed_low, full_router, preferred_element_type=jnp.float32)
    gates = masked_softmax(logits, own_mask)
    grad_gates = (
        grad_sent[:, MODEL_WIDTH : MODEL_WIDTH + devices]
        + grad_sent[:, MODEL_WIDTH + devices : MODEL_WIDTH + 2 * devices]
    )
    grad_logits = (
        gates * (grad_gates - jnp.sum(gates * grad_gates, axis=-1, keepdims=True))
    ).astype(jnp.bfloat16)
    grad_mixed = grad_sent[:, :MODEL_WIDTH] + outer_cols(grad_logits, full_router)
    grad_router_w = inner_rows(mixed_low, grad_logits)
    _, pull_two = jax.vjp(rms_norm, hidden1, gain_two)
    grad_hidden_norm, grad_gain_two = pull_two(grad_mixed)
    grad_hidden1 = grad_result + grad_hidden_norm
    grad_branch = grad_hidden1.astype(jnp.bfloat16)
    normed_total, shard_out, column_sums, gain_totals = attention_backward(
        sequence_number,
        planes,
        per_device,
        shard,
        grad_branch,
        out_rows,
        own_cols,
        normed_full,
        jnp.transpose(
            heads_low.reshape(sequence_length, planes, query_columns // planes), (1, 0, 2)
        ),
        jnp.transpose(query_heads, (1, 0, 2)),
        jnp.stack([key_heads, value_heads]),
        jnp.transpose(
            projected_rows.reshape(sequence_length, per_device + 2, HEAD_SIZE), (1, 0, 2)
        ),
        log_totals.reshape(-1, per_device, sequence_length // log_totals.shape[0])
        .transpose(1, 0, 2)
        .reshape(per_device, 1, sequence_length),
        jnp.concatenate([cosine, cosine], axis=1),
        jnp.concatenate([sine_table, -sine_table], axis=1),
        jnp.pad(jnp.stack([gain_query, gain_key]), ((0, 6), (0, 0))),
    )
    column_sums = column_sums.astype(jnp.float32)
    shard_query = jnp.transpose(column_sums[:, :, :query_columns], (1, 0, 2)).reshape(
        shard, QUERY_HEADS * HEAD_SIZE
    )
    shard_paired = jnp.sum(
        column_sums[:, :, query_columns:].reshape(
            KEY_VALUE_HEADS, head_replicas, shard, 2, HEAD_SIZE
        ),
        axis=1,
    )
    shard_paired = jnp.transpose(shard_paired, (1, 2, 0, 3)).reshape(
        shard, 2 * KEY_VALUE_HEADS * HEAD_SIZE
    )
    shard_qkv = jnp.concatenate([shard_query, shard_paired], axis=1)
    _, pull_one = jax.vjp(rms_norm, residual, gain_one)
    grad_residual_norm, grad_gain_one = pull_one(normed_total)
    grad_input = grad_hidden1 + grad_residual_norm

    small = jnp.concatenate(
        [
            grad_gain_one.reshape(devices, shard),
            grad_gain_two.reshape(devices, shard),
            gain_totals[0].reshape(devices, small_shard),
            gain_totals[1].reshape(devices, small_shard),
            grad_router_w.reshape(devices, shard * devices),
        ],
        axis=1,
    )
    small = jnp.pad(small, ((0, 0), (0, small_rows * 128 - small_width)))
    small = lax.psum_scatter(
        small.reshape(devices * small_rows, 128), ("seq", "dp"), scatter_dimension=0, tiled=True
    ).reshape(-1)
    cut = 0
    pieces = []
    for width in (shard, shard, small_shard, small_shard, shard * devices):
        pieces.append(small[cut : cut + width])
        cut += width
    return (
        output[None],
        grad_input[None],
        pieces[0],
        pieces[2],
        pieces[3],
        shard_qkv,
        shard_out,
        pieces[1],
        pieces[4].reshape(shard, devices),
        grad_weight_in[None],
        grad_weight_back[None],
    )


def solution(mesh):
    in_specs = (
        P("dp", "seq", None),
        P("dp", "seq", None),
        P(("seq", "dp")),
        P(("seq", "dp")),
        P(("seq", "dp")),
        P(("seq", "dp"), None),
        P(("seq", "dp"), None),
        P(("seq", "dp")),
        P(("seq", "dp"), None),
        P(("seq", "dp"), None, None),
        P(("seq", "dp"), None, None),
        P("dp", "seq", None),
    )
    out_specs = (
        P("dp", "seq", None),
        P("dp", "seq", None),
        P(("seq", "dp")),
        P(("seq", "dp")),
        P(("seq", "dp")),
        P(("seq", "dp"), None),
        P(("seq", "dp"), None),
        P(("seq", "dp")),
        P(("seq", "dp"), None),
        P(("seq", "dp"), None, None),
        P(("seq", "dp"), None, None),
    )
    return jax.shard_map(body, mesh=mesh, in_specs=in_specs, out_specs=out_specs, check_vma=False)
```

```python
import functools
import jax
import jax.numpy as jnp
from jax import lax
from jax.experimental import pallas as pl
from jax.experimental.pallas import tpu as pltpu
from jax.sharding import PartitionSpec as P


MODEL_WIDTH = 2048
QUERY_HEADS = 32
KEY_VALUE_HEADS = 4
HEAD_SIZE = 128
FF = 768
TOP = 8


EPSILON = 1e-06
ROPE_BASE = 1000000.0
FILLER = -1e30
QUERY_BLOCK = 512


MESH = pl.DeviceIdType.MESH
VMEM_BYTES = 63 * 1024 * 1024


def dot_nn(left, right):
    return jnp.dot(left, right, preferred_element_type=jnp.float32)


def dot_nt(left, right):
    return lax.dot_general(
        left, right, (((1,), (1,)), ((), ())), preferred_element_type=jnp.float32
    )


def dot_tn(left, right):
    return lax.dot_general(
        left, right, (((0,), (0,)), ((), ())), preferred_element_type=jnp.float32
    )


def greet(peers):
    barrier = pltpu.get_barrier_semaphore()
    for peer in peers:
        pl.semaphore_signal(barrier, inc=1, device_id=peer, device_id_type=MESH)
    pl.semaphore_wait(barrier, len(peers))


def remote(source, target, send_sem, recv_sem, device):
    return pltpu.make_async_remote_copy(
        src_ref=source,
        dst_ref=target,
        send_sem=send_sem,
        recv_sem=recv_sem,
        device_id=device,
        device_id_type=MESH,
    )


def line_gather_step(step, count, place, column, blocks, send_sems, recv_sems):
    right, left = place + 1, place - 1
    if step > 0:

        @pl.when(place - step >= 0)
        def _():
            block = blocks.at[place - step]
            remote(block, block, send_sems.at[0, step], recv_sems.at[0, step], (right, column)).wait_recv()

        @pl.when(place + step < count)
        def _():
            block = blocks.at[place + step]
            remote(block, block, send_sems.at[1, step], recv_sems.at[1, step], (left, column)).wait_recv()

    if step < count - 1:

        @pl.when((place - step >= 0) & (place + 1 < count))
        def _():
            block = blocks.at[place - step]
            remote(block, block, send_sems.at[0, step], recv_sems.at[0, step + 1], (right, column)).start()

        @pl.when((place + step < count) & (place - 1 >= 0))
        def _():
            block = blocks.at[place + step]
            remote(block, block, send_sems.at[1, step], recv_sems.at[1, step + 1], (left, column)).start()


def line_gather_end(count, place, column, blocks, send_sems, recv_sems):
    for step in range(count - 1):

        @pl.when((place - step >= 0) & (place + 1 < count))
        def _():
            block = blocks.at[place - step]
            remote(block, block, send_sems.at[0, step], recv_sems.at[0, step], (place + 1, column)).wait_send()

        @pl.when((place + step < count) & (place - 1 >= 0))
        def _():
            block = blocks.at[place + step]
            remote(block, block, send_sems.at[1, step], recv_sems.at[1, step], (place - 1, column)).wait_send()


def line_sum_step(step, count, place, column, own, sums, send_sems, recv_sems):
    turn = step - place
    last = count - 1 - turn

    @pl.when((turn >= 0) & (last > place))
    def _():
        block = sums.at[last]

        @pl.when(place > 0)
        def _():
            remote(block, block, send_sems.at[0, last], recv_sems.at[0, last], (place, column)).wait_recv()
            sums[last] = (
                sums[last].astype(jnp.float32) + own[last].astype(jnp.float32)
            ).astype(jnp.bfloat16)

        @pl.when(place == 0)
        def _():
            sums[last] = own[last]

        remote(block, block, send_sems.at[0, last], recv_sems.at[0, last], (place + 1, column)).start()

    first = step - (count - 1 - place)

    @pl.when((first >= 0) & (first < place))
    def _():
        block = sums.at[first]

        @pl.when(place < count - 1)
        def _():
            remote(block, block, send_sems.at[1, first], recv_sems.at[1, first], (place, column)).wait_recv()
            sums[first] = (
                sums[first].astype(jnp.float32) + own[first].astype(jnp.float32)
            ).astype(jnp.bfloat16)

        @pl.when(place == count - 1)
        def _():
            sums[first] = own[first]

        target = sums.at[jnp.where(first == place - 1, count, first)]
        remote(block, target, send_sems.at[1, first], recv_sems.at[1, first], (place - 1, column)).start()


def line_sum_end(count, place, column, own, sums, send_sems, recv_sems, total):
    total[...] = own[place].astype(jnp.float32)

    @pl.when(place > 0)
    def _():
        block = sums.at[place]
        remote(block, block, send_sems.at[0, place], recv_sems.at[0, place], (place, column)).wait_recv()
        total[...] += sums[place].astype(jnp.float32)

    @pl.when(place < count - 1)
    def _():
        block = sums.at[count]
        remote(block, block, send_sems.at[1, place], recv_sems.at[1, place], (place, column)).wait_recv()
        total[...] += sums[count].astype(jnp.float32)

    for step in range(count - 1):
        last = count - 1 - step

        @pl.when(last > place)
        def _():
            block = sums.at[last]
            remote(block, block, send_sems.at[0, last], recv_sems.at[0, last], (place + 1, column)).wait_send()

        @pl.when(step < place)
        def _():
            block = sums.at[step]
            remote(block, block, send_sems.at[1, step], recv_sems.at[1, step], (place - 1, column)).wait_send()


def backward_kernel(
    count, planes, tokens, heads, shard,
    branch_ref, out_rows_hbm, own_cols_hbm, normed_hbm, heads_hbm, query_hbm, pair_hbm,
    proj_hbm, lse_ref, turn_cos_ref, turn_sin_ref, gain_ref,
    normed_total, out_total, columns_out, gain_total,
    out_rows, own_cols, normed, heads_low, queries, pair, proj, local_sems,
    branch_full, ag_send, ag_recv,
    grad_heads, grad_proj, grad_pair,
    grad_out, out_pair, out_far, out_sems,
    grad_cols, col_pair, col_far, col_sums, col_sems,
    normed_part, normed_sums, rs_send, rs_recv, z_sems,
):
    place = lax.axis_index("seq")
    member = lax.axis_index("dp")
    core = lax.rem(member, 2)
    chip = member // 2
    chips = planes // 2
    partner = member + 1 - 2 * core
    length = count * tokens
    query_columns = heads * HEAD_SIZE
    out_block = query_columns // planes
    scale = HEAD_SIZE ** (-0.5)

    loads = [
        pltpu.make_async_copy(source, target, local_sems.at[index])
        for index, (source, target) in enumerate(
            [
                (out_rows_hbm, out_rows),
                (query_hbm, queries),
                (pair_hbm, pair),
                (heads_hbm, heads_low),
                (proj_hbm, proj),
                (own_cols_hbm, own_cols),
                (normed_hbm, normed),
            ]
        )
    ]
    for load in loads:
        load.start()
    branch_full[place] = branch_ref[...]

    far_chips = [lax.rem(chip + k, chips) for k in range(1, chips)]
    far_places = [lax.rem(place + k, count) for k in range(1, count)]
    greet(
        [(place, partner)]
        + [(place, 2 * other + core) for other in far_chips]
        + [(other, member) for other in far_places]
    )

    line = (count, place, member, branch_full, ag_send, ag_recv)
    line_gather_step(0, *line)
    for load in loads:
        load.wait()

    def head_gradients(block):
        partial_heads = dot_nt(branch_full[block], out_rows[...]).astype(jnp.bfloat16)
        for head in range(heads):
            grad_heads[head, pl.ds(pl.multiple_of(block * tokens, tokens), tokens), :] = (
                partial_heads[:, head * HEAD_SIZE : (head + 1) * HEAD_SIZE]
            )

    head_gradients(place)
    for step in range(1, count):
        line_gather_step(step, *line)

        @pl.when(place - step >= 0)
        def _():
            head_gradients(place - step)

        @pl.when(place + step < count)
        def _():
            head_gradients(place + step)

    def out_copy(target, k):
        rows = grad_out.at[2 * k + 1 - core]
        return remote(rows, out_pair.at[k], out_sems.at[0, k], out_sems.at[1, k], (place, partner))

    def out_gradient(block):
        all_branch = branch_full[...].reshape(length, MODEL_WIDTH)
        columns = heads_low[block]
        grad_out[block] = dot_tn(columns, all_branch).astype(jnp.bfloat16)

    for k in range(chips):
        out_gradient(2 * k + 1 - core)
        out_copy(None, k).start()
    for k in range(chips):
        out_gradient(2 * k + core)

    def out_far_copy(k):
        other = lax.rem(chip + k, chips)
        return remote(
            out_pair.at[other], out_far.at[k - 1], out_sems.at[2, k], out_sems.at[3, k],
            (place, 2 * other + core),
        )

    for k in range(chips):
        out_copy(None, k).wait_recv()
        out_pair[k] = (
            out_pair[k].astype(jnp.float32) + grad_out[2 * k + core].astype(jnp.float32)
        ).astype(jnp.bfloat16)
    for k in range(1, chips):
        out_far_copy(k).start()

    grad_pair[...] = jnp.zeros_like(grad_pair)
    gain_total[...] = jnp.zeros_like(gain_total)
    block_rows = min(256, length)

    def unprepare(grad, raw, gain):
        turned = grad * turn_cos_ref[...] + pltpu.roll(grad, HEAD_SIZE // 2, 1) * turn_sin_ref[...]
        inverse = lax.rsqrt(jnp.mean(raw * raw, axis=-1, keepdims=True) + EPSILON)
        unit = raw * inverse
        gain_part = jnp.sum(turned * unit, axis=0, keepdims=True)
        turned = turned * gain
        middle = jnp.mean(turned * unit, axis=-1, keepdims=True)
        return inverse * (turned - unit * middle), gain_part

    def one_head(head, carry):
        lse = lse_ref[head]
        grads = []
        for block in range(length // block_rows):
            low, high = block * block_rows, (block + 1) * block_rows
            query = queries[head, low:high, :]
            grad = grad_heads[head, low:high, :]
            key = pair[0, :high, :]
            scores = dot_nt(key, query) * scale
            row_ids = lax.broadcasted_iota(jnp.int32, (high, block_rows), 0)
            col_ids = lax.broadcasted_iota(jnp.int32, (high, block_rows), 1) + low
            scores = jnp.where(row_ids <= col_ids, scores, FILLER)
            probs = jnp.exp(scores - lse[:, low:high])
            grad_probs = dot_nt(pair[1, :high, :], grad)
            delta = jnp.sum(probs * grad_probs, axis=0, keepdims=True)
            grad_scores = (probs * (grad_probs - delta)).astype(jnp.bfloat16)
            grad_pair[0, :high, :] += dot_nn(grad_scores, query) * scale
            grad_pair[1, :high, :] += dot_nn(probs.astype(jnp.bfloat16), grad)
            grads.append(dot_tn(grad_scores, key) * scale)
        grad_query = jnp.concatenate(grads, axis=0)
        grad_raw, gain_part = unprepare(grad_query, proj[head], gain_ref[0:1, :])
        gain_total[0:1, :] += gain_part
        grad_proj[head] = grad_raw.astype(jnp.bfloat16)
        return carry

    lax.fori_loop(0, heads, one_head, 0)
    grad_raw, gain_part = unprepare(grad_pair[0], proj[heads], gain_ref[1:2, :])
    gain_total[1:2, :] += gain_part
    grad_proj[heads] = grad_raw.astype(jnp.bfloat16)
    grad_proj[heads + 1] = grad_pair[1].astype(jnp.bfloat16)
    grad_rows = jnp.concatenate([grad_proj[head] for head in range(heads + 2)], axis=1)

    for block in range(count):
        normed_part[block] = dot_nt(
            grad_rows[block * tokens : (block + 1) * tokens, :], own_cols[...]
        ).astype(jnp.bfloat16)
    sums = (count, place, member, normed_part, normed_sums, rs_send, rs_recv)
    line_sum_step(0, *sums)

    for block in range(count):
        width = planes * shard
        part = dot_tn(normed[:, block * width : (block + 1) * width], grad_rows).astype(jnp.bfloat16)
        grad_cols[block] = part.reshape(planes, shard, part.shape[-1])

    def col_copy(k):
        rows = grad_cols.at[:, 2 * k + 1 - core]
        return remote(rows, col_pair.at[k], col_sems.at[0, k], col_sems.at[1, k], (place, partner))

    def col_far_copy(k):
        other = lax.rem(chip + k, chips)
        return remote(
            col_pair.at[other], col_far.at[k - 1], col_sems.at[2, k], col_sems.at[3, k],
            (place, 2 * other + core),
        )

    for k in range(chips):
        col_copy(k).start()
    for k in range(chips):
        col_copy(k).wait_recv()
        col_pair[k] = (
            col_pair[k].astype(jnp.float32) + grad_cols[:, 2 * k + core].astype(jnp.float32)
        ).astype(jnp.bfloat16)
    for k in range(1, chips):
        col_far_copy(k).start()

    if count > 2:
        line_sum_step(1, *sums)

    total = out_pair[chip].astype(jnp.float32)
    for k in range(1, chips):
        out_far_copy(k).wait_recv()
        total += out_far[k - 1].astype(jnp.float32)
    out_total[...] = total

    for step in range(2, count - 1):
        line_sum_step(step, *sums)

    columns = col_pair[chip].astype(jnp.float32)
    for k in range(1, chips):
        col_far_copy(k).wait_recv()
        columns += col_far[k - 1].astype(jnp.float32)
    col_sums[...] = columns.astype(jnp.bfloat16)

    def z_copy(k):
        other = lax.rem(place + k, count)
        return remote(
            col_sums.at[other], columns_out.at[place], z_sems.at[0, k], z_sems.at[1, k], (other, member)
        )

    for k in range(1, count):
        z_copy(k).start()
    columns_out[place] = col_sums[place]

    line_sum_end(*sums, normed_total)
    for k in range(1, count):
        z_copy(k).wait_recv()
    for k in range(1, count):
        z_copy(k).wait_send()
    for k in range(chips):
        out_copy(None, k).wait_send()
        col_copy(k).wait_send()
    for k in range(1, chips):
        out_far_copy(k).wait_send()
        col_far_copy(k).wait_send()
    line_gather_end(*line)


def attention_backward(
    count, planes, heads, shard, branch, out_rows, own_cols, normed, heads_low, queries, pair, proj,
    lse, turn_cos, turn_sin, gains,
):
    tokens = branch.shape[0]
    length = count * tokens
    width = (heads + 2) * HEAD_SIZE
    chips = planes // 2
    out_block = heads * HEAD_SIZE // planes
    low = jnp.bfloat16
    vmem = pl.BlockSpec(memory_space=pltpu.VMEM)
    anywhere = pl.BlockSpec(memory_space=pl.ANY)
    dma = pltpu.SemaphoreType.DMA
    return pl.pallas_call(
        functools.partial(backward_kernel, count, planes, tokens, heads, shard),
        out_shape=(
            jax.ShapeDtypeStruct((tokens, MODEL_WIDTH), jnp.float32),
            jax.ShapeDtypeStruct((out_block, MODEL_WIDTH), jnp.float32),
            jax.ShapeDtypeStruct((count, shard, width), low),
            jax.ShapeDtypeStruct((8, HEAD_SIZE), jnp.float32),
        ),
        in_specs=[vmem] + [anywhere] * 7 + [vmem] * 4,
        out_specs=(vmem,) * 4,
        scratch_shapes=[
            pltpu.VMEM(out_rows.shape, low),
            pltpu.VMEM(own_cols.shape, low),
            pltpu.VMEM(normed.shape, low),
            pltpu.VMEM(heads_low.shape, low),
            pltpu.VMEM(queries.shape, low),
            pltpu.VMEM(pair.shape, low),
            pltpu.VMEM(proj.shape, jnp.float32),
            dma((7,)),
            pltpu.VMEM((count, tokens, MODEL_WIDTH), low),
            dma((2, count)),
            dma((2, count)),
            pltpu.VMEM((heads, length, HEAD_SIZE), low),
            pltpu.VMEM((heads + 2, length, HEAD_SIZE), low),
            pltpu.VMEM((2, length, HEAD_SIZE), jnp.float32),
            pltpu.VMEM((planes, out_block, MODEL_WIDTH), low),
            pltpu.VMEM((chips, out_block, MODEL_WIDTH), low),
            pltpu.VMEM((chips - 1, out_block, MODEL_WIDTH), low),
            dma((4, chips)),
            pltpu.VMEM((count, planes, shard, width), low),
            pltpu.VMEM((chips, count, shard, width), low),
            pltpu.VMEM((chips - 1, count, shard, width), low),
            pltpu.VMEM((count, shard, width), low),
            dma((4, chips)),
            pltpu.VMEM((count, tokens, MODEL_WIDTH), low),
            pltpu.VMEM((count + 1, tokens, MODEL_WIDTH), low),
            dma((2, count)),
            dma((2, count)),
            dma((2, count)),
        ],
        compiler_params=pltpu.CompilerParams(
            collective_id=3, has_side_effects=True, vmem_limit_bytes=VMEM_BYTES
        ),
        name="attention_backward",
    )(branch, out_rows, own_cols, normed, heads_low, queries, pair, proj, lse, turn_cos, turn_sin, gains)


def expert_kernel(
    count, planes, tokens, slots, chunks,
    mixed_ref, masks_ref, spreader_hbm, grad_hbm, router_hbm, in_hbm, back_hbm,
    total_ref, gate_total_ref, grad_in_hbm, grad_back_hbm, combined_hbm,
    spreader, grad_rows, router, weight_in, weight_back, local_sems,
    full, ag_send, ag_recv,
    sent, arrived, x_send, x_recv,
    gate_up, act, grad_gate_up, logits,
    back_arrived, b_send, b_recv,
    gate_sent, gate_arrived, gate_own, gate_sums, g_send, g_recv, gs_send, gs_recv,
    sums, rs_send, rs_recv, tile_sems, combined_sems,
):
    place = lax.axis_index("seq")
    member = lax.axis_index("dp")
    rows = planes * slots
    length = count * tokens
    wide = MODEL_WIDTH // chunks
    half = rows // 2
    own_expert = place * planes + member
    low = jnp.bfloat16

    loads = [
        pltpu.make_async_copy(spreader_hbm, spreader, local_sems.at[0]),
        pltpu.make_async_copy(router_hbm, router, local_sems.at[1]),
        pltpu.make_async_copy(in_hbm, weight_in, local_sems.at[2]),
        pltpu.make_async_copy(grad_hbm, grad_rows, local_sems.at[3]),
    ] + [
        pltpu.make_async_copy(
            back_hbm.at[:, pl.ds(c * wide, wide)], weight_back.at[c], local_sems.at[4 + c]
        )
        for c in range(chunks)
    ]
    for load in loads:
        load.start()
    for c in range(chunks):
        full[c, place] = mixed_ref[:, c * wide : (c + 1) * wide]
    greet(
        [(place, lax.rem(member + j, planes)) for j in range(1, planes)]
        + [(lax.rem(place + k, count), member) for k in range(1, count)]
    )

    def line(c):
        return (count, place, member, full.at[c], ag_send.at[c], ag_recv.at[c])

    def row_copy(c, j):
        other = lax.rem(member + j, planes)
        return remote(
            sent.at[c, other], arrived.at[c, member], x_send.at[c, j], x_recv.at[c, j], (place, other)
        )

    for c in range(chunks):
        line_gather_step(0, *line(c))
    gate_up[...] = jnp.zeros_like(gate_up)
    logits[...] = jnp.zeros_like(logits)
    loads[0].wait()

    def dispatch(c, carry):
        for step in range(1, count):
            line_gather_step(step, *line(c))
        picked = dot_tn(spreader[...], full[c].reshape(length, wide)).astype(low)
        sent[c] = picked.reshape(planes, slots, wide)
        for j in range(1, planes):
            row_copy(c, j).start()
        arrived[c, member] = sent[c, member]
        return carry

    lax.fori_loop(0, chunks, dispatch, 0)
    for load in loads[1:]:
        load.wait()

    def forward(c, carry):
        for j in range(1, planes):
            row_copy(c, j).wait_recv()
        part = pl.ds(pl.multiple_of(c * wide, wide), wide)
        x = arrived[c].reshape(rows, wide)
        for piece in range(2):
            at = slice(piece * half, (piece + 1) * half)
            gate_up[at, :] += dot_nn(x[at], weight_in[part, :])
            logits[at, :] += dot_nn(x[at], router[part, :])
        return carry

    lax.fori_loop(0, chunks, forward, 0)

    def settle(c, carry):
        for j in range(1, planes):
            row_copy(c, j).wait_send()
        line_gather_end(*line(c))
        return carry

    lax.fori_loop(0, chunks, settle, 0)

    mask = masks_ref[:, : logits.shape[-1]].astype(jnp.float32)
    shifted = jnp.where(mask > 0, logits[...], FILLER)
    powers = jnp.where(mask > 0, jnp.exp(shifted - jnp.max(shifted, axis=-1, keepdims=True)), 0.0)
    powers_total = jnp.sum(powers, axis=-1, keepdims=True)
    lanes = lax.broadcasted_iota(jnp.int32, powers.shape, 1)
    own = jnp.sum(jnp.where(lanes == own_expert, powers, 0.0), axis=-1, keepdims=True)
    gate = own / jnp.where(powers_total > 0, powers_total, 1.0)
    gate_column = logits
    gate_column[...] = jnp.broadcast_to(gate, gate_column.shape)

    blocks = 4 if rows % 64 == 0 else 2
    step_rows = rows // blocks

    def backward(index, carry):
        at = pl.ds(pl.multiple_of(index * step_rows, step_rows), step_rows)
        scale = gate_column[at, 0:1]
        grad_act = jnp.zeros((step_rows, FF), jnp.float32)
        for c in range(chunks):
            scaled = (grad_rows[c, at, :].astype(jnp.float32) * scale).astype(low)
            grad_act += dot_nt(scaled, weight_back[c])
        gate_part = gate_up[at, :FF]
        up_part = gate_up[at, FF:]
        chance = jax.nn.sigmoid(gate_part)
        silu = gate_part * chance
        act[at, :] = (silu * up_part).astype(low)
        slope = chance + silu * (1.0 - chance)
        grad_gate_up[at, :FF] = (grad_act * up_part * slope).astype(low)
        grad_gate_up[at, FF:] = (grad_act * silu).astype(low)
        return carry

    lax.fori_loop(0, blocks, backward, 0)

    def back_copy(c, j):
        other = lax.rem(member + j, planes)
        return remote(
            sent.at[c, other], back_arrived.at[c, member], b_send.at[c, j], b_recv.at[c, j], (place, other)
        )

    def gate_copy(j):
        other = lax.rem(member + j, planes)
        return remote(
            gate_sent.at[other], gate_arrived.at[member], g_send.at[j], g_recv.at[j], (place, other)
        )

    def send_back(c, carry):
        part = pl.ds(pl.multiple_of(c * wide, wide), wide)
        back = dot_nt(grad_gate_up[...], weight_in[part, :]).astype(low)
        sent[c] = back.reshape(planes, slots, wide)
        for j in range(1, planes):
            back_copy(c, j).start()
        back_arrived[c, member] = sent[c, member]
        return carry

    lax.fori_loop(0, chunks, send_back, 0)

    in_tiles = [gate_up.at[part * wide : (part + 1) * wide, :FF] for part in range(2)]
    back_tile = gate_up.at[:FF, FF : FF + wide]

    def in_copy(slot, c, part):
        return pltpu.make_async_copy(
            in_tiles[slot],
            grad_in_hbm.at[pl.ds(pl.multiple_of(c * wide, wide), wide), pl.ds(part * FF, FF)],
            tile_sems.at[slot],
        )

    def in_gradient(c, carry):
        x = arrived[c].reshape(rows, wide)
        for part in range(2):

            @pl.when(c > 0)
            def _():
                in_copy(part, c, part).wait()

            in_tiles[part][...] = dot_tn(x, grad_gate_up[:, part * FF : (part + 1) * FF])
            in_copy(part, c, part).start()
        return carry

    lax.fori_loop(0, chunks, in_gradient, 0)

    def combined_copy(c):
        return pltpu.make_async_copy(arrived.at[c], combined_hbm.at[c], combined_sems.at[c])

    def outputs(c, grad_gate):
        result = dot_nn(act[...], weight_back[c]).astype(low).astype(jnp.float32)
        grads = grad_rows[c].astype(jnp.float32)
        scale = gate_column[:, 0:1]
        grad_rows[c] = (grads * scale).astype(low)
        arrived[c] = (result * scale).astype(low).reshape(planes, slots, wide)
        combined_copy(c).start()
        return grad_gate + jnp.sum(result * grads, axis=-1, keepdims=True)

    grad_gate = lax.fori_loop(0, chunks, outputs, jnp.zeros((rows, 1), jnp.float32))
    high = grad_gate.astype(low).astype(jnp.float32)
    rest = grad_gate - high
    experts = count * planes
    wide_lanes = lax.broadcasted_iota(jnp.int32, (rows, gate_sent.shape[-1]), 1)
    columns = jnp.where(
        wide_lanes == own_expert, high, jnp.where(wide_lanes == own_expert + experts, rest, 0.0)
    )
    gate_sent[...] = columns.astype(low).reshape(gate_sent.shape)
    for j in range(1, planes):
        gate_copy(j).start()
    gate_arrived[member] = gate_sent[member]

    def back_tile_copy(c):
        return pltpu.make_async_copy(
            back_tile,
            grad_back_hbm.at[:, pl.ds(pl.multiple_of(c * wide, wide), wide)],
            tile_sems.at[2],
        )

    def back_gradient(c, carry):
        result = dot_tn(act[...], grad_rows[c])

        @pl.when(c > 0)
        def _():
            back_tile_copy(c).wait()

        back_tile[...] = result
        back_tile_copy(c).start()
        return carry

    lax.fori_loop(0, chunks, back_gradient, 0)

    def sums_line(c):
        return (count, place, member, full.at[c], sums.at[c], rs_send.at[c], rs_recv.at[c])

    for c in range(chunks):
        for j in range(1, planes):
            back_copy(c, j).wait_recv()
        own_sums = dot_nn(spreader[...], back_arrived[c].reshape(rows, wide)).astype(low)
        full[c] = own_sums.reshape(count, tokens, wide)
        for step in range(count - 1):
            line_sum_step(step, *sums_line(c))
    for j in range(1, planes):
        gate_copy(j).wait_recv()
    extra = gate_sent.shape[-1]
    gate_own[...] = (
        dot_nn(spreader[...], gate_arrived[...].reshape(rows, extra))
        .astype(low)
        .reshape(count, tokens, extra)
    )
    gate_line = (count, place, member, gate_own, gate_sums, gs_send, gs_recv)
    for step in range(count - 1):
        line_sum_step(step, *gate_line)
    for c in range(chunks):
        line_sum_end(*sums_line(c), total_ref.at[:, c * wide : (c + 1) * wide])
    line_sum_end(*gate_line, gate_total_ref)
    for c in range(chunks):
        for j in range(1, planes):
            back_copy(c, j).wait_send()
        combined_copy(c).wait()
    for j in range(1, planes):
        gate_copy(j).wait_send()
    in_copy(0, 0, 0).wait()
    in_copy(1, 0, 1).wait()
    back_tile_copy(0).wait()


def expert_layer(
    count, planes, mixed, masks, spreader, grad_rows, router, weight_in, weight_back
):
    tokens = mixed.shape[0]
    length = count * tokens
    chunks, rows, wide = grad_rows.shape
    slots = rows // planes
    extra = masks.shape[-1]
    experts = router.shape[-1]
    low = jnp.bfloat16
    vmem = pl.BlockSpec(memory_space=pltpu.VMEM)
    anywhere = pl.BlockSpec(memory_space=pl.ANY)
    dma = pltpu.SemaphoreType.DMA
    return pl.pallas_call(
        functools.partial(expert_kernel, count, planes, tokens, slots, chunks),
        out_shape=(
            jax.ShapeDtypeStruct((tokens, MODEL_WIDTH), jnp.float32),
            jax.ShapeDtypeStruct((tokens, extra), jnp.float32),
            jax.ShapeDtypeStruct(weight_in.shape, jnp.float32),
            jax.ShapeDtypeStruct(weight_back.shape, jnp.float32),
            jax.ShapeDtypeStruct((chunks, planes, slots, wide), low),
        ),
        in_specs=[vmem] * 2 + [anywhere] * 5,
        out_specs=(vmem, vmem, anywhere, anywhere, anywhere),
        scratch_shapes=[
            pltpu.VMEM(spreader.shape, low),
            pltpu.VMEM(grad_rows.shape, low),
            pltpu.VMEM(router.shape, low),
            pltpu.VMEM(weight_in.shape, low),
            pltpu.VMEM((chunks, FF, wide), low),
            dma((4 + chunks,)),
            pltpu.VMEM((chunks, count, tokens, wide), low),
            dma((chunks, 2, count)),
            dma((chunks, 2, count)),
            pltpu.VMEM((chunks, planes, slots, wide), low),
            pltpu.VMEM((chunks, planes, slots, wide), low),
            dma((chunks, planes)),
            dma((chunks, planes)),
            pltpu.VMEM((rows, 2 * FF), jnp.float32),
            pltpu.VMEM((rows, FF), low),
            pltpu.VMEM((rows, 2 * FF), low),
            pltpu.VMEM((rows, experts), jnp.float32),
            pltpu.VMEM((chunks, planes, slots, wide), low),
            dma((chunks, planes)),
            dma((chunks, planes)),
            pltpu.VMEM((planes, slots, extra), low),
            pltpu.VMEM((planes, slots, extra), low),
            pltpu.VMEM((count, tokens, extra), low),
            pltpu.VMEM((count + 1, tokens, extra), low),
            dma((planes,)),
            dma((planes,)),
            dma((2, count)),
            dma((2, count)),
            pltpu.VMEM((chunks, count + 1, tokens, wide), low),
            dma((chunks, 2, count)),
            dma((chunks, 2, count)),
            dma((3,)),
            dma((chunks,)),
        ],
        compiler_params=pltpu.CompilerParams(
            collective_id=2, has_side_effects=True, vmem_limit_bytes=VMEM_BYTES
        ),
        name="expert_layer",
    )(mixed, masks, spreader, grad_rows, router, weight_in, weight_back)


def small_kernel(
    count, chips, own_ref, total_ref, line_got, line_sum, chip_got, core_sum, core_got,
    z_send, z_recv, c_send, c_recv, p_send, p_recv,
):
    place = lax.axis_index("seq")
    member = lax.axis_index("dp")
    core = lax.rem(member, 2)
    chip = member // 2
    partner = member + 1 - 2 * core
    far_places = [lax.rem(place + k, count) for k in range(1, count)]
    far_chips = [lax.rem(chip + k, chips) for k in range(1, chips)]
    greet(
        [(other, member) for other in far_places]
        + [(place, 2 * other + core) for other in far_chips]
        + [(place, partner)]
    )
    copies = [
        remote(own_ref.at[other], line_got.at[k], z_send.at[k], z_recv.at[k], (other, member))
        for k, other in enumerate(far_places)
    ]
    for copy in copies:
        copy.start()
    total = own_ref[place]
    for k, copy in enumerate(copies):
        copy.wait_recv()
        total += line_got[k]
    line_sum[...] = total
    chip_copies = [
        remote(line_sum.at[other], chip_got.at[k], c_send.at[k], c_recv.at[k], (place, 2 * other + core))
        for k, other in enumerate(far_chips)
    ]
    for copy in chip_copies:
        copy.start()
    mine = line_sum[chip]
    for k, copy in enumerate(chip_copies):
        copy.wait_recv()
        mine += chip_got[k]
    core_sum[...] = mine
    pair = remote(core_sum, core_got, p_send, p_recv, (place, partner))
    pair.start()
    pair.wait_recv()
    total_ref[...] = core_sum[...] + core_got[...]
    pair.wait_send()
    for copy in copies + chip_copies:
        copy.wait_send()


def small_sums(count, chips, own):
    shape = own.shape[2:]
    vmem = pl.BlockSpec(memory_space=pltpu.VMEM)
    dma = pltpu.SemaphoreType.DMA
    kind = jnp.float32
    return pl.pallas_call(
        functools.partial(small_kernel, count, chips),
        out_shape=jax.ShapeDtypeStruct(shape, kind),
        in_specs=[vmem],
        out_specs=vmem,
        scratch_shapes=[
            pltpu.VMEM((count - 1, chips) + shape, kind),
            pltpu.VMEM((chips,) + shape, kind),
            pltpu.VMEM((chips - 1,) + shape, kind),
            pltpu.VMEM(shape, kind),
            pltpu.VMEM(shape, kind),
            dma((count - 1,)),
            dma((count - 1,)),
            dma((chips - 1,)),
            dma((chips - 1,)),
            dma(()),
            dma(()),
        ],
        compiler_params=pltpu.CompilerParams(collective_id=4, has_side_effects=True),
        name="small_sums",
    )(own)


def rms_norm(values, gain):
    return values * lax.rsqrt(jnp.mean(values * values, axis=-1, keepdims=True) + EPSILON) * gain


def rope_tables(positions, width):
    half_width = width // 2
    freqs = ROPE_BASE ** (-(jnp.arange(half_width, dtype=jnp.float32) * (2.0 / width)))
    angles = positions[:, None] * freqs[None, :]
    return (jnp.cos(angles), jnp.sin(angles))


def rotate(values, cosine, sine_table):
    half_width = values.shape[-1] // 2
    first = values[..., :half_width]
    second = values[..., half_width:]
    cosine = cosine[:, None, :]
    sine_table = sine_table[:, None, :]
    return jnp.concatenate(
        [first * cosine - second * sine_table, second * cosine + first * sine_table], axis=-1
    )


def prepare_heads(projected_rows, gain_query, gain_key, cosine, sine_table):
    row_count = projected_rows.shape[0]
    query_columns = projected_rows.shape[1] - 2 * HEAD_SIZE
    queries = projected_rows[:, :query_columns].reshape(
        row_count, query_columns // HEAD_SIZE, HEAD_SIZE
    )
    key_head = projected_rows[:, query_columns : query_columns + HEAD_SIZE].reshape(
        row_count, 1, HEAD_SIZE
    )
    value_head = projected_rows[:, query_columns + HEAD_SIZE :]
    queries = rotate(rms_norm(queries, gain_query), cosine, sine_table)
    key_head = rotate(rms_norm(key_head, gain_key), cosine, sine_table).reshape(
        row_count, HEAD_SIZE
    )
    return (queries, key_head, value_head)


def inner_rows(left, right):
    return lax.dot_general(
        left, right, (((0,), (0,)), ((), ())), preferred_element_type=jnp.float32
    )


def outer_cols(left, right):
    return lax.dot_general(
        left, right, (((1,), (1,)), ((), ())), preferred_element_type=jnp.float32
    )


def block_slice(array, index, block_rows):
    return lax.dynamic_slice_in_dim(array, index * block_rows, block_rows, 0)


def block_scores(query_block, key_block, i, j, block_rows):
    scores = jnp.einsum(
        "qhd,kd->hqk", query_block, key_block, preferred_element_type=jnp.float32
    ) * HEAD_SIZE ** (-0.5)
    row_ids = i * block_rows + jnp.arange(block_rows)
    col_ids = j * block_rows + jnp.arange(block_rows)
    return jnp.where((row_ids[:, None] >= col_ids[None, :])[None], scores, FILLER)


def attend_forward(queries, keys_in, values_in):
    sequence_length, head_count = (queries.shape[0], queries.shape[1])
    block_rows = min(QUERY_BLOCK, sequence_length)
    block_count = sequence_length // block_rows

    def one_block(i):
        query_block = block_slice(queries, i, block_rows)

        def max_step(j, carry):
            row_top, row_total = carry
            scores = block_scores(
                query_block, block_slice(keys_in, j, block_rows), i, j, block_rows
            )
            new_top = jnp.maximum(row_top, jnp.max(scores, axis=-1))
            row_total = row_total * jnp.exp(row_top - new_top) + jnp.sum(
                jnp.exp(scores - new_top[..., None]), axis=-1
            )
            return (new_top, row_total)

        start = (
            jnp.full((head_count, block_rows), FILLER, jnp.float32),
            jnp.zeros((head_count, block_rows), jnp.float32),
        )
        row_top, row_total = lax.fori_loop(0, i + 1, max_step, start)
        log_totals = row_top + jnp.log(row_total)

        def out_step(j, accum_out):
            scores = block_scores(
                query_block, block_slice(keys_in, j, block_rows), i, j, block_rows
            )
            probabilities = jnp.exp(scores - log_totals[..., None]).astype(jnp.bfloat16)
            return accum_out + jnp.einsum(
                "hqk,kd->qhd",
                probabilities,
                block_slice(values_in, j, block_rows),
                preferred_element_type=jnp.float32,
            )

        accum_out = lax.fori_loop(
            0, i + 1, out_step, jnp.zeros((block_rows, head_count, HEAD_SIZE), jnp.float32)
        )
        return (accum_out, log_totals)

    outputs, log_totals = lax.map(one_block, jnp.arange(block_count))
    return (outputs.reshape(sequence_length, head_count, HEAD_SIZE), log_totals)


def masked_softmax(logits, mask):
    shifted = jnp.where(mask > 0, logits, FILLER)
    top = jnp.max(shifted, axis=-1, keepdims=True)
    powers = jnp.where(mask > 0, jnp.exp(shifted - top), 0.0)
    total = jnp.sum(powers, axis=-1, keepdims=True)
    return powers / jnp.where(total > 0, total, 1.0)


def body(
    hidden_in,
    routes,
    norm1_gain,
    query_gain,
    key_gain,
    qkv_weight,
    out_weight,
    norm2_gain,
    router,
    gate_up_weight,
    down_weight,
    cotangent,
):
    tokens = hidden_in.shape[1]
    sequence_number = lax.axis_size("seq")
    planes = lax.axis_size("dp")
    devices = sequence_number * planes
    group = lax.axis_index("seq")
    member = lax.axis_index("dp")
    per_device = QUERY_HEADS // sequence_number
    query_columns = per_device * HEAD_SIZE
    own_width = query_columns + 2 * HEAD_SIZE
    head_replicas = sequence_number // KEY_VALUE_HEADS
    capacity = (tokens * TOP * 9 + 8 * devices - 1) // (8 * devices)
    slots = -(-sequence_number * capacity // 16) * 16
    chunks = 4
    wide = MODEL_WIDTH // chunks
    sequence_length = sequence_number * tokens
    extra = -(-2 * devices // 128) * 128

    shard = norm1_gain.shape[0]
    small_shard = query_gain.shape[0]
    small_width = 2 * shard + 2 * small_shard + shard * devices
    small_rows = -(-small_width // 2048) * 16
    packed = jnp.concatenate(
        [norm1_gain, norm2_gain, query_gain, key_gain, router.reshape(-1)]
    )
    packed = jnp.pad(packed, (0, small_rows * 128 - small_width)).reshape(small_rows, 128)
    packed = lax.all_gather(packed, ("seq", "dp"), axis=0, tiled=True)
    packed = packed.reshape(devices, small_rows * 128)
    cut = 0
    pieces = []
    for width in (shard, shard, small_shard, small_shard, shard * devices):
        pieces.append(packed[:, cut : cut + width])
        cut += width
    gain_one = pieces[0].reshape(-1).astype(jnp.float32)
    gain_two = pieces[1].reshape(-1).astype(jnp.float32)
    gain_query = pieces[2].reshape(-1).astype(jnp.float32)
    gain_key = pieces[3].reshape(-1).astype(jnp.float32)
    full_router = pieces[4].reshape(MODEL_WIDTH, devices)

    query_part = qkv_weight[:, : QUERY_HEADS * HEAD_SIZE].reshape(
        shard, sequence_number, query_columns
    )
    paired_portion = jnp.repeat(
        qkv_weight[:, QUERY_HEADS * HEAD_SIZE :].reshape(shard, 2, KEY_VALUE_HEADS, HEAD_SIZE),
        head_replicas,
        axis=2,
    )
    paired_portion = jnp.transpose(paired_portion, (0, 2, 1, 3)).reshape(
        shard, sequence_number, 2 * HEAD_SIZE
    )
    column_send = jnp.transpose(
        jnp.concatenate([query_part, paired_portion], axis=-1), (1, 0, 2)
    )
    own_part = lax.all_to_all(column_send, "seq", split_axis=0, concat_axis=0, tiled=True)
    own_cols = lax.all_gather(own_part, "dp", axis=1, tiled=True).reshape(MODEL_WIDTH, own_width)
    out_rows = lax.all_gather(out_weight, "dp", axis=0, tiled=True)

    full_routes = lax.all_gather(routes[0], "seq", axis=0, tiled=True)
    expert_ids = jnp.arange(devices, dtype=jnp.int32)
    route_mask = jnp.sum(
        (full_routes[:, :, None] == expert_ids[None, None, :]).astype(jnp.float32), axis=1
    )
    before = (
        jnp.arange(tokens)[:, None] > jnp.arange(tokens)[None, :]
    ).astype(jnp.bfloat16)
    places = jnp.einsum(
        "tu,sue->ste",
        before,
        route_mask.astype(jnp.bfloat16).reshape(sequence_number, tokens, devices),
        preferred_element_type=jnp.float32,
    ).astype(jnp.int32)
    places = places + (jnp.arange(sequence_number, dtype=jnp.int32) * capacity)[:, None, None]
    places = jnp.where(route_mask > 0, places.reshape(sequence_length, devices), -1)
    plane_places = lax.dynamic_slice_in_dim(places, group * planes, planes, 1)
    column_ids = jnp.arange(planes * slots, dtype=jnp.int32)
    column_places = jnp.full((sequence_length, planes * slots), -2, jnp.int32)
    for other in range(planes):
        column_places = jnp.where(
            (column_ids // slots == other)[None, :], plane_places[:, other : other + 1], column_places
        )
    spreader = (column_places == (column_ids % slots)[None, :]).astype(jnp.bfloat16)

    def dispatch(rows):
        sent = inner_rows(spreader, rows).astype(jnp.bfloat16)
        return lax.all_to_all(
            sent.reshape(planes, slots, rows.shape[-1]), "dp", split_axis=0, concat_axis=0, tiled=True
        ).reshape(planes * slots, rows.shape[-1])

    def combine(rows):
        back = lax.all_to_all(rows, "dp", split_axis=1, concat_axis=1, tiled=True)
        back = jnp.transpose(
            back.reshape(chunks, planes * slots, wide), (1, 0, 2)
        ).reshape(planes * slots, MODEL_WIDTH)
        sums = jnp.dot(spreader, back, preferred_element_type=jnp.float32).astype(jnp.bfloat16)
        return lax.psum_scatter(sums, "seq", scatter_dimension=0, tiled=True).astype(jnp.float32)

    mask_columns = jnp.pad(route_mask.astype(jnp.bfloat16), ((0, 0), (0, extra - devices)))
    cotangent_full = lax.all_gather(cotangent[0], "seq", axis=0, tiled=True)
    grad_arrived = dispatch(jnp.concatenate([cotangent_full, mask_columns], axis=1))

    hidden_full = lax.all_gather(hidden_in[0], "seq", axis=0, tiled=True)
    residual = hidden_in[0].astype(jnp.float32)
    normed_full = rms_norm(hidden_full.astype(jnp.float32), gain_one).astype(jnp.bfloat16)
    cosine, sine_table = rope_tables(jnp.arange(sequence_length).astype(jnp.float32), HEAD_SIZE)
    projected_rows = jnp.dot(normed_full, own_cols, preferred_element_type=jnp.float32)
    queries, key_head, value_head = prepare_heads(
        projected_rows, gain_query, gain_key, cosine, sine_table
    )
    query_heads = queries.astype(jnp.bfloat16)
    key_heads = key_head.astype(jnp.bfloat16)
    value_heads = value_head.astype(jnp.bfloat16)
    out_full, log_totals = attend_forward(query_heads, key_heads, value_heads)
    heads_low = out_full.astype(jnp.bfloat16).reshape(sequence_length, query_columns)
    branch_part = jnp.dot(heads_low, out_rows, preferred_element_type=jnp.float32)
    hidden1 = residual + lax.psum_scatter(
        branch_part.astype(jnp.bfloat16), "seq", scatter_dimension=0, tiled=True
    ).astype(jnp.float32)
    mixed_low = rms_norm(hidden1, gain_two).astype(jnp.bfloat16)
    grad_sent, gate_sent, grad_weight_in, grad_weight_back, combined_rows = expert_layer(
        sequence_number,
        planes,
        mixed_low,
        grad_arrived[:, MODEL_WIDTH:],
        spreader,
        jnp.transpose(
            grad_arrived[:, :MODEL_WIDTH].reshape(planes * slots, chunks, wide), (1, 0, 2)
        ),
        jnp.pad(full_router, ((0, 0), (0, -devices % 128))),
        gate_up_weight[0],
        down_weight[0],
    )
    output = (hidden1 + combine(combined_rows)).astype(jnp.bfloat16)

    grad_result = cotangent[0].astype(jnp.float32)
    own_mask = lax.dynamic_slice_in_dim(route_mask, group * tokens, tokens, 0)
    logits = jnp.dot(mixed_low, full_router, preferred_element_type=jnp.float32)
    gates = masked_softmax(logits, own_mask)
    grad_gates = (
        gate_sent[:, :devices] + gate_sent[:, devices : 2 * devices]
    )
    grad_logits = (
        gates * (grad_gates - jnp.sum(gates * grad_gates, axis=-1, keepdims=True))
    ).astype(jnp.bfloat16)
    grad_mixed = grad_sent + outer_cols(grad_logits, full_router)
    grad_router_t = inner_rows(grad_logits, mixed_low)
    _, pull_two = jax.vjp(rms_norm, hidden1, gain_two)
    grad_hidden_norm, grad_gain_two = pull_two(grad_mixed)
    grad_hidden1 = grad_result + grad_hidden_norm
    grad_branch = grad_hidden1.astype(jnp.bfloat16)
    normed_total, shard_out, column_sums, gain_totals = attention_backward(
        sequence_number,
        planes,
        per_device,
        shard,
        grad_branch,
        out_rows,
        own_cols,
        normed_full,
        jnp.transpose(
            heads_low.reshape(sequence_length, planes, query_columns // planes), (1, 0, 2)
        ),
        jnp.transpose(query_heads, (1, 0, 2)),
        jnp.stack([key_heads, value_heads]),
        jnp.transpose(
            projected_rows.reshape(sequence_length, per_device + 2, HEAD_SIZE), (1, 0, 2)
        ),
        log_totals.reshape(-1, per_device, sequence_length // log_totals.shape[0])
        .transpose(1, 0, 2)
        .reshape(per_device, 1, sequence_length),
        jnp.concatenate([cosine, cosine], axis=1),
        jnp.concatenate([sine_table, -sine_table], axis=1),
        jnp.pad(jnp.stack([gain_query, gain_key]), ((0, 6), (0, 0))),
    )
    column_sums = column_sums.astype(jnp.float32)
    shard_query = jnp.transpose(column_sums[:, :, :query_columns], (1, 0, 2)).reshape(
        shard, QUERY_HEADS * HEAD_SIZE
    )
    shard_paired = jnp.sum(
        column_sums[:, :, query_columns:].reshape(
            KEY_VALUE_HEADS, head_replicas, shard, 2, HEAD_SIZE
        ),
        axis=1,
    )
    shard_paired = jnp.transpose(shard_paired, (1, 2, 0, 3)).reshape(
        shard, 2 * KEY_VALUE_HEADS * HEAD_SIZE
    )
    shard_qkv = jnp.concatenate([shard_query, shard_paired], axis=1)
    _, pull_one = jax.vjp(rms_norm, residual, gain_one)
    grad_residual_norm, grad_gain_one = pull_one(normed_total)
    grad_input = grad_hidden1 + grad_residual_norm

    chips = planes // 2

    def by_chip(values):
        columns = values.reshape(-1, sequence_number, chips, values.shape[-1] // devices * 2)
        columns = jnp.pad(columns, ((0, 0),) * 3 + ((0, 2 * shard - columns.shape[-1]),))
        return jnp.transpose(columns, (1, 2, 0, 3))

    small = jnp.concatenate(
        [
            by_chip(grad_router_t),
            by_chip(grad_gain_two),
            by_chip(grad_gain_one),
            by_chip(gain_totals[0]),
            by_chip(gain_totals[1]),
            jnp.zeros((sequence_number, chips, 4, 2 * shard), jnp.float32),
        ],
        axis=2,
    )
    small = small_sums(sequence_number, chips, small)
    core = lax.rem(member, 2)
    small_core = lax.dynamic_slice_in_dim(small, core * shard, shard, 1)
    small_gains = lax.dynamic_slice_in_dim(
        small[devices + 2 : devices + 4, : 2 * small_shard], core * small_shard, small_shard, 1
    )
    return (
        output[None],
        grad_input[None],
        small_core[devices + 1],
        small_gains[0],
        small_gains[1],
        shard_qkv,
        shard_out,
        small_core[devices],
        small_core[:devices].T,
        grad_weight_in[None],
        grad_weight_back[None],
    )


def solution(mesh):
    in_specs = (
        P("dp", "seq", None),
        P("dp", "seq", None),
        P(("seq", "dp")),
        P(("seq", "dp")),
        P(("seq", "dp")),
        P(("seq", "dp"), None),
        P(("seq", "dp"), None),
        P(("seq", "dp")),
        P(("seq", "dp"), None),
        P(("seq", "dp"), None, None),
        P(("seq", "dp"), None, None),
        P("dp", "seq", None),
    )
    out_specs = (
        P("dp", "seq", None),
        P("dp", "seq", None),
        P(("seq", "dp")),
        P(("seq", "dp")),
        P(("seq", "dp")),
        P(("seq", "dp"), None),
        P(("seq", "dp"), None),
        P(("seq", "dp")),
        P(("seq", "dp"), None),
        P(("seq", "dp"), None, None),
        P(("seq", "dp"), None, None),
    )
    return jax.shard_map(body, mesh=mesh, in_specs=in_specs, out_specs=out_specs, check_vma=False)
```

```python
import functools
import jax
import jax.numpy as jnp
import numpy as np
from jax import lax
from jax.experimental import pallas as pl
from jax.experimental.pallas import tpu as pltpu
from jax.sharding import PartitionSpec as P


MODEL_WIDTH = 2048
QUERY_HEADS = 32
KEY_VALUE_HEADS = 4
HEAD_SIZE = 128
FF = 768
TOP = 8


EPSILON = 1e-06
ROPE_BASE = 1000000.0
FILLER = -1e30
QUERY_BLOCK = 512


MESH = pl.DeviceIdType.MESH
VMEM_BYTES = 63 * 1024 * 1024


def dot_nn(left, right):
    return jnp.dot(left, right, preferred_element_type=jnp.float32)


def dot_nt(left, right):
    return lax.dot_general(
        left, right, (((1,), (1,)), ((), ())), preferred_element_type=jnp.float32
    )


def dot_tn(left, right):
    return lax.dot_general(
        left, right, (((0,), (0,)), ((), ())), preferred_element_type=jnp.float32
    )


def greet(peers):
    barrier = pltpu.get_barrier_semaphore()
    for peer in peers:
        pl.semaphore_signal(barrier, inc=1, device_id=peer, device_id_type=MESH)
    pl.semaphore_wait(barrier, len(peers))


def remote(source, target, send_sem, recv_sem, device):
    return pltpu.make_async_remote_copy(
        src_ref=source,
        dst_ref=target,
        send_sem=send_sem,
        recv_sem=recv_sem,
        device_id=device,
        device_id_type=MESH,
    )


def line_gather_step(step, count, place, column, blocks, send_sems, recv_sems):
    right, left = place + 1, place - 1
    if step > 0:

        @pl.when(place - step >= 0)
        def _():
            block = blocks.at[place - step]
            remote(block, block, send_sems.at[0, step], recv_sems.at[0, step], (right, column)).wait_recv()

        @pl.when(place + step < count)
        def _():
            block = blocks.at[place + step]
            remote(block, block, send_sems.at[1, step], recv_sems.at[1, step], (left, column)).wait_recv()

    if step < count - 1:

        @pl.when((place - step >= 0) & (place + 1 < count))
        def _():
            block = blocks.at[place - step]
            remote(block, block, send_sems.at[0, step], recv_sems.at[0, step + 1], (right, column)).start()

        @pl.when((place + step < count) & (place - 1 >= 0))
        def _():
            block = blocks.at[place + step]
            remote(block, block, send_sems.at[1, step], recv_sems.at[1, step + 1], (left, column)).start()


def line_gather_end(count, place, column, blocks, send_sems, recv_sems):
    for step in range(count - 1):

        @pl.when((place - step >= 0) & (place + 1 < count))
        def _():
            block = blocks.at[place - step]
            remote(block, block, send_sems.at[0, step], recv_sems.at[0, step], (place + 1, column)).wait_send()

        @pl.when((place + step < count) & (place - 1 >= 0))
        def _():
            block = blocks.at[place + step]
            remote(block, block, send_sems.at[1, step], recv_sems.at[1, step], (place - 1, column)).wait_send()


def line_sum_step(step, count, place, column, own, sums, send_sems, recv_sems):
    turn = step - place
    last = count - 1 - turn

    @pl.when((turn >= 0) & (last > place))
    def _():
        block = sums.at[last]

        @pl.when(place > 0)
        def _():
            remote(block, block, send_sems.at[0, last], recv_sems.at[0, last], (place, column)).wait_recv()
            sums[last] = (
                sums[last].astype(jnp.float32) + own[last].astype(jnp.float32)
            ).astype(jnp.bfloat16)

        @pl.when(place == 0)
        def _():
            sums[last] = own[last]

        remote(block, block, send_sems.at[0, last], recv_sems.at[0, last], (place + 1, column)).start()

    first = step - (count - 1 - place)

    @pl.when((first >= 0) & (first < place))
    def _():
        block = sums.at[first]

        @pl.when(place < count - 1)
        def _():
            remote(block, block, send_sems.at[1, first], recv_sems.at[1, first], (place, column)).wait_recv()
            sums[first] = (
                sums[first].astype(jnp.float32) + own[first].astype(jnp.float32)
            ).astype(jnp.bfloat16)

        @pl.when(place == count - 1)
        def _():
            sums[first] = own[first]

        target = sums.at[jnp.where(first == place - 1, count, first)]
        remote(block, target, send_sems.at[1, first], recv_sems.at[1, first], (place - 1, column)).start()


def line_sum_end(count, place, column, own, sums, send_sems, recv_sems, total):
    total[...] = own[place].astype(jnp.float32)

    @pl.when(place > 0)
    def _():
        block = sums.at[place]
        remote(block, block, send_sems.at[0, place], recv_sems.at[0, place], (place, column)).wait_recv()
        total[...] += sums[place].astype(jnp.float32)

    @pl.when(place < count - 1)
    def _():
        block = sums.at[count]
        remote(block, block, send_sems.at[1, place], recv_sems.at[1, place], (place, column)).wait_recv()
        total[...] += sums[count].astype(jnp.float32)

    for step in range(count - 1):
        last = count - 1 - step

        @pl.when(last > place)
        def _():
            block = sums.at[last]
            remote(block, block, send_sems.at[0, last], recv_sems.at[0, last], (place + 1, column)).wait_send()

        @pl.when(step < place)
        def _():
            block = sums.at[step]
            remote(block, block, send_sems.at[1, step], recv_sems.at[1, step], (place - 1, column)).wait_send()


def backward_kernel(
    count, planes, tokens, heads, shard,
    branch_ref, out_rows_hbm, own_cols_hbm, normed_hbm, heads_hbm, query_hbm, pair_hbm,
    proj_hbm, spreader_hbm, combined_hbm, lse_ref, turn_cos_ref, turn_sin_ref, gain_ref,
    normed_total, out_total, columns_out, gain_total, mixed_total, mixed_arrived,
    out_rows, own_cols, normed, heads_low, queries, pair, proj, local_sems,
    branch_full, ag_send, ag_recv,
    grad_heads, grad_proj, grad_pair,
    grad_out, out_pair, out_far, out_sems,
    grad_cols, col_pair, col_far, col_sums, col_sems,
    normed_part, normed_sums, rs_send, rs_recv, z_sems,
    spreader, mixed_rows, mixed_sums, mix_send, mix_recv, mix_local, ms_send, ms_recv,
):
    place = lax.axis_index("seq")
    member = lax.axis_index("dp")
    core = lax.rem(member, 2)
    chip = member // 2
    chips = planes // 2
    partner = member + 1 - 2 * core
    length = count * tokens
    query_columns = heads * HEAD_SIZE
    out_block = query_columns // planes
    scale = HEAD_SIZE ** (-0.5)

    loads = [
        pltpu.make_async_copy(source, target, local_sems.at[index])
        for index, (source, target) in enumerate(
            [
                (out_rows_hbm, out_rows),
                (query_hbm, queries),
                (pair_hbm, pair),
                (heads_hbm, heads_low),
                (proj_hbm, proj),
                (own_cols_hbm, own_cols),
                (normed_hbm, normed),
                (spreader_hbm, spreader),
            ]
        )
    ]
    for load in loads:
        load.start()
    branch_full[place] = branch_ref[...]

    far_chips = [lax.rem(chip + k, chips) for k in range(1, chips)]
    far_places = [lax.rem(place + k, count) for k in range(1, count)]
    others = [(j, lax.rem(member + j, planes)) for j in range(1, planes)]
    greet([(place, other) for _, other in others] + [(other, member) for other in far_places])

    line = (count, place, member, branch_full, ag_send, ag_recv)
    line_gather_step(0, *line)

    def mixed_copy(j, other):
        return remote(
            combined_hbm.at[:, other], mixed_arrived.at[:, member], mix_send.at[j], mix_recv.at[j],
            (place, other),
        )

    for j, other in others:
        mixed_copy(j, other).start()
    mixed_own = pltpu.make_async_copy(
        combined_hbm.at[:, member], mixed_arrived.at[:, member], mix_local.at[0]
    )
    mixed_own.start()
    for load in loads:
        load.wait()

    def head_gradients(block):
        partial_heads = dot_nt(
            branch_full[block], out_rows[...].reshape(query_columns, MODEL_WIDTH)
        ).astype(jnp.bfloat16)
        for head in range(heads):
            grad_heads[head, pl.ds(pl.multiple_of(block * tokens, tokens), tokens), :] = (
                partial_heads[:, head * HEAD_SIZE : (head + 1) * HEAD_SIZE]
            )

    head_gradients(place)
    for step in range(1, count):
        line_gather_step(step, *line)

        @pl.when(place - step >= 0)
        def _():
            head_gradients(place - step)

        @pl.when(place + step < count)
        def _():
            head_gradients(place + step)

    def out_copy(target, k):
        rows = grad_out.at[2 * k + 1 - core]
        return remote(rows, out_pair.at[k], out_sems.at[0, k], out_sems.at[1, k], (place, partner))

    def out_gradient(block):
        all_branch = branch_full[...].reshape(length, MODEL_WIDTH)
        columns = heads_low[block]
        grad_out[block] = dot_tn(columns, all_branch).astype(jnp.bfloat16)

    for k in range(chips):
        out_gradient(2 * k + 1 - core)
        out_copy(None, k).start()
    for k in range(chips):
        out_gradient(2 * k + core)

    def out_far_copy(k):
        other = lax.rem(chip + k, chips)
        return remote(
            out_pair.at[other], out_far.at[k - 1], out_sems.at[2, k], out_sems.at[3, k],
            (place, 2 * other + core),
        )

    for k in range(chips):
        out_copy(None, k).wait_recv()
        out_pair[k] = (
            out_pair[k].astype(jnp.float32) + grad_out[2 * k + core].astype(jnp.float32)
        ).astype(jnp.bfloat16)
    for k in range(1, chips):
        out_far_copy(k).start()

    grad_pair[...] = jnp.zeros_like(grad_pair)
    gain_total[...] = jnp.zeros_like(gain_total)
    block_rows = min(256, length)

    def unprepare(grad, raw, gain):
        turned = grad * turn_cos_ref[...] + pltpu.roll(grad, HEAD_SIZE // 2, 1) * -turn_sin_ref[...]
        inverse = lax.rsqrt(jnp.mean(raw * raw, axis=-1, keepdims=True) + EPSILON)
        unit = raw * inverse
        gain_part = jnp.sum(turned * unit, axis=0, keepdims=True)
        turned = turned * gain
        middle = jnp.mean(turned * unit, axis=-1, keepdims=True)
        return inverse * (turned - unit * middle), gain_part

    key_turned = jnp.transpose(pair[0].astype(jnp.float32)).astype(jnp.bfloat16)

    def one_head(head, carry):
        lse = lse_ref[head]
        grads = []
        for block in range(length // block_rows):
            low, high = block * block_rows, (block + 1) * block_rows
            query = queries[head, low:high, :]
            grad = grad_heads[head, low:high, :]
            key = pair[0, :high, :]
            scores = dot_nt(key, query) * scale
            row_ids = lax.broadcasted_iota(jnp.int32, (high, block_rows), 0)
            col_ids = lax.broadcasted_iota(jnp.int32, (high, block_rows), 1) + low
            scores = jnp.where(row_ids <= col_ids, scores, FILLER)
            probs = jnp.exp(scores - lse[:, low:high])
            grad_probs = dot_nt(pair[1, :high, :], grad)
            delta = jnp.sum(probs * grad_probs, axis=0, keepdims=True)
            grad_scores = (probs * (grad_probs - delta)).astype(jnp.bfloat16)
            grad_pair[0, :high, :] += dot_nn(grad_scores, query) * scale
            grad_pair[1, :high, :] += dot_nn(probs.astype(jnp.bfloat16), grad)
            grads.append(jnp.transpose(dot_nn(key_turned[:, :high], grad_scores)) * scale)
        grad_query = jnp.concatenate(grads, axis=0)
        grad_raw, gain_part = unprepare(grad_query, proj[head], gain_ref[0:1, :])
        gain_total[0:1, :] += gain_part
        grad_proj[head] = grad_raw.astype(jnp.bfloat16)
        return carry

    lax.fori_loop(0, heads // 2, one_head, 0)

    for j, other in others:
        mixed_copy(j, other).wait_recv()
    mixed_own.wait()
    line_gather_end(*line)
    chunks, _, slots, wide = mixed_arrived.shape

    def mixed_load(c):
        return pltpu.make_async_copy(mixed_arrived.at[c], mixed_rows.at[c % 2], mix_local.at[1 + c % 2])

    mixed_load(0).start()
    for c in range(chunks):
        mixed_load(c).wait()
        if c + 1 < chunks:
            mixed_load(c + 1).start()
        part = dot_nn(spreader[...], mixed_rows[c % 2].reshape(planes * slots, wide))
        branch_full[:, :, c * wide : (c + 1) * wide] = part.astype(jnp.bfloat16).reshape(
            count, tokens, wide
        )
    mixed_line = (count, place, member, branch_full, mixed_sums, ms_send, ms_recv)
    line_sum_step(0, *mixed_line)
    lax.fori_loop(heads // 2, heads, one_head, 0)
    line_sum_step(1, *mixed_line)
    grad_raw, gain_part = unprepare(grad_pair[0], proj[heads], gain_ref[1:2, :])
    gain_total[1:2, :] += gain_part
    grad_proj[heads] = grad_raw.astype(jnp.bfloat16)
    grad_proj[heads + 1] = grad_pair[1].astype(jnp.bfloat16)
    grad_rows = jnp.concatenate([grad_proj[head] for head in range(heads + 2)], axis=1)

    for block in range(count):
        normed_part[block] = dot_nt(
            grad_rows[block * tokens : (block + 1) * tokens, :],
            own_cols[...].reshape(MODEL_WIDTH, grad_rows.shape[-1]),
        ).astype(jnp.bfloat16)
    sums = (count, place, member, normed_part, normed_sums, rs_send, rs_recv)
    line_sum_step(0, *sums)

    for block in range(count):
        width = planes * shard
        part = dot_tn(normed[:, block * width : (block + 1) * width], grad_rows).astype(jnp.bfloat16)
        grad_cols[block] = part.reshape(planes, shard, part.shape[-1])

    def col_copy(k):
        rows = grad_cols.at[:, 2 * k + 1 - core]
        return remote(rows, col_pair.at[k], col_sems.at[0, k], col_sems.at[1, k], (place, partner))

    def col_far_copy(k):
        other = lax.rem(chip + k, chips)
        return remote(
            col_pair.at[other], col_far.at[k - 1], col_sems.at[2, k], col_sems.at[3, k],
            (place, 2 * other + core),
        )

    for k in range(chips):
        col_copy(k).start()
    for k in range(chips):
        col_copy(k).wait_recv()
        col_pair[k] = (
            col_pair[k].astype(jnp.float32) + grad_cols[:, 2 * k + core].astype(jnp.float32)
        ).astype(jnp.bfloat16)
    for k in range(1, chips):
        col_far_copy(k).start()

    for step in range(2, count - 1):
        line_sum_step(step, *mixed_line)
    if count > 2:
        line_sum_step(1, *sums)

    total = out_pair[chip].astype(jnp.float32)
    for k in range(1, chips):
        out_far_copy(k).wait_recv()
        total += out_far[k - 1].astype(jnp.float32)
    out_total[...] = total

    for step in range(2, count - 1):
        line_sum_step(step, *sums)

    columns = col_pair[chip].astype(jnp.float32)
    for k in range(1, chips):
        col_far_copy(k).wait_recv()
        columns += col_far[k - 1].astype(jnp.float32)
    col_sums[...] = columns.astype(jnp.bfloat16)

    def z_copy(k):
        other = lax.rem(place + k, count)
        return remote(
            col_sums.at[other], columns_out.at[place], z_sems.at[0, k], z_sems.at[1, k], (other, member)
        )

    for k in range(1, count):
        z_copy(k).start()
    columns_out[place] = col_sums[place]

    line_sum_end(*mixed_line, mixed_total)
    line_sum_end(*sums, normed_total)
    for j, other in others:
        mixed_copy(j, other).wait_send()
    for k in range(1, count):
        z_copy(k).wait_recv()
    for k in range(1, count):
        z_copy(k).wait_send()
    for k in range(chips):
        out_copy(None, k).wait_send()
        col_copy(k).wait_send()
    for k in range(1, chips):
        out_far_copy(k).wait_send()
        col_far_copy(k).wait_send()


def attention_backward(
    count, planes, heads, shard, branch, out_rows, own_cols, normed, heads_low, queries, pair, proj,
    spreader, combined, lse, turn_cos, turn_sin, gains,
):
    tokens = branch.shape[0]
    length = count * tokens
    width = (heads + 2) * HEAD_SIZE
    chips = planes // 2
    out_block = heads * HEAD_SIZE // planes
    low = jnp.bfloat16
    vmem = pl.BlockSpec(memory_space=pltpu.VMEM)
    anywhere = pl.BlockSpec(memory_space=pl.ANY)
    dma = pltpu.SemaphoreType.DMA
    return pl.pallas_call(
        functools.partial(backward_kernel, count, planes, tokens, heads, shard),
        out_shape=(
            jax.ShapeDtypeStruct((tokens, MODEL_WIDTH), jnp.float32),
            jax.ShapeDtypeStruct((out_block, MODEL_WIDTH), jnp.float32),
            jax.ShapeDtypeStruct((count, shard, width), low),
            jax.ShapeDtypeStruct((8, HEAD_SIZE), jnp.float32),
            jax.ShapeDtypeStruct((tokens, MODEL_WIDTH), jnp.float32),
            jax.ShapeDtypeStruct(combined.shape, low),
        ),
        in_specs=[vmem] + [anywhere] * 9 + [vmem] * 4,
        out_specs=(vmem,) * 5 + (anywhere,),
        scratch_shapes=[
            pltpu.VMEM(out_rows.shape, low),
            pltpu.VMEM(own_cols.shape, low),
            pltpu.VMEM(normed.shape, low),
            pltpu.VMEM(heads_low.shape, low),
            pltpu.VMEM(queries.shape, low),
            pltpu.VMEM(pair.shape, low),
            pltpu.VMEM(proj.shape, jnp.float32),
            dma((8,)),
            pltpu.VMEM((count, tokens, MODEL_WIDTH), low),
            dma((2, count)),
            dma((2, count)),
            pltpu.VMEM((heads, length, HEAD_SIZE), low),
            pltpu.VMEM((heads + 2, length, HEAD_SIZE), low),
            pltpu.VMEM((2, length, HEAD_SIZE), jnp.float32),
            pltpu.VMEM((planes, out_block, MODEL_WIDTH), low),
            pltpu.VMEM((chips, out_block, MODEL_WIDTH), low),
            pltpu.VMEM((chips - 1, out_block, MODEL_WIDTH), low),
            dma((4, chips)),
            pltpu.VMEM((count, planes, shard, width), low),
            pltpu.VMEM((chips, count, shard, width), low),
            pltpu.VMEM((chips - 1, count, shard, width), low),
            pltpu.VMEM((count, shard, width), low),
            dma((4, chips)),
            pltpu.VMEM((count, tokens, MODEL_WIDTH), low),
            pltpu.VMEM((count + 1, tokens, MODEL_WIDTH), low),
            dma((2, count)),
            dma((2, count)),
            dma((2, count)),
            pltpu.VMEM(spreader.shape, low),
            pltpu.VMEM((2,) + combined.shape[1:], low),
            pltpu.VMEM((count + 1, tokens, MODEL_WIDTH), low),
            dma((planes,)),
            dma((planes,)),
            dma((3,)),
            dma((2, count)),
            dma((2, count)),
        ],
        compiler_params=pltpu.CompilerParams(
            collective_id=3, has_side_effects=True, vmem_limit_bytes=VMEM_BYTES
        ),
        name="attention_backward",
    )(
        branch, out_rows, own_cols, normed, heads_low, queries, pair, proj, spreader, combined,
        lse, turn_cos, turn_sin, gains,
    )


def forward_kernel(
    count, planes, tokens, heads, shard, capacity, chunks,
    hidden_ref, routes_ref, small_ref, router_ref, qkv_ref, out_ref, cotangent_ref,
    turn_cos_ref, turn_sin_ref,
    hidden1_ref, mixed_ref, lse_ref, gains_ref, spreader_ref,
    router_out, own_cols_hbm, out_rows_hbm, normed_hbm, heads_hbm, query_hbm, pair_hbm, proj_hbm,
    grad_hbm, masks_hbm,
    column_send, own_cols, c_send, c_recv,
    out_rows, o_send, o_recv,
    hidden_full, h_send, h_recv,
    gains_all, gz_send, gz_recv, gd_send, gd_recv,
    router_all, rz_send, rz_recv, rd_send, rd_recv,
    places_all, p_send, p_recv,
    normed, proj, queries, pair, heads_low,
    grad_full, dy_send, dy_recv,
    grad_sent, d_send, d_recv, mask_sent, m_send, m_recv,
    branch, sums, rs_send, rs_recv, local_sems,
):
    place = lax.axis_index("seq")
    member = lax.axis_index("dp")
    core = lax.rem(member, 2)
    chip = member // 2
    chips = planes // 2
    partner = member + 1 - 2 * core
    length = count * tokens
    query_columns = heads * HEAD_SIZE
    replicas = count // KEY_VALUE_HEADS
    wide = MODEL_WIDTH // chunks
    slots = grad_sent.shape[2]
    rows = planes * slots
    low = jnp.bfloat16
    scale = HEAD_SIZE ** (-0.5)
    far_places = [(k, lax.rem(place + k, count)) for k in range(1, count)]
    far_chips = [(k, lax.rem(chip + k, chips)) for k in range(1, chips)]
    others = [(j, lax.rem(member + j, planes)) for j in range(1, planes)]

    hidden_full[place] = hidden_ref[...]
    gains_all[place, member] = small_ref[...]
    router_all[place, member] = router_ref[...]
    for part in range(count):
        head = part // replicas
        keys = QUERY_HEADS * HEAD_SIZE + head * HEAD_SIZE
        values = keys + KEY_VALUE_HEADS * HEAD_SIZE
        column_send[part, :, :query_columns] = qkv_ref[
            :, part * query_columns : (part + 1) * query_columns
        ]
        column_send[part, :, query_columns : query_columns + HEAD_SIZE] = qkv_ref[
            :, keys : keys + HEAD_SIZE
        ]
        column_send[part, :, query_columns + HEAD_SIZE :] = qkv_ref[:, values : values + HEAD_SIZE]
    lanes = lax.broadcasted_iota(jnp.int32, (tokens, places_all.shape[-1]), 1)
    named = jnp.zeros(lanes.shape, jnp.float32)
    for k in range(TOP):
        named += jnp.where(routes_ref[:, k : k + 1] == lanes, 1.0, 0.0)
    row_ids = lax.broadcasted_iota(jnp.int32, (tokens, tokens), 0)
    col_ids = lax.broadcasted_iota(jnp.int32, (tokens, tokens), 1)
    before = jnp.where(row_ids > col_ids, 1.0, 0.0).astype(low)
    earlier = dot_nn(before, named.astype(low)) + (place * capacity).astype(jnp.float32)
    places_all[place] = jnp.where(named > 0, earlier, -1.0).astype(low)
    for c in range(chunks):
        grad_full[c, place] = cotangent_ref[:, c * wide : (c + 1) * wide]

    greet([(place, other) for _, other in others] + [(other, member) for _, other in far_places])

    def column_copy(k, other):
        return remote(
            column_send.at[other], own_cols.at[place, member], c_send.at[0, k], c_recv.at[0, k],
            (other, member),
        )

    def gain_line(k, other):
        mine = gains_all.at[place, member]
        return remote(mine, mine, gz_send.at[k], gz_recv.at[k], (other, member))

    def router_line(k, other):
        mine = router_all.at[place, member]
        return remote(mine, mine, rz_send.at[k], rz_recv.at[k], (other, member))

    def places_line(k, other):
        mine = places_all.at[place]
        return remote(mine, mine, p_send.at[k], p_recv.at[k], (other, member))

    def out_copy(k, other):
        return remote(
            out_ref, out_rows.at[member], o_send.at[0, k], o_recv.at[0, k], (place, 2 * other + core)
        )

    def out_pair(k, other):
        source = out_ref if k == 0 else out_rows.at[2 * other + core]
        return remote(
            source, out_rows.at[2 * other + core], o_send.at[1, k], o_recv.at[1, k], (place, partner)
        )

    def block_copy(k, other):
        mine = own_cols.at[:, member]
        return remote(mine, mine, c_send.at[1, k], c_recv.at[1, k], (place, 2 * other + core))

    def block_pair(k, other):
        block = own_cols.at[:, 2 * other + core]
        return remote(block, block, c_send.at[2, k], c_recv.at[2, k], (place, partner))

    for k, other in far_places:
        gain_line(k, other).start()
        column_copy(k, other).start()
    for k, other in far_chips:
        out_copy(k, other).start()
    out_pair(0, chip).start()
    hidden_line = (count, place, member, hidden_full, h_send, h_recv)
    line_gather_step(0, *hidden_line)
    for k, other in far_places:
        places_line(k, other).start()
        router_line(k, other).start()
    own_cols[place, member] = column_send[place]
    out_rows[member] = out_ref[...]

    def gain_plane(j, other):
        mine = gains_all.at[:, member]
        return remote(mine, mine, gd_send.at[j], gd_recv.at[j], (place, other))

    def router_plane(j, other):
        mine = router_all.at[:, member]
        return remote(mine, mine, rd_send.at[j], rd_recv.at[j], (place, other))

    for k, other in far_places:
        gain_line(k, other).wait_recv()
    for j, other in others:
        gain_plane(j, other).start()
    for k, other in far_places:
        column_copy(k, other).wait_recv()
    for k, other in far_chips:
        block_copy(k, other).start()
    block_pair(0, chip).start()
    line_gather_step(1, *hidden_line)

    for k, other in far_places:
        places_line(k, other).wait_recv()
    experts = places_all.shape[-1]
    pick_rows = lax.broadcasted_iota(jnp.int32, (experts, rows), 0)
    pick_cols = lax.broadcasted_iota(jnp.int32, (experts, rows), 1)
    slot_ids = lax.broadcasted_iota(jnp.int32, (length, rows), 1)
    slot_base = jnp.zeros((length, rows), jnp.int32)
    choose = jnp.zeros((experts, rows), jnp.float32)
    for other in range(planes):
        inside = (pick_cols >= other * slots) & (pick_cols < (other + 1) * slots)
        choose += jnp.where(inside & (pick_rows == place * planes + other), 1.0, 0.0)
        slot_base = jnp.where(slot_ids >= other * slots, other * slots, slot_base)
    wanted = dot_nn(places_all[...].reshape(length, experts), choose.astype(low))
    spreader_ref[...] = jnp.where(
        wanted == (slot_ids - slot_base).astype(jnp.float32), 1.0, 0.0
    ).astype(low)
    mask_full = jnp.where(places_all[...].reshape(length, experts).astype(jnp.float32) >= 0, 1.0, 0.0)
    mask_sent[...] = (
        dot_tn(spreader_ref[...], mask_full.astype(low)).astype(low).reshape(mask_sent.shape)
    )

    for k, other in far_places:
        router_line(k, other).wait_recv()
    for j, other in others:
        router_plane(j, other).start()

    def mask_copy(j, other):
        return remote(
            mask_sent.at[other], masks_hbm.at[member], m_send.at[j], m_recv.at[j], (place, other)
        )

    for j, other in others:
        mask_copy(j, other).start()
    masks_own = pltpu.make_async_copy(mask_sent.at[member], masks_hbm.at[member], local_sems.at[0])
    masks_own.start()

    for k, other in far_chips:
        out_copy(k, other).wait_recv()
    for k, other in far_chips:
        out_pair(k, lax.rem(chip + chips - k, chips)).start()
    for step in range(2, count):
        line_gather_step(step, *hidden_line)

    def grad_line(c):
        return (count, place, member, grad_full.at[c], dy_send.at[c], dy_recv.at[c])

    def grad_copy(c, j, other):
        return remote(
            grad_sent.at[c, other], grad_hbm.at[c, member], d_send.at[c, j], d_recv.at[c, j], (place, other)
        )

    def grad_own(c):
        return pltpu.make_async_copy(
            grad_sent.at[c, member], grad_hbm.at[c, member], local_sems.at[16 + c]
        )

    def grad_tick(tick):
        for c in range(chunks):
            step = tick - c
            if 0 <= step < count:
                line_gather_step(step, *grad_line(c))
            if step == count - 1:
                picked = dot_tn(spreader_ref[...], grad_full[c].reshape(length, wide)).astype(low)
                grad_sent[c] = picked.reshape(planes, slots, wide)
                for j, other in others:
                    grad_copy(c, j, other).start()
                grad_own(c).start()

    ticks = list(range(chunks + count - 1))
    grad_tick(ticks.pop(0))

    for j, other in others:
        gain_plane(j, other).wait_recv()
    per_row = HEAD_SIZE // shard
    small_total = jnp.sum(gains_all[...].astype(jnp.float32), axis=(0, 1))
    gain_rows = []
    for row in range(2):
        parts = []
        for group in range(MODEL_WIDTH // HEAD_SIZE):
            part = jnp.zeros((1, HEAD_SIZE), jnp.float32)
            for index in range(group * per_row, (group + 1) * per_row):
                part += gains_all[index // planes, index % planes, row : row + 1, :].astype(jnp.float32)
            parts.append(part)
        gain_rows.append(jnp.concatenate(parts, axis=1))
    gains_ref[0:1, :] = gain_rows[0]
    gains_ref[1:2, :] = gain_rows[1]
    gain_query = small_total[2:3, :]
    gain_key = small_total[3:4, :]
    gains_ref[2:3, :HEAD_SIZE] = gain_query
    gains_ref[3:4, :HEAD_SIZE] = gain_key

    def normalize(values, gain):
        return (
            values
            * lax.rsqrt(jnp.mean(values * values, axis=-1, keepdims=True) + EPSILON)
            * gain
        )

    for block in range(count):
        values = hidden_full[block].astype(jnp.float32)
        normed[block * tokens : (block + 1) * tokens, :] = normalize(values, gain_rows[0]).astype(low)
    stores = [pltpu.make_async_copy(normed, normed_hbm, local_sems.at[1])]
    stores[-1].start()

    for k, other in far_chips:
        block_copy(k, other).wait_recv()
    for k, other in far_chips:
        block_pair(k, lax.rem(chip + chips - k, chips)).start()
    block_pair(0, chip).wait_recv()
    for k, other in far_chips:
        block_pair(k, lax.rem(chip + chips - k, chips)).wait_recv()
    weights = own_cols[...].reshape(MODEL_WIDTH, query_columns + 2 * HEAD_SIZE)
    stores.append(pltpu.make_async_copy(own_cols, own_cols_hbm, local_sems.at[2]))
    stores[-1].start()

    def prepare(values, gain):
        turned = normalize(values, gain)
        return turned * turn_cos_ref[...] + pltpu.roll(turned, HEAD_SIZE // 2, 1) * turn_sin_ref[...]

    paired = dot_nn(normed[...], weights[:, query_columns:])
    proj[heads] = paired[:, :HEAD_SIZE]
    proj[heads + 1] = paired[:, HEAD_SIZE:]
    pair[0] = prepare(paired[:, :HEAD_SIZE], gain_key).astype(low)
    pair[1] = paired[:, HEAD_SIZE:].astype(low)
    projected = dot_nn(normed[...], weights[:, :query_columns])
    for head in range(heads):
        proj[head] = projected[:, head * HEAD_SIZE : (head + 1) * HEAD_SIZE]
    value_turned = jnp.transpose(paired[:, HEAD_SIZE:]).astype(low)
    stores.append(pltpu.make_async_copy(proj, proj_hbm, local_sems.at[3]))
    stores[-1].start()
    stores.append(pltpu.make_async_copy(pair, pair_hbm, local_sems.at[4]))
    stores[-1].start()
    block_rows = min(256, length)

    def one_head(head, carry):
        queries[head] = prepare(proj[head], gain_query).astype(low)
        for block in range(length // block_rows):
            begin, end = block * block_rows, (block + 1) * block_rows
            scores = dot_nt(pair[0, :end, :], queries[head, begin:end, :]) * scale
            key_ids = lax.broadcasted_iota(jnp.int32, (end, block_rows), 0)
            query_ids = lax.broadcasted_iota(jnp.int32, (end, block_rows), 1) + begin
            scores = jnp.where(key_ids <= query_ids, scores, FILLER)
            top = jnp.max(scores, axis=0, keepdims=True)
            powers = jnp.exp(scores - top)
            total = jnp.sum(powers, axis=0, keepdims=True)
            lse_ref[head, :, begin:end] = top + jnp.log(total)
            probs = (powers * (1.0 / total)).astype(low)
            mixed = dot_nn(value_turned[:, :end], probs)
            heads_low[head, begin:end, :] = jnp.transpose(mixed).astype(low)
        return carry

    halves = 4
    for part in range(halves):
        lax.fori_loop(part * heads // halves, (part + 1) * heads // halves, one_head, 0)
        if ticks:
            grad_tick(ticks.pop(0))
    stores.append(pltpu.make_async_copy(queries, query_hbm, local_sems.at[5]))
    stores[-1].start()
    stores.append(pltpu.make_async_copy(heads_low, heads_hbm, local_sems.at[6]))
    stores[-1].start()

    out_pair(0, chip).wait_recv()
    for k, other in far_chips:
        out_pair(k, lax.rem(chip + chips - k, chips)).wait_recv()
    out_all = out_rows[...].reshape(query_columns, MODEL_WIDTH)
    stores.append(pltpu.make_async_copy(out_rows, out_rows_hbm, local_sems.at[7]))
    stores[-1].start()

    def project(block, carry):
        at = pl.ds(pl.multiple_of(block * tokens, tokens), tokens)
        mixed = jnp.concatenate([heads_low[head, at, :] for head in range(heads)], axis=1)
        branch[block] = dot_nn(mixed, out_all).astype(low)
        return carry

    lax.fori_loop(0, count, project, 0)
    line = (count, place, member, branch, sums, rs_send, rs_recv)
    for step in range(count - 1):
        line_sum_step(step, *line)
        for _ in range(-(-len(ticks) // (count - 1 - step))):
            grad_tick(ticks.pop(0))
    line_sum_end(*line, hidden1_ref)
    hidden1 = hidden_ref[...].astype(jnp.float32) + hidden1_ref[...]
    hidden1_ref[...] = hidden1
    mixed_ref[...] = normalize(hidden1, gain_rows[1]).astype(low)

    for j, other in others:
        router_plane(j, other).wait_recv()
    router_out[...] = router_all[...].reshape(router_out.shape)
    for j, other in others:
        mask_copy(j, other).wait_recv()
        for c in range(chunks):
            grad_copy(c, j, other).wait_recv()
    for k, other in far_places:
        gain_line(k, other).wait_send()
        column_copy(k, other).wait_send()
        places_line(k, other).wait_send()
        router_line(k, other).wait_send()
    for k, other in far_chips:
        out_copy(k, other).wait_send()
        block_copy(k, other).wait_send()
        out_pair(k, other).wait_send()
        block_pair(k, other).wait_send()
    out_pair(0, chip).wait_send()
    block_pair(0, chip).wait_send()
    for j, other in others:
        gain_plane(j, other).wait_send()
        router_plane(j, other).wait_send()
        mask_copy(j, other).wait_send()
        for c in range(chunks):
            grad_copy(c, j, other).wait_send()
    for c in range(chunks):
        grad_own(c).wait()
        line_gather_end(*grad_line(c))
    line_gather_end(*hidden_line)
    masks_own.wait()
    for store in stores:
        store.wait()


def attention_forward(
    count, planes, heads, shard, capacity, slots, chunks,
    hidden, routes, small, router, qkv, out_weight, cotangent, turn_cos, turn_sin,
):
    tokens = hidden.shape[0]
    length = count * tokens
    width = (heads + 2) * HEAD_SIZE
    chips = planes // 2
    rows = planes * slots
    wide = MODEL_WIDTH // chunks
    experts = router.shape[-1]
    small_rows = small.shape[0]
    out_block = out_weight.shape[0]
    low, full = jnp.bfloat16, jnp.float32
    vmem = pl.BlockSpec(memory_space=pltpu.VMEM)
    anywhere = pl.BlockSpec(memory_space=pl.ANY)
    dma = pltpu.SemaphoreType.DMA
    shape = jax.ShapeDtypeStruct
    return pl.pallas_call(
        functools.partial(forward_kernel, count, planes, tokens, heads, shard, capacity, chunks),
        out_shape=(
            shape((tokens, MODEL_WIDTH), full),
            shape((tokens, MODEL_WIDTH), low),
            shape((heads, 1, length), full),
            shape((8, MODEL_WIDTH), full),
            shape((length, rows), low),
            shape((MODEL_WIDTH, experts), low),
            shape((count, planes, shard, width), low),
            shape((planes, out_block, MODEL_WIDTH), low),
            shape((length, MODEL_WIDTH), low),
            shape((heads, length, HEAD_SIZE), low),
            shape((heads, length, HEAD_SIZE), low),
            shape((2, length, HEAD_SIZE), low),
            shape((heads + 2, length, HEAD_SIZE), full),
            shape((chunks, planes, slots, wide), low),
            shape((planes, slots, experts), low),
        ),
        in_specs=[vmem] * 9,
        out_specs=(vmem,) * 6 + (anywhere,) * 9,
        scratch_shapes=[
            pltpu.VMEM((count, shard, width), low),
            pltpu.VMEM((count, planes, shard, width), low),
            dma((3, max(count, chips))),
            dma((3, max(count, chips))),
            pltpu.VMEM((planes, out_block, MODEL_WIDTH), low),
            dma((2, chips)),
            dma((2, chips)),
            pltpu.VMEM((count, tokens, MODEL_WIDTH), low),
            dma((2, count)),
            dma((2, count)),
            pltpu.VMEM((count, planes, small_rows, HEAD_SIZE), low),
            dma((count,)),
            dma((count,)),
            dma((planes,)),
            dma((planes,)),
            pltpu.VMEM((count, planes, shard, experts), low),
            dma((count,)),
            dma((count,)),
            dma((planes,)),
            dma((planes,)),
            pltpu.VMEM((count, tokens, experts), low),
            dma((count,)),
            dma((count,)),
            pltpu.VMEM((length, MODEL_WIDTH), low),
            pltpu.VMEM((heads + 2, length, HEAD_SIZE), full),
            pltpu.VMEM((heads, length, HEAD_SIZE), low),
            pltpu.VMEM((2, length, HEAD_SIZE), low),
            pltpu.VMEM((heads, length, HEAD_SIZE), low),
            pltpu.VMEM((chunks, count, tokens, wide), low),
            dma((chunks, 2, count)),
            dma((chunks, 2, count)),
            pltpu.VMEM((chunks, planes, slots, wide), low),
            dma((chunks, planes)),
            dma((chunks, planes)),
            pltpu.VMEM((planes, slots, experts), low),
            dma((planes,)),
            dma((planes,)),
            pltpu.VMEM((count, tokens, MODEL_WIDTH), low),
            pltpu.VMEM((count + 1, tokens, MODEL_WIDTH), low),
            dma((2, count)),
            dma((2, count)),
            dma((16 + chunks,)),
        ],
        compiler_params=pltpu.CompilerParams(
            collective_id=1, has_side_effects=True, vmem_limit_bytes=VMEM_BYTES
        ),
        name="attention_forward",
    )(hidden, routes, small, router, qkv, out_weight, cotangent, turn_cos, turn_sin)


def expert_kernel(
    count, planes, tokens, slots, chunks,
    mixed_ref, masks_ref, spreader_hbm, grad_hbm, router_hbm, in_hbm, back_hbm,
    total_ref, gate_total_ref, grad_in_hbm, grad_back_hbm, combined_hbm,
    spreader, grad_rows, router, weight_in, weight_back, local_sems,
    full, ag_send, ag_recv,
    sent, arrived, x_send, x_recv,
    gate_up, act, grad_gate_up, logits,
    back_arrived, b_send, b_recv,
    gate_sent, gate_arrived, gate_own, gate_sums, g_send, g_recv, gs_send, gs_recv,
    sums, rs_send, rs_recv, tile_sems, combined_sems,
):
    place = lax.axis_index("seq")
    member = lax.axis_index("dp")
    rows = planes * slots
    length = count * tokens
    wide = MODEL_WIDTH // chunks
    half = rows // 2
    own_expert = place * planes + member
    low = jnp.bfloat16

    loads = [
        pltpu.make_async_copy(spreader_hbm, spreader, local_sems.at[0]),
        pltpu.make_async_copy(router_hbm, router, local_sems.at[1]),
        pltpu.make_async_copy(in_hbm, weight_in, local_sems.at[2]),
        pltpu.make_async_copy(grad_hbm, grad_rows, local_sems.at[3]),
    ] + [
        pltpu.make_async_copy(
            back_hbm.at[:, pl.ds(c * wide, wide)], weight_back.at[c], local_sems.at[4 + c]
        )
        for c in range(chunks)
    ]
    for load in loads:
        load.start()
    for c in range(chunks):
        full[c, place] = mixed_ref[:, c * wide : (c + 1) * wide]
    greet(
        [(place, lax.rem(member + j, planes)) for j in range(1, planes)]
        + [(lax.rem(place + k, count), member) for k in range(1, count)]
    )

    def line(c):
        return (count, place, member, full.at[c], ag_send.at[c], ag_recv.at[c])

    def row_copy(c, j):
        other = lax.rem(member + j, planes)
        return remote(
            sent.at[c, other], arrived.at[c, member], x_send.at[c, j], x_recv.at[c, j], (place, other)
        )

    for c in range(chunks):
        line_gather_step(0, *line(c))
    gate_up[...] = jnp.zeros_like(gate_up)
    logits[...] = jnp.zeros_like(logits)
    loads[0].wait()

    def dispatch(c, carry):
        for step in range(1, count):
            line_gather_step(step, *line(c))
        picked = dot_tn(spreader[...], full[c].reshape(length, wide)).astype(low)
        sent[c] = picked.reshape(planes, slots, wide)
        for j in range(1, planes):
            row_copy(c, j).start()
        arrived[c, member] = sent[c, member]
        return carry

    lax.fori_loop(0, chunks, dispatch, 0)
    for load in loads[1:]:
        load.wait()

    def forward(c, carry):
        for j in range(1, planes):
            row_copy(c, j).wait_recv()
        part = pl.ds(pl.multiple_of(c * wide, wide), wide)
        x = arrived[c].reshape(rows, wide)
        for piece in range(2):
            at = slice(piece * half, (piece + 1) * half)
            gate_up[at, :] += dot_nn(x[at], weight_in[part, :])
            logits[at, :] += dot_nn(x[at], router[part, :])
        return carry

    lax.fori_loop(0, chunks, forward, 0)

    def settle(c, carry):
        for j in range(1, planes):
            row_copy(c, j).wait_send()
        line_gather_end(*line(c))
        return carry

    lax.fori_loop(0, chunks, settle, 0)

    mask = masks_ref[:, : logits.shape[-1]].astype(jnp.float32)
    shifted = jnp.where(mask > 0, logits[...], FILLER)
    powers = jnp.where(mask > 0, jnp.exp(shifted - jnp.max(shifted, axis=-1, keepdims=True)), 0.0)
    powers_total = jnp.sum(powers, axis=-1, keepdims=True)
    lanes = lax.broadcasted_iota(jnp.int32, powers.shape, 1)
    own = jnp.sum(jnp.where(lanes == own_expert, powers, 0.0), axis=-1, keepdims=True)
    gate = own / jnp.where(powers_total > 0, powers_total, 1.0)
    gate_column = logits
    gate_column[...] = jnp.broadcast_to(gate, gate_column.shape)

    blocks = 4 if rows % 64 == 0 else 2
    step_rows = rows // blocks

    def backward(index, carry):
        at = pl.ds(pl.multiple_of(index * step_rows, step_rows), step_rows)
        scale = gate_column[at, 0:1]
        grad_act = jnp.zeros((step_rows, FF), jnp.float32)
        for c in range(chunks):
            scaled = (grad_rows[c, at, :].astype(jnp.float32) * scale).astype(low)
            grad_act += dot_nt(scaled, weight_back[c])
        gate_part = gate_up[at, :FF]
        up_part = gate_up[at, FF:]
        chance = jax.nn.sigmoid(gate_part)
        silu = gate_part * chance
        act[at, :] = (silu * up_part).astype(low)
        slope = chance + silu * (1.0 - chance)
        grad_gate_up[at, :FF] = (grad_act * up_part * slope).astype(low)
        grad_gate_up[at, FF:] = (grad_act * silu).astype(low)
        return carry

    lax.fori_loop(0, blocks, backward, 0)

    def back_copy(c, j):
        other = lax.rem(member + j, planes)
        return remote(
            sent.at[c, other], back_arrived.at[c, member], b_send.at[c, j], b_recv.at[c, j], (place, other)
        )

    def gate_copy(j):
        other = lax.rem(member + j, planes)
        return remote(
            gate_sent.at[other], gate_arrived.at[member], g_send.at[j], g_recv.at[j], (place, other)
        )

    def send_back(c, carry):
        part = pl.ds(pl.multiple_of(c * wide, wide), wide)
        back = dot_nt(grad_gate_up[...], weight_in[part, :]).astype(low)
        sent[c] = back.reshape(planes, slots, wide)
        for j in range(1, planes):
            back_copy(c, j).start()
        back_arrived[c, member] = sent[c, member]
        return carry

    lax.fori_loop(0, chunks, send_back, 0)

    in_tiles = [gate_up.at[part * wide : (part + 1) * wide, :FF] for part in range(2)]
    back_tile = gate_up.at[:FF, FF : FF + wide]

    def in_copy(slot, c, part):
        return pltpu.make_async_copy(
            in_tiles[slot],
            grad_in_hbm.at[pl.ds(pl.multiple_of(c * wide, wide), wide), pl.ds(part * FF, FF)],
            tile_sems.at[slot],
        )

    def in_gradient(c, carry):
        x = arrived[c].reshape(rows, wide)
        for part in range(2):

            @pl.when(c > 0)
            def _():
                in_copy(part, c, part).wait()

            in_tiles[part][...] = dot_tn(x, grad_gate_up[:, part * FF : (part + 1) * FF])
            in_copy(part, c, part).start()
        return carry

    lax.fori_loop(0, chunks, in_gradient, 0)

    def combined_copy(c):
        return pltpu.make_async_copy(arrived.at[c], combined_hbm.at[c], combined_sems.at[c])

    def outputs(c, grad_gate):
        result = dot_nn(act[...], weight_back[c]).astype(low).astype(jnp.float32)
        grads = grad_rows[c].astype(jnp.float32)
        scale = gate_column[:, 0:1]
        grad_rows[c] = (grads * scale).astype(low)
        arrived[c] = (result * scale).astype(low).reshape(planes, slots, wide)
        combined_copy(c).start()
        return grad_gate + jnp.sum(result * grads, axis=-1, keepdims=True)

    grad_gate = lax.fori_loop(0, chunks, outputs, jnp.zeros((rows, 1), jnp.float32))
    high = grad_gate.astype(low).astype(jnp.float32)
    rest = grad_gate - high
    experts = count * planes
    wide_lanes = lax.broadcasted_iota(jnp.int32, (rows, gate_sent.shape[-1]), 1)
    columns = jnp.where(
        wide_lanes == own_expert, high, jnp.where(wide_lanes == own_expert + experts, rest, 0.0)
    )
    gate_sent[...] = columns.astype(low).reshape(gate_sent.shape)
    for j in range(1, planes):
        gate_copy(j).start()
    gate_arrived[member] = gate_sent[member]

    def back_tile_copy(c):
        return pltpu.make_async_copy(
            back_tile,
            grad_back_hbm.at[:, pl.ds(pl.multiple_of(c * wide, wide), wide)],
            tile_sems.at[2],
        )

    def back_gradient(c, carry):
        result = dot_tn(act[...], grad_rows[c])

        @pl.when(c > 0)
        def _():
            back_tile_copy(c).wait()

        back_tile[...] = result
        back_tile_copy(c).start()
        return carry

    lax.fori_loop(0, chunks, back_gradient, 0)

    def sums_line(c):
        return (count, place, member, full.at[c], sums.at[c], rs_send.at[c], rs_recv.at[c])

    for c in range(chunks):
        for j in range(1, planes):
            back_copy(c, j).wait_recv()
        own_sums = dot_nn(spreader[...], back_arrived[c].reshape(rows, wide)).astype(low)
        full[c] = own_sums.reshape(count, tokens, wide)
        for step in range(count - 1):
            line_sum_step(step, *sums_line(c))
    for j in range(1, planes):
        gate_copy(j).wait_recv()
    extra = gate_sent.shape[-1]
    gate_own[...] = (
        dot_nn(spreader[...], gate_arrived[...].reshape(rows, extra))
        .astype(low)
        .reshape(count, tokens, extra)
    )
    gate_line = (count, place, member, gate_own, gate_sums, gs_send, gs_recv)
    for step in range(count - 1):
        line_sum_step(step, *gate_line)
    for c in range(chunks):
        line_sum_end(*sums_line(c), total_ref.at[:, c * wide : (c + 1) * wide])
    line_sum_end(*gate_line, gate_total_ref)
    for c in range(chunks):
        for j in range(1, planes):
            back_copy(c, j).wait_send()
        combined_copy(c).wait()
    for j in range(1, planes):
        gate_copy(j).wait_send()
    in_copy(0, 0, 0).wait()
    in_copy(1, 0, 1).wait()
    back_tile_copy(0).wait()


def expert_layer(
    count, planes, mixed, masks, spreader, grad_rows, router, weight_in, weight_back
):
    tokens = mixed.shape[0]
    length = count * tokens
    chunks, rows, wide = grad_rows.shape
    slots = rows // planes
    extra = -(-2 * count * planes // 128) * 128
    experts = router.shape[-1]
    low = jnp.bfloat16
    vmem = pl.BlockSpec(memory_space=pltpu.VMEM)
    anywhere = pl.BlockSpec(memory_space=pl.ANY)
    dma = pltpu.SemaphoreType.DMA
    return pl.pallas_call(
        functools.partial(expert_kernel, count, planes, tokens, slots, chunks),
        out_shape=(
            jax.ShapeDtypeStruct((tokens, MODEL_WIDTH), jnp.float32),
            jax.ShapeDtypeStruct((tokens, extra), jnp.float32),
            jax.ShapeDtypeStruct(weight_in.shape, jnp.float32),
            jax.ShapeDtypeStruct(weight_back.shape, jnp.float32),
            jax.ShapeDtypeStruct((chunks, planes, slots, wide), low),
        ),
        in_specs=[vmem] * 2 + [anywhere] * 5,
        out_specs=(vmem, vmem, anywhere, anywhere, anywhere),
        scratch_shapes=[
            pltpu.VMEM(spreader.shape, low),
            pltpu.VMEM(grad_rows.shape, low),
            pltpu.VMEM(router.shape, low),
            pltpu.VMEM(weight_in.shape, low),
            pltpu.VMEM((chunks, FF, wide), low),
            dma((4 + chunks,)),
            pltpu.VMEM((chunks, count, tokens, wide), low),
            dma((chunks, 2, count)),
            dma((chunks, 2, count)),
            pltpu.VMEM((chunks, planes, slots, wide), low),
            pltpu.VMEM((chunks, planes, slots, wide), low),
            dma((chunks, planes)),
            dma((chunks, planes)),
            pltpu.VMEM((rows, 2 * FF), jnp.float32),
            pltpu.VMEM((rows, FF), low),
            pltpu.VMEM((rows, 2 * FF), low),
            pltpu.VMEM((rows, experts), jnp.float32),
            pltpu.VMEM((chunks, planes, slots, wide), low),
            dma((chunks, planes)),
            dma((chunks, planes)),
            pltpu.VMEM((planes, slots, extra), low),
            pltpu.VMEM((planes, slots, extra), low),
            pltpu.VMEM((count, tokens, extra), low),
            pltpu.VMEM((count + 1, tokens, extra), low),
            dma((planes,)),
            dma((planes,)),
            dma((2, count)),
            dma((2, count)),
            pltpu.VMEM((chunks, count + 1, tokens, wide), low),
            dma((chunks, 2, count)),
            dma((chunks, 2, count)),
            dma((3,)),
            dma((chunks,)),
        ],
        compiler_params=pltpu.CompilerParams(
            collective_id=2, has_side_effects=True, vmem_limit_bytes=VMEM_BYTES
        ),
        name="expert_layer",
    )(mixed, masks, spreader, grad_rows, router, weight_in, weight_back)


def small_kernel(
    count, chips, own_ref, total_ref, line_got, line_sum, chip_got, core_sum, core_got,
    z_send, z_recv, c_send, c_recv, p_send, p_recv,
):
    place = lax.axis_index("seq")
    member = lax.axis_index("dp")
    core = lax.rem(member, 2)
    chip = member // 2
    partner = member + 1 - 2 * core
    far_places = [lax.rem(place + k, count) for k in range(1, count)]
    far_chips = [lax.rem(chip + k, chips) for k in range(1, chips)]
    greet(
        [(other, member) for other in far_places]
        + [(place, 2 * other + core) for other in far_chips]
        + [(place, partner)]
    )
    copies = [
        remote(own_ref.at[other], line_got.at[k], z_send.at[k], z_recv.at[k], (other, member))
        for k, other in enumerate(far_places)
    ]
    for copy in copies:
        copy.start()
    total = own_ref[place]
    for k, copy in enumerate(copies):
        copy.wait_recv()
        total += line_got[k]
    line_sum[...] = total
    chip_copies = [
        remote(line_sum.at[other], chip_got.at[k], c_send.at[k], c_recv.at[k], (place, 2 * other + core))
        for k, other in enumerate(far_chips)
    ]
    for copy in chip_copies:
        copy.start()
    mine = line_sum[chip]
    for k, copy in enumerate(chip_copies):
        copy.wait_recv()
        mine += chip_got[k]
    core_sum[...] = mine
    pair = remote(core_sum, core_got, p_send, p_recv, (place, partner))
    pair.start()
    pair.wait_recv()
    total_ref[...] = core_sum[...] + core_got[...]
    pair.wait_send()
    for copy in copies + chip_copies:
        copy.wait_send()


def small_sums(count, chips, own):
    shape = own.shape[2:]
    vmem = pl.BlockSpec(memory_space=pltpu.VMEM)
    dma = pltpu.SemaphoreType.DMA
    kind = jnp.float32
    return pl.pallas_call(
        functools.partial(small_kernel, count, chips),
        out_shape=jax.ShapeDtypeStruct(shape, kind),
        in_specs=[vmem],
        out_specs=vmem,
        scratch_shapes=[
            pltpu.VMEM((count - 1, chips) + shape, kind),
            pltpu.VMEM((chips,) + shape, kind),
            pltpu.VMEM((chips - 1,) + shape, kind),
            pltpu.VMEM(shape, kind),
            pltpu.VMEM(shape, kind),
            dma((count - 1,)),
            dma((count - 1,)),
            dma((chips - 1,)),
            dma((chips - 1,)),
            dma(()),
            dma(()),
        ],
        compiler_params=pltpu.CompilerParams(collective_id=4, has_side_effects=True),
        name="small_sums",
    )(own)


def rms_norm(values, gain):
    return values * lax.rsqrt(jnp.mean(values * values, axis=-1, keepdims=True) + EPSILON) * gain


def turn_tables(length):
    half = HEAD_SIZE // 2
    freqs = np.float32(ROPE_BASE) ** (-(np.arange(half, dtype=np.float32) * np.float32(2 / HEAD_SIZE)))
    angles = np.arange(length, dtype=np.float32)[:, None] * freqs[None, :]
    cosine, sine = np.cos(angles), np.sin(angles)
    return (
        jnp.asarray(np.concatenate([cosine, cosine], axis=1), jnp.float32),
        jnp.asarray(np.concatenate([-sine, sine], axis=1), jnp.float32),
    )


def inner_rows(left, right):
    return dot_tn(left, right)


def outer_cols(left, right):
    return dot_nt(left, right)


def masked_softmax(logits, mask):
    shifted = jnp.where(mask > 0, logits, FILLER)
    top = jnp.max(shifted, axis=-1, keepdims=True)
    powers = jnp.where(mask > 0, jnp.exp(shifted - top), 0.0)
    total = jnp.sum(powers, axis=-1, keepdims=True)
    return powers / jnp.where(total > 0, total, 1.0)


def body(
    hidden_in,
    routes,
    norm1_gain,
    query_gain,
    key_gain,
    qkv_weight,
    out_weight,
    norm2_gain,
    router,
    gate_up_weight,
    down_weight,
    cotangent,
):
    tokens = hidden_in.shape[1]
    sequence_number = lax.axis_size("seq")
    planes = lax.axis_size("dp")
    devices = sequence_number * planes
    group = lax.axis_index("seq")
    member = lax.axis_index("dp")
    index = group * planes + member
    heads = QUERY_HEADS // sequence_number
    query_columns = heads * HEAD_SIZE
    head_replicas = sequence_number // KEY_VALUE_HEADS
    capacity = (tokens * TOP * 9 + 8 * devices - 1) // (8 * devices)
    slots = -(-sequence_number * capacity // 16) * 16
    chunks = 4
    sequence_length = sequence_number * tokens
    shard = norm1_gain.shape[0]
    small_shard = query_gain.shape[0]
    lane_count = -(-devices // 128) * 128

    def placed(values):
        width = values.shape[0]
        at = jnp.arange(HEAD_SIZE, dtype=jnp.int32) // width == index % (HEAD_SIZE // width)
        return jnp.where(at, jnp.tile(values, HEAD_SIZE // width), jnp.zeros((), values.dtype))

    small = jnp.stack([placed(value) for value in (norm1_gain, norm2_gain, query_gain, key_gain)])
    small = jnp.pad(small, ((0, 12), (0, 0)))
    turn_cos, turn_sin = turn_tables(sequence_length)
    (
        hidden1, mixed_low, lse, gains, spreader, full_router, own_cols, out_rows, normed_full,
        heads_low, queries, pair, projected, grad_rows, masks,
    ) = attention_forward(
        sequence_number,
        planes,
        heads,
        shard,
        capacity,
        slots,
        chunks,
        hidden_in[0],
        routes[0],
        small,
        jnp.pad(router, ((0, 0), (0, lane_count - devices))),
        qkv_weight,
        out_weight,
        cotangent[0],
        turn_cos,
        turn_sin,
    )
    gain_one, gain_two = gains[0], gains[1]
    residual = hidden_in[0].astype(jnp.float32)

    grad_sent, gate_sent, grad_weight_in, grad_weight_back, combined_rows = expert_layer(
        sequence_number,
        planes,
        mixed_low,
        masks.reshape(planes * slots, lane_count),
        spreader,
        grad_rows.reshape(chunks, planes * slots, MODEL_WIDTH // chunks),
        full_router,
        gate_up_weight[0],
        down_weight[0],
    )
    grad_result = cotangent[0].astype(jnp.float32)
    own_mask = jnp.sum(
        (routes[0][:, :, None] == jnp.arange(devices, dtype=jnp.int32)[None, None, :]).astype(
            jnp.float32
        ),
        axis=1,
    )
    full_router = full_router[:, :devices]
    logits = jnp.dot(mixed_low, full_router, preferred_element_type=jnp.float32)
    gates = masked_softmax(logits, own_mask)
    grad_gates = (
        gate_sent[:, :devices] + gate_sent[:, devices : 2 * devices]
    )
    grad_logits = (
        gates * (grad_gates - jnp.sum(gates * grad_gates, axis=-1, keepdims=True))
    ).astype(jnp.bfloat16)
    grad_mixed = grad_sent + outer_cols(grad_logits, full_router)
    grad_router_t = inner_rows(grad_logits, mixed_low)
    _, pull_two = jax.vjp(rms_norm, hidden1, gain_two)
    grad_hidden_norm, grad_gain_two = pull_two(grad_mixed)
    grad_hidden1 = grad_result + grad_hidden_norm
    grad_branch = grad_hidden1.astype(jnp.bfloat16)
    out_block = query_columns // planes
    heads_low = jnp.transpose(
        heads_low.reshape(heads, sequence_length, HEAD_SIZE // out_block, out_block), (0, 2, 1, 3)
    ).reshape(planes, sequence_length, out_block)
    (
        normed_total, shard_out, column_sums, gain_totals, mixed_total, _,
    ) = attention_backward(
        sequence_number,
        planes,
        heads,
        shard,
        grad_branch,
        out_rows,
        own_cols,
        normed_full,
        heads_low,
        queries,
        pair,
        projected,
        spreader,
        combined_rows,
        lse,
        turn_cos,
        turn_sin,
        gains[2:4, :HEAD_SIZE],
    )
    output = (hidden1 + mixed_total).astype(jnp.bfloat16)
    column_sums = column_sums.astype(jnp.float32)
    shard_query = jnp.transpose(column_sums[:, :, :query_columns], (1, 0, 2)).reshape(
        shard, QUERY_HEADS * HEAD_SIZE
    )
    shard_paired = jnp.sum(
        column_sums[:, :, query_columns:].reshape(
            KEY_VALUE_HEADS, head_replicas, shard, 2, HEAD_SIZE
        ),
        axis=1,
    )
    shard_paired = jnp.transpose(shard_paired, (1, 2, 0, 3)).reshape(
        shard, 2 * KEY_VALUE_HEADS * HEAD_SIZE
    )
    shard_qkv = jnp.concatenate([shard_query, shard_paired], axis=1)
    _, pull_one = jax.vjp(rms_norm, residual, gain_one)
    grad_residual_norm, grad_gain_one = pull_one(normed_total)
    grad_input = grad_hidden1 + grad_residual_norm

    chips = planes // 2

    def by_chip(values):
        columns = values.reshape(-1, sequence_number, chips, values.shape[-1] // devices * 2)
        columns = jnp.pad(columns, ((0, 0),) * 3 + ((0, 2 * shard - columns.shape[-1]),))
        return jnp.transpose(columns, (1, 2, 0, 3))

    small = jnp.concatenate(
        [
            by_chip(grad_router_t),
            by_chip(grad_gain_two),
            by_chip(grad_gain_one),
            by_chip(gain_totals[0]),
            by_chip(gain_totals[1]),
            jnp.zeros((sequence_number, chips, 4, 2 * shard), jnp.float32),
        ],
        axis=2,
    )
    small = small_sums(sequence_number, chips, small)
    core = lax.rem(member, 2)
    small_core = lax.dynamic_slice_in_dim(small, core * shard, shard, 1)
    small_gains = lax.dynamic_slice_in_dim(
        small[devices + 2 : devices + 4, : 2 * small_shard], core * small_shard, small_shard, 1
    )
    return (
        output[None],
        grad_input[None],
        small_core[devices + 1],
        small_gains[0],
        small_gains[1],
        shard_qkv,
        shard_out,
        small_core[devices],
        small_core[:devices].T,
        grad_weight_in[None],
        grad_weight_back[None],
    )


def solution(mesh):
    in_specs = (
        P("dp", "seq", None),
        P("dp", "seq", None),
        P(("seq", "dp")),
        P(("seq", "dp")),
        P(("seq", "dp")),
        P(("seq", "dp"), None),
        P(("seq", "dp"), None),
        P(("seq", "dp")),
        P(("seq", "dp"), None),
        P(("seq", "dp"), None, None),
        P(("seq", "dp"), None, None),
        P("dp", "seq", None),
    )
    out_specs = (
        P("dp", "seq", None),
        P("dp", "seq", None),
        P(("seq", "dp")),
        P(("seq", "dp")),
        P(("seq", "dp")),
        P(("seq", "dp"), None),
        P(("seq", "dp"), None),
        P(("seq", "dp")),
        P(("seq", "dp"), None),
        P(("seq", "dp"), None, None),
        P(("seq", "dp"), None, None),
    )
    return jax.shard_map(body, mesh=mesh, in_specs=in_specs, out_specs=out_specs, check_vma=False)
```

```python
import functools
import jax
import jax.numpy as jnp
import numpy as np
from jax import lax
from jax.experimental import pallas as pl
from jax.experimental.pallas import tpu as pltpu
from jax.sharding import PartitionSpec as P


MODEL_WIDTH = 2048
QUERY_HEADS = 32
KEY_VALUE_HEADS = 4
HEAD_SIZE = 128
FF = 768
TOP = 8


EPSILON = 1e-06
ROPE_BASE = 1000000.0
FILLER = -1e30
QUERY_BLOCK = 512


MESH = pl.DeviceIdType.MESH
VMEM_BYTES = 63 * 1024 * 1024


def dot_nn(left, right):
    return jnp.dot(left, right, preferred_element_type=jnp.float32)


def dot_nt(left, right):
    return lax.dot_general(
        left, right, (((1,), (1,)), ((), ())), preferred_element_type=jnp.float32
    )


def dot_tn(left, right):
    return lax.dot_general(
        left, right, (((0,), (0,)), ((), ())), preferred_element_type=jnp.float32
    )


def greet(peers):
    barrier = pltpu.get_barrier_semaphore()
    for peer in peers:
        pl.semaphore_signal(barrier, inc=1, device_id=peer, device_id_type=MESH)
    pl.semaphore_wait(barrier, len(peers))


def remote(source, target, send_sem, recv_sem, device):
    return pltpu.make_async_remote_copy(
        src_ref=source,
        dst_ref=target,
        send_sem=send_sem,
        recv_sem=recv_sem,
        device_id=device,
        device_id_type=MESH,
    )


def line_gather_step(step, count, place, column, blocks, send_sems, recv_sems):
    right, left = place + 1, place - 1
    if step > 0:

        @pl.when(place - step >= 0)
        def _():
            block = blocks.at[place - step]
            remote(block, block, send_sems.at[0, step], recv_sems.at[0, step], (right, column)).wait_recv()

        @pl.when(place + step < count)
        def _():
            block = blocks.at[place + step]
            remote(block, block, send_sems.at[1, step], recv_sems.at[1, step], (left, column)).wait_recv()

    if step < count - 1:

        @pl.when((place - step >= 0) & (place + 1 < count))
        def _():
            block = blocks.at[place - step]
            remote(block, block, send_sems.at[0, step], recv_sems.at[0, step + 1], (right, column)).start()

        @pl.when((place + step < count) & (place - 1 >= 0))
        def _():
            block = blocks.at[place + step]
            remote(block, block, send_sems.at[1, step], recv_sems.at[1, step + 1], (left, column)).start()


def line_gather_end(count, place, column, blocks, send_sems, recv_sems):
    for step in range(count - 1):

        @pl.when((place - step >= 0) & (place + 1 < count))
        def _():
            block = blocks.at[place - step]
            remote(block, block, send_sems.at[0, step], recv_sems.at[0, step], (place + 1, column)).wait_send()

        @pl.when((place + step < count) & (place - 1 >= 0))
        def _():
            block = blocks.at[place + step]
            remote(block, block, send_sems.at[1, step], recv_sems.at[1, step], (place - 1, column)).wait_send()


def line_sum_step(step, count, place, column, own, sums, send_sems, recv_sems):
    turn = step - place
    last = count - 1 - turn

    @pl.when((turn >= 0) & (last > place))
    def _():
        block = sums.at[last]

        @pl.when(place > 0)
        def _():
            remote(block, block, send_sems.at[0, last], recv_sems.at[0, last], (place, column)).wait_recv()
            sums[last] = (
                sums[last].astype(jnp.float32) + own[last].astype(jnp.float32)
            ).astype(jnp.bfloat16)

        @pl.when(place == 0)
        def _():
            sums[last] = own[last]

        remote(block, block, send_sems.at[0, last], recv_sems.at[0, last], (place + 1, column)).start()

    first = step - (count - 1 - place)

    @pl.when((first >= 0) & (first < place))
    def _():
        block = sums.at[first]

        @pl.when(place < count - 1)
        def _():
            remote(block, block, send_sems.at[1, first], recv_sems.at[1, first], (place, column)).wait_recv()
            sums[first] = (
                sums[first].astype(jnp.float32) + own[first].astype(jnp.float32)
            ).astype(jnp.bfloat16)

        @pl.when(place == count - 1)
        def _():
            sums[first] = own[first]

        target = sums.at[jnp.where(first == place - 1, count, first)]
        remote(block, target, send_sems.at[1, first], recv_sems.at[1, first], (place - 1, column)).start()


def line_sum_end(count, place, column, own, sums, send_sems, recv_sems, total):
    total[...] = own[place].astype(jnp.float32)

    @pl.when(place > 0)
    def _():
        block = sums.at[place]
        remote(block, block, send_sems.at[0, place], recv_sems.at[0, place], (place, column)).wait_recv()
        total[...] += sums[place].astype(jnp.float32)

    @pl.when(place < count - 1)
    def _():
        block = sums.at[count]
        remote(block, block, send_sems.at[1, place], recv_sems.at[1, place], (place, column)).wait_recv()
        total[...] += sums[count].astype(jnp.float32)

    for step in range(count - 1):
        last = count - 1 - step

        @pl.when(last > place)
        def _():
            block = sums.at[last]
            remote(block, block, send_sems.at[0, last], recv_sems.at[0, last], (place + 1, column)).wait_send()

        @pl.when(step < place)
        def _():
            block = sums.at[step]
            remote(block, block, send_sems.at[1, step], recv_sems.at[1, step], (place - 1, column)).wait_send()


def backward_kernel(
    count, planes, tokens, heads, shard,
    branch_ref, grad_hidden_ref, hidden_ref, gains_ref, router_ref,
    out_rows_hbm, own_cols_hbm, normed_hbm, heads_hbm, query_hbm, pair_hbm,
    proj_hbm, picker_hbm, combined_hbm, lse_ref, turn_cos_ref, turn_sin_ref,
    grad_input_ref, out_total, columns_out, mixed_total, router_total, gain_total, mixed_arrived,
    out_rows, own_cols, normed, heads_low, queries, pair, proj, picker, local_sems,
    branch_full, ag_send, ag_recv,
    grad_heads, grad_proj, grad_pair, gain_parts,
    grad_out, out_pair, out_far, out_sems,
    grad_cols, col_pair, col_far, col_sums, col_sems,
    normed_sums, rs_send, rs_recv, z_sems,
    mixed_rows, mixed_part, mixed_sums, mix_send, mix_recv, mix_local, ms_send, ms_recv,
    router_line, router_sum, router_chip, router_pair, router_sems,
    gain_own, gain_line, gain_chip, gain_pair, gain_sems,
):
    place = lax.axis_index("seq")
    member = lax.axis_index("dp")
    core = lax.rem(member, 2)
    chip = member // 2
    chips = planes // 2
    partner = member + 1 - 2 * core
    length = count * tokens
    query_columns = heads * HEAD_SIZE
    width = query_columns + 2 * HEAD_SIZE
    out_block = query_columns // planes
    scale = HEAD_SIZE ** (-0.5)
    chunks = mixed_part.shape[0]
    wide = MODEL_WIDTH // chunks
    slots = mixed_rows.shape[1]
    low = jnp.bfloat16

    loads = [
        pltpu.make_async_copy(source, target, local_sems.at[index])
        for index, (source, target) in enumerate(
            [
                (out_rows_hbm, out_rows),
                (query_hbm, queries),
                (pair_hbm, pair),
                (heads_hbm, heads_low),
                (proj_hbm, proj),
                (own_cols_hbm, own_cols),
                (normed_hbm, normed),
                (picker_hbm, picker),
            ]
        )
    ]
    for load in loads:
        load.start()
    branch_full[place] = branch_ref[...]

    far_chips = [(k, lax.rem(chip + k, chips)) for k in range(1, chips)]
    far_places = [(k, lax.rem(place + k, count)) for k in range(1, count)]
    others = [(j, lax.rem(member + j, planes)) for j in range(1, planes)]
    greet([(place, other) for _, other in others] + [(other, member) for _, other in far_places])

    line = (count, place, member, branch_full, ag_send, ag_recv)
    line_gather_step(0, *line)

    def mixed_copy(c, j, other):
        part = pl.ds(c * wide, wide)
        return remote(
            combined_hbm.at[other, :, part], mixed_arrived.at[member, :, part],
            mix_send.at[c, j], mix_recv.at[c, j], (place, other),
        )

    for c in range(chunks):
        for j, other in others:
            mixed_copy(c, j, other).start()
    mixed_own = pltpu.make_async_copy(
        combined_hbm.at[member], mixed_arrived.at[member], mix_local.at[0]
    )
    mixed_own.start()
    for load in loads:
        load.wait()

    def head_gradients(block):
        partial_heads = dot_nt(
            branch_full[block], out_rows[...].reshape(query_columns, MODEL_WIDTH)
        ).astype(low)
        for head in range(heads):
            grad_heads[head, pl.ds(pl.multiple_of(block * tokens, tokens), tokens), :] = (
                partial_heads[:, head * HEAD_SIZE : (head + 1) * HEAD_SIZE]
            )

    def gather(step):
        line_gather_step(step, *line)

        @pl.when(place - step >= 0)
        def _():
            head_gradients(place - step)

        @pl.when(place + step < count)
        def _():
            head_gradients(place + step)

    def mixed_line(c):
        return (count, place, member, mixed_part.at[c], mixed_sums.at[c], ms_send.at[c], ms_recv.at[c])

    def mixed_chunk(c):
        for j, other in others:
            mixed_copy(c, j, other).wait_recv()
        if c == 0:
            mixed_own.wait()
        load = pltpu.make_async_copy(
            mixed_arrived.at[:, :, pl.ds(c * wide, wide)], mixed_rows, mix_local.at[1]
        )
        load.start()
        load.wait()
        part = dot_tn(
            picker[...].reshape(planes * slots, length), mixed_rows[...].reshape(planes * slots, wide)
        )
        mixed_part[c] = part.astype(low).reshape(count, tokens, wide)

    waves = list(range(chunks + count - 2))

    def mixed_wave():
        wave = waves.pop(0)
        for c in range(chunks):
            if 0 <= wave - c < count - 1:
                line_sum_step(wave - c, *mixed_line(c))

    head_gradients(place)
    spread = min(chunks, count) - 1
    for step in range(1, count):
        gather(step)
        if step <= spread - 1:
            mixed_chunk(step - 1)
            mixed_wave()

    per_head = HEAD_SIZE // out_block

    def out_gradient(head):
        all_branch = branch_full[...].reshape(length, MODEL_WIDTH)
        part = dot_tn(heads_low[head], all_branch).astype(low)
        if per_head == 1:
            grad_out[head] = part
        else:
            grad_out[head * per_head : (head + 1) * per_head] = part.reshape(
                per_head, out_block, MODEL_WIDTH
            )

    def out_copy(k):
        return remote(
            grad_out.at[2 * k + 1 - core], out_pair.at[k], out_sems.at[0, k], out_sems.at[1, k],
            (place, partner),
        )

    def out_far_copy(k, other):
        return remote(
            out_pair.at[other], out_far.at[k - 1], out_sems.at[2, k], out_sems.at[3, k],
            (place, 2 * other + core),
        )

    if per_head == 1:
        for k in range(chips):
            out_gradient(2 * k + 1 - core)
            out_copy(k).start()
        for k in range(chips):
            out_gradient(2 * k + core)
    else:
        for head in range(heads):
            out_gradient(head)
        for k in range(chips):
            out_copy(k).start()

    done = spread - 1
    while done < chunks - 1:
        mixed_chunk(done)
        mixed_wave()
        done += 1

    lane_part = MODEL_WIDTH // count

    def router_far(k, other):
        return remote(
            router_ref.at[:, pl.ds(pl.multiple_of(other * lane_part, lane_part), lane_part)],
            router_line.at[k - 1], router_sems.at[0, k], router_sems.at[1, k], (other, member),
        )

    def router_near(k, other):
        return remote(
            router_sum.at[0], router_chip.at[k - 1], router_sems.at[2, k], router_sems.at[3, k],
            (place, 2 * other + core),
        )

    def router_last():
        return remote(
            router_sum.at[1], router_pair, router_sems.at[2, 0], router_sems.at[3, 0], (place, partner)
        )

    for k, other in far_places:
        router_far(k, other).start()

    grad_pair[...] = jnp.zeros_like(grad_pair)
    gain_parts[...] = jnp.zeros_like(gain_parts)
    block_rows = min(256, length)
    gain_query = gains_ref[2:3, :HEAD_SIZE]
    gain_key = gains_ref[3:4, :HEAD_SIZE]

    def unprepare(grad, raw, gain):
        turned = grad * turn_cos_ref[...] - pltpu.roll(grad, HEAD_SIZE // 2, 1) * turn_sin_ref[...]
        inverse = lax.rsqrt(jnp.mean(raw * raw, axis=-1, keepdims=True) + EPSILON)
        unit = raw * inverse
        gain_part = jnp.sum(turned * unit, axis=0, keepdims=True)
        turned = turned * gain
        middle = jnp.mean(turned * unit, axis=-1, keepdims=True)
        return inverse * (turned - unit * middle), gain_part

    key_turned = jnp.transpose(pair[0].astype(jnp.float32)).astype(low)

    def one_head(head, carry):
        lse = lse_ref[head]
        grads = []
        for block in range(length // block_rows):
            begin, end = block * block_rows, (block + 1) * block_rows
            query = queries[head, begin:end, :]
            grad = grad_heads[head, begin:end, :]
            scores = dot_nt(pair[0, :end, :], query) * scale
            key_ids = lax.broadcasted_iota(jnp.int32, (end, block_rows), 0)
            query_ids = lax.broadcasted_iota(jnp.int32, (end, block_rows), 1) + begin
            scores = jnp.where(key_ids <= query_ids, scores, FILLER)
            probs = jnp.exp(scores - lse[:, begin:end])
            grad_probs = dot_nt(pair[1, :end, :], grad)
            delta = jnp.sum(probs * grad_probs, axis=0, keepdims=True)
            grad_scores = (probs * (grad_probs - delta)).astype(low)
            grad_pair[0, :end, :] += dot_nn(grad_scores, query) * scale
            grad_pair[1, :end, :] += dot_nn(probs.astype(low), grad)
            grads.append(jnp.transpose(dot_nn(key_turned[:, :end], grad_scores)) * scale)
        grad_query = jnp.concatenate(grads, axis=0)
        grad_raw, gain_part = unprepare(grad_query, proj[head], gain_query)
        gain_parts[0:1, :] += gain_part
        grad_proj[:, pl.ds(pl.multiple_of(head * HEAD_SIZE, HEAD_SIZE), HEAD_SIZE)] = grad_raw.astype(low)
        return carry

    split = heads // 2
    groups = [(0, split), (split, heads + 2)]

    def columns_of(group):
        return pl.ds(groups[group][0] * HEAD_SIZE, (groups[group][1] - groups[group][0]) * HEAD_SIZE)

    def col_copy(group, k):
        part = columns_of(group)
        return remote(
            grad_cols.at[:, 2 * k + 1 - core, :, part], col_pair.at[k, :, :, part],
            col_sems.at[group, 0, k], col_sems.at[group, 1, k], (place, partner),
        )

    def col_far_copy(group, k, other):
        part = columns_of(group)
        return remote(
            col_pair.at[other, :, :, part], col_far.at[k - 1, :, :, part],
            col_sems.at[group, 2, k], col_sems.at[group, 3, k], (place, 2 * other + core),
        )

    def z_copy(group, k, other):
        part = columns_of(group)
        return remote(
            col_sums.at[other, :, part], columns_out.at[place, :, part],
            z_sems.at[group, 0, k], z_sems.at[group, 1, k], (other, member),
        )

    def col_gradient(group):
        first, final = groups[group]
        grads = grad_proj[:, first * HEAD_SIZE : final * HEAD_SIZE]
        block_width = planes * shard
        for block in range(count):
            part = dot_tn(normed[:, block * block_width : (block + 1) * block_width], grads)
            grad_cols[block, :, :, first * HEAD_SIZE : final * HEAD_SIZE] = part.astype(low).reshape(
                planes, shard, (final - first) * HEAD_SIZE
            )
        for k in range(chips):
            col_copy(group, k).start()

    def col_pairs(group):
        first, final = groups[group]
        columns = slice(first * HEAD_SIZE, final * HEAD_SIZE)
        for k in range(chips):
            col_copy(group, k).wait_recv()
            col_pair[k, :, :, columns] = (
                col_pair[k, :, :, columns].astype(jnp.float32)
                + grad_cols[:, 2 * k + core, :, columns].astype(jnp.float32)
            ).astype(low)
        for k, other in far_chips:
            col_far_copy(group, k, other).start()

    def col_totals(group):
        first, final = groups[group]
        columns = slice(first * HEAD_SIZE, final * HEAD_SIZE)
        total = col_pair[chip, :, :, columns].astype(jnp.float32)
        for k, other in far_chips:
            col_far_copy(group, k, other).wait_recv()
            total += col_far[k - 1, :, :, columns].astype(jnp.float32)
        col_sums[:, :, columns] = total.astype(low)
        for k, other in far_places:
            z_copy(group, k, other).start()
        columns_out[place, :, columns] = col_sums[place, :, columns]

    lax.fori_loop(0, split, one_head, 0)
    col_gradient(0)
    for k in range(chips):
        out_copy(k).wait_recv()
        out_pair[k] = (
            out_pair[k].astype(jnp.float32) + grad_out[2 * k + core].astype(jnp.float32)
        ).astype(low)
    for k, other in far_chips:
        out_far_copy(k, other).start()
    mixed_chunk(chunks - 1)
    mixed_wave()
    col_pairs(0)
    lax.fori_loop(split, heads, one_head, 0)
    grad_raw, gain_part = unprepare(grad_pair[0], proj[heads], gain_key)
    gain_parts[1:2, :] += gain_part
    grad_proj[:, query_columns : query_columns + HEAD_SIZE] = grad_raw.astype(low)
    grad_proj[:, query_columns + HEAD_SIZE :] = grad_pair[1].astype(low)
    col_gradient(1)

    line_gather_end(*line)
    normed_part = branch_full
    for block in range(count):
        normed_part[block] = dot_nt(
            grad_proj[block * tokens : (block + 1) * tokens, :],
            own_cols[...].reshape(MODEL_WIDTH, width),
        ).astype(low)
    sums = (count, place, member, normed_part, normed_sums, rs_send, rs_recv)
    line_sum_step(0, *sums)
    col_pairs(1)
    if waves:
        mixed_wave()

    for k, other in far_places:
        router_far(k, other).wait_recv()
    own_lanes = pl.ds(pl.multiple_of(place * lane_part, lane_part), lane_part)
    total = router_ref[:, own_lanes]
    for k, other in far_places:
        total += router_line[k - 1]
    router_sum[0] = total
    for k, other in far_chips:
        router_near(k, other).start()
    for step in range(1, count - 1):
        line_sum_step(step, *sums)
        if waves:
            mixed_wave()
        if step == 1:
            total = out_pair[chip].astype(jnp.float32)
            for k, other in far_chips:
                out_far_copy(k, other).wait_recv()
                total += out_far[k - 1].astype(jnp.float32)
            out_total[...] = total
            col_totals(0)
            total = router_sum[0]
            for k, other in far_chips:
                router_near(k, other).wait_recv()
                total += router_chip[k - 1]
            router_sum[1] = total
            router_last().start()
    while waves:
        mixed_wave()
    for c in range(chunks):
        line_sum_end(*mixed_line(c), mixed_total.at[:, c * wide : (c + 1) * wide])
    col_totals(1)
    router_last().wait_recv()
    router_total[...] = router_sum[1] + router_pair[...]
    line_sum_end(*sums, grad_input_ref)

    hidden = hidden_ref[...].astype(jnp.float32)
    inverse = lax.rsqrt(jnp.mean(hidden * hidden, axis=-1, keepdims=True) + EPSILON)
    unit = hidden * inverse
    grad_normed = grad_input_ref[...]
    gain_row = jnp.sum(grad_normed * unit, axis=0, keepdims=True)
    for k in range(MODEL_WIDTH // HEAD_SIZE):
        gain_own[0, k : k + 1, :] = gain_row[:, k * HEAD_SIZE : (k + 1) * HEAD_SIZE]
    gain_own[0, MODEL_WIDTH // HEAD_SIZE :, :] = gain_parts[...]

    def gain_far(k, other):
        return remote(
            gain_own.at[0], gain_line.at[k - 1], gain_sems.at[0, k], gain_sems.at[1, k], (other, member)
        )

    def gain_near(k, other):
        return remote(
            gain_own.at[1], gain_chip.at[k - 1], gain_sems.at[2, k], gain_sems.at[3, k],
            (place, 2 * other + core),
        )

    def gain_last():
        return remote(
            gain_own.at[2], gain_pair, gain_sems.at[2, 0], gain_sems.at[3, 0], (place, partner)
        )

    for k, other in far_places:
        gain_far(k, other).start()
    turned = grad_normed * gains_ref[0:1, :]
    grad_input_ref[...] = grad_hidden_ref[...] + inverse * (
        turned - unit * jnp.mean(turned * unit, axis=-1, keepdims=True)
    )
    total = gain_own[0]
    for k, other in far_places:
        gain_far(k, other).wait_recv()
        total += gain_line[k - 1]
    gain_own[1] = total
    for k, other in far_chips:
        gain_near(k, other).start()
    for k, other in far_chips:
        gain_near(k, other).wait_recv()
        total += gain_chip[k - 1]
    gain_own[2] = total
    gain_last().start()
    gain_last().wait_recv()
    gain_total[...] = gain_own[2] + gain_pair[...]

    for group in range(2):
        for k, other in far_places:
            z_copy(group, k, other).wait_recv()
            z_copy(group, k, other).wait_send()
        for k in range(chips):
            col_copy(group, k).wait_send()
        for k, other in far_chips:
            col_far_copy(group, k, other).wait_send()
    for k in range(chips):
        out_copy(k).wait_send()
    for k, other in far_chips:
        out_far_copy(k, other).wait_send()
        router_near(k, other).wait_send()
        gain_near(k, other).wait_send()
    for k, other in far_places:
        router_far(k, other).wait_send()
        gain_far(k, other).wait_send()
    router_last().wait_send()
    gain_last().wait_send()
    for c in range(chunks):
        for j, other in others:
            mixed_copy(c, j, other).wait_send()


def attention_backward(
    count, planes, heads, shard, branch, grad_hidden, hidden, gains, router, out_rows, own_cols, normed,
    heads_low, queries, pair, proj, picker, combined, lse, turn_cos, turn_sin,
):
    tokens = branch.shape[0]
    length = count * tokens
    width = (heads + 2) * HEAD_SIZE
    chips = planes // 2
    out_block = heads * HEAD_SIZE // planes
    chunks = 4
    wide = MODEL_WIDTH // chunks
    gain_rows = MODEL_WIDTH // HEAD_SIZE + 8
    router_part = (router.shape[0], MODEL_WIDTH // count)
    low, kind = jnp.bfloat16, jnp.float32
    vmem = pl.BlockSpec(memory_space=pltpu.VMEM)
    anywhere = pl.BlockSpec(memory_space=pl.ANY)
    dma = pltpu.SemaphoreType.DMA
    shape = jax.ShapeDtypeStruct
    most = max(count, chips)
    return pl.pallas_call(
        functools.partial(backward_kernel, count, planes, tokens, heads, shard),
        out_shape=(
            shape((tokens, MODEL_WIDTH), kind),
            shape((out_block, MODEL_WIDTH), kind),
            shape((count, shard, width), low),
            shape((tokens, MODEL_WIDTH), kind),
            shape(router_part, kind),
            shape((gain_rows, HEAD_SIZE), kind),
            shape(combined.shape, low),
        ),
        in_specs=[vmem] * 5 + [anywhere] * 9 + [vmem] * 3,
        out_specs=(vmem,) * 6 + (anywhere,),
        scratch_shapes=[
            pltpu.VMEM(out_rows.shape, low),
            pltpu.VMEM(own_cols.shape, low),
            pltpu.VMEM(normed.shape, low),
            pltpu.VMEM(heads_low.shape, low),
            pltpu.VMEM(queries.shape, low),
            pltpu.VMEM(pair.shape, low),
            pltpu.VMEM(proj.shape, kind),
            pltpu.VMEM(picker.shape, low),
            dma((8,)),
            pltpu.VMEM((count, tokens, MODEL_WIDTH), low),
            dma((2, count)),
            dma((2, count)),
            pltpu.VMEM((heads, length, HEAD_SIZE), low),
            pltpu.VMEM((length, width), low),
            pltpu.VMEM((2, length, HEAD_SIZE), kind),
            pltpu.VMEM((8, HEAD_SIZE), kind),
            pltpu.VMEM((planes, out_block, MODEL_WIDTH), low),
            pltpu.VMEM((chips, out_block, MODEL_WIDTH), low),
            pltpu.VMEM((chips - 1, out_block, MODEL_WIDTH), low),
            dma((4, chips)),
            pltpu.VMEM((count, planes, shard, width), low),
            pltpu.VMEM((chips, count, shard, width), low),
            pltpu.VMEM((chips - 1, count, shard, width), low),
            pltpu.VMEM((count, shard, width), low),
            dma((2, 4, chips)),
            pltpu.VMEM((count + 1, tokens, MODEL_WIDTH), low),
            dma((2, count)),
            dma((2, count)),
            dma((2, 2, count)),
            pltpu.VMEM(combined.shape[:2] + (wide,), low),
            pltpu.VMEM((chunks, count, tokens, wide), low),
            pltpu.VMEM((chunks, count + 1, tokens, wide), low),
            dma((chunks, planes)),
            dma((chunks, planes)),
            dma((2,)),
            dma((chunks, 2, count)),
            dma((chunks, 2, count)),
            pltpu.VMEM((count - 1,) + router_part, kind),
            pltpu.VMEM((2,) + router_part, kind),
            pltpu.VMEM((chips - 1,) + router_part, kind),
            pltpu.VMEM(router_part, kind),
            dma((4, most)),
            pltpu.VMEM((3, gain_rows, HEAD_SIZE), kind),
            pltpu.VMEM((count - 1, gain_rows, HEAD_SIZE), kind),
            pltpu.VMEM((chips - 1, gain_rows, HEAD_SIZE), kind),
            pltpu.VMEM((gain_rows, HEAD_SIZE), kind),
            dma((4, most)),
        ],
        compiler_params=pltpu.CompilerParams(
            collective_id=3, has_side_effects=True, vmem_limit_bytes=VMEM_BYTES
        ),
        name="attention_backward",
    )(
        branch, grad_hidden, hidden, gains, router, out_rows, own_cols, normed, heads_low, queries,
        pair, proj, picker, combined, lse, turn_cos, turn_sin,
    )


def forward_kernel(
    count, planes, tokens, heads, shard, capacity, chunks,
    hidden_ref, routes_ref, gain1_ref, gain2_ref, query_gain_ref, key_gain_ref, router_ref, qkv_ref,
    out_ref, cotangent_ref, turn_cos_ref, turn_sin_ref,
    hidden1_ref, mixed_ref, lse_ref, gains_ref, picker_ref,
    router_out, own_cols_hbm, out_rows_hbm, normed_hbm, heads_hbm, query_hbm, pair_hbm, proj_hbm,
    grad_hbm, masks_hbm,
    column_send, own_cols, c_send, c_recv,
    out_rows, o_send, o_recv,
    hidden_full, h_send, h_recv,
    gains_all, gz_send, gz_recv, gd_send, gd_recv,
    router_all, rz_send, rz_recv, rd_send, rd_recv,
    places_all, p_send, p_recv,
    normed, proj, queries, pair, heads_low,
    grad_full, dy_send, dy_recv,
    grad_sent, d_send, d_recv, mask_sent, m_send, m_recv,
    branch, sums, rs_send, rs_recv, local_sems,
):
    place = lax.axis_index("seq")
    member = lax.axis_index("dp")
    core = lax.rem(member, 2)
    chip = member // 2
    chips = planes // 2
    partner = member + 1 - 2 * core
    length = count * tokens
    query_columns = heads * HEAD_SIZE
    replicas = count // KEY_VALUE_HEADS
    wide = MODEL_WIDTH // chunks
    slots = grad_sent.shape[2]
    rows = planes * slots
    low = jnp.bfloat16
    scale = HEAD_SIZE ** (-0.5)
    far_places = [(k, lax.rem(place + k, count)) for k in range(1, count)]
    far_chips = [(k, lax.rem(chip + k, chips)) for k in range(1, chips)]
    others = [(j, lax.rem(member + j, planes)) for j in range(1, planes)]

    hidden_full[place] = hidden_ref[...]
    index = place * planes + member
    row_lanes = lax.broadcasted_iota(jnp.int32, (1, HEAD_SIZE), 1)
    pieces = []
    for ref in (gain1_ref, gain2_ref, query_gain_ref, key_gain_ref):
        width = ref.shape[1]
        values = ref[...].astype(jnp.float32)
        begin = lax.rem(index, HEAD_SIZE // width) * width
        piece = jnp.zeros((1, HEAD_SIZE), jnp.float32)
        for k in range(width):
            piece += jnp.where(row_lanes == begin + k, values[:, k : k + 1], 0.0)
        pieces.append(piece)
    pieces.append(jnp.zeros((gains_all.shape[2] - 4, HEAD_SIZE), jnp.float32))
    gains_all[place, member] = jnp.concatenate(pieces, axis=0).astype(low)
    router_all[place, member] = jnp.zeros(router_all.shape[2:], low)
    router_all[place, member, :, : router_ref.shape[1]] = router_ref[...]
    for part in range(count):
        head = part // replicas
        keys = QUERY_HEADS * HEAD_SIZE + head * HEAD_SIZE
        values = keys + KEY_VALUE_HEADS * HEAD_SIZE
        column_send[part, :, :query_columns] = qkv_ref[
            :, part * query_columns : (part + 1) * query_columns
        ]
        column_send[part, :, query_columns : query_columns + HEAD_SIZE] = qkv_ref[
            :, keys : keys + HEAD_SIZE
        ]
        column_send[part, :, query_columns + HEAD_SIZE :] = qkv_ref[:, values : values + HEAD_SIZE]
    lanes = lax.broadcasted_iota(jnp.int32, (tokens, places_all.shape[-1]), 1)
    named = jnp.zeros(lanes.shape, jnp.float32)
    for k in range(TOP):
        named += jnp.where(routes_ref[:, k : k + 1] == lanes, 1.0, 0.0)
    row_ids = lax.broadcasted_iota(jnp.int32, (tokens, tokens), 0)
    col_ids = lax.broadcasted_iota(jnp.int32, (tokens, tokens), 1)
    before = jnp.where(row_ids > col_ids, 1.0, 0.0).astype(low)
    earlier = dot_nn(before, named.astype(low))
    places_all[place] = jnp.where(named > 0, earlier, -512.0).astype(low)
    for c in range(chunks):
        grad_full[c, place] = cotangent_ref[:, c * wide : (c + 1) * wide]

    greet([(place, other) for _, other in others] + [(other, member) for _, other in far_places])

    def column_copy(k, other):
        return remote(
            column_send.at[other], own_cols.at[place, member], c_send.at[0, k], c_recv.at[0, k],
            (other, member),
        )

    def gain_line(k, other):
        mine = gains_all.at[place, member]
        return remote(mine, mine, gz_send.at[k], gz_recv.at[k], (other, member))

    def router_line(k, other):
        mine = router_all.at[place, member]
        return remote(mine, mine, rz_send.at[k], rz_recv.at[k], (other, member))

    def places_line(k, other):
        mine = places_all.at[place]
        return remote(mine, mine, p_send.at[k], p_recv.at[k], (other, member))

    def out_copy(k, other):
        return remote(
            out_ref, out_rows.at[member], o_send.at[0, k], o_recv.at[0, k], (place, 2 * other + core)
        )

    def out_pair(k, other):
        source = out_ref if k == 0 else out_rows.at[2 * other + core]
        return remote(
            source, out_rows.at[2 * other + core], o_send.at[1, k], o_recv.at[1, k], (place, partner)
        )

    def block_copy(k, other):
        mine = own_cols.at[:, member]
        return remote(mine, mine, c_send.at[1, k], c_recv.at[1, k], (place, 2 * other + core))

    def block_pair(k, other):
        block = own_cols.at[:, 2 * other + core]
        return remote(block, block, c_send.at[2, k], c_recv.at[2, k], (place, partner))

    for k, other in far_places:
        gain_line(k, other).start()
        column_copy(k, other).start()
    for k, other in far_chips:
        out_copy(k, other).start()
    out_pair(0, chip).start()
    hidden_line = (count, place, member, hidden_full, h_send, h_recv)
    line_gather_step(0, *hidden_line)
    for k, other in far_places:
        places_line(k, other).start()
        router_line(k, other).start()
    own_cols[place, member] = column_send[place]
    out_rows[member] = out_ref[...]

    def gain_plane(j, other):
        mine = gains_all.at[:, member]
        return remote(mine, mine, gd_send.at[j], gd_recv.at[j], (place, other))

    def router_plane(j, other):
        mine = router_all.at[:, member]
        return remote(mine, mine, rd_send.at[j], rd_recv.at[j], (place, other))

    for k, other in far_places:
        gain_line(k, other).wait_recv()
    for j, other in others:
        gain_plane(j, other).start()
    for k, other in far_places:
        column_copy(k, other).wait_recv()
    for k, other in far_chips:
        block_copy(k, other).start()
    block_pair(0, chip).start()
    line_gather_step(1, *hidden_line)

    for k, other in far_places:
        places_line(k, other).wait_recv()
    experts = places_all.shape[-1]
    pick_rows = lax.broadcasted_iota(jnp.int32, (rows, experts), 0)
    pick_experts = lax.broadcasted_iota(jnp.int32, (rows, experts), 1) - place * planes
    slot_ids = lax.broadcasted_iota(jnp.int32, (rows, length), 0)
    token_ids = lax.broadcasted_iota(jnp.int32, (rows, length), 1)
    offsets = jnp.zeros((rows, length), jnp.int32)
    choose = jnp.zeros((rows, experts), jnp.float32)
    for other in range(planes):
        inside = (pick_rows >= other * slots) & (pick_rows < (other + 1) * slots)
        choose += jnp.where(inside & (pick_experts == other), 1.0, 0.0)
        offsets = jnp.where(slot_ids >= other * slots, other * slots, offsets)
    before_block = jnp.zeros((rows, length), jnp.int32)
    for block in range(count):
        before_block = jnp.where(
            token_ids >= block * tokens, block_rank(block, place, count) * capacity, before_block
        )
    wanted = dot_nt(choose.astype(low), places_all[...].reshape(length, experts))
    picker_rows = jnp.where(
        wanted == (slot_ids - offsets - before_block).astype(jnp.float32), 1.0, 0.0
    ).astype(low)
    picker_ref[...] = picker_rows.reshape(planes, slots, length)
    mask_full = jnp.where(places_all[...].reshape(length, experts).astype(jnp.float32) >= 0, 1.0, 0.0)
    mask_sent[...] = (
        dot_nn(picker_rows, mask_full.astype(low)).astype(low).reshape(mask_sent.shape)
    )

    for k, other in far_places:
        router_line(k, other).wait_recv()
    for j, other in others:
        router_plane(j, other).start()

    def mask_copy(j, other):
        return remote(
            mask_sent.at[other], masks_hbm.at[member], m_send.at[j], m_recv.at[j], (place, other)
        )

    for j, other in others:
        mask_copy(j, other).start()
    masks_own = pltpu.make_async_copy(mask_sent.at[member], masks_hbm.at[member], local_sems.at[0])
    masks_own.start()

    for k, other in far_chips:
        out_copy(k, other).wait_recv()
    for k, other in far_chips:
        out_pair(k, lax.rem(chip + chips - k, chips)).start()
    for step in range(2, count):
        line_gather_step(step, *hidden_line)

    def grad_line(c):
        return (count, place, member, grad_full.at[c], dy_send.at[c], dy_recv.at[c])

    def grad_copy(c, j, other):
        return remote(
            grad_sent.at[c, other], grad_hbm.at[c, member], d_send.at[c, j], d_recv.at[c, j], (place, other)
        )

    def grad_own(c):
        return pltpu.make_async_copy(
            grad_sent.at[c, member], grad_hbm.at[c, member], local_sems.at[16 + c]
        )

    def grad_tick(tick):
        for c in range(chunks):
            step = tick - c
            if 0 <= step < count:
                line_gather_step(step, *grad_line(c))
            if step == count - 1:
                picked = dot_nn(
                    picker_ref[...].reshape(rows, length), grad_full[c].reshape(length, wide)
                ).astype(low)
                grad_sent[c] = picked.reshape(planes, slots, wide)
                for j, other in others:
                    grad_copy(c, j, other).start()
                grad_own(c).start()

    ticks = list(range(chunks + count - 1))
    grad_tick(ticks.pop(0))

    for j, other in others:
        gain_plane(j, other).wait_recv()
    per_row = HEAD_SIZE // shard
    small_total = jnp.sum(gains_all[...].astype(jnp.float32), axis=(0, 1))
    gain_rows = []
    for row in range(2):
        parts = []
        for group in range(MODEL_WIDTH // HEAD_SIZE):
            part = jnp.zeros((1, HEAD_SIZE), jnp.float32)
            for index in range(group * per_row, (group + 1) * per_row):
                part += gains_all[index // planes, index % planes, row : row + 1, :].astype(jnp.float32)
            parts.append(part)
        gain_rows.append(jnp.concatenate(parts, axis=1))
    gains_ref[0:1, :] = gain_rows[0]
    gains_ref[1:2, :] = gain_rows[1]
    gain_query = small_total[2:3, :]
    gain_key = small_total[3:4, :]
    gains_ref[2:3, :HEAD_SIZE] = gain_query
    gains_ref[3:4, :HEAD_SIZE] = gain_key

    def normalize(values, gain):
        return (
            values
            * lax.rsqrt(jnp.mean(values * values, axis=-1, keepdims=True) + EPSILON)
            * gain
        )

    for block in range(count):
        values = hidden_full[block].astype(jnp.float32)
        normed[block * tokens : (block + 1) * tokens, :] = normalize(values, gain_rows[0]).astype(low)
    stores = [pltpu.make_async_copy(normed, normed_hbm, local_sems.at[1])]
    stores[-1].start()

    for k, other in far_chips:
        block_copy(k, other).wait_recv()
    for k, other in far_chips:
        block_pair(k, lax.rem(chip + chips - k, chips)).start()
    block_pair(0, chip).wait_recv()
    for k, other in far_chips:
        block_pair(k, lax.rem(chip + chips - k, chips)).wait_recv()
    weights = own_cols[...].reshape(MODEL_WIDTH, query_columns + 2 * HEAD_SIZE)
    stores.append(pltpu.make_async_copy(own_cols, own_cols_hbm, local_sems.at[2]))
    stores[-1].start()

    def prepare(values, gain):
        turned = normalize(values, gain)
        return turned * turn_cos_ref[...] + pltpu.roll(turned, HEAD_SIZE // 2, 1) * turn_sin_ref[...]

    paired = dot_nn(normed[...], weights[:, query_columns:])
    proj[heads] = paired[:, :HEAD_SIZE]
    proj[heads + 1] = paired[:, HEAD_SIZE:]
    pair[0] = prepare(paired[:, :HEAD_SIZE], gain_key).astype(low)
    pair[1] = paired[:, HEAD_SIZE:].astype(low)
    projected = dot_nn(normed[...], weights[:, :query_columns])
    for head in range(heads):
        proj[head] = projected[:, head * HEAD_SIZE : (head + 1) * HEAD_SIZE]
    value_turned = jnp.transpose(paired[:, HEAD_SIZE:]).astype(low)
    stores.append(pltpu.make_async_copy(proj, proj_hbm, local_sems.at[3]))
    stores[-1].start()
    stores.append(pltpu.make_async_copy(pair, pair_hbm, local_sems.at[4]))
    stores[-1].start()
    block_rows = min(256, length)

    def one_head(head, carry):
        queries[head] = prepare(proj[head], gain_query).astype(low)
        for block in range(length // block_rows):
            begin, end = block * block_rows, (block + 1) * block_rows
            scores = dot_nt(pair[0, :end, :], queries[head, begin:end, :]) * scale
            key_ids = lax.broadcasted_iota(jnp.int32, (end, block_rows), 0)
            query_ids = lax.broadcasted_iota(jnp.int32, (end, block_rows), 1) + begin
            scores = jnp.where(key_ids <= query_ids, scores, FILLER)
            top = jnp.max(scores, axis=0, keepdims=True)
            powers = jnp.exp(scores - top)
            total = jnp.sum(powers, axis=0, keepdims=True)
            lse_ref[head, :, begin:end] = top + jnp.log(total)
            probs = (powers * (1.0 / total)).astype(low)
            mixed = dot_nn(value_turned[:, :end], probs)
            heads_low[head, begin:end, :] = jnp.transpose(mixed).astype(low)
        return carry

    halves = 4
    for part in range(halves):
        lax.fori_loop(part * heads // halves, (part + 1) * heads // halves, one_head, 0)
        if ticks:
            grad_tick(ticks.pop(0))
    stores.append(pltpu.make_async_copy(queries, query_hbm, local_sems.at[5]))
    stores[-1].start()
    stores.append(pltpu.make_async_copy(heads_low, heads_hbm, local_sems.at[6]))
    stores[-1].start()

    out_pair(0, chip).wait_recv()
    for k, other in far_chips:
        out_pair(k, lax.rem(chip + chips - k, chips)).wait_recv()
    out_all = out_rows[...].reshape(query_columns, MODEL_WIDTH)
    stores.append(pltpu.make_async_copy(out_rows, out_rows_hbm, local_sems.at[7]))
    stores[-1].start()

    def project(block, carry):
        at = pl.ds(pl.multiple_of(block * tokens, tokens), tokens)
        mixed = jnp.concatenate([heads_low[head, at, :] for head in range(heads)], axis=1)
        branch[block] = dot_nn(mixed, out_all).astype(low)
        return carry

    lax.fori_loop(0, count, project, 0)
    line = (count, place, member, branch, sums, rs_send, rs_recv)
    for step in range(count - 1):
        line_sum_step(step, *line)
        for _ in range(-(-len(ticks) // (count - 1 - step))):
            grad_tick(ticks.pop(0))
    line_sum_end(*line, hidden1_ref)
    hidden1 = hidden_ref[...].astype(jnp.float32) + hidden1_ref[...]
    hidden1_ref[...] = hidden1
    mixed_ref[...] = normalize(hidden1, gain_rows[1]).astype(low)

    for j, other in others:
        router_plane(j, other).wait_recv()
    router_out[...] = router_all[...].reshape(router_out.shape)
    for j, other in others:
        mask_copy(j, other).wait_recv()
        for c in range(chunks):
            grad_copy(c, j, other).wait_recv()
    for k, other in far_places:
        gain_line(k, other).wait_send()
        column_copy(k, other).wait_send()
        places_line(k, other).wait_send()
        router_line(k, other).wait_send()
    for k, other in far_chips:
        out_copy(k, other).wait_send()
        block_copy(k, other).wait_send()
        out_pair(k, other).wait_send()
        block_pair(k, other).wait_send()
    out_pair(0, chip).wait_send()
    block_pair(0, chip).wait_send()
    for j, other in others:
        gain_plane(j, other).wait_send()
        router_plane(j, other).wait_send()
        mask_copy(j, other).wait_send()
        for c in range(chunks):
            grad_copy(c, j, other).wait_send()
    for c in range(chunks):
        grad_own(c).wait()
        line_gather_end(*grad_line(c))
    line_gather_end(*hidden_line)
    masks_own.wait()
    for store in stores:
        store.wait()


def attention_forward(
    count, planes, heads, shard, capacity, slots, chunks,
    hidden, routes, gain_one, gain_two, query_gain, key_gain, router, qkv, out_weight, cotangent,
    turn_cos, turn_sin,
):
    tokens = hidden.shape[0]
    length = count * tokens
    width = (heads + 2) * HEAD_SIZE
    chips = planes // 2
    wide = MODEL_WIDTH // chunks
    experts = -(-router.shape[-1] // 128) * 128
    small_rows = 16
    out_block = out_weight.shape[0]
    low, full = jnp.bfloat16, jnp.float32
    vmem = pl.BlockSpec(memory_space=pltpu.VMEM)
    anywhere = pl.BlockSpec(memory_space=pl.ANY)
    dma = pltpu.SemaphoreType.DMA
    shape = jax.ShapeDtypeStruct
    return pl.pallas_call(
        functools.partial(forward_kernel, count, planes, tokens, heads, shard, capacity, chunks),
        out_shape=(
            shape((tokens, MODEL_WIDTH), full),
            shape((tokens, MODEL_WIDTH), low),
            shape((heads, 1, length), full),
            shape((8, MODEL_WIDTH), full),
            shape((planes, slots, length), low),
            shape((MODEL_WIDTH, experts), low),
            shape((count, planes, shard, width), low),
            shape((planes, out_block, MODEL_WIDTH), low),
            shape((length, MODEL_WIDTH), low),
            shape((heads, length, HEAD_SIZE), low),
            shape((heads, length, HEAD_SIZE), low),
            shape((2, length, HEAD_SIZE), low),
            shape((heads + 2, length, HEAD_SIZE), full),
            shape((chunks, planes, slots, wide), low),
            shape((planes, slots, experts), low),
        ),
        in_specs=[vmem] * 12,
        out_specs=(vmem,) * 6 + (anywhere,) * 9,
        scratch_shapes=[
            pltpu.VMEM((count, shard, width), low),
            pltpu.VMEM((count, planes, shard, width), low),
            dma((3, max(count, chips))),
            dma((3, max(count, chips))),
            pltpu.VMEM((planes, out_block, MODEL_WIDTH), low),
            dma((2, chips)),
            dma((2, chips)),
            pltpu.VMEM((count, tokens, MODEL_WIDTH), low),
            dma((2, count)),
            dma((2, count)),
            pltpu.VMEM((count, planes, small_rows, HEAD_SIZE), low),
            dma((count,)),
            dma((count,)),
            dma((planes,)),
            dma((planes,)),
            pltpu.VMEM((count, planes, shard, experts), low),
            dma((count,)),
            dma((count,)),
            dma((planes,)),
            dma((planes,)),
            pltpu.VMEM((count, tokens, experts), low),
            dma((count,)),
            dma((count,)),
            pltpu.VMEM((length, MODEL_WIDTH), low),
            pltpu.VMEM((heads + 2, length, HEAD_SIZE), full),
            pltpu.VMEM((heads, length, HEAD_SIZE), low),
            pltpu.VMEM((2, length, HEAD_SIZE), low),
            pltpu.VMEM((heads, length, HEAD_SIZE), low),
            pltpu.VMEM((chunks, count, tokens, wide), low),
            dma((chunks, 2, count)),
            dma((chunks, 2, count)),
            pltpu.VMEM((chunks, planes, slots, wide), low),
            dma((chunks, planes)),
            dma((chunks, planes)),
            pltpu.VMEM((planes, slots, experts), low),
            dma((planes,)),
            dma((planes,)),
            pltpu.VMEM((count, tokens, MODEL_WIDTH), low),
            pltpu.VMEM((count + 1, tokens, MODEL_WIDTH), low),
            dma((2, count)),
            dma((2, count)),
            dma((16 + chunks,)),
        ],
        compiler_params=pltpu.CompilerParams(
            collective_id=1, has_side_effects=True, vmem_limit_bytes=VMEM_BYTES
        ),
        name="attention_forward",
    )(
        hidden, routes, gain_one, gain_two, query_gain, key_gain, router, qkv, out_weight, cotangent,
        turn_cos, turn_sin,
    )


def segments(slots):
    step = max(16, slots // 4 // 16 * 16)
    starts = [step * k for k in range(slots // step)]
    return list(zip(starts, starts[1:] + [slots]))


def ranked_block(rank, place, count):
    short = jnp.minimum(place, count - 1 - place)
    near = (rank + 1) // 2
    side = -1 if rank % 2 else 1
    far = rank - short
    far_side = jnp.where(place < count - 1 - place, 1, -1)
    return jnp.where(rank <= 2 * short, place + side * near, place + far_side * far)


def block_rank(block, place, count):
    short = jnp.minimum(place, count - 1 - place)
    away = jnp.abs(block - place)
    near = 2 * away - jnp.where(block < place, 1, 0)
    return jnp.where(away <= short, near, short + away)


def expert_kernel(
    count, planes, tokens, capacity, chunks,
    mixed_ref, hidden1_ref, cotangent_ref, gains_ref, routes_ref, masks_ref,
    picker_hbm, grad_hbm, router_hbm, in_hbm, back_hbm,
    grad_hidden_ref, branch_ref, router_ref, grad_in_hbm, grad_back_hbm, combined_hbm,
    picker, grad_rows, router, weight_in, weight_back, local_sems,
    full, ag_send, ag_recv,
    sent, arrived, x_send, x_recv,
    gate_up, act, grad_gate_up, gate_rows,
    back_arrived, b_send, b_recv,
    gate_sent, gate_arrived, gate_own, gate_sums, gate_total, g_send, g_recv, gs_send, gs_recv,
    sums, rs_send, rs_recv, in_tiles, back_tile, tile_sems,
):
    place = lax.axis_index("seq")
    member = lax.axis_index("dp")
    slots = sent.shape[1]
    rows = planes * slots
    length = count * tokens
    wide = MODEL_WIDTH // chunks
    own_expert = place * planes + member
    experts = count * planes
    lanes = router.shape[-1]
    extra = gate_sent.shape[-1]
    low = jnp.bfloat16
    pieces = segments(slots)
    others = [(j, lax.rem(member + j, planes)) for j in range(1, planes)]

    loads = [
        pltpu.make_async_copy(picker_hbm, picker, local_sems.at[0]),
        pltpu.make_async_copy(in_hbm, weight_in, local_sems.at[1]),
        pltpu.make_async_copy(router_hbm, router, local_sems.at[2]),
        pltpu.make_async_copy(back_hbm, weight_back, local_sems.at[3]),
    ] + [
        pltpu.make_async_copy(
            grad_hbm.at[c], grad_rows.at[:, :, pl.ds(c * wide, wide)], local_sems.at[4 + c]
        )
        for c in range(chunks)
    ]
    for load in loads:
        load.start()
    full[place] = mixed_ref[...]
    greet([(place, other) for _, other in others] + [(lax.rem(place + k, count), member) for k in range(1, count)])

    line = (count, place, member, full, ag_send, ag_recv)

    def row_copy(i, j, other):
        low_row, high_row = pieces[i]
        part = pl.ds(low_row, high_row - low_row)
        return remote(
            sent.at[other, part], arrived.at[member, part], x_send.at[i, j], x_recv.at[i, j], (place, other)
        )

    def back_copy(i, j, other):
        low_row, high_row = pieces[i]
        part = pl.ds(low_row, high_row - low_row)
        return remote(
            sent.at[other, part], back_arrived.at[member, part], b_send.at[i, j], b_recv.at[i, j],
            (place, other),
        )

    def lanes_of(block):
        return pl.ds(pl.multiple_of(block * tokens, tokens), tokens)

    line_gather_step(0, *line)
    loads[0].wait()
    done = 0
    for i, (begin, end) in enumerate(pieces):
        needed = count - 1 if i == len(pieces) - 1 else min((end - 1) // capacity, count - 1)
        while done < needed:
            done += 1
            line_gather_step(done, *line)
        height = planes * (end - begin)
        picked = jnp.zeros((height, MODEL_WIDTH), jnp.float32)
        for rank in range(begin // capacity, min((end - 1) // capacity, count - 1) + 1):
            block = ranked_block(rank, place, count)
            choice = picker[:, begin:end, lanes_of(block)].reshape(height, tokens)
            picked += dot_nn(choice, full[block])
        sent[:, begin:end, :] = picked.astype(low).reshape(planes, end - begin, MODEL_WIDTH)
        for j, other in others:
            row_copy(i, j, other).start()
        arrived[member, begin:end, :] = sent[member, begin:end, :]
    for load in loads[1:]:
        load.wait()

    own_lanes = lax.broadcasted_iota(jnp.int32, (tokens, lanes), 1)
    named = jnp.zeros((tokens, lanes), jnp.float32)
    for k in range(TOP):
        named += jnp.where(routes_ref[:, k : k + 1] == own_lanes, 1.0, 0.0)

    def masked_gates(scores, mask):
        shifted = jnp.where(mask > 0, scores, FILLER)
        powers = jnp.where(mask > 0, jnp.exp(shifted - jnp.max(shifted, axis=-1, keepdims=True)), 0.0)
        total = jnp.sum(powers, axis=-1, keepdims=True)
        return powers / jnp.where(total > 0, total, 1.0)

    own_gates = masked_gates(dot_nn(mixed_ref[...], router[...]), named)

    def work(i):
        begin, end = pieces[i]
        height = planes * (end - begin)
        x = arrived[:, begin:end, :].reshape(height, MODEL_WIDTH)
        gate_up[:height, :] = dot_nn(x, weight_in[...])
        mask = masks_ref[:, begin:end, :].reshape(height, lanes).astype(jnp.float32)
        gates = masked_gates(dot_nn(x, router[...]), mask)
        lane_ids = lax.broadcasted_iota(jnp.int32, (height, lanes), 1)
        gate = jnp.sum(jnp.where(lane_ids == own_expert, gates, 0.0), axis=-1, keepdims=True)
        gate_rows[:, begin:end, :] = jnp.broadcast_to(gate, (height, HEAD_SIZE)).reshape(
            planes, end - begin, HEAD_SIZE
        )
        grads = grad_rows[:, begin:end, :].reshape(height, MODEL_WIDTH).astype(jnp.float32)
        grad_act = dot_nt((grads * gate).astype(low), weight_back[...])
        gate_part = gate_up[:height, :FF]
        up_part = gate_up[:height, FF:]
        chance = jax.nn.sigmoid(gate_part)
        silu = gate_part * chance
        act[:, begin:end, :] = (silu * up_part).astype(low).reshape(planes, end - begin, FF)
        slope = chance + silu * (1.0 - chance)
        grad_gate = (grad_act * up_part * slope).astype(low)
        grad_up = (grad_act * silu).astype(low)
        grad_gate_up[:, begin:end, :FF] = grad_gate.reshape(planes, end - begin, FF)
        grad_gate_up[:, begin:end, FF:] = grad_up.reshape(planes, end - begin, FF)
        for j, other in others:
            row_copy(i, j, other).wait_send()
        back = jnp.concatenate([grad_gate, grad_up], axis=1)
        for c in range(chunks):
            columns = slice(c * wide, (c + 1) * wide)
            sent[:, begin:end, columns] = (
                dot_nt(back, weight_in[columns, :]).astype(low).reshape(planes, end - begin, wide)
            )
        back_arrived[member, begin:end, :] = sent[member, begin:end, :]

    def send_back(i):
        for j, other in others:
            back_copy(i, j, other).start()

    last = len(pieces) - 1
    for i in range(last):
        for j, other in others:
            row_copy(i, j, other).wait_recv()
        work(i)
    for j, other in others:
        row_copy(last, j, other).wait_recv()
    send_back(last - 1)
    work(last)
    send_back(last)
    line_gather_end(*line)

    tile = in_tiles.shape[1]

    def in_copy(slot, index):
        return pltpu.make_async_copy(
            in_tiles.at[slot],
            grad_in_hbm.at[pl.ds(pl.multiple_of(index * tile, tile), tile), pl.ds(slot * FF, FF)],
            tile_sems.at[slot],
        )

    def in_gradient(index, carry):
        x = arrived[:, :, pl.ds(pl.multiple_of(index * tile, tile), tile)].reshape(rows, tile)
        for slot in range(2):

            @pl.when(index > 0)
            def _():
                in_copy(slot, index).wait()

            grads = grad_gate_up[:, :, slot * FF : (slot + 1) * FF].reshape(rows, FF)
            in_tiles[slot] = dot_tn(x, grads)
            in_copy(slot, index).start()
        return carry

    def outputs(c, grad_gate):
        columns = pl.ds(pl.multiple_of(c * wide, wide), wide)
        result = dot_nn(act[...].reshape(rows, FF), weight_back[:, columns])
        result = result.astype(low).astype(jnp.float32)
        grads = grad_rows[:, :, columns].reshape(rows, wide).astype(jnp.float32)
        scale = gate_rows[...].reshape(rows, HEAD_SIZE)[:, 0:1]
        grad_rows[:, :, columns] = (grads * scale).astype(low).reshape(planes, slots, wide)
        arrived[:, :, columns] = (result * scale).astype(low).reshape(planes, slots, wide)
        return grad_gate + jnp.sum(result * grads, axis=-1, keepdims=True)

    def gate_copy(j, other):
        return remote(
            gate_sent.at[other], gate_arrived.at[member], g_send.at[j], g_recv.at[j], (place, other)
        )

    def back_tile_copy(index):
        return pltpu.make_async_copy(
            back_tile,
            grad_back_hbm.at[:, pl.ds(pl.multiple_of(index * tile, tile), tile)],
            tile_sems.at[2],
        )

    def back_gradient(index, carry):
        grads = grad_rows[:, :, pl.ds(pl.multiple_of(index * tile, tile), tile)].reshape(rows, tile)
        result = dot_tn(act[...].reshape(rows, FF), grads)

        @pl.when(index > 0)
        def _():
            back_tile_copy(index).wait()

        back_tile[...] = result
        back_tile_copy(index).start()
        return carry

    tiles = MODEL_WIDTH // tile
    lax.fori_loop(0, tiles, in_gradient, 0)
    grad_gate = lax.fori_loop(0, chunks, outputs, jnp.zeros((rows, 1), jnp.float32))
    combined = pltpu.make_async_copy(arrived, combined_hbm, tile_sems.at[3])
    combined.start()
    high = grad_gate.astype(low).astype(jnp.float32)
    rest = grad_gate - high
    wide_lanes = lax.broadcasted_iota(jnp.int32, (rows, extra), 1)
    columns = jnp.where(
        wide_lanes == own_expert, high, jnp.where(wide_lanes == own_expert + experts, rest, 0.0)
    )
    gate_sent[...] = columns.astype(low).reshape(gate_sent.shape)
    for j, other in others:
        gate_copy(j, other).start()
    gate_arrived[member] = gate_sent[member]
    for i in range(last - 2, -1, -1):
        send_back(i)
    lax.fori_loop(0, tiles, back_gradient, 0)

    for j, other in others:
        gate_copy(j, other).wait_recv()
    gate_own[...] = (
        dot_tn(picker[...].reshape(rows, length), gate_arrived[...].reshape(rows, extra))
        .astype(low)
        .reshape(count, tokens, extra)
    )
    gate_line = (count, place, member, gate_own, gate_sums, gs_send, gs_recv)
    sums_line = (count, place, member, full, sums, rs_send, rs_recv)
    come = set()
    for step in range(count):
        rank = count - 1 - step
        first = rank * capacity // 16 * 16
        final = min(-(-(rank + 1) * capacity // 16) * 16, slots)
        for i in range(last, -1, -1):
            begin, end = pieces[i]
            if i not in come and begin < final and end > first:
                come.add(i)
                for j, other in others:
                    back_copy(i, j, other).wait_recv()
        block = ranked_block(rank, place, count)
        height = planes * (final - first)
        choice = picker[:, first:final, lanes_of(block)].reshape(height, tokens)
        full[block] = dot_tn(
            choice, back_arrived[:, first:final, :].reshape(height, MODEL_WIDTH)
        ).astype(low)
        if step < count - 1:
            line_sum_step(step, *gate_line)
            line_sum_step(step, *sums_line)
    for i in range(len(pieces)):
        if i not in come:
            for j, other in others:
                back_copy(i, j, other).wait_recv()
    line_sum_end(*gate_line, gate_total)
    line_sum_end(*sums_line, grad_hidden_ref)

    if experts % 128 == 0:
        grad_gates = gate_total[:, :experts] + gate_total[:, experts:]
    else:
        grad_gates = gate_total[...] + pltpu.roll(gate_total[...], extra - experts, 1)
    middle = jnp.sum(own_gates * grad_gates, axis=-1, keepdims=True)
    grad_logits = (own_gates * (grad_gates - middle)).astype(low)
    grad_mixed = grad_hidden_ref[...] + dot_nt(grad_logits, router[...])
    router_ref[:experts, :] = dot_tn(grad_logits, mixed_ref[...])[:experts]
    hidden = hidden1_ref[...]
    inverse = lax.rsqrt(jnp.mean(hidden * hidden, axis=-1, keepdims=True) + EPSILON)
    unit = hidden * inverse
    router_ref[experts:, :] = jnp.broadcast_to(
        jnp.sum(grad_mixed * unit, axis=0, keepdims=True), (8, MODEL_WIDTH)
    )
    turned = grad_mixed * gains_ref[1:2, :]
    grad_norm = inverse * (turned - unit * jnp.mean(turned * unit, axis=-1, keepdims=True))
    grad_hidden = cotangent_ref[...].astype(jnp.float32) + grad_norm
    grad_hidden_ref[...] = grad_hidden
    branch_ref[...] = grad_hidden.astype(low)

    for j, other in others:
        for i in range(len(pieces)):
            back_copy(i, j, other).wait_send()
        gate_copy(j, other).wait_send()
    in_copy(0, 0).wait()
    in_copy(1, 0).wait()
    back_tile_copy(0).wait()
    combined.wait()


def expert_layer(
    count, planes, capacity, mixed, hidden1, cotangent, gains, routes, masks, picker, grad_rows,
    router, weight_in, weight_back,
):
    tokens = mixed.shape[0]
    chunks, _, slots, wide = grad_rows.shape
    rows = planes * slots
    extra = -(-2 * count * planes // 128) * 128
    lanes = router.shape[-1]
    height = planes * max(end - begin for begin, end in segments(slots))
    tile = 256 if rows < 1280 else 128
    pieces = len(segments(slots))
    low, kind = jnp.bfloat16, jnp.float32
    vmem = pl.BlockSpec(memory_space=pltpu.VMEM)
    anywhere = pl.BlockSpec(memory_space=pl.ANY)
    dma = pltpu.SemaphoreType.DMA
    shape = jax.ShapeDtypeStruct
    blocks = (planes, slots, MODEL_WIDTH)
    return pl.pallas_call(
        functools.partial(expert_kernel, count, planes, tokens, capacity, chunks),
        out_shape=(
            shape((tokens, MODEL_WIDTH), kind),
            shape((tokens, MODEL_WIDTH), low),
            shape((count * planes + 8, MODEL_WIDTH), kind),
            shape(weight_in.shape, kind),
            shape(weight_back.shape, kind),
            shape(blocks, low),
        ),
        in_specs=[vmem] * 6 + [anywhere] * 5,
        out_specs=(vmem,) * 3 + (anywhere,) * 3,
        scratch_shapes=[
            pltpu.VMEM(picker.shape, low),
            pltpu.VMEM(blocks, low),
            pltpu.VMEM(router.shape, low),
            pltpu.VMEM(weight_in.shape, low),
            pltpu.VMEM(weight_back.shape, low),
            dma((4 + chunks,)),
            pltpu.VMEM((count, tokens, MODEL_WIDTH), low),
            dma((2, count)),
            dma((2, count)),
            pltpu.VMEM(blocks, low),
            pltpu.VMEM(blocks, low),
            dma((pieces, planes)),
            dma((pieces, planes)),
            pltpu.VMEM((height, 2 * FF), kind),
            pltpu.VMEM((planes, slots, FF), low),
            pltpu.VMEM((planes, slots, 2 * FF), low),
            pltpu.VMEM((planes, slots, HEAD_SIZE), kind),
            pltpu.VMEM(blocks, low),
            dma((pieces, planes)),
            dma((pieces, planes)),
            pltpu.VMEM((planes, slots, extra), low),
            pltpu.VMEM((planes, slots, extra), low),
            pltpu.VMEM((count, tokens, extra), low),
            pltpu.VMEM((count + 1, tokens, extra), low),
            pltpu.VMEM((tokens, extra), kind),
            dma((planes,)),
            dma((planes,)),
            dma((2, count)),
            dma((2, count)),
            pltpu.VMEM((count + 1, tokens, MODEL_WIDTH), low),
            dma((2, count)),
            dma((2, count)),
            pltpu.VMEM((2, tile, FF), kind),
            pltpu.VMEM((FF, tile), kind),
            dma((4,)),
        ],
        compiler_params=pltpu.CompilerParams(
            collective_id=2, has_side_effects=True, vmem_limit_bytes=VMEM_BYTES
        ),
        name="expert_layer",
    )(
        mixed, hidden1, cotangent, gains, routes, masks, picker, grad_rows, router, weight_in,
        weight_back,
    )


def turn_tables(length):
    half = HEAD_SIZE // 2
    freqs = np.float32(ROPE_BASE) ** (-(np.arange(half, dtype=np.float32) * np.float32(2 / HEAD_SIZE)))
    angles = np.arange(length, dtype=np.float32)[:, None] * freqs[None, :]
    cosine, sine = np.cos(angles), np.sin(angles)
    return (
        jnp.asarray(np.concatenate([cosine, cosine], axis=1), jnp.float32),
        jnp.asarray(np.concatenate([-sine, sine], axis=1), jnp.float32),
    )


def body(
    hidden_in,
    routes,
    norm1_gain,
    query_gain,
    key_gain,
    qkv_weight,
    out_weight,
    norm2_gain,
    router,
    gate_up_weight,
    down_weight,
    cotangent,
):
    tokens = hidden_in.shape[1]
    sequence_number = lax.axis_size("seq")
    planes = lax.axis_size("dp")
    devices = sequence_number * planes
    group = lax.axis_index("seq")
    member = lax.axis_index("dp")
    index = group * planes + member
    heads = QUERY_HEADS // sequence_number
    query_columns = heads * HEAD_SIZE
    head_replicas = sequence_number // KEY_VALUE_HEADS
    capacity = (tokens * TOP * 9 + 8 * devices - 1) // (8 * devices)
    slots = -(-sequence_number * capacity // 16) * 16
    chunks = 4
    sequence_length = sequence_number * tokens
    shard = norm1_gain.shape[0]
    small_shard = query_gain.shape[0]

    turn_cos, turn_sin = turn_tables(sequence_length)
    (
        hidden1, mixed_low, lse, gains, picker, full_router, own_cols, out_rows, normed_full,
        heads_low, queries, pair, projected, grad_rows, masks,
    ) = attention_forward(
        sequence_number,
        planes,
        heads,
        shard,
        capacity,
        slots,
        chunks,
        hidden_in[0],
        routes[0],
        norm1_gain[None],
        norm2_gain[None],
        query_gain[None],
        key_gain[None],
        router,
        qkv_weight,
        out_weight,
        cotangent[0],
        turn_cos,
        turn_sin,
    )
    (
        grad_hidden1, grad_branch, grad_router, grad_weight_in, grad_weight_back, combined_rows,
    ) = expert_layer(
        sequence_number,
        planes,
        capacity,
        mixed_low,
        hidden1,
        cotangent[0],
        gains,
        routes[0],
        masks,
        picker,
        grad_rows,
        full_router,
        gate_up_weight[0],
        down_weight[0],
    )
    (
        grad_input, shard_out, column_sums, mixed_total, router_total, gain_total, _,
    ) = attention_backward(
        sequence_number,
        planes,
        heads,
        shard,
        grad_branch,
        grad_hidden1,
        hidden_in[0],
        gains,
        grad_router,
        out_rows,
        own_cols,
        normed_full,
        heads_low,
        queries,
        pair,
        projected,
        picker,
        combined_rows,
        lse,
        turn_cos,
        turn_sin,
    )
    output = (hidden1 + mixed_total).astype(jnp.bfloat16)
    column_sums = column_sums.astype(jnp.float32)
    shard_query = jnp.transpose(column_sums[:, :, :query_columns], (1, 0, 2)).reshape(
        shard, QUERY_HEADS * HEAD_SIZE
    )
    shard_paired = jnp.sum(
        column_sums[:, :, query_columns:].reshape(
            KEY_VALUE_HEADS, head_replicas, shard, 2, HEAD_SIZE
        ),
        axis=1,
    )
    shard_paired = jnp.transpose(shard_paired, (1, 2, 0, 3)).reshape(
        shard, 2 * KEY_VALUE_HEADS * HEAD_SIZE
    )
    shard_qkv = jnp.concatenate([shard_query, shard_paired], axis=1)
    index = group * planes + member
    router_own = lax.dynamic_slice_in_dim(router_total, member * shard, shard, 1)
    gain_own = lax.dynamic_slice_in_dim(
        gain_total[: MODEL_WIDTH // HEAD_SIZE].reshape(1, MODEL_WIDTH), index * shard, shard, 1
    )
    head_gains = lax.dynamic_slice_in_dim(
        gain_total[MODEL_WIDTH // HEAD_SIZE :][:2], index * small_shard, small_shard, 1
    )
    return (
        output[None],
        grad_input[None],
        gain_own[0],
        head_gains[0],
        head_gains[1],
        shard_qkv,
        shard_out,
        router_own[devices],
        router_own[:devices].T,
        grad_weight_in[None],
        grad_weight_back[None],
    )


def solution(mesh):
    in_specs = (
        P("dp", "seq", None),
        P("dp", "seq", None),
        P(("seq", "dp")),
        P(("seq", "dp")),
        P(("seq", "dp")),
        P(("seq", "dp"), None),
        P(("seq", "dp"), None),
        P(("seq", "dp")),
        P(("seq", "dp"), None),
        P(("seq", "dp"), None, None),
        P(("seq", "dp"), None, None),
        P("dp", "seq", None),
    )
    out_specs = (
        P("dp", "seq", None),
        P("dp", "seq", None),
        P(("seq", "dp")),
        P(("seq", "dp")),
        P(("seq", "dp")),
        P(("seq", "dp"), None),
        P(("seq", "dp"), None),
        P(("seq", "dp")),
        P(("seq", "dp"), None),
        P(("seq", "dp"), None, None),
        P(("seq", "dp"), None, None),
    )
    return jax.shard_map(body, mesh=mesh, in_specs=in_specs, out_specs=out_specs, check_vma=False)
```

```python
import functools
import jax
import jax.numpy as jnp
import numpy as np
from jax import lax
from jax.experimental import pallas as pl
from jax.experimental.pallas import tpu as pltpu
from jax.sharding import PartitionSpec as P


MODEL_WIDTH = 2048
QUERY_HEADS = 32
KEY_VALUE_HEADS = 4
HEAD_SIZE = 128
FF = 768
TOP = 8


EPSILON = 1e-06
ROPE_BASE = 1000000.0
FILLER = -1e30
QUERY_BLOCK = 512


MESH = pl.DeviceIdType.MESH
VMEM_BYTES = 63 * 1024 * 1024


def dot_nn(left, right):
    return jnp.dot(left, right, preferred_element_type=jnp.float32)


def dot_nt(left, right):
    return lax.dot_general(
        left, right, (((1,), (1,)), ((), ())), preferred_element_type=jnp.float32
    )


def dot_tn(left, right):
    return lax.dot_general(
        left, right, (((0,), (0,)), ((), ())), preferred_element_type=jnp.float32
    )


def greet(peers, between=None):
    barrier = pltpu.get_barrier_semaphore()
    for peer in peers:
        pl.semaphore_signal(barrier, inc=1, device_id=peer, device_id_type=MESH)
    if between is not None:
        between()
    pl.semaphore_wait(barrier, len(peers))


def remote(source, target, send_sem, recv_sem, device):
    return pltpu.make_async_remote_copy(
        src_ref=source,
        dst_ref=target,
        send_sem=send_sem,
        recv_sem=recv_sem,
        device_id=device,
        device_id_type=MESH,
    )


def line_gather_step(step, count, place, column, blocks, send_sems, recv_sems):
    right, left = place + 1, place - 1
    if step > 0:

        @pl.when(place - step >= 0)
        def _():
            block = blocks.at[place - step]
            remote(block, block, send_sems.at[0, step], recv_sems.at[0, step], (right, column)).wait_recv()

        @pl.when(place + step < count)
        def _():
            block = blocks.at[place + step]
            remote(block, block, send_sems.at[1, step], recv_sems.at[1, step], (left, column)).wait_recv()

    if step < count - 1:

        @pl.when((place - step >= 0) & (place + 1 < count))
        def _():
            block = blocks.at[place - step]
            remote(block, block, send_sems.at[0, step], recv_sems.at[0, step + 1], (right, column)).start()

        @pl.when((place + step < count) & (place - 1 >= 0))
        def _():
            block = blocks.at[place + step]
            remote(block, block, send_sems.at[1, step], recv_sems.at[1, step + 1], (left, column)).start()


def line_gather_end(count, place, column, blocks, send_sems, recv_sems):
    for step in range(count - 1):

        @pl.when((place - step >= 0) & (place + 1 < count))
        def _():
            block = blocks.at[place - step]
            remote(block, block, send_sems.at[0, step], recv_sems.at[0, step], (place + 1, column)).wait_send()

        @pl.when((place + step < count) & (place - 1 >= 0))
        def _():
            block = blocks.at[place + step]
            remote(block, block, send_sems.at[1, step], recv_sems.at[1, step], (place - 1, column)).wait_send()


def line_sum_step(step, count, place, column, own, sums, send_sems, recv_sems):
    turn = step - place
    last = count - 1 - turn

    @pl.when((turn >= 0) & (last > place))
    def _():
        block = sums.at[last]

        @pl.when(place > 0)
        def _():
            remote(block, block, send_sems.at[0, last], recv_sems.at[0, last], (place, column)).wait_recv()
            sums[last] = (
                sums[last].astype(jnp.float32) + own[last].astype(jnp.float32)
            ).astype(jnp.bfloat16)

        @pl.when(place == 0)
        def _():
            sums[last] = own[last]

        remote(block, block, send_sems.at[0, last], recv_sems.at[0, last], (place + 1, column)).start()

    first = step - (count - 1 - place)

    @pl.when((first >= 0) & (first < place))
    def _():
        block = sums.at[first]

        @pl.when(place < count - 1)
        def _():
            remote(block, block, send_sems.at[1, first], recv_sems.at[1, first], (place, column)).wait_recv()
            sums[first] = (
                sums[first].astype(jnp.float32) + own[first].astype(jnp.float32)
            ).astype(jnp.bfloat16)

        @pl.when(place == count - 1)
        def _():
            sums[first] = own[first]

        target = sums.at[jnp.where(first == place - 1, count, first)]
        remote(block, target, send_sems.at[1, first], recv_sems.at[1, first], (place - 1, column)).start()


def line_sum_end(count, place, column, own, sums, send_sems, recv_sems, total):
    total[...] = own[place].astype(jnp.float32)

    @pl.when(place > 0)
    def _():
        block = sums.at[place]
        remote(block, block, send_sems.at[0, place], recv_sems.at[0, place], (place, column)).wait_recv()
        total[...] += sums[place].astype(jnp.float32)

    @pl.when(place < count - 1)
    def _():
        block = sums.at[count]
        remote(block, block, send_sems.at[1, place], recv_sems.at[1, place], (place, column)).wait_recv()
        total[...] += sums[count].astype(jnp.float32)

    for step in range(count - 1):
        last = count - 1 - step

        @pl.when(last > place)
        def _():
            block = sums.at[last]
            remote(block, block, send_sems.at[0, last], recv_sems.at[0, last], (place + 1, column)).wait_send()

        @pl.when(step < place)
        def _():
            block = sums.at[step]
            remote(block, block, send_sems.at[1, step], recv_sems.at[1, step], (place - 1, column)).wait_send()


def backward_kernel(
    count, planes, tokens, heads, shard, capacity,
    branch_ref, grad_hidden_ref, hidden_ref, gains_ref, router_ref,
    out_rows_hbm, own_cols_hbm, normed_hbm, heads_hbm, query_hbm, pair_hbm,
    proj_hbm, picker_hbm, combined_hbm, lse_ref, turn_cos_ref, turn_sin_ref,
    grad_input_ref, out_total, qkv_total, mixed_total, router_total, gain_total, mixed_arrived,
    out_rows, own_cols, normed, heads_low, queries, pair, proj, picker, local_sems,
    branch_full, ag_send, ag_recv,
    grad_heads, grad_proj, grad_pair, gain_parts,
    grad_out, out_pair, out_far, out_sems,
    grad_cols, col_pair, col_far, col_sums, columns_out, col_sems,
    normed_room, normed_sums, rs_send, rs_recv, z_sems,
    mixed_rows, mixed_part, mixed_sums, mix_send, mix_recv, mix_local, ms_send, ms_recv,
    router_line, router_sum, router_chip, router_pair, router_sems,
    gain_own, gain_line, gain_chip, gain_pair, gain_sems,
):
    place = lax.axis_index("seq")
    member = lax.axis_index("dp")
    core = lax.rem(member, 2)
    chip = member // 2
    chips = planes // 2
    partner = member + 1 - 2 * core
    length = count * tokens
    query_columns = heads * HEAD_SIZE
    width = query_columns + 2 * HEAD_SIZE
    out_block = query_columns // planes
    scale = HEAD_SIZE ** (-0.5)
    chunks = mixed_part.shape[0]
    wide = MODEL_WIDTH // chunks
    shared = normed_room.shape[0] == 1
    normed_part = branch_full if shared else normed_room
    slots = mixed_rows.shape[1]
    low = jnp.bfloat16

    loads = [
        pltpu.make_async_copy(source, target, local_sems.at[index])
        for index, (source, target) in enumerate(
            [
                (out_rows_hbm, out_rows),
                (query_hbm, queries),
                (pair_hbm, pair),
                (heads_hbm, heads_low),
                (proj_hbm, proj),
                (own_cols_hbm, own_cols),
                (normed_hbm, normed),
                (picker_hbm, picker),
            ]
        )
    ]
    for load in loads:
        load.start()
    branch_full[place] = branch_ref[...]

    far_chips = [(k, lax.rem(chip + k, chips)) for k in range(1, chips)]
    far_places = [(k, lax.rem(place + k, count)) for k in range(1, count)]
    others = [(j, lax.rem(member + j, planes)) for j in range(1, planes)]
    greet([(place, other) for _, other in others] + [(other, member) for _, other in far_places])

    line = (count, place, member, branch_full, ag_send, ag_recv)
    line_gather_step(0, *line)

    def mixed_copy(c, j, other):
        part = pl.ds(c * wide, wide)
        return remote(
            combined_hbm.at[other, :, part], mixed_arrived.at[member, :, part],
            mix_send.at[c, j], mix_recv.at[c, j], (place, other),
        )

    def mixed_send(c):
        for j, other in others:
            mixed_copy(c, j, other).start()

    mixed_send(0)
    mixed_own = pltpu.make_async_copy(
        combined_hbm.at[member], mixed_arrived.at[member], mix_local.at[0]
    )
    mixed_own.start()
    for load in loads:
        load.wait()

    gain_query = gains_ref[2:3, :HEAD_SIZE]
    gain_key = gains_ref[3:4, :HEAD_SIZE]
    grad_pair[...] = jnp.zeros_like(grad_pair)
    gain_parts[...] = jnp.zeros_like(gain_parts)
    key_turned = jnp.transpose(pair[0].astype(jnp.float32)).astype(low)

    def unprepare(grad, raw, gain, cosine, sine):
        turned = grad * cosine - pltpu.roll(grad, HEAD_SIZE // 2, 1) * sine
        inverse = lax.rsqrt(jnp.mean(raw * raw, axis=-1, keepdims=True) + EPSILON)
        unit = raw * inverse
        gain_part = jnp.sum(turned * unit, axis=0, keepdims=True)
        turned = turned * gain
        middle = jnp.mean(turned * unit, axis=-1, keepdims=True)
        return inverse * (turned - unit * middle), gain_part

    together = min(max(1, 2048 // length), heads)

    def process(block):
        at = pl.ds(pl.multiple_of(block * tokens, tokens), tokens)
        partial_heads = dot_nt(
            branch_full[block], out_rows[...].reshape(query_columns, MODEL_WIDTH)
        ).astype(low)
        for head in range(heads):
            grad_heads[head] = partial_heads[:, head * HEAD_SIZE : (head + 1) * HEAD_SIZE]

        cosine, sine = turn_cos_ref[at, :], turn_sin_ref[at, :]

        def some_heads(index, carry):
            first = index * together
            some = pl.ds(first, together)
            query = queries[some, at, :].reshape(together * tokens, HEAD_SIZE)
            grad = grad_heads[some].reshape(together * tokens, HEAD_SIZE)
            scores = dot_nt(pair[0], query) * scale
            shape = (length, together * tokens)
            key_ids = lax.broadcasted_iota(jnp.int32, shape, 0) - block * tokens
            query_ids = lax.rem(lax.broadcasted_iota(jnp.int32, shape, 1), tokens)
            scores = jnp.where(key_ids <= query_ids, scores, FILLER)
            lse = jnp.concatenate([lse_ref[first + k, :, at] for k in range(together)], axis=1)
            probs = jnp.exp(scores - lse)
            grad_probs = dot_nt(pair[1], grad)
            delta = jnp.sum(probs * grad_probs, axis=0, keepdims=True)
            grad_scores = (probs * (grad_probs - delta)).astype(low)
            grad_pair[0] += dot_nn(grad_scores, query) * scale
            grad_pair[1] += dot_nn(probs.astype(low), grad)
            grad_query = jnp.transpose(dot_nn(key_turned, grad_scores)) * scale
            for k in range(together):
                grad_raw, gain_part = unprepare(
                    grad_query[k * tokens : (k + 1) * tokens],
                    proj[first + k, at, :],
                    gain_query,
                    cosine,
                    sine,
                )
                gain_parts[0:1, :] += gain_part
                columns = pl.ds(pl.multiple_of((first + k) * HEAD_SIZE, HEAD_SIZE), HEAD_SIZE)
                grad_proj[at, columns] = grad_raw.astype(low)
            return carry

        lax.fori_loop(0, heads // together, some_heads, 0)

    def gather(step):
        line_gather_step(step, *line)

        def side(index, carry):
            block = place - step + 2 * step * index

            @pl.when((block >= 0) & (block < count))
            def _():
                process(block)

            return carry

        lax.fori_loop(0, 2, side, 0)

    def mixed_line(c):
        return (count, place, member, mixed_part.at[c], mixed_sums.at[c], ms_send.at[c], ms_recv.at[c])

    def mixed_chunk(c):
        for j, other in others:
            mixed_copy(c, j, other).wait_recv()
        if c == 0:
            mixed_own.wait()
        load = pltpu.make_async_copy(
            mixed_arrived.at[:, :, pl.ds(c * wide, wide)], mixed_rows, mix_local.at[1]
        )
        load.start()
        load.wait()
        for rank in range(count):
            block = ranked_block(rank, place, count)
            first = rank * capacity // 16 * 16
            final = min(-(-(rank + 1) * capacity // 16) * 16, slots)
            height = planes * (final - first)
            at = pl.ds(pl.multiple_of(block * tokens, tokens), tokens)
            choice = picker[:, first:final, at].reshape(height, tokens)
            mixed_part[c, block] = dot_tn(
                choice, mixed_rows[:, first:final, :].reshape(height, wide)
            ).astype(low)

    waves = list(range(chunks + count - 2))

    def mixed_wave():
        wave = waves.pop(0)
        for c in range(chunks):
            if 0 <= wave - c < count - 1:
                line_sum_step(wave - c, *mixed_line(c))

    process(place)
    mixed_send(1)
    for step in range(1, count):
        gather(step)
        if step < count - 1 and step <= chunks - 2:
            mixed_send(step + 1)
            mixed_chunk(step - 1)
            mixed_wave()
    mixed_done = min(chunks - 2, count - 2)
    for c in range(mixed_done + 2, chunks):
        mixed_send(c)
    line_gather_end(*line)

    per_head = HEAD_SIZE // out_block

    def out_gradient(head):
        all_branch = branch_full[...].reshape(length, MODEL_WIDTH)
        part = dot_tn(heads_low[head], all_branch).astype(low)
        if per_head == 1:
            grad_out[head] = part
        else:
            grad_out[head * per_head : (head + 1) * per_head] = part.reshape(
                per_head, out_block, MODEL_WIDTH
            )

    def out_copy(k):
        return remote(
            grad_out.at[2 * k + 1 - core], out_pair.at[k], out_sems.at[0, k], out_sems.at[1, k],
            (place, partner),
        )

    def out_far_copy(k, other):
        return remote(
            out_pair.at[other], out_far.at[k - 1], out_sems.at[2, k], out_sems.at[3, k],
            (place, 2 * other + core),
        )

    def out_gradients():
        if per_head == 1:
            for k in range(chips):
                out_gradient(2 * k + 1 - core)
                out_copy(k).start()

            def rest(k, carry):
                out_gradient(2 * k + core)
                return carry

            lax.fori_loop(0, chips, rest, 0)
        else:
            for head in range(heads):
                out_gradient(head)
            for k in range(chips):
                out_copy(k).start()

    def out_pairs():
        for k in range(chips):
            out_copy(k).wait_recv()
            out_pair[k] = (
                out_pair[k].astype(jnp.float32) + grad_out[2 * k + core].astype(jnp.float32)
            ).astype(low)
        for k, other in far_chips:
            out_far_copy(k, other).start()

    lane_part = MODEL_WIDTH // count

    def router_far(k, other):
        return remote(
            router_ref.at[:, pl.ds(pl.multiple_of(other * lane_part, lane_part), lane_part)],
            router_line.at[k - 1], router_sems.at[0, k], router_sems.at[1, k], (other, member),
        )

    def router_near(k, other):
        return remote(
            router_sum.at[0], router_chip.at[k - 1], router_sems.at[2, k], router_sems.at[3, k],
            (place, 2 * other + core),
        )

    def router_last():
        return remote(
            router_sum.at[1], router_pair, router_sems.at[2, 0], router_sems.at[3, 0], (place, partner)
        )

    groups = [(0, heads + 2)]

    def columns_of(group):
        return pl.ds(groups[group][0] * HEAD_SIZE, (groups[group][1] - groups[group][0]) * HEAD_SIZE)

    def col_copy(group, k):
        part = columns_of(group)
        return remote(
            grad_cols.at[:, 2 * k + 1 - core, :, part], col_pair.at[k, :, :, part],
            col_sems.at[group, 0, k], col_sems.at[group, 1, k], (place, partner),
        )

    def col_far_copy(group, k, other):
        part = columns_of(group)
        return remote(
            col_pair.at[other, :, :, part], col_far.at[k - 1, :, :, part],
            col_sems.at[group, 2, k], col_sems.at[group, 3, k], (place, 2 * other + core),
        )

    def z_copy(group, k, other):
        part = columns_of(group)
        return remote(
            col_sums.at[other, :, part], columns_out.at[place, :, part],
            z_sems.at[group, 0, k], z_sems.at[group, 1, k], (other, member),
        )

    def col_gradient(group):
        first, final = groups[group]
        grads = grad_proj[:, first * HEAD_SIZE : final * HEAD_SIZE]
        block_width = planes * shard
        for block in range(count):
            part = dot_tn(normed[:, block * block_width : (block + 1) * block_width], grads)
            grad_cols[block, :, :, first * HEAD_SIZE : final * HEAD_SIZE] = part.astype(low).reshape(
                planes, shard, (final - first) * HEAD_SIZE
            )
        for k in range(chips):
            col_copy(group, k).start()

    def col_pairs(group):
        first, final = groups[group]
        columns = slice(first * HEAD_SIZE, final * HEAD_SIZE)
        for k in range(chips):
            col_copy(group, k).wait_recv()
            col_pair[k, :, :, columns] = (
                col_pair[k, :, :, columns].astype(jnp.float32)
                + grad_cols[:, 2 * k + core, :, columns].astype(jnp.float32)
            ).astype(low)
        for k, other in far_chips:
            col_far_copy(group, k, other).start()

    def col_totals(group):
        first, final = groups[group]
        columns = slice(first * HEAD_SIZE, final * HEAD_SIZE)
        total = col_pair[chip, :, :, columns].astype(jnp.float32)
        for k, other in far_chips:
            col_far_copy(group, k, other).wait_recv()
            total += col_far[k - 1, :, :, columns].astype(jnp.float32)
        col_sums[:, :, columns] = total.astype(low)
        for k, other in far_places:
            z_copy(group, k, other).start()
        columns_out[place, :, columns] = col_sums[place, :, columns]

    grad_raw, gain_part = unprepare(
        grad_pair[0], proj[heads], gain_key, turn_cos_ref[...], turn_sin_ref[...]
    )
    gain_parts[1:2, :] += gain_part
    grad_proj[:, query_columns : query_columns + HEAD_SIZE] = grad_raw.astype(low)
    grad_proj[:, query_columns + HEAD_SIZE :] = grad_pair[1].astype(low)

    def gain_far(k, other):
        return remote(
            gain_own.at[0], gain_line.at[k - 1], gain_sems.at[0, k], gain_sems.at[1, k], (other, member)
        )

    def gain_near(k, other):
        return remote(
            gain_own.at[1], gain_chip.at[k - 1], gain_sems.at[2, k], gain_sems.at[3, k],
            (place, 2 * other + core),
        )

    def gain_last():
        return remote(
            gain_own.at[2], gain_pair, gain_sems.at[2, 0], gain_sems.at[3, 0], (place, partner)
        )

    sums = (count, place, member, normed_part, normed_sums, rs_send, rs_recv)

    def normed_step(step):
        block = ranked_block(count - 1 - step, place, count)
        at = pl.ds(pl.multiple_of(block * tokens, tokens), tokens)
        part = dot_nt(grad_proj[at, :], own_cols[...].reshape(MODEL_WIDTH, width))
        normed_part[block] = part.astype(low)
        if step < count - 1:
            line_sum_step(step, *sums)
        return jnp.sum(part * normed[at, :].astype(jnp.float32), axis=0, keepdims=True)

    if shared:
        out_gradients()
    gain_row = normed_step(0)
    col_gradient(0)
    col_pairs(0)
    for c in range(mixed_done, chunks):
        mixed_chunk(c)
        mixed_wave()
    gain_row += normed_step(1)
    if not shared:
        out_gradients()
    out_pairs()
    for k, other in far_places:
        router_far(k, other).start()
    if waves:
        mixed_wave()
    for step in range(2, count):
        gain_row += normed_step(step)
    gain_row = gain_row / gains_ref[0:1, :]
    for k in range(MODEL_WIDTH // HEAD_SIZE):
        gain_own[0, k : k + 1, :] = gain_row[:, k * HEAD_SIZE : (k + 1) * HEAD_SIZE]
    gain_own[0, MODEL_WIDTH // HEAD_SIZE :, :] = gain_parts[...]
    for k, other in far_places:
        gain_far(k, other).start()
    while waves:
        mixed_wave()
    own_lanes = pl.ds(pl.multiple_of(place * lane_part, lane_part), lane_part)
    total = router_ref[:, own_lanes]
    for k, other in far_places:
        router_far(k, other).wait_recv()
        total += router_line[k - 1]
    router_sum[0] = total
    for k, other in far_chips:
        router_near(k, other).start()
    total = gain_own[0]
    for k, other in far_places:
        gain_far(k, other).wait_recv()
        total += gain_line[k - 1]
    gain_own[1] = total
    for k, other in far_chips:
        gain_near(k, other).start()
    col_totals(0)
    for c in range(chunks):
        line_sum_end(*mixed_line(c), mixed_total.at[:, c * wide : (c + 1) * wide])
    line_sum_end(*sums, grad_input_ref)
    total = out_pair[chip].astype(jnp.float32)
    for k, other in far_chips:
        out_far_copy(k, other).wait_recv()
        total += out_far[k - 1].astype(jnp.float32)
    out_total[...] = total
    total = router_sum[0]
    for k, other in far_chips:
        router_near(k, other).wait_recv()
        total += router_chip[k - 1]
    router_sum[1] = total
    router_last().start()
    total = gain_own[1]
    for k, other in far_chips:
        gain_near(k, other).wait_recv()
        total += gain_chip[k - 1]
    gain_own[2] = total
    gain_last().start()
    gain_last().wait_recv()
    gain_total[...] = gain_own[2] + gain_pair[...]
    router_last().wait_recv()
    router_total[...] = router_sum[1] + router_pair[...]

    hidden = hidden_ref[...].astype(jnp.float32)
    inverse = lax.rsqrt(jnp.mean(hidden * hidden, axis=-1, keepdims=True) + EPSILON)
    unit = hidden * inverse
    grad_normed = grad_input_ref[...]
    turned = grad_normed * gains_ref[0:1, :]
    grad_input_ref[...] = grad_hidden_ref[...] + inverse * (
        turned - unit * jnp.mean(turned * unit, axis=-1, keepdims=True)
    )
    for group in range(len(groups)):
        for k, other in far_places:
            z_copy(group, k, other).wait_recv()
            z_copy(group, k, other).wait_send()
        for part in range(count):
            qkv_total[:, part * query_columns : (part + 1) * query_columns] = columns_out[
                part, :, :query_columns
            ].astype(jnp.float32)
        replicas = count // KEY_VALUE_HEADS
        for head in range(2 * KEY_VALUE_HEADS):
            kind, pair_head = head // KEY_VALUE_HEADS, head % KEY_VALUE_HEADS
            begin = query_columns + kind * HEAD_SIZE
            total = jnp.zeros((shard, HEAD_SIZE), jnp.float32)
            for part in range(pair_head * replicas, (pair_head + 1) * replicas):
                total += columns_out[part, :, begin : begin + HEAD_SIZE].astype(jnp.float32)
            begin = (QUERY_HEADS + head) * HEAD_SIZE
            qkv_total[:, begin : begin + HEAD_SIZE] = total
        for k in range(chips):
            col_copy(group, k).wait_send()
        for k, other in far_chips:
            col_far_copy(group, k, other).wait_send()
    for k in range(chips):
        out_copy(k).wait_send()
    for k, other in far_chips:
        out_far_copy(k, other).wait_send()
        router_near(k, other).wait_send()
        gain_near(k, other).wait_send()
    for k, other in far_places:
        router_far(k, other).wait_send()
        gain_far(k, other).wait_send()
    router_last().wait_send()
    gain_last().wait_send()
    for c in range(chunks):
        for j, other in others:
            mixed_copy(c, j, other).wait_send()


def attention_backward(
    count, planes, heads, shard, capacity, branch, grad_hidden, hidden, gains, router, out_rows, own_cols, normed,
    heads_low, queries, pair, proj, picker, combined, lse, turn_cos, turn_sin,
):
    tokens = branch.shape[0]
    length = count * tokens
    width = (heads + 2) * HEAD_SIZE
    chips = planes // 2
    out_block = heads * HEAD_SIZE // planes
    chunks = 4
    wide = MODEL_WIDTH // chunks
    gain_rows = MODEL_WIDTH // HEAD_SIZE + 8
    router_part = (router.shape[0], MODEL_WIDTH // count)
    low, kind = jnp.bfloat16, jnp.float32
    vmem = pl.BlockSpec(memory_space=pltpu.VMEM)
    anywhere = pl.BlockSpec(memory_space=pl.ANY)
    dma = pltpu.SemaphoreType.DMA
    shape = jax.ShapeDtypeStruct
    most = max(count, chips)
    return pl.pallas_call(
        functools.partial(backward_kernel, count, planes, tokens, heads, shard, capacity),
        out_shape=(
            shape((tokens, MODEL_WIDTH), kind),
            shape((out_block, MODEL_WIDTH), kind),
            shape((shard, (QUERY_HEADS + 2 * KEY_VALUE_HEADS) * HEAD_SIZE), kind),
            shape((tokens, MODEL_WIDTH), kind),
            shape(router_part, kind),
            shape((gain_rows, HEAD_SIZE), kind),
            shape(combined.shape, low),
        ),
        in_specs=[vmem] * 5 + [anywhere] * 9 + [vmem] * 3,
        out_specs=(vmem,) * 6 + (anywhere,),
        scratch_shapes=[
            pltpu.VMEM(out_rows.shape, low),
            pltpu.VMEM(own_cols.shape, low),
            pltpu.VMEM(normed.shape, low),
            pltpu.VMEM(heads_low.shape, low),
            pltpu.VMEM(queries.shape, low),
            pltpu.VMEM(pair.shape, low),
            pltpu.VMEM(proj.shape, kind),
            pltpu.VMEM(picker.shape, low),
            dma((8,)),
            pltpu.VMEM((count, tokens, MODEL_WIDTH), low),
            dma((2, count)),
            dma((2, count)),
            pltpu.VMEM((heads, tokens, HEAD_SIZE), low),
            pltpu.VMEM((length, width), low),
            pltpu.VMEM((2, length, HEAD_SIZE), kind),
            pltpu.VMEM((8, HEAD_SIZE), kind),
            pltpu.VMEM((planes, out_block, MODEL_WIDTH), low),
            pltpu.VMEM((chips, out_block, MODEL_WIDTH), low),
            pltpu.VMEM((chips - 1, out_block, MODEL_WIDTH), low),
            dma((4, chips)),
            pltpu.VMEM((count, planes, shard, width), low),
            pltpu.VMEM((chips, count, shard, width), low),
            pltpu.VMEM((chips - 1, count, shard, width), low),
            pltpu.VMEM((count, shard, width), low),
            pltpu.VMEM((count, shard, width), low),
            dma((2, 4, chips)),
            pltpu.VMEM((count if count <= 4 else 1, tokens, MODEL_WIDTH), low),
            pltpu.VMEM((count + 1, tokens, MODEL_WIDTH), low),
            dma((2, count)),
            dma((2, count)),
            dma((2, 2, count)),
            pltpu.VMEM(combined.shape[:2] + (wide,), low),
            pltpu.VMEM((chunks, count, tokens, wide), low),
            pltpu.VMEM((chunks, count + 1, tokens, wide), low),
            dma((chunks, planes)),
            dma((chunks, planes)),
            dma((2,)),
            dma((chunks, 2, count)),
            dma((chunks, 2, count)),
            pltpu.VMEM((count - 1,) + router_part, kind),
            pltpu.VMEM((2,) + router_part, kind),
            pltpu.VMEM((chips - 1,) + router_part, kind),
            pltpu.VMEM(router_part, kind),
            dma((4, most)),
            pltpu.VMEM((3, gain_rows, HEAD_SIZE), kind),
            pltpu.VMEM((count - 1, gain_rows, HEAD_SIZE), kind),
            pltpu.VMEM((chips - 1, gain_rows, HEAD_SIZE), kind),
            pltpu.VMEM((gain_rows, HEAD_SIZE), kind),
            dma((4, most)),
        ],
        compiler_params=pltpu.CompilerParams(
            collective_id=3, has_side_effects=True, vmem_limit_bytes=VMEM_BYTES
        ),
        name="attention_backward",
    )(
        branch, grad_hidden, hidden, gains, router, out_rows, own_cols, normed, heads_low, queries,
        pair, proj, picker, combined, lse, turn_cos, turn_sin,
    )


def forward_kernel(
    count, planes, tokens, heads, shard, capacity, chunks,
    hidden_ref, routes_ref, gain1_ref, gain2_ref, query_gain_ref, key_gain_ref, router_ref, qkv_ref,
    out_ref, cotangent_ref, turn_cos_ref, turn_sin_ref,
    hidden1_ref, mixed_ref, lse_ref, gains_ref, picker_ref,
    router_out, own_cols_hbm, out_rows_hbm, normed_hbm, heads_hbm, query_hbm, pair_hbm, proj_hbm,
    grad_hbm, masks_hbm,
    column_send, own_cols, c_send, c_recv,
    out_rows, o_send, o_recv,
    hidden_full, h_send, h_recv,
    gains_all, gz_send, gz_recv, gd_send, gd_recv,
    router_all, rz_send, rz_recv, rd_send, rd_recv,
    places_all, p_send, p_recv,
    normed, proj, queries, pair, heads_low,
    grad_full, dy_send, dy_recv,
    grad_sent, d_send, d_recv, mask_sent, m_send, m_recv,
    branch, sums, rs_send, rs_recv, local_sems,
):
    place = lax.axis_index("seq")
    member = lax.axis_index("dp")
    core = lax.rem(member, 2)
    chip = member // 2
    chips = planes // 2
    partner = member + 1 - 2 * core
    length = count * tokens
    query_columns = heads * HEAD_SIZE
    replicas = count // KEY_VALUE_HEADS
    wide = MODEL_WIDTH // chunks
    slots = grad_sent.shape[2]
    rows = planes * slots
    low = jnp.bfloat16
    scale = HEAD_SIZE ** (-0.5)
    far_places = [(k, lax.rem(place + k, count)) for k in range(1, count)]
    far_chips = [(k, lax.rem(chip + k, chips)) for k in range(1, chips)]
    others = [(j, lax.rem(member + j, planes)) for j in range(1, planes)]

    def column_parts():
        for part in range(count):
            head = part // replicas
            keys = QUERY_HEADS * HEAD_SIZE + head * HEAD_SIZE
            values = keys + KEY_VALUE_HEADS * HEAD_SIZE
            column_send[part, :, :query_columns] = qkv_ref[
                :, part * query_columns : (part + 1) * query_columns
            ]
            column_send[part, :, query_columns : query_columns + HEAD_SIZE] = qkv_ref[
                :, keys : keys + HEAD_SIZE
            ]
            column_send[part, :, query_columns + HEAD_SIZE :] = qkv_ref[
                :, values : values + HEAD_SIZE
            ]

    greet(
        [(place, other) for _, other in others] + [(other, member) for _, other in far_places],
        column_parts,
    )

    def column_copy(k, other):
        return remote(
            column_send.at[other], own_cols.at[place, member], c_send.at[0, k], c_recv.at[0, k],
            (other, member),
        )

    def gain_line(k, other):
        mine = gains_all.at[place, member]
        return remote(mine, mine, gz_send.at[k], gz_recv.at[k], (other, member))

    def router_line(k, other):
        mine = router_all.at[place, member]
        return remote(mine, mine, rz_send.at[k], rz_recv.at[k], (other, member))

    def places_line(k, other):
        mine = places_all.at[place]
        return remote(mine, mine, p_send.at[k], p_recv.at[k], (other, member))

    def out_copy(k, other):
        return remote(
            out_ref, out_rows.at[member], o_send.at[0, k], o_recv.at[0, k], (place, 2 * other + core)
        )

    def out_pair(k, other):
        source = out_ref if k == 0 else out_rows.at[2 * other + core]
        return remote(
            source, out_rows.at[2 * other + core], o_send.at[1, k], o_recv.at[1, k], (place, partner)
        )

    def block_copy(k, other):
        mine = own_cols.at[:, member]
        return remote(mine, mine, c_send.at[1, k], c_recv.at[1, k], (place, 2 * other + core))

    def block_pair(k, other):
        block = own_cols.at[:, 2 * other + core]
        return remote(block, block, c_send.at[2, k], c_recv.at[2, k], (place, partner))

    for k, other in far_places:
        column_copy(k, other).start()
    for k, other in far_chips:
        out_copy(k, other).start()
    out_pair(0, chip).start()

    hidden_line = (count, place, member, hidden_full, h_send, h_recv)
    index = place * planes + member
    row_lanes = lax.broadcasted_iota(jnp.int32, (1, HEAD_SIZE), 1)
    pieces = []
    for ref in (gain1_ref, gain2_ref, query_gain_ref, key_gain_ref):
        gain_width = ref.shape[1]
        values = ref[...].astype(jnp.float32)
        begin = lax.rem(index, HEAD_SIZE // gain_width) * gain_width
        piece = jnp.zeros((1, HEAD_SIZE), jnp.float32)
        for k in range(gain_width):
            piece += jnp.where(row_lanes == begin + k, values[:, k : k + 1], 0.0)
        pieces.append(piece)
    pieces.append(jnp.zeros((gains_all.shape[2] - 4, HEAD_SIZE), jnp.float32))
    gains_all[place, member] = jnp.concatenate(pieces, axis=0).astype(low)
    for k, other in far_places:
        gain_line(k, other).start()
    hidden_full[place] = hidden_ref[...]
    line_gather_step(0, *hidden_line)
    router_all[place, member] = jnp.zeros(router_all.shape[2:], low)
    router_all[place, member, :, : router_ref.shape[1]] = router_ref[...]
    lanes = lax.broadcasted_iota(jnp.int32, (tokens, places_all.shape[-1]), 1)
    named = jnp.zeros(lanes.shape, jnp.float32)
    for k in range(TOP):
        named += jnp.where(routes_ref[:, k : k + 1] == lanes, 1.0, 0.0)
    row_ids = lax.broadcasted_iota(jnp.int32, (tokens, tokens), 0)
    col_ids = lax.broadcasted_iota(jnp.int32, (tokens, tokens), 1)
    before = jnp.where(row_ids > col_ids, 1.0, 0.0).astype(low)
    earlier = dot_nn(before, named.astype(low))
    places_all[place] = jnp.where(named > 0, earlier, -512.0).astype(low)
    for c in range(chunks):
        grad_full[c, place] = cotangent_ref[:, c * wide : (c + 1) * wide]
    for k, other in far_places:
        places_line(k, other).start()
        router_line(k, other).start()
    own_cols[place, member] = column_send[place]
    out_rows[member] = out_ref[...]

    def gain_plane(j, other):
        mine = gains_all.at[:, member]
        return remote(mine, mine, gd_send.at[j], gd_recv.at[j], (place, other))

    def router_plane(j, other):
        mine = router_all.at[:, member]
        return remote(mine, mine, rd_send.at[j], rd_recv.at[j], (place, other))

    for k, other in far_places:
        gain_line(k, other).wait_recv()
    for j, other in others:
        gain_plane(j, other).start()
    for k, other in far_places:
        column_copy(k, other).wait_recv()
    for k, other in far_chips:
        block_copy(k, other).start()
    block_pair(0, chip).start()
    line_gather_step(1, *hidden_line)

    for k, other in far_places:
        places_line(k, other).wait_recv()
    experts = places_all.shape[-1]
    pick_rows = lax.broadcasted_iota(jnp.int32, (rows, experts), 0)
    pick_experts = lax.broadcasted_iota(jnp.int32, (rows, experts), 1) - place * planes
    slot_ids = lax.broadcasted_iota(jnp.int32, (rows, length), 0)
    token_ids = lax.broadcasted_iota(jnp.int32, (rows, length), 1)
    offsets = jnp.zeros((rows, length), jnp.int32)
    choose = jnp.zeros((rows, experts), jnp.float32)
    for other in range(planes):
        inside = (pick_rows >= other * slots) & (pick_rows < (other + 1) * slots)
        choose += jnp.where(inside & (pick_experts == other), 1.0, 0.0)
        offsets = jnp.where(slot_ids >= other * slots, other * slots, offsets)
    before_block = jnp.zeros((rows, length), jnp.int32)
    for block in range(count):
        before_block = jnp.where(
            token_ids >= block * tokens, block_rank(block, place, count) * capacity, before_block
        )
    wanted = dot_nt(choose.astype(low), places_all[...].reshape(length, experts))
    picker_rows = jnp.where(
        wanted == (slot_ids - offsets - before_block).astype(jnp.float32), 1.0, 0.0
    ).astype(low)
    picker_ref[...] = picker_rows.reshape(planes, slots, length)
    mask_full = jnp.where(places_all[...].reshape(length, experts).astype(jnp.float32) >= 0, 1.0, 0.0)
    mask_sent[...] = (
        dot_nn(picker_rows, mask_full.astype(low)).astype(low).reshape(mask_sent.shape)
    )

    for k, other in far_places:
        router_line(k, other).wait_recv()
    for j, other in others:
        router_plane(j, other).start()

    def mask_copy(j, other):
        return remote(
            mask_sent.at[other], masks_hbm.at[member], m_send.at[j], m_recv.at[j], (place, other)
        )

    for j, other in others:
        mask_copy(j, other).start()
    masks_own = pltpu.make_async_copy(mask_sent.at[member], masks_hbm.at[member], local_sems.at[0])
    masks_own.start()

    for k, other in far_chips:
        out_copy(k, other).wait_recv()
    for k, other in far_chips:
        out_pair(k, lax.rem(chip + chips - k, chips)).start()
    for step in range(2, count - 1):
        line_gather_step(step, *hidden_line)

    def grad_line(c):
        return (count, place, member, grad_full.at[c], dy_send.at[c], dy_recv.at[c])

    def grad_copy(c, j, other):
        return remote(
            grad_sent.at[c, other], grad_hbm.at[c, member], d_send.at[c, j], d_recv.at[c, j], (place, other)
        )

    def grad_own(c):
        return pltpu.make_async_copy(
            grad_sent.at[c, member], grad_hbm.at[c, member], local_sems.at[16 + c]
        )

    def grad_tick(tick):
        for c in range(chunks):
            step = tick - c
            if 0 <= step < count:
                line_gather_step(step, *grad_line(c))
            if step == count - 1:
                picked = dot_nn(
                    picker_ref[...].reshape(rows, length), grad_full[c].reshape(length, wide)
                ).astype(low)
                grad_sent[c] = picked.reshape(planes, slots, wide)
                for j, other in others:
                    grad_copy(c, j, other).start()
                grad_own(c).start()

    ticks = list(range(chunks + count - 1))
    grad_tick(ticks.pop(0))
    line_gather_step(count - 1, *hidden_line)

    for j, other in others:
        gain_plane(j, other).wait_recv()
    per_row = HEAD_SIZE // shard
    small_total = jnp.sum(gains_all[...].astype(jnp.float32), axis=(0, 1))
    gain_rows = []
    for row in range(2):
        parts = []
        for group in range(MODEL_WIDTH // HEAD_SIZE):
            part = jnp.zeros((1, HEAD_SIZE), jnp.float32)
            for index in range(group * per_row, (group + 1) * per_row):
                part += gains_all[index // planes, index % planes, row : row + 1, :].astype(jnp.float32)
            parts.append(part)
        gain_rows.append(jnp.concatenate(parts, axis=1))
    gains_ref[0:1, :] = gain_rows[0]
    gains_ref[1:2, :] = gain_rows[1]
    gain_query = small_total[2:3, :]
    gain_key = small_total[3:4, :]
    gains_ref[2:3, :HEAD_SIZE] = gain_query
    gains_ref[3:4, :HEAD_SIZE] = gain_key

    def normalize(values, gain):
        return (
            values
            * lax.rsqrt(jnp.mean(values * values, axis=-1, keepdims=True) + EPSILON)
            * gain
        )

    for block in range(count):
        values = hidden_full[block].astype(jnp.float32)
        normed[block * tokens : (block + 1) * tokens, :] = normalize(values, gain_rows[0]).astype(low)
    stores = [pltpu.make_async_copy(normed, normed_hbm, local_sems.at[1])]
    stores[-1].start()

    for k, other in far_chips:
        block_copy(k, other).wait_recv()
    for k, other in far_chips:
        block_pair(k, lax.rem(chip + chips - k, chips)).start()
    block_pair(0, chip).wait_recv()
    for k, other in far_chips:
        block_pair(k, lax.rem(chip + chips - k, chips)).wait_recv()
    weights = own_cols[...].reshape(MODEL_WIDTH, query_columns + 2 * HEAD_SIZE)
    stores.append(pltpu.make_async_copy(own_cols, own_cols_hbm, local_sems.at[2]))
    stores[-1].start()

    def prepare(values, gain):
        turned = normalize(values, gain)
        return turned * turn_cos_ref[...] + pltpu.roll(turned, HEAD_SIZE // 2, 1) * turn_sin_ref[...]

    paired = dot_nn(normed[...], weights[:, query_columns:])
    proj[heads] = paired[:, :HEAD_SIZE]
    proj[heads + 1] = paired[:, HEAD_SIZE:]
    pair[0] = prepare(paired[:, :HEAD_SIZE], gain_key).astype(low)
    pair[1] = paired[:, HEAD_SIZE:].astype(low)
    projected = dot_nn(normed[...], weights[:, :query_columns])
    for head in range(heads):
        proj[head] = projected[:, head * HEAD_SIZE : (head + 1) * HEAD_SIZE]
    value_turned = jnp.transpose(paired[:, HEAD_SIZE:]).astype(low)
    stores.append(pltpu.make_async_copy(proj, proj_hbm, local_sems.at[3]))
    stores[-1].start()
    stores.append(pltpu.make_async_copy(pair, pair_hbm, local_sems.at[4]))
    stores[-1].start()
    together = min(max(1, 2048 // length), heads)

    def some_heads(index, carry):
        first = index * together
        some = pl.ds(first, together)
        for k in range(together):
            queries[first + k] = prepare(proj[first + k], gain_query).astype(low)
        for block in range(count):
            begin, end = block * tokens, (block + 1) * tokens
            query = queries[some, begin:end, :].reshape(together * tokens, HEAD_SIZE)
            scores = dot_nt(pair[0, :end, :], query) * scale
            shape = (end, together * tokens)
            key_ids = lax.broadcasted_iota(jnp.int32, shape, 0) - begin
            query_ids = lax.rem(lax.broadcasted_iota(jnp.int32, shape, 1), tokens)
            scores = jnp.where(key_ids <= query_ids, scores, FILLER)
            top = jnp.max(scores, axis=0, keepdims=True)
            powers = jnp.exp(scores - top)
            total = jnp.sum(powers, axis=0, keepdims=True)
            lse = top + jnp.log(total)
            for k in range(together):
                lse_ref[first + k, :, begin:end] = lse[:, k * tokens : (k + 1) * tokens]
            probs = (powers * (1.0 / total)).astype(low)
            mixed = dot_nn(value_turned[:, :end], probs)
            heads_low[some, begin:end, :] = (
                jnp.transpose(mixed).astype(low).reshape(together, tokens, HEAD_SIZE)
            )
        return carry

    for part in range(heads // together):
        some_heads(part, 0)
        for _ in range(4 * together // heads):
            if ticks:
                grad_tick(ticks.pop(0))
    stores.append(pltpu.make_async_copy(queries, query_hbm, local_sems.at[5]))
    stores[-1].start()
    stores.append(pltpu.make_async_copy(heads_low, heads_hbm, local_sems.at[6]))
    stores[-1].start()

    out_pair(0, chip).wait_recv()
    for k, other in far_chips:
        out_pair(k, lax.rem(chip + chips - k, chips)).wait_recv()
    out_all = out_rows[...].reshape(query_columns, MODEL_WIDTH)
    stores.append(pltpu.make_async_copy(out_rows, out_rows_hbm, local_sems.at[7]))
    stores[-1].start()

    def project(block, carry):
        at = pl.ds(pl.multiple_of(block * tokens, tokens), tokens)
        mixed = jnp.concatenate([heads_low[head, at, :] for head in range(heads)], axis=1)
        branch[block] = dot_nn(mixed, out_all).astype(low)
        return carry

    lax.fori_loop(0, count, project, 0)
    line = (count, place, member, branch, sums, rs_send, rs_recv)
    for step in range(count - 1):
        line_sum_step(step, *line)
        for _ in range(-(-len(ticks) // (count - 1 - step))):
            grad_tick(ticks.pop(0))
    line_sum_end(*line, hidden1_ref)
    hidden1 = hidden_ref[...].astype(jnp.float32) + hidden1_ref[...]
    hidden1_ref[...] = hidden1
    mixed_ref[...] = normalize(hidden1, gain_rows[1]).astype(low)

    for j, other in others:
        router_plane(j, other).wait_recv()
    router_out[...] = router_all[...].reshape(router_out.shape)
    for j, other in others:
        mask_copy(j, other).wait_recv()
        for c in range(chunks):
            grad_copy(c, j, other).wait_recv()
    for k, other in far_places:
        gain_line(k, other).wait_send()
        column_copy(k, other).wait_send()
        places_line(k, other).wait_send()
        router_line(k, other).wait_send()
    for k, other in far_chips:
        out_copy(k, other).wait_send()
        block_copy(k, other).wait_send()
        out_pair(k, other).wait_send()
        block_pair(k, other).wait_send()
    out_pair(0, chip).wait_send()
    block_pair(0, chip).wait_send()
    for j, other in others:
        gain_plane(j, other).wait_send()
        router_plane(j, other).wait_send()
        mask_copy(j, other).wait_send()
        for c in range(chunks):
            grad_copy(c, j, other).wait_send()
    for c in range(chunks):
        grad_own(c).wait()
        line_gather_end(*grad_line(c))
    line_gather_end(*hidden_line)
    masks_own.wait()
    for store in stores:
        store.wait()


def attention_forward(
    count, planes, heads, shard, capacity, slots, chunks,
    hidden, routes, gain_one, gain_two, query_gain, key_gain, router, qkv, out_weight, cotangent,
    turn_cos, turn_sin,
):
    tokens = hidden.shape[0]
    length = count * tokens
    width = (heads + 2) * HEAD_SIZE
    chips = planes // 2
    wide = MODEL_WIDTH // chunks
    experts = -(-router.shape[-1] // 128) * 128
    small_rows = 16
    out_block = out_weight.shape[0]
    low, full = jnp.bfloat16, jnp.float32
    vmem = pl.BlockSpec(memory_space=pltpu.VMEM)
    anywhere = pl.BlockSpec(memory_space=pl.ANY)
    dma = pltpu.SemaphoreType.DMA
    shape = jax.ShapeDtypeStruct
    return pl.pallas_call(
        functools.partial(forward_kernel, count, planes, tokens, heads, shard, capacity, chunks),
        out_shape=(
            shape((tokens, MODEL_WIDTH), full),
            shape((tokens, MODEL_WIDTH), low),
            shape((heads, 1, length), full),
            shape((8, MODEL_WIDTH), full),
            shape((planes, slots, length), low),
            shape((MODEL_WIDTH, experts), low),
            shape((count, planes, shard, width), low),
            shape((planes, out_block, MODEL_WIDTH), low),
            shape((length, MODEL_WIDTH), low),
            shape((heads, length, HEAD_SIZE), low),
            shape((heads, length, HEAD_SIZE), low),
            shape((2, length, HEAD_SIZE), low),
            shape((heads + 2, length, HEAD_SIZE), full),
            shape((chunks, planes, slots, wide), low),
            shape((planes, slots, experts), low),
        ),
        in_specs=[vmem] * 12,
        out_specs=(vmem,) * 6 + (anywhere,) * 9,
        scratch_shapes=[
            pltpu.VMEM((count, shard, width), low),
            pltpu.VMEM((count, planes, shard, width), low),
            dma((3, max(count, chips))),
            dma((3, max(count, chips))),
            pltpu.VMEM((planes, out_block, MODEL_WIDTH), low),
            dma((2, chips)),
            dma((2, chips)),
            pltpu.VMEM((count, tokens, MODEL_WIDTH), low),
            dma((2, count)),
            dma((2, count)),
            pltpu.VMEM((count, planes, small_rows, HEAD_SIZE), low),
            dma((count,)),
            dma((count,)),
            dma((planes,)),
            dma((planes,)),
            pltpu.VMEM((count, planes, shard, experts), low),
            dma((count,)),
            dma((count,)),
            dma((planes,)),
            dma((planes,)),
            pltpu.VMEM((count, tokens, experts), low),
            dma((count,)),
            dma((count,)),
            pltpu.VMEM((length, MODEL_WIDTH), low),
            pltpu.VMEM((heads + 2, length, HEAD_SIZE), full),
            pltpu.VMEM((heads, length, HEAD_SIZE), low),
            pltpu.VMEM((2, length, HEAD_SIZE), low),
            pltpu.VMEM((heads, length, HEAD_SIZE), low),
            pltpu.VMEM((chunks, count, tokens, wide), low),
            dma((chunks, 2, count)),
            dma((chunks, 2, count)),
            pltpu.VMEM((chunks, planes, slots, wide), low),
            dma((chunks, planes)),
            dma((chunks, planes)),
            pltpu.VMEM((planes, slots, experts), low),
            dma((planes,)),
            dma((planes,)),
            pltpu.VMEM((count, tokens, MODEL_WIDTH), low),
            pltpu.VMEM((count + 1, tokens, MODEL_WIDTH), low),
            dma((2, count)),
            dma((2, count)),
            dma((16 + chunks,)),
        ],
        compiler_params=pltpu.CompilerParams(
            collective_id=1, has_side_effects=True, vmem_limit_bytes=VMEM_BYTES
        ),
        name="attention_forward",
    )(
        hidden, routes, gain_one, gain_two, query_gain, key_gain, router, qkv, out_weight, cotangent,
        turn_cos, turn_sin,
    )


def segments(slots):
    step = max(16, slots // 4 // 16 * 16)
    starts = [step * k for k in range(slots // step)]
    return list(zip(starts, starts[1:] + [slots]))


def ranked_block(rank, place, count):
    short = jnp.minimum(place, count - 1 - place)
    near = (rank + 1) // 2
    side = -1 if rank % 2 else 1
    far = rank - short
    far_side = jnp.where(place < count - 1 - place, 1, -1)
    return jnp.where(rank <= 2 * short, place + side * near, place + far_side * far)


def block_rank(block, place, count):
    short = jnp.minimum(place, count - 1 - place)
    away = jnp.abs(block - place)
    near = 2 * away - jnp.where(block < place, 1, 0)
    return jnp.where(away <= short, near, short + away)


def expert_kernel(
    count, planes, tokens, capacity, chunks,
    mixed_ref, hidden1_ref, cotangent_ref, gains_ref, routes_ref, masks_ref,
    picker_hbm, grad_hbm, router_hbm, in_hbm, back_hbm,
    grad_hidden_ref, branch_ref, router_ref, grad_in_hbm, grad_back_hbm, combined_hbm,
    picker, grad_rows, router, weight_in, weight_back, local_sems,
    full, ag_send, ag_recv,
    sent, arrived, x_send, x_recv,
    gate_up, act, grad_gate_up, gate_rows,
    back_arrived, b_send, b_recv,
    gate_sent, gate_arrived, gate_own, gate_sums, gate_total, g_send, g_recv, gs_send, gs_recv,
    sums, rs_send, rs_recv, in_tiles, back_tile, tile_sems,
):
    place = lax.axis_index("seq")
    member = lax.axis_index("dp")
    slots = sent.shape[1]
    rows = planes * slots
    length = count * tokens
    wide = MODEL_WIDTH // chunks
    own_expert = place * planes + member
    experts = count * planes
    lanes = router.shape[-1]
    extra = gate_sent.shape[-1]
    low = jnp.bfloat16
    pieces = segments(slots)
    others = [(j, lax.rem(member + j, planes)) for j in range(1, planes)]

    loads = [
        pltpu.make_async_copy(picker_hbm, picker, local_sems.at[0]),
        pltpu.make_async_copy(in_hbm, weight_in, local_sems.at[1]),
        pltpu.make_async_copy(router_hbm, router, local_sems.at[2]),
        pltpu.make_async_copy(back_hbm, weight_back, local_sems.at[3]),
    ] + [
        pltpu.make_async_copy(
            grad_hbm.at[c], grad_rows.at[:, :, pl.ds(c * wide, wide)], local_sems.at[4 + c]
        )
        for c in range(chunks)
    ]
    for load in loads:
        load.start()
    full[place] = mixed_ref[...]
    greet([(place, other) for _, other in others] + [(lax.rem(place + k, count), member) for k in range(1, count)])

    line = (count, place, member, full, ag_send, ag_recv)

    def row_copy(i, j, other):
        low_row, high_row = pieces[i]
        part = pl.ds(low_row, high_row - low_row)
        return remote(
            sent.at[other, part], arrived.at[member, part], x_send.at[i, j], x_recv.at[i, j], (place, other)
        )

    def back_copy(i, j, other):
        low_row, high_row = pieces[i]
        part = pl.ds(low_row, high_row - low_row)
        return remote(
            sent.at[other, part], back_arrived.at[member, part], b_send.at[i, j], b_recv.at[i, j],
            (place, other),
        )

    def lanes_of(block):
        return pl.ds(pl.multiple_of(block * tokens, tokens), tokens)

    line_gather_step(0, *line)
    loads[0].wait()
    done = 0
    for i, (begin, end) in enumerate(pieces):
        needed = count - 1 if i == len(pieces) - 1 else min((end - 1) // capacity, count - 1)
        while done < needed:
            done += 1
            line_gather_step(done, *line)
        height = planes * (end - begin)
        picked = jnp.zeros((height, MODEL_WIDTH), jnp.float32)
        for rank in range(begin // capacity, min((end - 1) // capacity, count - 1) + 1):
            block = ranked_block(rank, place, count)
            choice = picker[:, begin:end, lanes_of(block)].reshape(height, tokens)
            picked += dot_nn(choice, full[block])
        sent[:, begin:end, :] = picked.astype(low).reshape(planes, end - begin, MODEL_WIDTH)
        for j, other in others:
            row_copy(i, j, other).start()
        arrived[member, begin:end, :] = sent[member, begin:end, :]
    for load in loads[1:]:
        load.wait()

    own_lanes = lax.broadcasted_iota(jnp.int32, (tokens, lanes), 1)
    named = jnp.zeros((tokens, lanes), jnp.float32)
    for k in range(TOP):
        named += jnp.where(routes_ref[:, k : k + 1] == own_lanes, 1.0, 0.0)

    def masked_gates(scores, mask):
        shifted = jnp.where(mask > 0, scores, FILLER)
        powers = jnp.where(mask > 0, jnp.exp(shifted - jnp.max(shifted, axis=-1, keepdims=True)), 0.0)
        total = jnp.sum(powers, axis=-1, keepdims=True)
        return powers / jnp.where(total > 0, total, 1.0)

    own_gates = masked_gates(dot_nn(mixed_ref[...], router[...]), named)

    def work(i):
        begin, end = pieces[i]
        height = planes * (end - begin)
        x = arrived[:, begin:end, :].reshape(height, MODEL_WIDTH)
        gate_up[:height, :] = dot_nn(x, weight_in[...])
        mask = masks_ref[:, begin:end, :].reshape(height, lanes).astype(jnp.float32)
        gates = masked_gates(dot_nn(x, router[...]), mask)
        lane_ids = lax.broadcasted_iota(jnp.int32, (height, lanes), 1)
        gate = jnp.sum(jnp.where(lane_ids == own_expert, gates, 0.0), axis=-1, keepdims=True)
        gate_rows[:, begin:end, :] = jnp.broadcast_to(gate, (height, HEAD_SIZE)).reshape(
            planes, end - begin, HEAD_SIZE
        )
        grads = grad_rows[:, begin:end, :].reshape(height, MODEL_WIDTH).astype(jnp.float32)
        grad_act = dot_nt((grads * gate).astype(low), weight_back[...])
        gate_part = gate_up[:height, :FF]
        up_part = gate_up[:height, FF:]
        chance = jax.nn.sigmoid(gate_part)
        silu = gate_part * chance
        act[:, begin:end, :] = (silu * up_part).astype(low).reshape(planes, end - begin, FF)
        slope = chance + silu * (1.0 - chance)
        grad_gate = (grad_act * up_part * slope).astype(low)
        grad_up = (grad_act * silu).astype(low)
        grad_gate_up[:, begin:end, :FF] = grad_gate.reshape(planes, end - begin, FF)
        grad_gate_up[:, begin:end, FF:] = grad_up.reshape(planes, end - begin, FF)
        for j, other in others:
            row_copy(i, j, other).wait_send()
        back = jnp.concatenate([grad_gate, grad_up], axis=1)
        for c in range(chunks):
            columns = slice(c * wide, (c + 1) * wide)
            sent[:, begin:end, columns] = (
                dot_nt(back, weight_in[columns, :]).astype(low).reshape(planes, end - begin, wide)
            )
        back_arrived[member, begin:end, :] = sent[member, begin:end, :]

    def send_back(i):
        for j, other in others:
            back_copy(i, j, other).start()

    last = len(pieces) - 1
    for i in range(last):
        for j, other in others:
            row_copy(i, j, other).wait_recv()
        work(i)
    for j, other in others:
        row_copy(last, j, other).wait_recv()
    send_back(last - 1)
    work(last)
    send_back(last)
    line_gather_end(*line)

    tile = in_tiles.shape[1]

    def in_copy(slot, index):
        return pltpu.make_async_copy(
            in_tiles.at[slot],
            grad_in_hbm.at[pl.ds(pl.multiple_of(index * tile, tile), tile), pl.ds(slot * FF, FF)],
            tile_sems.at[slot],
        )

    def in_gradient(index, carry):
        x = arrived[:, :, pl.ds(pl.multiple_of(index * tile, tile), tile)].reshape(rows, tile)
        for slot in range(2):

            @pl.when(index > 0)
            def _():
                in_copy(slot, index).wait()

            grads = grad_gate_up[:, :, slot * FF : (slot + 1) * FF].reshape(rows, FF)
            in_tiles[slot] = dot_tn(x, grads).astype(low)
            in_copy(slot, index).start()
        return carry

    def outputs(c, grad_gate):
        columns = pl.ds(pl.multiple_of(c * wide, wide), wide)
        result = dot_nn(act[...].reshape(rows, FF), weight_back[:, columns])
        result = result.astype(low).astype(jnp.float32)
        grads = grad_rows[:, :, columns].reshape(rows, wide).astype(jnp.float32)
        scale = gate_rows[...].reshape(rows, HEAD_SIZE)[:, 0:1]
        grad_rows[:, :, columns] = (grads * scale).astype(low).reshape(planes, slots, wide)
        arrived[:, :, columns] = (result * scale).astype(low).reshape(planes, slots, wide)
        return grad_gate + jnp.sum(result * grads, axis=-1, keepdims=True)

    def gate_copy(j, other):
        return remote(
            gate_sent.at[other], gate_arrived.at[member], g_send.at[j], g_recv.at[j], (place, other)
        )

    def back_tile_copy(index):
        return pltpu.make_async_copy(
            back_tile,
            grad_back_hbm.at[:, pl.ds(pl.multiple_of(index * tile, tile), tile)],
            tile_sems.at[2],
        )

    def back_gradient(index, carry):
        grads = grad_rows[:, :, pl.ds(pl.multiple_of(index * tile, tile), tile)].reshape(rows, tile)
        result = dot_tn(act[...].reshape(rows, FF), grads)

        @pl.when(index > 0)
        def _():
            back_tile_copy(index).wait()

        back_tile[...] = result.astype(low)
        back_tile_copy(index).start()
        return carry

    tiles = MODEL_WIDTH // tile
    lax.fori_loop(0, tiles, in_gradient, 0)
    grad_gate = lax.fori_loop(0, chunks, outputs, jnp.zeros((rows, 1), jnp.float32))
    combined = pltpu.make_async_copy(arrived, combined_hbm, tile_sems.at[3])
    combined.start()
    high = grad_gate.astype(low).astype(jnp.float32)
    rest = grad_gate - high
    wide_lanes = lax.broadcasted_iota(jnp.int32, (rows, extra), 1)
    columns = jnp.where(
        wide_lanes == own_expert, high, jnp.where(wide_lanes == own_expert + experts, rest, 0.0)
    )
    gate_sent[...] = columns.astype(low).reshape(gate_sent.shape)
    for j, other in others:
        gate_copy(j, other).start()
    gate_arrived[member] = gate_sent[member]
    for i in range(last - 2, -1, -1):
        send_back(i)
    lax.fori_loop(0, tiles, back_gradient, 0)

    for j, other in others:
        gate_copy(j, other).wait_recv()
    gate_own[...] = (
        dot_tn(picker[...].reshape(rows, length), gate_arrived[...].reshape(rows, extra))
        .astype(low)
        .reshape(count, tokens, extra)
    )
    gate_line = (count, place, member, gate_own, gate_sums, gs_send, gs_recv)
    sums_line = (count, place, member, full, sums, rs_send, rs_recv)
    come = set()
    for step in range(count):
        rank = count - 1 - step
        first = rank * capacity // 16 * 16
        final = min(-(-(rank + 1) * capacity // 16) * 16, slots)
        for i in range(last, -1, -1):
            begin, end = pieces[i]
            if i not in come and begin < final and end > first:
                come.add(i)
                for j, other in others:
                    back_copy(i, j, other).wait_recv()
        block = ranked_block(rank, place, count)
        height = planes * (final - first)
        choice = picker[:, first:final, lanes_of(block)].reshape(height, tokens)
        full[block] = dot_tn(
            choice, back_arrived[:, first:final, :].reshape(height, MODEL_WIDTH)
        ).astype(low)
        if step < count - 1:
            line_sum_step(step, *gate_line)
            line_sum_step(step, *sums_line)
    for i in range(len(pieces)):
        if i not in come:
            for j, other in others:
                back_copy(i, j, other).wait_recv()
    line_sum_end(*gate_line, gate_total)
    line_sum_end(*sums_line, grad_hidden_ref)

    if experts % 128 == 0:
        grad_gates = gate_total[:, :experts] + gate_total[:, experts:]
    else:
        grad_gates = gate_total[...] + pltpu.roll(gate_total[...], extra - experts, 1)
    middle = jnp.sum(own_gates * grad_gates, axis=-1, keepdims=True)
    grad_logits = (own_gates * (grad_gates - middle)).astype(low)
    grad_mixed = grad_hidden_ref[...] + dot_nt(grad_logits, router[...])
    router_ref[:experts, :] = dot_tn(grad_logits, mixed_ref[...])[:experts]
    hidden = hidden1_ref[...]
    inverse = lax.rsqrt(jnp.mean(hidden * hidden, axis=-1, keepdims=True) + EPSILON)
    unit = hidden * inverse
    router_ref[experts:, :] = jnp.broadcast_to(
        jnp.sum(grad_mixed * unit, axis=0, keepdims=True), (8, MODEL_WIDTH)
    )
    turned = grad_mixed * gains_ref[1:2, :]
    grad_norm = inverse * (turned - unit * jnp.mean(turned * unit, axis=-1, keepdims=True))
    grad_hidden = cotangent_ref[...].astype(jnp.float32) + grad_norm
    grad_hidden_ref[...] = grad_hidden
    branch_ref[...] = grad_hidden.astype(low)

    for j, other in others:
        for i in range(len(pieces)):
            back_copy(i, j, other).wait_send()
        gate_copy(j, other).wait_send()
    in_copy(0, 0).wait()
    in_copy(1, 0).wait()
    back_tile_copy(0).wait()
    combined.wait()


def expert_layer(
    count, planes, capacity, mixed, hidden1, cotangent, gains, routes, masks, picker, grad_rows,
    router, weight_in, weight_back,
):
    tokens = mixed.shape[0]
    chunks, _, slots, wide = grad_rows.shape
    rows = planes * slots
    extra = -(-2 * count * planes // 128) * 128
    lanes = router.shape[-1]
    height = planes * max(end - begin for begin, end in segments(slots))
    tile = 256 if rows < 1280 else 128
    pieces = len(segments(slots))
    low, kind = jnp.bfloat16, jnp.float32
    vmem = pl.BlockSpec(memory_space=pltpu.VMEM)
    anywhere = pl.BlockSpec(memory_space=pl.ANY)
    dma = pltpu.SemaphoreType.DMA
    shape = jax.ShapeDtypeStruct
    blocks = (planes, slots, MODEL_WIDTH)
    return pl.pallas_call(
        functools.partial(expert_kernel, count, planes, tokens, capacity, chunks),
        out_shape=(
            shape((tokens, MODEL_WIDTH), kind),
            shape((tokens, MODEL_WIDTH), low),
            shape((count * planes + 8, MODEL_WIDTH), kind),
            shape(weight_in.shape, low),
            shape(weight_back.shape, low),
            shape(blocks, low),
        ),
        in_specs=[vmem] * 6 + [anywhere] * 5,
        out_specs=(vmem,) * 3 + (anywhere,) * 3,
        scratch_shapes=[
            pltpu.VMEM(picker.shape, low),
            pltpu.VMEM(blocks, low),
            pltpu.VMEM(router.shape, low),
            pltpu.VMEM(weight_in.shape, low),
            pltpu.VMEM(weight_back.shape, low),
            dma((4 + chunks,)),
            pltpu.VMEM((count, tokens, MODEL_WIDTH), low),
            dma((2, count)),
            dma((2, count)),
            pltpu.VMEM(blocks, low),
            pltpu.VMEM(blocks, low),
            dma((pieces, planes)),
            dma((pieces, planes)),
            pltpu.VMEM((height, 2 * FF), kind),
            pltpu.VMEM((planes, slots, FF), low),
            pltpu.VMEM((planes, slots, 2 * FF), low),
            pltpu.VMEM((planes, slots, HEAD_SIZE), kind),
            pltpu.VMEM(blocks, low),
            dma((pieces, planes)),
            dma((pieces, planes)),
            pltpu.VMEM((planes, slots, extra), low),
            pltpu.VMEM((planes, slots, extra), low),
            pltpu.VMEM((count, tokens, extra), low),
            pltpu.VMEM((count + 1, tokens, extra), low),
            pltpu.VMEM((tokens, extra), kind),
            dma((planes,)),
            dma((planes,)),
            dma((2, count)),
            dma((2, count)),
            pltpu.VMEM((count + 1, tokens, MODEL_WIDTH), low),
            dma((2, count)),
            dma((2, count)),
            pltpu.VMEM((2, tile, FF), low),
            pltpu.VMEM((FF, tile), low),
            dma((4,)),
        ],
        compiler_params=pltpu.CompilerParams(
            collective_id=2, has_side_effects=True, vmem_limit_bytes=VMEM_BYTES
        ),
        name="expert_layer",
    )(
        mixed, hidden1, cotangent, gains, routes, masks, picker, grad_rows, router, weight_in,
        weight_back,
    )


def turn_tables(length):
    half = HEAD_SIZE // 2
    freqs = np.float32(ROPE_BASE) ** (-(np.arange(half, dtype=np.float32) * np.float32(2 / HEAD_SIZE)))
    angles = np.arange(length, dtype=np.float32)[:, None] * freqs[None, :]
    cosine, sine = np.cos(angles), np.sin(angles)
    return (
        jnp.asarray(np.concatenate([cosine, cosine], axis=1), jnp.float32),
        jnp.asarray(np.concatenate([-sine, sine], axis=1), jnp.float32),
    )


def body(
    hidden_in,
    routes,
    norm1_gain,
    query_gain,
    key_gain,
    qkv_weight,
    out_weight,
    norm2_gain,
    router,
    gate_up_weight,
    down_weight,
    cotangent,
):
    tokens = hidden_in.shape[1]
    sequence_number = lax.axis_size("seq")
    planes = lax.axis_size("dp")
    devices = sequence_number * planes
    group = lax.axis_index("seq")
    member = lax.axis_index("dp")
    index = group * planes + member
    heads = QUERY_HEADS // sequence_number
    query_columns = heads * HEAD_SIZE
    head_replicas = sequence_number // KEY_VALUE_HEADS
    capacity = (tokens * TOP * 9 + 8 * devices - 1) // (8 * devices)
    slots = -(-sequence_number * capacity // 16) * 16
    chunks = 4
    sequence_length = sequence_number * tokens
    shard = norm1_gain.shape[0]
    small_shard = query_gain.shape[0]

    turn_cos, turn_sin = turn_tables(sequence_length)
    (
        hidden1, mixed_low, lse, gains, picker, full_router, own_cols, out_rows, normed_full,
        heads_low, queries, pair, projected, grad_rows, masks,
    ) = attention_forward(
        sequence_number,
        planes,
        heads,
        shard,
        capacity,
        slots,
        chunks,
        hidden_in[0],
        routes[0],
        norm1_gain[None],
        norm2_gain[None],
        query_gain[None],
        key_gain[None],
        router,
        qkv_weight,
        out_weight,
        cotangent[0],
        turn_cos,
        turn_sin,
    )
    (
        grad_hidden1, grad_branch, grad_router, grad_weight_in, grad_weight_back, combined_rows,
    ) = expert_layer(
        sequence_number,
        planes,
        capacity,
        mixed_low,
        hidden1,
        cotangent[0],
        gains,
        routes[0],
        masks,
        picker,
        grad_rows,
        full_router,
        gate_up_weight[0],
        down_weight[0],
    )
    (
        grad_input, shard_out, shard_qkv, mixed_total, router_total, gain_total, _,
    ) = attention_backward(
        sequence_number,
        planes,
        heads,
        shard,
        capacity,
        grad_branch,
        grad_hidden1,
        hidden_in[0],
        gains,
        grad_router,
        out_rows,
        own_cols,
        normed_full,
        heads_low,
        queries,
        pair,
        projected,
        picker,
        combined_rows,
        lse,
        turn_cos,
        turn_sin,
    )
    output = (hidden1 + mixed_total).astype(jnp.bfloat16)
    index = group * planes + member
    router_own = lax.dynamic_slice_in_dim(router_total, member * shard, shard, 1)
    gain_own = lax.dynamic_slice_in_dim(
        gain_total[: MODEL_WIDTH // HEAD_SIZE].reshape(1, MODEL_WIDTH), index * shard, shard, 1
    )
    head_gains = lax.dynamic_slice_in_dim(
        gain_total[MODEL_WIDTH // HEAD_SIZE :][:2], index * small_shard, small_shard, 1
    )
    return (
        output[None],
        grad_input[None],
        gain_own[0],
        head_gains[0],
        head_gains[1],
        shard_qkv,
        shard_out,
        router_own[devices],
        router_own[:devices].T,
        grad_weight_in.astype(jnp.float32)[None],
        grad_weight_back.astype(jnp.float32)[None],
    )


def solution(mesh):
    in_specs = (
        P("dp", "seq", None),
        P("dp", "seq", None),
        P(("seq", "dp")),
        P(("seq", "dp")),
        P(("seq", "dp")),
        P(("seq", "dp"), None),
        P(("seq", "dp"), None),
        P(("seq", "dp")),
        P(("seq", "dp"), None),
        P(("seq", "dp"), None, None),
        P(("seq", "dp"), None, None),
        P("dp", "seq", None),
    )
    out_specs = (
        P("dp", "seq", None),
        P("dp", "seq", None),
        P(("seq", "dp")),
        P(("seq", "dp")),
        P(("seq", "dp")),
        P(("seq", "dp"), None),
        P(("seq", "dp"), None),
        P(("seq", "dp")),
        P(("seq", "dp"), None),
        P(("seq", "dp"), None, None),
        P(("seq", "dp"), None, None),
    )
    return jax.shard_map(body, mesh=mesh, in_specs=in_specs, out_specs=out_specs, check_vma=False)
```

```python
import functools
import jax
import jax.numpy as jnp
import numpy as np
from jax import lax
from jax.experimental import pallas as pl
from jax.experimental.pallas import tpu as pltpu
from jax.sharding import PartitionSpec as P


MODEL_WIDTH = 2048
QUERY_HEADS = 32
KEY_VALUE_HEADS = 4
HEAD_SIZE = 128
FF = 768
TOP = 8


EPSILON = 1e-06
ROPE_BASE = 1000000.0
FILLER = -1e30
QUERY_BLOCK = 512


MESH = pl.DeviceIdType.MESH
VMEM_BYTES = 63 * 1024 * 1024


def dot_nn(left, right):
    return jnp.dot(left, right, preferred_element_type=jnp.float32)


def dot_nt(left, right):
    return lax.dot_general(
        left, right, (((1,), (1,)), ((), ())), preferred_element_type=jnp.float32
    )


def dot_tn(left, right):
    return lax.dot_general(
        left, right, (((0,), (0,)), ((), ())), preferred_element_type=jnp.float32
    )


def greet(peers, between=None):
    barrier = pltpu.get_barrier_semaphore()
    for peer in peers:
        pl.semaphore_signal(barrier, inc=1, device_id=peer, device_id_type=MESH)
    if between is not None:
        between()
    pl.semaphore_wait(barrier, len(peers))


def remote(source, target, send_sem, recv_sem, device):
    return pltpu.make_async_remote_copy(
        src_ref=source,
        dst_ref=target,
        send_sem=send_sem,
        recv_sem=recv_sem,
        device_id=device,
        device_id_type=MESH,
    )


def line_gather_step(step, count, place, column, blocks, send_sems, recv_sems):
    parts = send_sems.shape[-1]
    height = blocks.shape[1] // parts
    for part in range(parts):
        rows = pl.ds(part * height, height)
        for side, away in ((0, 1), (1, -1)):
            origin = place - away * step
            there = (origin >= 0) & (origin < count)
            target = place + away

            def copy(come, device):
                block = blocks.at[origin, rows]
                return remote(
                    block, block, send_sems.at[side, step, part], recv_sems.at[side, come, part],
                    (device, column),
                )

            if step > 0:

                @pl.when(there)
                def _():
                    copy(step, place).wait_recv()

            if step < count - 1:

                @pl.when(there & (target >= 0) & (target < count))
                def _():
                    copy(step + 1, target).start()


def line_gather_end(count, place, column, blocks, send_sems, recv_sems):
    parts = send_sems.shape[-1]
    height = blocks.shape[1] // parts
    for step in range(count - 1):
        for part in range(parts):
            rows = pl.ds(part * height, height)
            for side, away in ((0, 1), (1, -1)):
                origin = place - away * step
                target = place + away

                @pl.when((origin >= 0) & (origin < count) & (target >= 0) & (target < count))
                def _():
                    block = blocks.at[origin, rows]
                    remote(
                        block, block, send_sems.at[side, step, part], recv_sems.at[side, step, part],
                        (place, column),
                    ).wait_send()


def line_sum_step(step, count, place, column, own, sums, send_sems, recv_sems):
    parts = send_sems.shape[-1]
    height = own.shape[1] // parts
    for part in range(parts):
        rows = pl.ds(part * height, height)
        for side in range(2):
            if side == 0:
                turn = step - place
                index = count - 1 - turn
                active = (turn >= 0) & (index > place)
                target, slot = place + 1, index
            else:
                index = step - (count - 1 - place)
                active = (index >= 0) & (index < place)
                target, slot = place - 1, jnp.where(index == place - 1, count, index)
            fresh = place == (0 if side == 0 else count - 1)

            @pl.when(active)
            def _():
                block = sums.at[index, rows]

                def copy(goal, device):
                    return remote(
                        block, sums.at[goal, rows], send_sems.at[side, index, part],
                        recv_sems.at[side, index, part], (device, column),
                    )

                @pl.when(jnp.logical_not(fresh))
                def _():
                    copy(index, place).wait_recv()
                    sums[index, rows] = (
                        sums[index, rows].astype(jnp.float32) + own[index, rows].astype(jnp.float32)
                    ).astype(jnp.bfloat16)

                @pl.when(fresh)
                def _():
                    sums[index, rows] = own[index, rows]

                copy(slot, target).start()


def line_sum_end(count, place, column, own, sums, send_sems, recv_sems, total):
    parts = send_sems.shape[-1]
    height = own.shape[1] // parts
    for part in range(parts):
        rows = pl.ds(part * height, height)
        total[rows, :] = own[place, rows].astype(jnp.float32)
        for side, come in ((0, place > 0), (1, place < count - 1)):
            slot = place if side == 0 else count

            @pl.when(come)
            def _():
                block = sums.at[slot, rows]
                remote(
                    block, block, send_sems.at[side, place, part], recv_sems.at[side, place, part],
                    (place, column),
                ).wait_recv()
                total[rows, :] += sums[slot, rows].astype(jnp.float32)

    for step in range(count - 1):
        last = count - 1 - step
        for part in range(parts):
            rows = pl.ds(part * height, height)
            for side, index, sent in ((0, last, last > place), (1, step, step < place)):

                @pl.when(sent)
                def _():
                    block = sums.at[index, rows]
                    remote(
                        block, block, send_sems.at[side, index, part], recv_sems.at[side, index, part],
                        (place, column),
                    ).wait_send()


def backward_kernel(
    count, planes, tokens, heads, shard, capacity,
    branch_ref, grad_hidden_ref, hidden_ref, gains_ref, router_ref,
    out_rows_hbm, own_cols_hbm, normed_hbm, heads_hbm, query_hbm, pair_hbm,
    proj_hbm, picker_hbm, combined_hbm, lse_ref, turn_cos_ref, turn_sin_ref,
    grad_input_ref, out_total, qkv_total, mixed_total, router_total, gain_total, mixed_arrived,
    out_rows, own_cols, normed, heads_low, queries, pair, proj, picker, local_sems,
    branch_full, ag_send, ag_recv,
    grad_heads, grad_proj, grad_pair, gain_parts,
    grad_out, out_pair, out_far, out_sems,
    grad_cols, col_pair, col_far, col_sums, columns_out, col_sems,
    normed_room, normed_sums, rs_send, rs_recv, z_sems,
    mixed_rows, mixed_part, mixed_sums, mix_send, mix_recv, mix_local, ms_send, ms_recv,
    router_line, router_sum, router_chip, router_pair, router_sems,
    gain_own, gain_line, gain_chip, gain_pair, gain_sems,
):
    place = lax.axis_index("seq")
    member = lax.axis_index("dp")
    core = lax.rem(member, 2)
    chip = member // 2
    chips = planes // 2
    partner = member + 1 - 2 * core
    length = count * tokens
    query_columns = heads * HEAD_SIZE
    width = query_columns + 2 * HEAD_SIZE
    out_block = query_columns // planes
    scale = HEAD_SIZE ** (-0.5)
    chunks = mixed_part.shape[0]
    wide = MODEL_WIDTH // chunks
    shared = normed_room.shape[0] == 1
    normed_part = branch_full if shared else normed_room
    slots = mixed_rows.shape[1]
    low = jnp.bfloat16

    loads = [
        pltpu.make_async_copy(source, target, local_sems.at[index])
        for index, (source, target) in enumerate(
            [
                (out_rows_hbm, out_rows),
                (query_hbm, queries),
                (pair_hbm, pair),
                (heads_hbm, heads_low),
                (proj_hbm, proj),
                (own_cols_hbm, own_cols),
                (normed_hbm, normed),
                (picker_hbm, picker),
            ]
        )
    ]
    for load in loads:
        load.start()
    branch_full[place] = branch_ref[...]

    far_chips = [(k, lax.rem(chip + k, chips)) for k in range(1, chips)]
    far_places = [(k, lax.rem(place + k, count)) for k in range(1, count)]
    others = [(j, lax.rem(member + j, planes)) for j in range(1, planes)]
    greet([(place, other) for _, other in others] + [(other, member) for _, other in far_places])

    line = (count, place, member, branch_full, ag_send, ag_recv)
    line_gather_step(0, *line)

    def mixed_copy(c, j, other):
        part = pl.ds(c * wide, wide)
        return remote(
            combined_hbm.at[other, :, part], mixed_arrived.at[member, :, part],
            mix_send.at[c, j], mix_recv.at[c, j], (place, other),
        )

    def mixed_send(c):
        for j, other in others:
            mixed_copy(c, j, other).start()

    mixed_send(0)
    mixed_own = pltpu.make_async_copy(
        combined_hbm.at[member], mixed_arrived.at[member], mix_local.at[0]
    )
    mixed_own.start()
    for load in loads:
        load.wait()

    gain_query = gains_ref[2:3, :HEAD_SIZE]
    gain_key = gains_ref[3:4, :HEAD_SIZE]
    grad_pair[...] = jnp.zeros_like(grad_pair)
    gain_parts[...] = jnp.zeros_like(gain_parts)
    key_turned = jnp.transpose(pair[0].astype(jnp.float32)).astype(low)

    def unprepare(grad, raw, gain, cosine, sine):
        turned = grad * cosine - pltpu.roll(grad, HEAD_SIZE // 2, 1) * sine
        inverse = lax.rsqrt(jnp.mean(raw * raw, axis=-1, keepdims=True) + EPSILON)
        unit = raw * inverse
        gain_part = jnp.sum(turned * unit, axis=0, keepdims=True)
        turned = turned * gain
        middle = jnp.mean(turned * unit, axis=-1, keepdims=True)
        return inverse * (turned - unit * middle), gain_part

    together = min(max(1, 2048 // length), heads)

    def process(block):
        at = pl.ds(pl.multiple_of(block * tokens, tokens), tokens)
        partial_heads = dot_nt(
            branch_full[block], out_rows[...].reshape(query_columns, MODEL_WIDTH)
        ).astype(low)
        for head in range(heads):
            grad_heads[head] = partial_heads[:, head * HEAD_SIZE : (head + 1) * HEAD_SIZE]

        cosine, sine = turn_cos_ref[at, :], turn_sin_ref[at, :]

        def some_heads(index, carry):
            first = index * together
            some = pl.ds(first, together)
            query = queries[some, at, :].reshape(together * tokens, HEAD_SIZE)
            grad = grad_heads[some].reshape(together * tokens, HEAD_SIZE)
            scores = dot_nt(pair[0], query) * scale
            shape = (length, together * tokens)
            key_ids = lax.broadcasted_iota(jnp.int32, shape, 0) - block * tokens
            query_ids = lax.rem(lax.broadcasted_iota(jnp.int32, shape, 1), tokens)
            scores = jnp.where(key_ids <= query_ids, scores, FILLER)
            lse = jnp.concatenate([lse_ref[first + k, :, at] for k in range(together)], axis=1)
            probs = jnp.exp(scores - lse)
            grad_probs = dot_nt(pair[1], grad)
            delta = jnp.sum(probs * grad_probs, axis=0, keepdims=True)
            grad_scores = (probs * (grad_probs - delta)).astype(low)
            grad_pair[0] += dot_nn(grad_scores, query) * scale
            grad_pair[1] += dot_nn(probs.astype(low), grad)
            grad_query = jnp.transpose(dot_nn(key_turned, grad_scores)) * scale
            for k in range(together):
                grad_raw, gain_part = unprepare(
                    grad_query[k * tokens : (k + 1) * tokens],
                    proj[first + k, at, :],
                    gain_query,
                    cosine,
                    sine,
                )
                gain_parts[0:1, :] += gain_part
                columns = pl.ds(pl.multiple_of((first + k) * HEAD_SIZE, HEAD_SIZE), HEAD_SIZE)
                grad_proj[at, columns] = grad_raw.astype(low)
            return carry

        lax.fori_loop(0, heads // together, some_heads, 0)

    def gather(step):
        line_gather_step(step, *line)

        def side(index, carry):
            block = place - step + 2 * step * index

            @pl.when((block >= 0) & (block < count))
            def _():
                process(block)

            return carry

        lax.fori_loop(0, 2, side, 0)

    def mixed_line(c):
        return (count, place, member, mixed_part.at[c], mixed_sums.at[c], ms_send.at[c], ms_recv.at[c])

    def mixed_chunk(c):
        for j, other in others:
            mixed_copy(c, j, other).wait_recv()
        if c == 0:
            mixed_own.wait()
        load = pltpu.make_async_copy(
            mixed_arrived.at[:, :, pl.ds(c * wide, wide)], mixed_rows, mix_local.at[1]
        )
        load.start()
        load.wait()
        for rank in range(count):
            block = ranked_block(rank, place, count)
            first = rank * capacity // 16 * 16
            final = min(-(-(rank + 1) * capacity // 16) * 16, slots)
            height = planes * (final - first)
            at = pl.ds(pl.multiple_of(block * tokens, tokens), tokens)
            choice = picker[:, first:final, at].reshape(height, tokens)
            mixed_part[c, block] = dot_tn(
                choice, mixed_rows[:, first:final, :].reshape(height, wide)
            ).astype(low)

    waves = list(range(chunks + count - 2))

    def mixed_wave():
        wave = waves.pop(0)
        for c in range(chunks):
            if 0 <= wave - c < count - 1:
                line_sum_step(wave - c, *mixed_line(c))

    process(place)
    mixed_send(1)
    for step in range(1, count):
        gather(step)
        if step < count - 1 and step <= chunks - 2:
            mixed_send(step + 1)
            mixed_chunk(step - 1)
            mixed_wave()
    mixed_done = min(chunks - 2, count - 2)
    for c in range(mixed_done + 2, chunks):
        mixed_send(c)
    line_gather_end(*line)

    per_head = HEAD_SIZE // out_block

    def out_gradient(head):
        all_branch = branch_full[...].reshape(length, MODEL_WIDTH)
        part = dot_tn(heads_low[head], all_branch).astype(low)
        if per_head == 1:
            grad_out[head] = part
        else:
            grad_out[head * per_head : (head + 1) * per_head] = part.reshape(
                per_head, out_block, MODEL_WIDTH
            )

    def out_copy(k):
        return remote(
            grad_out.at[2 * k + 1 - core], out_pair.at[k], out_sems.at[0, k], out_sems.at[1, k],
            (place, partner),
        )

    def out_far_copy(k, other):
        return remote(
            out_pair.at[other], out_far.at[k - 1], out_sems.at[2, k], out_sems.at[3, k],
            (place, 2 * other + core),
        )

    def out_gradients():
        if per_head == 1:
            for k in range(chips):
                out_gradient(2 * k + 1 - core)
                out_copy(k).start()

            def rest(k, carry):
                out_gradient(2 * k + core)
                return carry

            lax.fori_loop(0, chips, rest, 0)
        else:
            for head in range(heads):
                out_gradient(head)
            for k in range(chips):
                out_copy(k).start()

    def out_pairs():
        for k in range(chips):
            out_copy(k).wait_recv()
            out_pair[k] = (
                out_pair[k].astype(jnp.float32) + grad_out[2 * k + core].astype(jnp.float32)
            ).astype(low)
        for k, other in far_chips:
            out_far_copy(k, other).start()

    lane_part = MODEL_WIDTH // count

    def router_far(k, other):
        return remote(
            router_ref.at[:, pl.ds(pl.multiple_of(other * lane_part, lane_part), lane_part)],
            router_line.at[k - 1], router_sems.at[0, k], router_sems.at[1, k], (other, member),
        )

    def router_near(k, other):
        return remote(
            router_sum.at[0], router_chip.at[k - 1], router_sems.at[2, k], router_sems.at[3, k],
            (place, 2 * other + core),
        )

    def router_last():
        return remote(
            router_sum.at[1], router_pair, router_sems.at[2, 0], router_sems.at[3, 0], (place, partner)
        )

    groups = [(0, heads + 2)]

    def columns_of(group):
        return pl.ds(groups[group][0] * HEAD_SIZE, (groups[group][1] - groups[group][0]) * HEAD_SIZE)

    def col_copy(group, k):
        part = columns_of(group)
        return remote(
            grad_cols.at[:, 2 * k + 1 - core, :, part], col_pair.at[k, :, :, part],
            col_sems.at[group, 0, k], col_sems.at[group, 1, k], (place, partner),
        )

    def col_far_copy(group, k, other):
        part = columns_of(group)
        return remote(
            col_pair.at[other, :, :, part], col_far.at[k - 1, :, :, part],
            col_sems.at[group, 2, k], col_sems.at[group, 3, k], (place, 2 * other + core),
        )

    def z_copy(group, k, other):
        part = columns_of(group)
        return remote(
            col_sums.at[other, :, part], columns_out.at[place, :, part],
            z_sems.at[group, 0, k], z_sems.at[group, 1, k], (other, member),
        )

    def col_gradient(group):
        first, final = groups[group]
        grads = grad_proj[:, first * HEAD_SIZE : final * HEAD_SIZE]
        block_width = planes * shard
        for block in range(count):
            part = dot_tn(normed[:, block * block_width : (block + 1) * block_width], grads)
            grad_cols[block, :, :, first * HEAD_SIZE : final * HEAD_SIZE] = part.astype(low).reshape(
                planes, shard, (final - first) * HEAD_SIZE
            )
        for k in range(chips):
            col_copy(group, k).start()

    def col_pairs(group):
        first, final = groups[group]
        columns = slice(first * HEAD_SIZE, final * HEAD_SIZE)
        for k in range(chips):
            col_copy(group, k).wait_recv()
            col_pair[k, :, :, columns] = (
                col_pair[k, :, :, columns].astype(jnp.float32)
                + grad_cols[:, 2 * k + core, :, columns].astype(jnp.float32)
            ).astype(low)
        for k, other in far_chips:
            col_far_copy(group, k, other).start()

    def col_totals(group):
        first, final = groups[group]
        columns = slice(first * HEAD_SIZE, final * HEAD_SIZE)
        total = col_pair[chip, :, :, columns].astype(jnp.float32)
        for k, other in far_chips:
            col_far_copy(group, k, other).wait_recv()
            total += col_far[k - 1, :, :, columns].astype(jnp.float32)
        col_sums[:, :, columns] = total.astype(low)
        for k, other in far_places:
            z_copy(group, k, other).start()
        columns_out[place, :, columns] = col_sums[place, :, columns]

    grad_raw, gain_part = unprepare(
        grad_pair[0], proj[heads], gain_key, turn_cos_ref[...], turn_sin_ref[...]
    )
    gain_parts[1:2, :] += gain_part
    grad_proj[:, query_columns : query_columns + HEAD_SIZE] = grad_raw.astype(low)
    grad_proj[:, query_columns + HEAD_SIZE :] = grad_pair[1].astype(low)

    def gain_far(k, other):
        return remote(
            gain_own.at[0], gain_line.at[k - 1], gain_sems.at[0, k], gain_sems.at[1, k], (other, member)
        )

    def gain_near(k, other):
        return remote(
            gain_own.at[1], gain_chip.at[k - 1], gain_sems.at[2, k], gain_sems.at[3, k],
            (place, 2 * other + core),
        )

    def gain_last():
        return remote(
            gain_own.at[2], gain_pair, gain_sems.at[2, 0], gain_sems.at[3, 0], (place, partner)
        )

    sums = (count, place, member, normed_part, normed_sums, rs_send, rs_recv)

    def normed_step(step):
        block = ranked_block(count - 1 - step, place, count)
        at = pl.ds(pl.multiple_of(block * tokens, tokens), tokens)
        part = dot_nt(grad_proj[at, :], own_cols[...].reshape(MODEL_WIDTH, width))
        normed_part[block] = part.astype(low)
        if step < count - 1:
            line_sum_step(step, *sums)
        return jnp.sum(part * normed[at, :].astype(jnp.float32), axis=0, keepdims=True)

    if shared:
        out_gradients()
    gain_row = normed_step(0)
    col_gradient(0)
    col_pairs(0)
    for c in range(mixed_done, chunks):
        mixed_chunk(c)
        mixed_wave()
    gain_row += normed_step(1)
    if not shared:
        out_gradients()
    out_pairs()
    for k, other in far_places:
        router_far(k, other).start()
    if waves:
        mixed_wave()
    for step in range(2, count):
        gain_row += normed_step(step)
    gain_row = gain_row / gains_ref[0:1, :]
    for k in range(MODEL_WIDTH // HEAD_SIZE):
        gain_own[0, k : k + 1, :] = gain_row[:, k * HEAD_SIZE : (k + 1) * HEAD_SIZE]
    gain_own[0, MODEL_WIDTH // HEAD_SIZE :, :] = gain_parts[...]
    for k, other in far_places:
        gain_far(k, other).start()
    while waves:
        mixed_wave()
    own_lanes = pl.ds(pl.multiple_of(place * lane_part, lane_part), lane_part)
    total = router_ref[:, own_lanes]
    for k, other in far_places:
        router_far(k, other).wait_recv()
        total += router_line[k - 1]
    router_sum[0] = total
    for k, other in far_chips:
        router_near(k, other).start()
    total = gain_own[0]
    for k, other in far_places:
        gain_far(k, other).wait_recv()
        total += gain_line[k - 1]
    gain_own[1] = total
    for k, other in far_chips:
        gain_near(k, other).start()
    col_totals(0)
    for c in range(chunks):
        line_sum_end(*mixed_line(c), mixed_total.at[:, c * wide : (c + 1) * wide])
    line_sum_end(*sums, grad_input_ref)
    total = out_pair[chip].astype(jnp.float32)
    for k, other in far_chips:
        out_far_copy(k, other).wait_recv()
        total += out_far[k - 1].astype(jnp.float32)
    out_total[...] = total
    total = router_sum[0]
    for k, other in far_chips:
        router_near(k, other).wait_recv()
        total += router_chip[k - 1]
    router_sum[1] = total
    router_last().start()
    total = gain_own[1]
    for k, other in far_chips:
        gain_near(k, other).wait_recv()
        total += gain_chip[k - 1]
    gain_own[2] = total
    gain_last().start()
    gain_last().wait_recv()
    gain_total[...] = gain_own[2] + gain_pair[...]
    router_last().wait_recv()
    router_total[...] = router_sum[1] + router_pair[...]

    hidden = hidden_ref[...].astype(jnp.float32)
    inverse = lax.rsqrt(jnp.mean(hidden * hidden, axis=-1, keepdims=True) + EPSILON)
    unit = hidden * inverse
    grad_normed = grad_input_ref[...]
    turned = grad_normed * gains_ref[0:1, :]
    grad_input_ref[...] = grad_hidden_ref[...] + inverse * (
        turned - unit * jnp.mean(turned * unit, axis=-1, keepdims=True)
    )
    for group in range(len(groups)):
        for k, other in far_places:
            z_copy(group, k, other).wait_recv()
            z_copy(group, k, other).wait_send()
        for part in range(count):
            qkv_total[:, part * query_columns : (part + 1) * query_columns] = columns_out[
                part, :, :query_columns
            ].astype(jnp.float32)
        replicas = count // KEY_VALUE_HEADS
        for head in range(2 * KEY_VALUE_HEADS):
            kind, pair_head = head // KEY_VALUE_HEADS, head % KEY_VALUE_HEADS
            begin = query_columns + kind * HEAD_SIZE
            total = jnp.zeros((shard, HEAD_SIZE), jnp.float32)
            for part in range(pair_head * replicas, (pair_head + 1) * replicas):
                total += columns_out[part, :, begin : begin + HEAD_SIZE].astype(jnp.float32)
            begin = (QUERY_HEADS + head) * HEAD_SIZE
            qkv_total[:, begin : begin + HEAD_SIZE] = total
        for k in range(chips):
            col_copy(group, k).wait_send()
        for k, other in far_chips:
            col_far_copy(group, k, other).wait_send()
    for k in range(chips):
        out_copy(k).wait_send()
    for k, other in far_chips:
        out_far_copy(k, other).wait_send()
        router_near(k, other).wait_send()
        gain_near(k, other).wait_send()
    for k, other in far_places:
        router_far(k, other).wait_send()
        gain_far(k, other).wait_send()
    router_last().wait_send()
    gain_last().wait_send()
    for c in range(chunks):
        for j, other in others:
            mixed_copy(c, j, other).wait_send()


def attention_backward(
    count, planes, heads, shard, capacity, branch, grad_hidden, hidden, gains, router, out_rows, own_cols, normed,
    heads_low, queries, pair, proj, picker, combined, lse, turn_cos, turn_sin,
):
    tokens = branch.shape[0]
    length = count * tokens
    width = (heads + 2) * HEAD_SIZE
    chips = planes // 2
    out_block = heads * HEAD_SIZE // planes
    chunks = 4
    wide = MODEL_WIDTH // chunks
    gain_rows = MODEL_WIDTH // HEAD_SIZE + 8
    router_part = (router.shape[0], MODEL_WIDTH // count)
    low, kind = jnp.bfloat16, jnp.float32
    vmem = pl.BlockSpec(memory_space=pltpu.VMEM)
    anywhere = pl.BlockSpec(memory_space=pl.ANY)
    dma = pltpu.SemaphoreType.DMA
    shape = jax.ShapeDtypeStruct
    most = max(count, chips)
    return pl.pallas_call(
        functools.partial(backward_kernel, count, planes, tokens, heads, shard, capacity),
        out_shape=(
            shape((tokens, MODEL_WIDTH), kind),
            shape((out_block, MODEL_WIDTH), kind),
            shape((shard, (QUERY_HEADS + 2 * KEY_VALUE_HEADS) * HEAD_SIZE), kind),
            shape((tokens, MODEL_WIDTH), kind),
            shape(router_part, kind),
            shape((gain_rows, HEAD_SIZE), kind),
            shape(combined.shape, low),
        ),
        in_specs=[vmem] * 5 + [anywhere] * 9 + [vmem] * 3,
        out_specs=(vmem,) * 6 + (anywhere,),
        scratch_shapes=[
            pltpu.VMEM(out_rows.shape, low),
            pltpu.VMEM(own_cols.shape, low),
            pltpu.VMEM(normed.shape, low),
            pltpu.VMEM(heads_low.shape, low),
            pltpu.VMEM(queries.shape, low),
            pltpu.VMEM(pair.shape, low),
            pltpu.VMEM(proj.shape, kind),
            pltpu.VMEM(picker.shape, low),
            dma((8,)),
            pltpu.VMEM((count, tokens, MODEL_WIDTH), low),
            dma((2, count, 2)),
            dma((2, count, 2)),
            pltpu.VMEM((heads, tokens, HEAD_SIZE), low),
            pltpu.VMEM((length, width), low),
            pltpu.VMEM((2, length, HEAD_SIZE), kind),
            pltpu.VMEM((8, HEAD_SIZE), kind),
            pltpu.VMEM((planes, out_block, MODEL_WIDTH), low),
            pltpu.VMEM((chips, out_block, MODEL_WIDTH), low),
            pltpu.VMEM((chips - 1, out_block, MODEL_WIDTH), low),
            dma((4, chips)),
            pltpu.VMEM((count, planes, shard, width), low),
            pltpu.VMEM((chips, count, shard, width), low),
            pltpu.VMEM((chips - 1, count, shard, width), low),
            pltpu.VMEM((count, shard, width), low),
            pltpu.VMEM((count, shard, width), low),
            dma((2, 4, chips)),
            pltpu.VMEM((count if count <= 4 else 1, tokens, MODEL_WIDTH), low),
            pltpu.VMEM((count + 1, tokens, MODEL_WIDTH), low),
            dma((2, count, 2)),
            dma((2, count, 2)),
            dma((2, 2, count)),
            pltpu.VMEM(combined.shape[:2] + (wide,), low),
            pltpu.VMEM((chunks, count, tokens, wide), low),
            pltpu.VMEM((chunks, count + 1, tokens, wide), low),
            dma((chunks, planes)),
            dma((chunks, planes)),
            dma((2,)),
            dma((chunks, 2, count, 1)),
            dma((chunks, 2, count, 1)),
            pltpu.VMEM((count - 1,) + router_part, kind),
            pltpu.VMEM((2,) + router_part, kind),
            pltpu.VMEM((chips - 1,) + router_part, kind),
            pltpu.VMEM(router_part, kind),
            dma((4, most)),
            pltpu.VMEM((3, gain_rows, HEAD_SIZE), kind),
            pltpu.VMEM((count - 1, gain_rows, HEAD_SIZE), kind),
            pltpu.VMEM((chips - 1, gain_rows, HEAD_SIZE), kind),
            pltpu.VMEM((gain_rows, HEAD_SIZE), kind),
            dma((4, most)),
        ],
        compiler_params=pltpu.CompilerParams(
            collective_id=3, has_side_effects=True, vmem_limit_bytes=VMEM_BYTES
        ),
        name="attention_backward",
    )(
        branch, grad_hidden, hidden, gains, router, out_rows, own_cols, normed, heads_low, queries,
        pair, proj, picker, combined, lse, turn_cos, turn_sin,
    )


def forward_kernel(
    count, planes, tokens, heads, shard, capacity, chunks,
    hidden_ref, routes_ref, gain1_ref, gain2_ref, query_gain_ref, key_gain_ref, router_ref, qkv_ref,
    out_ref, cotangent_ref, turn_cos_ref, turn_sin_ref,
    hidden1_ref, mixed_ref, lse_ref, gains_ref, picker_ref,
    router_out, own_cols_hbm, out_rows_hbm, normed_hbm, heads_hbm, query_hbm, pair_hbm, proj_hbm,
    grad_hbm, masks_hbm,
    column_send, own_cols, c_send, c_recv,
    out_rows, o_send, o_recv,
    hidden_full, h_send, h_recv,
    gains_all, gz_send, gz_recv, gd_send, gd_recv,
    router_all, rz_send, rz_recv, rd_send, rd_recv,
    places_all, p_send, p_recv,
    normed, proj, queries, pair, heads_low,
    grad_full, dy_send, dy_recv,
    grad_sent, d_send, d_recv, mask_sent, m_send, m_recv,
    branch, sums, rs_send, rs_recv, local_sems,
):
    place = lax.axis_index("seq")
    member = lax.axis_index("dp")
    core = lax.rem(member, 2)
    chip = member // 2
    chips = planes // 2
    partner = member + 1 - 2 * core
    length = count * tokens
    query_columns = heads * HEAD_SIZE
    replicas = count // KEY_VALUE_HEADS
    wide = MODEL_WIDTH // chunks
    slots = grad_sent.shape[2]
    rows = planes * slots
    low = jnp.bfloat16
    scale = HEAD_SIZE ** (-0.5)
    far_places = [(k, lax.rem(place + k, count)) for k in range(1, count)]
    far_chips = [(k, lax.rem(chip + k, chips)) for k in range(1, chips)]
    others = [(j, lax.rem(member + j, planes)) for j in range(1, planes)]

    def column_parts():
        for part in range(count):
            head = part // replicas
            keys = QUERY_HEADS * HEAD_SIZE + head * HEAD_SIZE
            values = keys + KEY_VALUE_HEADS * HEAD_SIZE
            column_send[part, :, :query_columns] = qkv_ref[
                :, part * query_columns : (part + 1) * query_columns
            ]
            column_send[part, :, query_columns : query_columns + HEAD_SIZE] = qkv_ref[
                :, keys : keys + HEAD_SIZE
            ]
            column_send[part, :, query_columns + HEAD_SIZE :] = qkv_ref[
                :, values : values + HEAD_SIZE
            ]

    greet(
        [(place, other) for _, other in others] + [(other, member) for _, other in far_places],
        column_parts,
    )

    def column_copy(k, other):
        return remote(
            column_send.at[other], own_cols.at[place, member], c_send.at[0, k], c_recv.at[0, k],
            (other, member),
        )

    def gain_line(k, other):
        mine = gains_all.at[place, member]
        return remote(mine, mine, gz_send.at[k], gz_recv.at[k], (other, member))

    def router_line(k, other):
        mine = router_all.at[place, member]
        return remote(mine, mine, rz_send.at[k], rz_recv.at[k], (other, member))

    def places_line(k, other):
        mine = places_all.at[place]
        return remote(mine, mine, p_send.at[k], p_recv.at[k], (other, member))

    def out_copy(k, other):
        return remote(
            out_ref, out_rows.at[member], o_send.at[0, k], o_recv.at[0, k], (place, 2 * other + core)
        )

    def out_pair(k, other):
        source = out_ref if k == 0 else out_rows.at[2 * other + core]
        return remote(
            source, out_rows.at[2 * other + core], o_send.at[1, k], o_recv.at[1, k], (place, partner)
        )

    def block_copy(k, other):
        mine = own_cols.at[:, member]
        return remote(mine, mine, c_send.at[1, k], c_recv.at[1, k], (place, 2 * other + core))

    def block_pair(k, other):
        block = own_cols.at[:, 2 * other + core]
        return remote(block, block, c_send.at[2, k], c_recv.at[2, k], (place, partner))

    for k, other in far_places:
        column_copy(k, other).start()
    for k, other in far_chips:
        out_copy(k, other).start()
    out_pair(0, chip).start()

    hidden_line = (count, place, member, hidden_full, h_send, h_recv)
    index = place * planes + member
    row_lanes = lax.broadcasted_iota(jnp.int32, (1, HEAD_SIZE), 1)
    pieces = []
    for ref in (gain1_ref, gain2_ref, query_gain_ref, key_gain_ref):
        gain_width = ref.shape[1]
        values = ref[...].astype(jnp.float32)
        begin = lax.rem(index, HEAD_SIZE // gain_width) * gain_width
        piece = jnp.zeros((1, HEAD_SIZE), jnp.float32)
        for k in range(gain_width):
            piece += jnp.where(row_lanes == begin + k, values[:, k : k + 1], 0.0)
        pieces.append(piece)
    pieces.append(jnp.zeros((gains_all.shape[2] - 4, HEAD_SIZE), jnp.float32))
    gains_all[place, member] = jnp.concatenate(pieces, axis=0).astype(low)
    for k, other in far_places:
        gain_line(k, other).start()
    hidden_full[place] = hidden_ref[...]
    line_gather_step(0, *hidden_line)
    router_all[place, member] = jnp.zeros(router_all.shape[2:], low)
    router_all[place, member, :, : router_ref.shape[1]] = router_ref[...]
    lanes = lax.broadcasted_iota(jnp.int32, (tokens, places_all.shape[-1]), 1)
    named = jnp.zeros(lanes.shape, jnp.float32)
    for k in range(TOP):
        named += jnp.where(routes_ref[:, k : k + 1] == lanes, 1.0, 0.0)
    row_ids = lax.broadcasted_iota(jnp.int32, (tokens, tokens), 0)
    col_ids = lax.broadcasted_iota(jnp.int32, (tokens, tokens), 1)
    before = jnp.where(row_ids > col_ids, 1.0, 0.0).astype(low)
    earlier = dot_nn(before, named.astype(low))
    places_all[place] = jnp.where(named > 0, earlier, -512.0).astype(low)
    for c in range(chunks):
        grad_full[c, place] = cotangent_ref[:, c * wide : (c + 1) * wide]
    for k, other in far_places:
        places_line(k, other).start()
        router_line(k, other).start()
    own_cols[place, member] = column_send[place]
    out_rows[member] = out_ref[...]

    def gain_plane(j, other):
        mine = gains_all.at[:, member]
        return remote(mine, mine, gd_send.at[j], gd_recv.at[j], (place, other))

    def router_plane(j, other):
        mine = router_all.at[:, member]
        return remote(mine, mine, rd_send.at[j], rd_recv.at[j], (place, other))

    for k, other in far_places:
        gain_line(k, other).wait_recv()
    for j, other in others:
        gain_plane(j, other).start()
    for k, other in far_places:
        column_copy(k, other).wait_recv()
    for k, other in far_chips:
        block_copy(k, other).start()
    block_pair(0, chip).start()
    line_gather_step(1, *hidden_line)

    for k, other in far_places:
        places_line(k, other).wait_recv()
    experts = places_all.shape[-1]
    pick_rows = lax.broadcasted_iota(jnp.int32, (rows, experts), 0)
    pick_experts = lax.broadcasted_iota(jnp.int32, (rows, experts), 1) - place * planes
    slot_ids = lax.broadcasted_iota(jnp.int32, (rows, length), 0)
    token_ids = lax.broadcasted_iota(jnp.int32, (rows, length), 1)
    offsets = jnp.zeros((rows, length), jnp.int32)
    choose = jnp.zeros((rows, experts), jnp.float32)
    for other in range(planes):
        inside = (pick_rows >= other * slots) & (pick_rows < (other + 1) * slots)
        choose += jnp.where(inside & (pick_experts == other), 1.0, 0.0)
        offsets = jnp.where(slot_ids >= other * slots, other * slots, offsets)
    before_block = jnp.zeros((rows, length), jnp.int32)
    for block in range(count):
        before_block = jnp.where(
            token_ids >= block * tokens, block_rank(block, place, count) * capacity, before_block
        )
    wanted = dot_nt(choose.astype(low), places_all[...].reshape(length, experts))
    picker_rows = jnp.where(
        wanted == (slot_ids - offsets - before_block).astype(jnp.float32), 1.0, 0.0
    ).astype(low)
    picker_ref[...] = picker_rows.reshape(planes, slots, length)
    mask_full = jnp.where(places_all[...].reshape(length, experts).astype(jnp.float32) >= 0, 1.0, 0.0)
    mask_sent[...] = (
        dot_nn(picker_rows, mask_full.astype(low)).astype(low).reshape(mask_sent.shape)
    )

    for k, other in far_places:
        router_line(k, other).wait_recv()
    for j, other in others:
        router_plane(j, other).start()

    def mask_copy(j, other):
        return remote(
            mask_sent.at[other], masks_hbm.at[member], m_send.at[j], m_recv.at[j], (place, other)
        )

    for j, other in others:
        mask_copy(j, other).start()
    masks_own = pltpu.make_async_copy(mask_sent.at[member], masks_hbm.at[member], local_sems.at[0])
    masks_own.start()

    for step in range(2, count - 1):
        line_gather_step(step, *hidden_line)

    def grad_line(c):
        return (count, place, member, grad_full.at[c], dy_send.at[c], dy_recv.at[c])

    def grad_copy(c, j, other):
        return remote(
            grad_sent.at[c, other], grad_hbm.at[c, member], d_send.at[c, j], d_recv.at[c, j], (place, other)
        )

    def grad_own(c):
        return pltpu.make_async_copy(
            grad_sent.at[c, member], grad_hbm.at[c, member], local_sems.at[16 + c]
        )

    def grad_tick(tick):
        for c in range(chunks):
            step = tick - c
            if 0 <= step < count:
                line_gather_step(step, *grad_line(c))
            if step == count - 1:
                picked = dot_nn(
                    picker_ref[...].reshape(rows, length), grad_full[c].reshape(length, wide)
                ).astype(low)
                grad_sent[c] = picked.reshape(planes, slots, wide)
                for j, other in others:
                    grad_copy(c, j, other).start()
                grad_own(c).start()

    ticks = list(range(chunks + count - 1))
    grad_tick(ticks.pop(0))
    line_gather_step(count - 1, *hidden_line)

    for j, other in others:
        gain_plane(j, other).wait_recv()
    per_row = HEAD_SIZE // shard
    small_total = jnp.sum(gains_all[...].astype(jnp.float32), axis=(0, 1))
    gain_rows = []
    for row in range(2):
        parts = []
        for group in range(MODEL_WIDTH // HEAD_SIZE):
            part = jnp.zeros((1, HEAD_SIZE), jnp.float32)
            for index in range(group * per_row, (group + 1) * per_row):
                part += gains_all[index // planes, index % planes, row : row + 1, :].astype(jnp.float32)
            parts.append(part)
        gain_rows.append(jnp.concatenate(parts, axis=1))
    gains_ref[0:1, :] = gain_rows[0]
    gains_ref[1:2, :] = gain_rows[1]
    gain_query = small_total[2:3, :]
    gain_key = small_total[3:4, :]
    gains_ref[2:3, :HEAD_SIZE] = gain_query
    gains_ref[3:4, :HEAD_SIZE] = gain_key

    def normalize(values, gain):
        return (
            values
            * lax.rsqrt(jnp.mean(values * values, axis=-1, keepdims=True) + EPSILON)
            * gain
        )

    for block in range(count):
        values = hidden_full[block].astype(jnp.float32)
        normed[block * tokens : (block + 1) * tokens, :] = normalize(values, gain_rows[0]).astype(low)
    stores = [pltpu.make_async_copy(normed, normed_hbm, local_sems.at[1])]
    stores[-1].start()

    for k, other in far_chips:
        block_copy(k, other).wait_recv()
    for k, other in far_chips:
        block_pair(k, lax.rem(chip + chips - k, chips)).start()
    for k, other in far_chips:
        out_copy(k, other).wait_recv()
    for k, other in far_chips:
        out_pair(k, lax.rem(chip + chips - k, chips)).start()
    block_pair(0, chip).wait_recv()
    for k, other in far_chips:
        block_pair(k, lax.rem(chip + chips - k, chips)).wait_recv()
    weights = own_cols[...].reshape(MODEL_WIDTH, query_columns + 2 * HEAD_SIZE)
    stores.append(pltpu.make_async_copy(own_cols, own_cols_hbm, local_sems.at[2]))
    stores[-1].start()

    def prepare(values, gain):
        turned = normalize(values, gain)
        return turned * turn_cos_ref[...] + pltpu.roll(turned, HEAD_SIZE // 2, 1) * turn_sin_ref[...]

    paired = dot_nn(normed[...], weights[:, query_columns:])
    proj[heads] = paired[:, :HEAD_SIZE]
    proj[heads + 1] = paired[:, HEAD_SIZE:]
    pair[0] = prepare(paired[:, :HEAD_SIZE], gain_key).astype(low)
    pair[1] = paired[:, HEAD_SIZE:].astype(low)
    projected = dot_nn(normed[...], weights[:, :query_columns])
    for head in range(heads):
        proj[head] = projected[:, head * HEAD_SIZE : (head + 1) * HEAD_SIZE]
    value_turned = jnp.transpose(paired[:, HEAD_SIZE:]).astype(low)
    stores.append(pltpu.make_async_copy(proj, proj_hbm, local_sems.at[3]))
    stores[-1].start()
    stores.append(pltpu.make_async_copy(pair, pair_hbm, local_sems.at[4]))
    stores[-1].start()
    together = min(max(1, 2048 // length), heads)

    def some_heads(index, carry):
        first = index * together
        some = pl.ds(first, together)
        for k in range(together):
            queries[first + k] = prepare(proj[first + k], gain_query).astype(low)
        for block in range(count):
            begin, end = block * tokens, (block + 1) * tokens
            query = queries[some, begin:end, :].reshape(together * tokens, HEAD_SIZE)
            scores = dot_nt(pair[0, :end, :], query) * scale
            shape = (end, together * tokens)
            key_ids = lax.broadcasted_iota(jnp.int32, shape, 0) - begin
            query_ids = lax.rem(lax.broadcasted_iota(jnp.int32, shape, 1), tokens)
            scores = jnp.where(key_ids <= query_ids, scores, FILLER)
            top = jnp.max(scores, axis=0, keepdims=True)
            powers = jnp.exp(scores - top)
            total = jnp.sum(powers, axis=0, keepdims=True)
            lse = top + jnp.log(total)
            for k in range(together):
                lse_ref[first + k, :, begin:end] = lse[:, k * tokens : (k + 1) * tokens]
            probs = (powers * (1.0 / total)).astype(low)
            mixed = dot_nn(value_turned[:, :end], probs)
            heads_low[some, begin:end, :] = (
                jnp.transpose(mixed).astype(low).reshape(together, tokens, HEAD_SIZE)
            )
        return carry

    for part in range(heads // together):
        some_heads(part, 0)
        for _ in range(4 * together // heads):
            if ticks:
                grad_tick(ticks.pop(0))
    stores.append(pltpu.make_async_copy(queries, query_hbm, local_sems.at[5]))
    stores[-1].start()
    stores.append(pltpu.make_async_copy(heads_low, heads_hbm, local_sems.at[6]))
    stores[-1].start()

    out_pair(0, chip).wait_recv()
    for k, other in far_chips:
        out_pair(k, lax.rem(chip + chips - k, chips)).wait_recv()
    out_all = out_rows[...].reshape(query_columns, MODEL_WIDTH)
    stores.append(pltpu.make_async_copy(out_rows, out_rows_hbm, local_sems.at[7]))
    stores[-1].start()

    def project(block, carry):
        at = pl.ds(pl.multiple_of(block * tokens, tokens), tokens)
        mixed = jnp.concatenate([heads_low[head, at, :] for head in range(heads)], axis=1)
        branch[block] = dot_nn(mixed, out_all).astype(low)
        return carry

    lax.fori_loop(0, count, project, 0)
    line = (count, place, member, branch, sums, rs_send, rs_recv)
    for step in range(count - 1):
        line_sum_step(step, *line)
        for _ in range(-(-len(ticks) // (count - 1 - step))):
            grad_tick(ticks.pop(0))
    line_sum_end(*line, hidden1_ref)
    hidden1 = hidden_ref[...].astype(jnp.float32) + hidden1_ref[...]
    hidden1_ref[...] = hidden1
    mixed_ref[...] = normalize(hidden1, gain_rows[1]).astype(low)

    for j, other in others:
        router_plane(j, other).wait_recv()
    router_out[...] = router_all[...].reshape(router_out.shape)
    for j, other in others:
        mask_copy(j, other).wait_recv()
        for c in range(chunks):
            grad_copy(c, j, other).wait_recv()
    for k, other in far_places:
        gain_line(k, other).wait_send()
        column_copy(k, other).wait_send()
        places_line(k, other).wait_send()
        router_line(k, other).wait_send()
    for k, other in far_chips:
        out_copy(k, other).wait_send()
        block_copy(k, other).wait_send()
        out_pair(k, other).wait_send()
        block_pair(k, other).wait_send()
    out_pair(0, chip).wait_send()
    block_pair(0, chip).wait_send()
    for j, other in others:
        gain_plane(j, other).wait_send()
        router_plane(j, other).wait_send()
        mask_copy(j, other).wait_send()
        for c in range(chunks):
            grad_copy(c, j, other).wait_send()
    for c in range(chunks):
        grad_own(c).wait()
        line_gather_end(*grad_line(c))
    line_gather_end(*hidden_line)
    masks_own.wait()
    for store in stores:
        store.wait()


def attention_forward(
    count, planes, heads, shard, capacity, slots, chunks,
    hidden, routes, gain_one, gain_two, query_gain, key_gain, router, qkv, out_weight, cotangent,
    turn_cos, turn_sin,
):
    tokens = hidden.shape[0]
    length = count * tokens
    width = (heads + 2) * HEAD_SIZE
    chips = planes // 2
    wide = MODEL_WIDTH // chunks
    experts = -(-router.shape[-1] // 128) * 128
    small_rows = 16
    out_block = out_weight.shape[0]
    low, full = jnp.bfloat16, jnp.float32
    vmem = pl.BlockSpec(memory_space=pltpu.VMEM)
    anywhere = pl.BlockSpec(memory_space=pl.ANY)
    dma = pltpu.SemaphoreType.DMA
    shape = jax.ShapeDtypeStruct
    return pl.pallas_call(
        functools.partial(forward_kernel, count, planes, tokens, heads, shard, capacity, chunks),
        out_shape=(
            shape((tokens, MODEL_WIDTH), full),
            shape((tokens, MODEL_WIDTH), low),
            shape((heads, 1, length), full),
            shape((8, MODEL_WIDTH), full),
            shape((planes, slots, length), low),
            shape((MODEL_WIDTH, experts), low),
            shape((count, planes, shard, width), low),
            shape((planes, out_block, MODEL_WIDTH), low),
            shape((length, MODEL_WIDTH), low),
            shape((heads, length, HEAD_SIZE), low),
            shape((heads, length, HEAD_SIZE), low),
            shape((2, length, HEAD_SIZE), low),
            shape((heads + 2, length, HEAD_SIZE), full),
            shape((chunks, planes, slots, wide), low),
            shape((planes, slots, experts), low),
        ),
        in_specs=[vmem] * 12,
        out_specs=(vmem,) * 6 + (anywhere,) * 9,
        scratch_shapes=[
            pltpu.VMEM((count, shard, width), low),
            pltpu.VMEM((count, planes, shard, width), low),
            dma((3, max(count, chips))),
            dma((3, max(count, chips))),
            pltpu.VMEM((planes, out_block, MODEL_WIDTH), low),
            dma((2, chips)),
            dma((2, chips)),
            pltpu.VMEM((count, tokens, MODEL_WIDTH), low),
            dma((2, count, 2)),
            dma((2, count, 2)),
            pltpu.VMEM((count, planes, small_rows, HEAD_SIZE), low),
            dma((count,)),
            dma((count,)),
            dma((planes,)),
            dma((planes,)),
            pltpu.VMEM((count, planes, shard, experts), low),
            dma((count,)),
            dma((count,)),
            dma((planes,)),
            dma((planes,)),
            pltpu.VMEM((count, tokens, experts), low),
            dma((count,)),
            dma((count,)),
            pltpu.VMEM((length, MODEL_WIDTH), low),
            pltpu.VMEM((heads + 2, length, HEAD_SIZE), full),
            pltpu.VMEM((heads, length, HEAD_SIZE), low),
            pltpu.VMEM((2, length, HEAD_SIZE), low),
            pltpu.VMEM((heads, length, HEAD_SIZE), low),
            pltpu.VMEM((chunks, count, tokens, wide), low),
            dma((chunks, 2, count, 1)),
            dma((chunks, 2, count, 1)),
            pltpu.VMEM((chunks, planes, slots, wide), low),
            dma((chunks, planes)),
            dma((chunks, planes)),
            pltpu.VMEM((planes, slots, experts), low),
            dma((planes,)),
            dma((planes,)),
            pltpu.VMEM((count, tokens, MODEL_WIDTH), low),
            pltpu.VMEM((count + 1, tokens, MODEL_WIDTH), low),
            dma((2, count, 2)),
            dma((2, count, 2)),
            dma((16 + chunks,)),
        ],
        compiler_params=pltpu.CompilerParams(
            collective_id=1, has_side_effects=True, vmem_limit_bytes=VMEM_BYTES
        ),
        name="attention_forward",
    )(
        hidden, routes, gain_one, gain_two, query_gain, key_gain, router, qkv, out_weight, cotangent,
        turn_cos, turn_sin,
    )


def segments(slots):
    step = max(16, slots // 4 // 16 * 16)
    starts = [step * k for k in range(slots // step)]
    return list(zip(starts, starts[1:] + [slots]))


def ranked_block(rank, place, count):
    short = jnp.minimum(place, count - 1 - place)
    near = (rank + 1) // 2
    side = -1 if rank % 2 else 1
    far = rank - short
    far_side = jnp.where(place < count - 1 - place, 1, -1)
    return jnp.where(rank <= 2 * short, place + side * near, place + far_side * far)


def block_rank(block, place, count):
    short = jnp.minimum(place, count - 1 - place)
    away = jnp.abs(block - place)
    near = 2 * away - jnp.where(block < place, 1, 0)
    return jnp.where(away <= short, near, short + away)


def expert_kernel(
    count, planes, tokens, capacity, chunks,
    mixed_ref, hidden1_ref, cotangent_ref, gains_ref, routes_ref, masks_ref,
    picker_hbm, grad_hbm, router_hbm, in_hbm, back_hbm,
    grad_hidden_ref, branch_ref, router_ref, grad_in_hbm, grad_back_hbm, combined_hbm,
    picker, grad_rows, router, weight_in, weight_back, local_sems,
    full, ag_send, ag_recv,
    sent, arrived, x_send, x_recv,
    gate_up, act, grad_gate_up, gate_rows,
    back_arrived, b_send, b_recv,
    gate_sent, gate_arrived, gate_own, gate_sums, gate_total, g_send, g_recv, gs_send, gs_recv,
    sums, rs_send, rs_recv, in_tiles, back_tile, tile_sems,
):
    place = lax.axis_index("seq")
    member = lax.axis_index("dp")
    slots = sent.shape[1]
    rows = planes * slots
    length = count * tokens
    wide = MODEL_WIDTH // chunks
    own_expert = place * planes + member
    experts = count * planes
    lanes = router.shape[-1]
    extra = gate_sent.shape[-1]
    low = jnp.bfloat16
    pieces = segments(slots)
    others = [(j, lax.rem(member + j, planes)) for j in range(1, planes)]

    loads = [
        pltpu.make_async_copy(picker_hbm, picker, local_sems.at[0]),
        pltpu.make_async_copy(in_hbm, weight_in, local_sems.at[1]),
        pltpu.make_async_copy(router_hbm, router, local_sems.at[2]),
        pltpu.make_async_copy(back_hbm, weight_back, local_sems.at[3]),
    ] + [
        pltpu.make_async_copy(
            grad_hbm.at[c], grad_rows.at[:, :, pl.ds(c * wide, wide)], local_sems.at[4 + c]
        )
        for c in range(chunks)
    ]
    for load in loads:
        load.start()
    full[place] = mixed_ref[...]
    greet([(place, other) for _, other in others] + [(lax.rem(place + k, count), member) for k in range(1, count)])

    line = (count, place, member, full, ag_send, ag_recv)

    def row_copy(i, j, other):
        low_row, high_row = pieces[i]
        part = pl.ds(low_row, high_row - low_row)
        return remote(
            sent.at[other, part], arrived.at[member, part], x_send.at[i, j], x_recv.at[i, j], (place, other)
        )

    def back_copy(i, j, other):
        low_row, high_row = pieces[i]
        part = pl.ds(low_row, high_row - low_row)
        return remote(
            sent.at[other, part], back_arrived.at[member, part], b_send.at[i, j], b_recv.at[i, j],
            (place, other),
        )

    def lanes_of(block):
        return pl.ds(pl.multiple_of(block * tokens, tokens), tokens)

    line_gather_step(0, *line)
    loads[0].wait()
    done = 0
    for i, (begin, end) in enumerate(pieces):
        needed = count - 1 if i == len(pieces) - 1 else min((end - 1) // capacity, count - 1)
        while done < needed:
            done += 1
            line_gather_step(done, *line)
        height = planes * (end - begin)
        picked = jnp.zeros((height, MODEL_WIDTH), jnp.float32)
        for rank in range(begin // capacity, min((end - 1) // capacity, count - 1) + 1):
            block = ranked_block(rank, place, count)
            choice = picker[:, begin:end, lanes_of(block)].reshape(height, tokens)
            picked += dot_nn(choice, full[block])
        sent[:, begin:end, :] = picked.astype(low).reshape(planes, end - begin, MODEL_WIDTH)
        for j, other in others:
            row_copy(i, j, other).start()
        arrived[member, begin:end, :] = sent[member, begin:end, :]
    for load in loads[1:]:
        load.wait()

    own_lanes = lax.broadcasted_iota(jnp.int32, (tokens, lanes), 1)
    named = jnp.zeros((tokens, lanes), jnp.float32)
    for k in range(TOP):
        named += jnp.where(routes_ref[:, k : k + 1] == own_lanes, 1.0, 0.0)

    def masked_gates(scores, mask):
        shifted = jnp.where(mask > 0, scores, FILLER)
        powers = jnp.where(mask > 0, jnp.exp(shifted - jnp.max(shifted, axis=-1, keepdims=True)), 0.0)
        total = jnp.sum(powers, axis=-1, keepdims=True)
        return powers / jnp.where(total > 0, total, 1.0)

    own_gates = masked_gates(dot_nn(mixed_ref[...], router[...]), named)

    def work(i):
        begin, end = pieces[i]
        height = planes * (end - begin)
        x = arrived[:, begin:end, :].reshape(height, MODEL_WIDTH)
        gate_up[:height, :] = dot_nn(x, weight_in[...])
        mask = masks_ref[:, begin:end, :].reshape(height, lanes).astype(jnp.float32)
        gates = masked_gates(dot_nn(x, router[...]), mask)
        lane_ids = lax.broadcasted_iota(jnp.int32, (height, lanes), 1)
        gate = jnp.sum(jnp.where(lane_ids == own_expert, gates, 0.0), axis=-1, keepdims=True)
        gate_rows[:, begin:end, :] = jnp.broadcast_to(gate, (height, HEAD_SIZE)).reshape(
            planes, end - begin, HEAD_SIZE
        )
        grads = grad_rows[:, begin:end, :].reshape(height, MODEL_WIDTH).astype(jnp.float32)
        grad_act = dot_nt((grads * gate).astype(low), weight_back[...])
        gate_part = gate_up[:height, :FF]
        up_part = gate_up[:height, FF:]
        chance = jax.nn.sigmoid(gate_part)
        silu = gate_part * chance
        act[:, begin:end, :] = (silu * up_part).astype(low).reshape(planes, end - begin, FF)
        slope = chance + silu * (1.0 - chance)
        grad_gate = (grad_act * up_part * slope).astype(low)
        grad_up = (grad_act * silu).astype(low)
        grad_gate_up[:, begin:end, :FF] = grad_gate.reshape(planes, end - begin, FF)
        grad_gate_up[:, begin:end, FF:] = grad_up.reshape(planes, end - begin, FF)
        for j, other in others:
            row_copy(i, j, other).wait_send()
        back = jnp.concatenate([grad_gate, grad_up], axis=1)
        for c in range(chunks):
            columns = slice(c * wide, (c + 1) * wide)
            sent[:, begin:end, columns] = (
                dot_nt(back, weight_in[columns, :]).astype(low).reshape(planes, end - begin, wide)
            )
        back_arrived[member, begin:end, :] = sent[member, begin:end, :]

    def send_back(i):
        for j, other in others:
            back_copy(i, j, other).start()

    last = len(pieces) - 1
    for i in range(last):
        for j, other in others:
            row_copy(i, j, other).wait_recv()
        work(i)
    for j, other in others:
        row_copy(last, j, other).wait_recv()
    send_back(last - 1)
    work(last)
    send_back(last)
    line_gather_end(*line)

    tile = in_tiles.shape[1]

    def in_copy(slot, index):
        return pltpu.make_async_copy(
            in_tiles.at[slot],
            grad_in_hbm.at[pl.ds(pl.multiple_of(index * tile, tile), tile), pl.ds(slot * FF, FF)],
            tile_sems.at[slot],
        )

    def in_gradient(index, carry):
        x = arrived[:, :, pl.ds(pl.multiple_of(index * tile, tile), tile)].reshape(rows, tile)
        for slot in range(2):

            @pl.when(index > 0)
            def _():
                in_copy(slot, index).wait()

            grads = grad_gate_up[:, :, slot * FF : (slot + 1) * FF].reshape(rows, FF)
            in_tiles[slot] = dot_tn(x, grads).astype(low)
            in_copy(slot, index).start()
        return carry

    def outputs(c, grad_gate):
        columns = pl.ds(pl.multiple_of(c * wide, wide), wide)
        result = dot_nn(act[...].reshape(rows, FF), weight_back[:, columns])
        result = result.astype(low).astype(jnp.float32)
        grads = grad_rows[:, :, columns].reshape(rows, wide).astype(jnp.float32)
        scale = gate_rows[...].reshape(rows, HEAD_SIZE)[:, 0:1]
        grad_rows[:, :, columns] = (grads * scale).astype(low).reshape(planes, slots, wide)
        arrived[:, :, columns] = (result * scale).astype(low).reshape(planes, slots, wide)
        return grad_gate + jnp.sum(result * grads, axis=-1, keepdims=True)

    def gate_copy(j, other):
        return remote(
            gate_sent.at[other], gate_arrived.at[member], g_send.at[j], g_recv.at[j], (place, other)
        )

    def back_tile_copy(index):
        return pltpu.make_async_copy(
            back_tile,
            grad_back_hbm.at[:, pl.ds(pl.multiple_of(index * tile, tile), tile)],
            tile_sems.at[2],
        )

    def back_gradient(index, carry):
        grads = grad_rows[:, :, pl.ds(pl.multiple_of(index * tile, tile), tile)].reshape(rows, tile)
        result = dot_tn(act[...].reshape(rows, FF), grads)

        @pl.when(index > 0)
        def _():
            back_tile_copy(index).wait()

        back_tile[...] = result.astype(low)
        back_tile_copy(index).start()
        return carry

    tiles = MODEL_WIDTH // tile
    lax.fori_loop(0, tiles, in_gradient, 0)
    grad_gate = lax.fori_loop(0, chunks, outputs, jnp.zeros((rows, 1), jnp.float32))
    combined = pltpu.make_async_copy(arrived, combined_hbm, tile_sems.at[3])
    combined.start()
    high = grad_gate.astype(low).astype(jnp.float32)
    rest = grad_gate - high
    wide_lanes = lax.broadcasted_iota(jnp.int32, (rows, extra), 1)
    columns = jnp.where(
        wide_lanes == own_expert, high, jnp.where(wide_lanes == own_expert + experts, rest, 0.0)
    )
    gate_sent[...] = columns.astype(low).reshape(gate_sent.shape)
    for j, other in others:
        gate_copy(j, other).start()
    gate_arrived[member] = gate_sent[member]
    for i in range(last - 2, -1, -1):
        send_back(i)
    lax.fori_loop(0, tiles, back_gradient, 0)

    for j, other in others:
        gate_copy(j, other).wait_recv()
    gate_own[...] = (
        dot_tn(picker[...].reshape(rows, length), gate_arrived[...].reshape(rows, extra))
        .astype(low)
        .reshape(count, tokens, extra)
    )
    gate_line = (count, place, member, gate_own, gate_sums, gs_send, gs_recv)
    sums_line = (count, place, member, full, sums, rs_send, rs_recv)
    come = set()
    for step in range(count):
        rank = count - 1 - step
        first = rank * capacity // 16 * 16
        final = min(-(-(rank + 1) * capacity // 16) * 16, slots)
        for i in range(last, -1, -1):
            begin, end = pieces[i]
            if i not in come and begin < final and end > first:
                come.add(i)
                for j, other in others:
                    back_copy(i, j, other).wait_recv()
        block = ranked_block(rank, place, count)
        height = planes * (final - first)
        choice = picker[:, first:final, lanes_of(block)].reshape(height, tokens)
        full[block] = dot_tn(
            choice, back_arrived[:, first:final, :].reshape(height, MODEL_WIDTH)
        ).astype(low)
        if step < count - 1:
            line_sum_step(step, *gate_line)
            line_sum_step(step, *sums_line)
    for i in range(len(pieces)):
        if i not in come:
            for j, other in others:
                back_copy(i, j, other).wait_recv()
    line_sum_end(*gate_line, gate_total)
    line_sum_end(*sums_line, grad_hidden_ref)

    if experts % 128 == 0:
        grad_gates = gate_total[:, :experts] + gate_total[:, experts:]
    else:
        grad_gates = gate_total[...] + pltpu.roll(gate_total[...], extra - experts, 1)
    middle = jnp.sum(own_gates * grad_gates, axis=-1, keepdims=True)
    grad_logits = (own_gates * (grad_gates - middle)).astype(low)
    grad_mixed = grad_hidden_ref[...] + dot_nt(grad_logits, router[...])
    router_ref[:experts, :] = dot_tn(grad_logits, mixed_ref[...])[:experts]
    hidden = hidden1_ref[...]
    inverse = lax.rsqrt(jnp.mean(hidden * hidden, axis=-1, keepdims=True) + EPSILON)
    unit = hidden * inverse
    router_ref[experts:, :] = jnp.broadcast_to(
        jnp.sum(grad_mixed * unit, axis=0, keepdims=True), (8, MODEL_WIDTH)
    )
    turned = grad_mixed * gains_ref[1:2, :]
    grad_norm = inverse * (turned - unit * jnp.mean(turned * unit, axis=-1, keepdims=True))
    grad_hidden = cotangent_ref[...].astype(jnp.float32) + grad_norm
    grad_hidden_ref[...] = grad_hidden
    branch_ref[...] = grad_hidden.astype(low)

    for j, other in others:
        for i in range(len(pieces)):
            back_copy(i, j, other).wait_send()
        gate_copy(j, other).wait_send()
    in_copy(0, 0).wait()
    in_copy(1, 0).wait()
    back_tile_copy(0).wait()
    combined.wait()


def expert_layer(
    count, planes, capacity, mixed, hidden1, cotangent, gains, routes, masks, picker, grad_rows,
    router, weight_in, weight_back,
):
    tokens = mixed.shape[0]
    chunks, _, slots, wide = grad_rows.shape
    rows = planes * slots
    extra = -(-2 * count * planes // 128) * 128
    lanes = router.shape[-1]
    height = planes * max(end - begin for begin, end in segments(slots))
    tile = 256 if rows < 1280 else 128
    pieces = len(segments(slots))
    low, kind = jnp.bfloat16, jnp.float32
    vmem = pl.BlockSpec(memory_space=pltpu.VMEM)
    anywhere = pl.BlockSpec(memory_space=pl.ANY)
    dma = pltpu.SemaphoreType.DMA
    shape = jax.ShapeDtypeStruct
    blocks = (planes, slots, MODEL_WIDTH)
    return pl.pallas_call(
        functools.partial(expert_kernel, count, planes, tokens, capacity, chunks),
        out_shape=(
            shape((tokens, MODEL_WIDTH), kind),
            shape((tokens, MODEL_WIDTH), low),
            shape((count * planes + 8, MODEL_WIDTH), kind),
            shape(weight_in.shape, low),
            shape(weight_back.shape, low),
            shape(blocks, low),
        ),
        in_specs=[vmem] * 6 + [anywhere] * 5,
        out_specs=(vmem,) * 3 + (anywhere,) * 3,
        scratch_shapes=[
            pltpu.VMEM(picker.shape, low),
            pltpu.VMEM(blocks, low),
            pltpu.VMEM(router.shape, low),
            pltpu.VMEM(weight_in.shape, low),
            pltpu.VMEM(weight_back.shape, low),
            dma((4 + chunks,)),
            pltpu.VMEM((count, tokens, MODEL_WIDTH), low),
            dma((2, count, 2)),
            dma((2, count, 2)),
            pltpu.VMEM(blocks, low),
            pltpu.VMEM(blocks, low),
            dma((pieces, planes)),
            dma((pieces, planes)),
            pltpu.VMEM((height, 2 * FF), kind),
            pltpu.VMEM((planes, slots, FF), low),
            pltpu.VMEM((planes, slots, 2 * FF), low),
            pltpu.VMEM((planes, slots, HEAD_SIZE), kind),
            pltpu.VMEM(blocks, low),
            dma((pieces, planes)),
            dma((pieces, planes)),
            pltpu.VMEM((planes, slots, extra), low),
            pltpu.VMEM((planes, slots, extra), low),
            pltpu.VMEM((count, tokens, extra), low),
            pltpu.VMEM((count + 1, tokens, extra), low),
            pltpu.VMEM((tokens, extra), kind),
            dma((planes,)),
            dma((planes,)),
            dma((2, count, 1)),
            dma((2, count, 1)),
            pltpu.VMEM((count + 1, tokens, MODEL_WIDTH), low),
            dma((2, count, 2)),
            dma((2, count, 2)),
            pltpu.VMEM((2, tile, FF), low),
            pltpu.VMEM((FF, tile), low),
            dma((4,)),
        ],
        compiler_params=pltpu.CompilerParams(
            collective_id=2, has_side_effects=True, vmem_limit_bytes=VMEM_BYTES
        ),
        name="expert_layer",
    )(
        mixed, hidden1, cotangent, gains, routes, masks, picker, grad_rows, router, weight_in,
        weight_back,
    )


def finish_kernel(
    in_ref, back_ref, hidden_ref, mixed_ref, input_ref, out_ref, qkv_ref,
    in_full, back_full, output, input_full, out_full, qkv_full,
):
    in_full[...] = in_ref[...].astype(jnp.float32)
    back_full[...] = back_ref[...].astype(jnp.float32)
    output[...] = (hidden_ref[...] + mixed_ref[...]).astype(jnp.bfloat16)
    input_full[...] = input_ref[...]
    out_full[...] = out_ref[...]
    qkv_full[...] = qkv_ref[...]


def finish(grad_in, grad_back, hidden1, mixed, grad_input, shard_out, shard_qkv):
    steps = 8
    arrays = (grad_in, grad_back, hidden1, mixed, grad_input, shard_out, shard_qkv)

    def by_rows(array):
        return pl.BlockSpec((array.shape[0] // steps, array.shape[1]), lambda i: (i, 0))

    def by_columns(array):
        return pl.BlockSpec((array.shape[0], array.shape[1] // steps), lambda i: (0, i))

    specs = [by_rows(array) for array in arrays[:5]] + [by_columns(array) for array in arrays[5:]]
    results = (grad_in, grad_back, hidden1, grad_input, shard_out, shard_qkv)
    kinds = (jnp.float32, jnp.float32, jnp.bfloat16) + (jnp.float32,) * 3
    return pl.pallas_call(
        finish_kernel,
        grid=(steps,),
        out_shape=tuple(jax.ShapeDtypeStruct(a.shape, k) for a, k in zip(results, kinds)),
        in_specs=specs,
        out_specs=tuple([specs[0], specs[1], specs[2], specs[4], specs[5], specs[6]]),
        compiler_params=pltpu.CompilerParams(vmem_limit_bytes=VMEM_BYTES // 2),
        name="finish",
    )(*arrays)


def turn_tables(length):
    half = HEAD_SIZE // 2
    freqs = np.float32(ROPE_BASE) ** (-(np.arange(half, dtype=np.float32) * np.float32(2 / HEAD_SIZE)))
    angles = np.arange(length, dtype=np.float32)[:, None] * freqs[None, :]
    cosine, sine = np.cos(angles), np.sin(angles)
    return (
        jnp.asarray(np.concatenate([cosine, cosine], axis=1), jnp.float32),
        jnp.asarray(np.concatenate([-sine, sine], axis=1), jnp.float32),
    )


def body(
    hidden_in,
    routes,
    norm1_gain,
    query_gain,
    key_gain,
    qkv_weight,
    out_weight,
    norm2_gain,
    router,
    gate_up_weight,
    down_weight,
    cotangent,
):
    tokens = hidden_in.shape[1]
    sequence_number = lax.axis_size("seq")
    planes = lax.axis_size("dp")
    devices = sequence_number * planes
    group = lax.axis_index("seq")
    member = lax.axis_index("dp")
    index = group * planes + member
    heads = QUERY_HEADS // sequence_number
    query_columns = heads * HEAD_SIZE
    head_replicas = sequence_number // KEY_VALUE_HEADS
    capacity = (tokens * TOP * 9 + 8 * devices - 1) // (8 * devices)
    slots = -(-sequence_number * capacity // 16) * 16
    chunks = 4
    sequence_length = sequence_number * tokens
    shard = norm1_gain.shape[0]
    small_shard = query_gain.shape[0]

    turn_cos, turn_sin = turn_tables(sequence_length)
    (
        hidden1, mixed_low, lse, gains, picker, full_router, own_cols, out_rows, normed_full,
        heads_low, queries, pair, projected, grad_rows, masks,
    ) = attention_forward(
        sequence_number,
        planes,
        heads,
        shard,
        capacity,
        slots,
        chunks,
        hidden_in[0],
        routes[0],
        norm1_gain[None],
        norm2_gain[None],
        query_gain[None],
        key_gain[None],
        router,
        qkv_weight,
        out_weight,
        cotangent[0],
        turn_cos,
        turn_sin,
    )
    (
        grad_hidden1, grad_branch, grad_router, grad_weight_in, grad_weight_back, combined_rows,
    ) = expert_layer(
        sequence_number,
        planes,
        capacity,
        mixed_low,
        hidden1,
        cotangent[0],
        gains,
        routes[0],
        masks,
        picker,
        grad_rows,
        full_router,
        gate_up_weight[0],
        down_weight[0],
    )
    (
        grad_input, shard_out, shard_qkv, mixed_total, router_total, gain_total, _,
    ) = attention_backward(
        sequence_number,
        planes,
        heads,
        shard,
        capacity,
        grad_branch,
        grad_hidden1,
        hidden_in[0],
        gains,
        grad_router,
        out_rows,
        own_cols,
        normed_full,
        heads_low,
        queries,
        pair,
        projected,
        picker,
        combined_rows,
        lse,
        turn_cos,
        turn_sin,
    )
    grad_weight_in, grad_weight_back, output, grad_input, shard_out, shard_qkv = finish(
        grad_weight_in, grad_weight_back, hidden1, mixed_total, grad_input, shard_out, shard_qkv
    )
    index = group * planes + member
    router_own = lax.dynamic_slice_in_dim(router_total, member * shard, shard, 1)
    gain_own = lax.dynamic_slice_in_dim(
        gain_total[: MODEL_WIDTH // HEAD_SIZE].reshape(1, MODEL_WIDTH), index * shard, shard, 1
    )
    head_gains = lax.dynamic_slice_in_dim(
        gain_total[MODEL_WIDTH // HEAD_SIZE :][:2], index * small_shard, small_shard, 1
    )
    return (
        output[None],
        grad_input[None],
        gain_own[0],
        head_gains[0],
        head_gains[1],
        shard_qkv,
        shard_out,
        router_own[devices],
        router_own[:devices].T,
        grad_weight_in[None],
        grad_weight_back[None],
    )


def solution(mesh):
    in_specs = (
        P("dp", "seq", None),
        P("dp", "seq", None),
        P(("seq", "dp")),
        P(("seq", "dp")),
        P(("seq", "dp")),
        P(("seq", "dp"), None),
        P(("seq", "dp"), None),
        P(("seq", "dp")),
        P(("seq", "dp"), None),
        P(("seq", "dp"), None, None),
        P(("seq", "dp"), None, None),
        P("dp", "seq", None),
    )
    out_specs = (
        P("dp", "seq", None),
        P("dp", "seq", None),
        P(("seq", "dp")),
        P(("seq", "dp")),
        P(("seq", "dp")),
        P(("seq", "dp"), None),
        P(("seq", "dp"), None),
        P(("seq", "dp")),
        P(("seq", "dp"), None),
        P(("seq", "dp"), None, None),
        P(("seq", "dp"), None, None),
    )
    return jax.shard_map(body, mesh=mesh, in_specs=in_specs, out_specs=out_specs, check_vma=False)
```

```python
import functools
import jax
import jax.numpy as jnp
import numpy as np
from jax import lax
from jax.experimental import pallas as pl
from jax.experimental.pallas import tpu as pltpu
from jax.sharding import PartitionSpec as P


MODEL_WIDTH = 2048
QUERY_HEADS = 32
KEY_VALUE_HEADS = 4
HEAD_SIZE = 128
FF = 768
TOP = 8


EPSILON = 1e-06
ROPE_BASE = 1000000.0
FILLER = -1e30
QUERY_BLOCK = 512


MESH = pl.DeviceIdType.MESH
VMEM_BYTES = 63 * 1024 * 1024


def dot_nn(left, right):
    return jnp.dot(left, right, preferred_element_type=jnp.float32)


def dot_nt(left, right):
    return lax.dot_general(
        left, right, (((1,), (1,)), ((), ())), preferred_element_type=jnp.float32
    )


def dot_tn(left, right):
    return lax.dot_general(
        left, right, (((0,), (0,)), ((), ())), preferred_element_type=jnp.float32
    )


def greet(peers, between=None):
    barrier = pltpu.get_barrier_semaphore()
    for peer in peers:
        pl.semaphore_signal(barrier, inc=1, device_id=peer, device_id_type=MESH)
    if between is not None:
        between()
    pl.semaphore_wait(barrier, len(peers))


def remote(source, target, send_sem, recv_sem, device):
    return pltpu.make_async_remote_copy(
        src_ref=source,
        dst_ref=target,
        send_sem=send_sem,
        recv_sem=recv_sem,
        device_id=device,
        device_id_type=MESH,
    )


def line_gather_step(step, count, place, column, blocks, send_sems, recv_sems):
    parts = send_sems.shape[-1]
    height = blocks.shape[1] // parts
    for part in range(parts):
        rows = pl.ds(part * height, height)
        for side, away in ((0, 1), (1, -1)):
            origin = place - away * step
            there = (origin >= 0) & (origin < count)
            target = place + away

            def copy(come, device):
                block = blocks.at[origin, rows]
                return remote(
                    block, block, send_sems.at[side, step, part], recv_sems.at[side, come, part],
                    (device, column),
                )

            if step > 0:

                @pl.when(there)
                def _():
                    copy(step, place).wait_recv()

            if step < count - 1:

                @pl.when(there & (target >= 0) & (target < count))
                def _():
                    copy(step + 1, target).start()


def line_gather_end(count, place, column, blocks, send_sems, recv_sems):
    parts = send_sems.shape[-1]
    height = blocks.shape[1] // parts
    for step in range(count - 1):
        for part in range(parts):
            rows = pl.ds(part * height, height)
            for side, away in ((0, 1), (1, -1)):
                origin = place - away * step
                target = place + away

                @pl.when((origin >= 0) & (origin < count) & (target >= 0) & (target < count))
                def _():
                    block = blocks.at[origin, rows]
                    remote(
                        block, block, send_sems.at[side, step, part], recv_sems.at[side, step, part],
                        (place, column),
                    ).wait_send()


def line_sum_step(step, count, place, column, own, sums, send_sems, recv_sems):
    parts = send_sems.shape[-1]
    height = own.shape[1] // parts
    for part in range(parts):
        rows = pl.ds(part * height, height)
        for side in range(2):
            if side == 0:
                turn = step - place
                index = count - 1 - turn
                active = (turn >= 0) & (index > place)
                target, slot = place + 1, index
            else:
                index = step - (count - 1 - place)
                active = (index >= 0) & (index < place)
                target, slot = place - 1, jnp.where(index == place - 1, count, index)
            fresh = place == (0 if side == 0 else count - 1)

            @pl.when(active)
            def _():
                block = sums.at[index, rows]

                def copy(goal, device):
                    return remote(
                        block, sums.at[goal, rows], send_sems.at[side, index, part],
                        recv_sems.at[side, index, part], (device, column),
                    )

                @pl.when(jnp.logical_not(fresh))
                def _():
                    copy(index, place).wait_recv()
                    sums[index, rows] = (
                        sums[index, rows].astype(jnp.float32) + own[index, rows].astype(jnp.float32)
                    ).astype(jnp.bfloat16)

                @pl.when(fresh)
                def _():
                    sums[index, rows] = own[index, rows]

                copy(slot, target).start()


def line_sum_end(count, place, column, own, sums, send_sems, recv_sems, total):
    parts = send_sems.shape[-1]
    height = own.shape[1] // parts
    for part in range(parts):
        rows = pl.ds(part * height, height)
        total[rows, :] = own[place, rows].astype(jnp.float32)
        for side, come in ((0, place > 0), (1, place < count - 1)):
            slot = place if side == 0 else count

            @pl.when(come)
            def _():
                block = sums.at[slot, rows]
                remote(
                    block, block, send_sems.at[side, place, part], recv_sems.at[side, place, part],
                    (place, column),
                ).wait_recv()
                total[rows, :] += sums[slot, rows].astype(jnp.float32)

    for step in range(count - 1):
        last = count - 1 - step
        for part in range(parts):
            rows = pl.ds(part * height, height)
            for side, index, sent in ((0, last, last > place), (1, step, step < place)):

                @pl.when(sent)
                def _():
                    block = sums.at[index, rows]
                    remote(
                        block, block, send_sems.at[side, index, part], recv_sems.at[side, index, part],
                        (place, column),
                    ).wait_send()


def backward_kernel(
    count, planes, tokens, heads, shard, capacity,
    branch_ref, grad_hidden_ref, hidden_ref, gains_ref, router_ref,
    out_rows_hbm, own_cols_hbm, normed_hbm, heads_hbm, query_hbm, pair_hbm,
    proj_hbm, picker_hbm, combined_hbm, lse_ref, turn_cos_ref, turn_sin_ref,
    grad_input_ref, out_total, qkv_total, mixed_total, router_total, gain_total, mixed_arrived,
    out_rows, own_cols, normed, heads_low, queries, pair, proj, picker, local_sems,
    branch_full, ag_send, ag_recv,
    grad_heads, grad_proj, grad_pair, gain_parts,
    grad_out, out_pair, out_far, out_sems,
    grad_cols, col_pair, col_far, col_sums, columns_out, col_sems,
    normed_room, normed_sums, rs_send, rs_recv, z_sems,
    mixed_rows, mixed_part, mixed_sums, mix_send, mix_recv, mix_local, ms_send, ms_recv,
    router_line, router_sum, router_chip, router_pair, router_sems,
    gain_own, gain_line, gain_chip, gain_pair, gain_sems,
):
    place = lax.axis_index("seq")
    member = lax.axis_index("dp")
    core = lax.rem(member, 2)
    chip = member // 2
    chips = planes // 2
    partner = member + 1 - 2 * core
    length = count * tokens
    query_columns = heads * HEAD_SIZE
    width = query_columns + 2 * HEAD_SIZE
    out_block = query_columns // planes
    scale = HEAD_SIZE ** (-0.5)
    chunks = mixed_part.shape[0]
    wide = MODEL_WIDTH // chunks
    shared = normed_room.shape[0] == 1
    normed_part = branch_full if shared else normed_room
    slots = mixed_rows.shape[1]
    low = jnp.bfloat16

    loads = [
        pltpu.make_async_copy(source, target, local_sems.at[index])
        for index, (source, target) in enumerate(
            [
                (out_rows_hbm, out_rows),
                (query_hbm, queries),
                (pair_hbm, pair),
                (heads_hbm, heads_low),
                (proj_hbm, proj),
                (own_cols_hbm, own_cols),
                (normed_hbm, normed),
                (picker_hbm, picker),
            ]
        )
    ]
    for load in loads:
        load.start()
    branch_full[place] = branch_ref[...]

    far_chips = [(k, lax.rem(chip + k, chips)) for k in range(1, chips)]
    far_places = [(k, lax.rem(place + k, count)) for k in range(1, count)]
    others = [(j, lax.rem(member + j, planes)) for j in range(1, planes)]
    greet([(place, other) for _, other in others] + [(other, member) for _, other in far_places])

    line = (count, place, member, branch_full, ag_send, ag_recv)
    line_gather_step(0, *line)

    def mixed_copy(c, j, other):
        part = pl.ds(c * wide, wide)
        return remote(
            combined_hbm.at[other, :, part], mixed_arrived.at[member, :, part],
            mix_send.at[c, j], mix_recv.at[c, j], (place, other),
        )

    def mixed_send(c):
        for j, other in others:
            mixed_copy(c, j, other).start()

    mixed_send(0)
    mixed_own = pltpu.make_async_copy(
        combined_hbm.at[member], mixed_arrived.at[member], mix_local.at[0]
    )
    mixed_own.start()
    for load in loads:
        load.wait()

    gain_query = gains_ref[2:3, :HEAD_SIZE]
    gain_key = gains_ref[3:4, :HEAD_SIZE]
    grad_pair[...] = jnp.zeros_like(grad_pair)
    gain_parts[...] = jnp.zeros_like(gain_parts)
    key_turned = jnp.transpose(pair[0].astype(jnp.float32)).astype(low)

    def unprepare(grad, raw, gain, cosine, sine):
        turned = grad * cosine - pltpu.roll(grad, HEAD_SIZE // 2, 1) * sine
        inverse = lax.rsqrt(jnp.mean(raw * raw, axis=-1, keepdims=True) + EPSILON)
        unit = raw * inverse
        gain_part = jnp.sum(turned * unit, axis=0, keepdims=True)
        turned = turned * gain
        middle = jnp.mean(turned * unit, axis=-1, keepdims=True)
        return inverse * (turned - unit * middle), gain_part

    together = min(max(1, 2048 // length), heads)

    def process(block):
        at = pl.ds(pl.multiple_of(block * tokens, tokens), tokens)
        partial_heads = dot_nt(
            branch_full[block], out_rows[...].reshape(query_columns, MODEL_WIDTH)
        ).astype(low)
        for head in range(heads):
            grad_heads[head] = partial_heads[:, head * HEAD_SIZE : (head + 1) * HEAD_SIZE]

        cosine, sine = turn_cos_ref[at, :], turn_sin_ref[at, :]

        def some_heads(index, carry):
            first = index * together
            some = pl.ds(first, together)
            query = queries[some, at, :].reshape(together * tokens, HEAD_SIZE)
            grad = grad_heads[some].reshape(together * tokens, HEAD_SIZE)
            scores = dot_nt(pair[0], query) * scale
            shape = (length, together * tokens)
            key_ids = lax.broadcasted_iota(jnp.int32, shape, 0) - block * tokens
            query_ids = lax.rem(lax.broadcasted_iota(jnp.int32, shape, 1), tokens)
            scores = jnp.where(key_ids <= query_ids, scores, FILLER)
            lse = jnp.concatenate([lse_ref[first + k, :, at] for k in range(together)], axis=1)
            probs = jnp.exp(scores - lse)
            grad_probs = dot_nt(pair[1], grad)
            delta = jnp.sum(probs * grad_probs, axis=0, keepdims=True)
            grad_scores = (probs * (grad_probs - delta)).astype(low)
            grad_pair[0] += dot_nn(grad_scores, query) * scale
            grad_pair[1] += dot_nn(probs.astype(low), grad)
            grad_query = jnp.transpose(dot_nn(key_turned, grad_scores)) * scale
            for k in range(together):
                grad_raw, gain_part = unprepare(
                    grad_query[k * tokens : (k + 1) * tokens],
                    proj[first + k, at, :],
                    gain_query,
                    cosine,
                    sine,
                )
                gain_parts[0:1, :] += gain_part
                columns = pl.ds(pl.multiple_of((first + k) * HEAD_SIZE, HEAD_SIZE), HEAD_SIZE)
                grad_proj[at, columns] = grad_raw.astype(low)
            return carry

        lax.fori_loop(0, heads // together, some_heads, 0)

    def gather(step):
        line_gather_step(step, *line)

        def side(index, carry):
            block = place - step + 2 * step * index

            @pl.when((block >= 0) & (block < count))
            def _():
                process(block)

            return carry

        lax.fori_loop(0, 2, side, 0)

    def mixed_line(c):
        return (count, place, member, mixed_part.at[c], mixed_sums.at[c], ms_send.at[c], ms_recv.at[c])

    def mixed_chunk(c):
        for j, other in others:
            mixed_copy(c, j, other).wait_recv()
        if c == 0:
            mixed_own.wait()
        load = pltpu.make_async_copy(
            mixed_arrived.at[:, :, pl.ds(c * wide, wide)], mixed_rows, mix_local.at[1]
        )
        load.start()
        load.wait()
        for rank in range(count):
            block = ranked_block(rank, place, count)
            first = rank * capacity // 16 * 16
            final = min(-(-(rank + 1) * capacity // 16) * 16, slots)
            height = planes * (final - first)
            at = pl.ds(pl.multiple_of(block * tokens, tokens), tokens)
            choice = picker[:, first:final, at].reshape(height, tokens)
            mixed_part[c, block] = dot_tn(
                choice, mixed_rows[:, first:final, :].reshape(height, wide)
            ).astype(low)

    waves = list(range(chunks + count - 2))

    def mixed_wave():
        wave = waves.pop(0)
        for c in range(chunks):
            if 0 <= wave - c < count - 1:
                line_sum_step(wave - c, *mixed_line(c))

    process(place)
    mixed_send(1)
    for step in range(1, count):
        gather(step)
        if step < count - 1 and step <= chunks - 2:
            mixed_send(step + 1)
            mixed_chunk(step - 1)
            mixed_wave()
    mixed_done = min(chunks - 2, count - 2)
    for c in range(mixed_done + 2, chunks):
        mixed_send(c)
    line_gather_end(*line)

    per_head = HEAD_SIZE // out_block

    def out_gradient(head):
        all_branch = branch_full[...].reshape(length, MODEL_WIDTH)
        part = dot_tn(heads_low[head], all_branch).astype(low)
        if per_head == 1:
            grad_out[head] = part
        else:
            grad_out[head * per_head : (head + 1) * per_head] = part.reshape(
                per_head, out_block, MODEL_WIDTH
            )

    def out_copy(k):
        return remote(
            grad_out.at[2 * k + 1 - core], out_pair.at[k], out_sems.at[0, k], out_sems.at[1, k],
            (place, partner),
        )

    def out_far_copy(k, other):
        return remote(
            out_pair.at[other], out_far.at[k - 1], out_sems.at[2, k], out_sems.at[3, k],
            (place, 2 * other + core),
        )

    def out_gradients():
        if per_head == 1:
            for k in range(chips):
                out_gradient(2 * k + 1 - core)
                out_copy(k).start()

            def rest(k, carry):
                out_gradient(2 * k + core)
                return carry

            lax.fori_loop(0, chips, rest, 0)
        else:
            for head in range(heads):
                out_gradient(head)
            for k in range(chips):
                out_copy(k).start()

    def out_pairs():
        for k in range(chips):
            out_copy(k).wait_recv()
            out_pair[k] = (
                out_pair[k].astype(jnp.float32) + grad_out[2 * k + core].astype(jnp.float32)
            ).astype(low)
        for k, other in far_chips:
            out_far_copy(k, other).start()

    lane_part = MODEL_WIDTH // count

    def router_far(k, other):
        return remote(
            router_ref.at[:, pl.ds(pl.multiple_of(other * lane_part, lane_part), lane_part)],
            router_line.at[k - 1], router_sems.at[0, k], router_sems.at[1, k], (other, member),
        )

    def router_near(k, other):
        return remote(
            router_sum.at[0], router_chip.at[k - 1], router_sems.at[2, k], router_sems.at[3, k],
            (place, 2 * other + core),
        )

    def router_last():
        return remote(
            router_sum.at[1], router_pair, router_sems.at[2, 0], router_sems.at[3, 0], (place, partner)
        )

    groups = [(0, heads + 2)]

    def columns_of(group):
        return pl.ds(groups[group][0] * HEAD_SIZE, (groups[group][1] - groups[group][0]) * HEAD_SIZE)

    def col_copy(group, k):
        part = columns_of(group)
        return remote(
            grad_cols.at[:, 2 * k + 1 - core, :, part], col_pair.at[k, :, :, part],
            col_sems.at[group, 0, k], col_sems.at[group, 1, k], (place, partner),
        )

    def col_far_copy(group, k, other):
        part = columns_of(group)
        return remote(
            col_pair.at[other, :, :, part], col_far.at[k - 1, :, :, part],
            col_sems.at[group, 2, k], col_sems.at[group, 3, k], (place, 2 * other + core),
        )

    def z_copy(group, k, other):
        part = columns_of(group)
        return remote(
            col_sums.at[other, :, part], columns_out.at[place, :, part],
            z_sems.at[group, 0, k], z_sems.at[group, 1, k], (other, member),
        )

    def col_gradient(group):
        first, final = groups[group]
        grads = grad_proj[:, first * HEAD_SIZE : final * HEAD_SIZE]
        block_width = planes * shard
        for block in range(count):
            part = dot_tn(normed[:, block * block_width : (block + 1) * block_width], grads)
            grad_cols[block, :, :, first * HEAD_SIZE : final * HEAD_SIZE] = part.astype(low).reshape(
                planes, shard, (final - first) * HEAD_SIZE
            )
        for k in range(chips):
            col_copy(group, k).start()

    def col_pairs(group):
        first, final = groups[group]
        columns = slice(first * HEAD_SIZE, final * HEAD_SIZE)
        for k in range(chips):
            col_copy(group, k).wait_recv()
            col_pair[k, :, :, columns] = (
                col_pair[k, :, :, columns].astype(jnp.float32)
                + grad_cols[:, 2 * k + core, :, columns].astype(jnp.float32)
            ).astype(low)
        for k, other in far_chips:
            col_far_copy(group, k, other).start()

    def col_totals(group):
        first, final = groups[group]
        columns = slice(first * HEAD_SIZE, final * HEAD_SIZE)
        total = col_pair[chip, :, :, columns].astype(jnp.float32)
        for k, other in far_chips:
            col_far_copy(group, k, other).wait_recv()
            total += col_far[k - 1, :, :, columns].astype(jnp.float32)
        col_sums[:, :, columns] = total.astype(low)
        for k, other in far_places:
            z_copy(group, k, other).start()
        columns_out[place, :, columns] = col_sums[place, :, columns]

    grad_raw, gain_part = unprepare(
        grad_pair[0], proj[heads], gain_key, turn_cos_ref[...], turn_sin_ref[...]
    )
    gain_parts[1:2, :] += gain_part
    grad_proj[:, query_columns : query_columns + HEAD_SIZE] = grad_raw.astype(low)
    grad_proj[:, query_columns + HEAD_SIZE :] = grad_pair[1].astype(low)

    def gain_far(k, other):
        return remote(
            gain_own.at[0], gain_line.at[k - 1], gain_sems.at[0, k], gain_sems.at[1, k], (other, member)
        )

    def gain_near(k, other):
        return remote(
            gain_own.at[1], gain_chip.at[k - 1], gain_sems.at[2, k], gain_sems.at[3, k],
            (place, 2 * other + core),
        )

    def gain_last():
        return remote(
            gain_own.at[2], gain_pair, gain_sems.at[2, 0], gain_sems.at[3, 0], (place, partner)
        )

    sums = (count, place, member, normed_part, normed_sums, rs_send, rs_recv)

    def normed_step(step):
        block = ranked_block(count - 1 - step, place, count)
        at = pl.ds(pl.multiple_of(block * tokens, tokens), tokens)
        part = dot_nt(grad_proj[at, :], own_cols[...].reshape(MODEL_WIDTH, width))
        normed_part[block] = part.astype(low)
        if step < count - 1:
            line_sum_step(step, *sums)
        return jnp.sum(part * normed[at, :].astype(jnp.float32), axis=0, keepdims=True)

    if shared:
        out_gradients()
    gain_row = normed_step(0)
    col_gradient(0)
    col_pairs(0)
    for c in range(mixed_done, chunks):
        mixed_chunk(c)
        mixed_wave()
    gain_row += normed_step(1)
    if not shared:
        out_gradients()
    out_pairs()
    for k, other in far_places:
        router_far(k, other).start()
    if waves:
        mixed_wave()
    for step in range(2, count):
        gain_row += normed_step(step)
    gain_row = gain_row / gains_ref[0:1, :]
    for k in range(MODEL_WIDTH // HEAD_SIZE):
        gain_own[0, k : k + 1, :] = gain_row[:, k * HEAD_SIZE : (k + 1) * HEAD_SIZE]
    gain_own[0, MODEL_WIDTH // HEAD_SIZE :, :] = gain_parts[...]
    for k, other in far_places:
        gain_far(k, other).start()
    while waves:
        mixed_wave()
    own_lanes = pl.ds(pl.multiple_of(place * lane_part, lane_part), lane_part)
    total = router_ref[:, own_lanes]
    for k, other in far_places:
        router_far(k, other).wait_recv()
        total += router_line[k - 1]
    router_sum[0] = total
    for k, other in far_chips:
        router_near(k, other).start()
    total = gain_own[0]
    for k, other in far_places:
        gain_far(k, other).wait_recv()
        total += gain_line[k - 1]
    gain_own[1] = total
    for k, other in far_chips:
        gain_near(k, other).start()
    col_totals(0)
    for c in range(chunks):
        line_sum_end(*mixed_line(c), mixed_total.at[:, c * wide : (c + 1) * wide])
    line_sum_end(*sums, grad_input_ref)
    total = out_pair[chip].astype(jnp.float32)
    for k, other in far_chips:
        out_far_copy(k, other).wait_recv()
        total += out_far[k - 1].astype(jnp.float32)
    out_total[...] = total
    total = router_sum[0]
    for k, other in far_chips:
        router_near(k, other).wait_recv()
        total += router_chip[k - 1]
    router_sum[1] = total
    router_last().start()
    total = gain_own[1]
    for k, other in far_chips:
        gain_near(k, other).wait_recv()
        total += gain_chip[k - 1]
    gain_own[2] = total
    gain_last().start()
    gain_last().wait_recv()
    gain_total[...] = gain_own[2] + gain_pair[...]
    router_last().wait_recv()
    router_total[...] = router_sum[1] + router_pair[...]

    hidden = hidden_ref[...].astype(jnp.float32)
    inverse = lax.rsqrt(jnp.mean(hidden * hidden, axis=-1, keepdims=True) + EPSILON)
    unit = hidden * inverse
    grad_normed = grad_input_ref[...]
    turned = grad_normed * gains_ref[0:1, :]
    grad_input_ref[...] = grad_hidden_ref[...] + inverse * (
        turned - unit * jnp.mean(turned * unit, axis=-1, keepdims=True)
    )
    for group in range(len(groups)):
        for k, other in far_places:
            z_copy(group, k, other).wait_recv()
            z_copy(group, k, other).wait_send()
        for part in range(count):
            qkv_total[:, part * query_columns : (part + 1) * query_columns] = columns_out[
                part, :, :query_columns
            ].astype(jnp.float32)
        replicas = count // KEY_VALUE_HEADS
        for head in range(2 * KEY_VALUE_HEADS):
            kind, pair_head = head // KEY_VALUE_HEADS, head % KEY_VALUE_HEADS
            begin = query_columns + kind * HEAD_SIZE
            total = jnp.zeros((shard, HEAD_SIZE), jnp.float32)
            for part in range(pair_head * replicas, (pair_head + 1) * replicas):
                total += columns_out[part, :, begin : begin + HEAD_SIZE].astype(jnp.float32)
            begin = (QUERY_HEADS + head) * HEAD_SIZE
            qkv_total[:, begin : begin + HEAD_SIZE] = total
        for k in range(chips):
            col_copy(group, k).wait_send()
        for k, other in far_chips:
            col_far_copy(group, k, other).wait_send()
    for k in range(chips):
        out_copy(k).wait_send()
    for k, other in far_chips:
        out_far_copy(k, other).wait_send()
        router_near(k, other).wait_send()
        gain_near(k, other).wait_send()
    for k, other in far_places:
        router_far(k, other).wait_send()
        gain_far(k, other).wait_send()
    router_last().wait_send()
    gain_last().wait_send()
    for c in range(chunks):
        for j, other in others:
            mixed_copy(c, j, other).wait_send()


def attention_backward(
    count, planes, heads, shard, capacity, branch, grad_hidden, hidden, gains, router, out_rows, own_cols, normed,
    heads_low, queries, pair, proj, picker, combined, lse, turn_cos, turn_sin,
):
    tokens = branch.shape[0]
    length = count * tokens
    width = (heads + 2) * HEAD_SIZE
    chips = planes // 2
    out_block = heads * HEAD_SIZE // planes
    chunks = 4
    wide = MODEL_WIDTH // chunks
    gain_rows = MODEL_WIDTH // HEAD_SIZE + 8
    router_part = (router.shape[0], MODEL_WIDTH // count)
    low, kind = jnp.bfloat16, jnp.float32
    vmem = pl.BlockSpec(memory_space=pltpu.VMEM)
    anywhere = pl.BlockSpec(memory_space=pl.ANY)
    dma = pltpu.SemaphoreType.DMA
    shape = jax.ShapeDtypeStruct
    most = max(count, chips)
    return pl.pallas_call(
        functools.partial(backward_kernel, count, planes, tokens, heads, shard, capacity),
        out_shape=(
            shape((tokens, MODEL_WIDTH), kind),
            shape((out_block, MODEL_WIDTH), kind),
            shape((shard, (QUERY_HEADS + 2 * KEY_VALUE_HEADS) * HEAD_SIZE), kind),
            shape((tokens, MODEL_WIDTH), kind),
            shape(router_part, kind),
            shape((gain_rows, HEAD_SIZE), kind),
            shape(combined.shape, low),
        ),
        in_specs=[vmem] * 5 + [anywhere] * 9 + [vmem] * 3,
        out_specs=(vmem,) * 6 + (anywhere,),
        scratch_shapes=[
            pltpu.VMEM(out_rows.shape, low),
            pltpu.VMEM(own_cols.shape, low),
            pltpu.VMEM(normed.shape, low),
            pltpu.VMEM(heads_low.shape, low),
            pltpu.VMEM(queries.shape, low),
            pltpu.VMEM(pair.shape, low),
            pltpu.VMEM(proj.shape, kind),
            pltpu.VMEM(picker.shape, low),
            dma((8,)),
            pltpu.VMEM((count, tokens, MODEL_WIDTH), low),
            dma((2, count, 2)),
            dma((2, count, 2)),
            pltpu.VMEM((heads, tokens, HEAD_SIZE), low),
            pltpu.VMEM((length, width), low),
            pltpu.VMEM((2, length, HEAD_SIZE), kind),
            pltpu.VMEM((8, HEAD_SIZE), kind),
            pltpu.VMEM((planes, out_block, MODEL_WIDTH), low),
            pltpu.VMEM((chips, out_block, MODEL_WIDTH), low),
            pltpu.VMEM((chips - 1, out_block, MODEL_WIDTH), low),
            dma((4, chips)),
            pltpu.VMEM((count, planes, shard, width), low),
            pltpu.VMEM((chips, count, shard, width), low),
            pltpu.VMEM((chips - 1, count, shard, width), low),
            pltpu.VMEM((count, shard, width), low),
            pltpu.VMEM((count, shard, width), low),
            dma((2, 4, chips)),
            pltpu.VMEM((count if count <= 4 else 1, tokens, MODEL_WIDTH), low),
            pltpu.VMEM((count + 1, tokens, MODEL_WIDTH), low),
            dma((2, count, 2)),
            dma((2, count, 2)),
            dma((2, 2, count)),
            pltpu.VMEM(combined.shape[:2] + (wide,), low),
            pltpu.VMEM((chunks, count, tokens, wide), low),
            pltpu.VMEM((chunks, count + 1, tokens, wide), low),
            dma((chunks, planes)),
            dma((chunks, planes)),
            dma((2,)),
            dma((chunks, 2, count, 1)),
            dma((chunks, 2, count, 1)),
            pltpu.VMEM((count - 1,) + router_part, kind),
            pltpu.VMEM((2,) + router_part, kind),
            pltpu.VMEM((chips - 1,) + router_part, kind),
            pltpu.VMEM(router_part, kind),
            dma((4, most)),
            pltpu.VMEM((3, gain_rows, HEAD_SIZE), kind),
            pltpu.VMEM((count - 1, gain_rows, HEAD_SIZE), kind),
            pltpu.VMEM((chips - 1, gain_rows, HEAD_SIZE), kind),
            pltpu.VMEM((gain_rows, HEAD_SIZE), kind),
            dma((4, most)),
        ],
        compiler_params=pltpu.CompilerParams(
            collective_id=3, has_side_effects=True, vmem_limit_bytes=VMEM_BYTES
        ),
        name="attention_backward",
    )(
        branch, grad_hidden, hidden, gains, router, out_rows, own_cols, normed, heads_low, queries,
        pair, proj, picker, combined, lse, turn_cos, turn_sin,
    )


def forward_kernel(
    count, planes, tokens, heads, shard, capacity, chunks,
    hidden_ref, routes_ref, gain1_ref, gain2_ref, query_gain_ref, key_gain_ref, router_ref, qkv_ref,
    out_ref, cotangent_ref, turn_cos_ref, turn_sin_ref,
    hidden1_ref, mixed_ref, lse_ref, gains_ref, picker_ref,
    router_out, own_cols_hbm, out_rows_hbm, normed_hbm, heads_hbm, query_hbm, pair_hbm, proj_hbm,
    grad_hbm, masks_hbm,
    column_send, own_cols, c_send, c_recv,
    out_rows, o_send, o_recv,
    hidden_full, h_send, h_recv,
    gains_all, gz_send, gz_recv, gd_send, gd_recv,
    router_all, rz_send, rz_recv, rd_send, rd_recv,
    places_all, p_send, p_recv,
    normed, proj, queries, pair, heads_low,
    grad_full, dy_send, dy_recv,
    grad_sent, d_send, d_recv, mask_sent, m_send, m_recv,
    branch, sums, rs_send, rs_recv, local_sems,
):
    place = lax.axis_index("seq")
    member = lax.axis_index("dp")
    core = lax.rem(member, 2)
    chip = member // 2
    chips = planes // 2
    partner = member + 1 - 2 * core
    length = count * tokens
    query_columns = heads * HEAD_SIZE
    replicas = count // KEY_VALUE_HEADS
    wide = MODEL_WIDTH // chunks
    slots = grad_sent.shape[2]
    rows = planes * slots
    low = jnp.bfloat16
    scale = HEAD_SIZE ** (-0.5)
    far_places = [(k, lax.rem(place + k, count)) for k in range(1, count)]
    far_chips = [(k, lax.rem(chip + k, chips)) for k in range(1, chips)]
    others = [(j, lax.rem(member + j, planes)) for j in range(1, planes)]

    def column_parts():
        for part in range(count):
            head = part // replicas
            keys = QUERY_HEADS * HEAD_SIZE + head * HEAD_SIZE
            values = keys + KEY_VALUE_HEADS * HEAD_SIZE
            column_send[part, :, :query_columns] = qkv_ref[
                :, part * query_columns : (part + 1) * query_columns
            ]
            column_send[part, :, query_columns : query_columns + HEAD_SIZE] = qkv_ref[
                :, keys : keys + HEAD_SIZE
            ]
            column_send[part, :, query_columns + HEAD_SIZE :] = qkv_ref[
                :, values : values + HEAD_SIZE
            ]

    greet(
        [(place, other) for _, other in others] + [(other, member) for _, other in far_places],
        column_parts,
    )

    def column_copy(k, other):
        return remote(
            column_send.at[other], own_cols.at[place, member], c_send.at[0, k], c_recv.at[0, k],
            (other, member),
        )

    def gain_line(k, other):
        mine = gains_all.at[place, member]
        return remote(mine, mine, gz_send.at[k], gz_recv.at[k], (other, member))

    def router_line(k, other):
        mine = router_all.at[place, member]
        return remote(mine, mine, rz_send.at[k], rz_recv.at[k], (other, member))

    def places_line(k, other):
        mine = places_all.at[place]
        return remote(mine, mine, p_send.at[k], p_recv.at[k], (other, member))

    def out_copy(k, other):
        return remote(
            out_ref, out_rows.at[member], o_send.at[0, k], o_recv.at[0, k], (place, 2 * other + core)
        )

    def out_pair(k, other):
        source = out_ref if k == 0 else out_rows.at[2 * other + core]
        return remote(
            source, out_rows.at[2 * other + core], o_send.at[1, k], o_recv.at[1, k], (place, partner)
        )

    def block_copy(k, other):
        mine = own_cols.at[:, member]
        return remote(mine, mine, c_send.at[1, k], c_recv.at[1, k], (place, 2 * other + core))

    def block_pair(k, other):
        block = own_cols.at[:, 2 * other + core]
        return remote(block, block, c_send.at[2, k], c_recv.at[2, k], (place, partner))

    for k, other in far_places:
        column_copy(k, other).start()
    for k, other in far_chips:
        out_copy(k, other).start()
    out_pair(0, chip).start()

    hidden_line = (count, place, member, hidden_full, h_send, h_recv)
    index = place * planes + member
    row_lanes = lax.broadcasted_iota(jnp.int32, (1, HEAD_SIZE), 1)
    pieces = []
    for ref in (gain1_ref, gain2_ref, query_gain_ref, key_gain_ref):
        gain_width = ref.shape[1]
        values = ref[...].astype(jnp.float32)
        begin = lax.rem(index, HEAD_SIZE // gain_width) * gain_width
        piece = jnp.zeros((1, HEAD_SIZE), jnp.float32)
        for k in range(gain_width):
            piece += jnp.where(row_lanes == begin + k, values[:, k : k + 1], 0.0)
        pieces.append(piece)
    pieces.append(jnp.zeros((gains_all.shape[2] - 4, HEAD_SIZE), jnp.float32))
    gains_all[place, member] = jnp.concatenate(pieces, axis=0).astype(low)
    for k, other in far_places:
        gain_line(k, other).start()
    hidden_full[place] = hidden_ref[...]
    line_gather_step(0, *hidden_line)
    router_all[place, member] = jnp.zeros(router_all.shape[2:], low)
    router_all[place, member, :, : router_ref.shape[1]] = router_ref[...]
    lanes = lax.broadcasted_iota(jnp.int32, (tokens, places_all.shape[-1]), 1)
    named = jnp.zeros(lanes.shape, jnp.float32)
    chosen = jnp.transpose(routes_ref[...].astype(jnp.float32))
    for k in range(TOP):
        named += jnp.where(chosen[:, k : k + 1] == lanes.astype(jnp.float32), 1.0, 0.0)
    row_ids = lax.broadcasted_iota(jnp.int32, (tokens, tokens), 0)
    col_ids = lax.broadcasted_iota(jnp.int32, (tokens, tokens), 1)
    before = jnp.where(row_ids > col_ids, 1.0, 0.0).astype(low)
    earlier = dot_nn(before, named.astype(low))
    places_all[place] = jnp.where(named > 0, earlier, -512.0).astype(low)
    for c in range(chunks):
        grad_full[c, place] = cotangent_ref[:, c * wide : (c + 1) * wide]
    for k, other in far_places:
        places_line(k, other).start()
        router_line(k, other).start()
    own_cols[place, member] = column_send[place]
    out_rows[member] = out_ref[...]

    def gain_plane(j, other):
        mine = gains_all.at[:, member]
        return remote(mine, mine, gd_send.at[j], gd_recv.at[j], (place, other))

    def router_plane(j, other):
        mine = router_all.at[:, member]
        return remote(mine, mine, rd_send.at[j], rd_recv.at[j], (place, other))

    for k, other in far_places:
        gain_line(k, other).wait_recv()
    for j, other in others:
        gain_plane(j, other).start()
    for k, other in far_places:
        column_copy(k, other).wait_recv()
    for k, other in far_chips:
        block_copy(k, other).start()
    block_pair(0, chip).start()
    line_gather_step(1, *hidden_line)

    for k, other in far_places:
        places_line(k, other).wait_recv()
    experts = places_all.shape[-1]
    pick_rows = lax.broadcasted_iota(jnp.int32, (rows, experts), 0)
    pick_experts = lax.broadcasted_iota(jnp.int32, (rows, experts), 1) - place * planes
    slot_ids = lax.broadcasted_iota(jnp.int32, (rows, length), 0)
    token_ids = lax.broadcasted_iota(jnp.int32, (rows, length), 1)
    offsets = jnp.zeros((rows, length), jnp.int32)
    choose = jnp.zeros((rows, experts), jnp.float32)
    for other in range(planes):
        inside = (pick_rows >= other * slots) & (pick_rows < (other + 1) * slots)
        choose += jnp.where(inside & (pick_experts == other), 1.0, 0.0)
        offsets = jnp.where(slot_ids >= other * slots, other * slots, offsets)
    before_block = jnp.zeros((rows, length), jnp.int32)
    for block in range(count):
        before_block = jnp.where(
            token_ids >= block * tokens, block_rank(block, place, count) * capacity, before_block
        )
    wanted = dot_nt(choose.astype(low), places_all[...].reshape(length, experts))
    picker_rows = jnp.where(
        wanted == (slot_ids - offsets - before_block).astype(jnp.float32), 1.0, 0.0
    ).astype(low)
    picker_ref[...] = picker_rows.reshape(planes, slots, length)
    mask_full = jnp.where(places_all[...].reshape(length, experts).astype(jnp.float32) >= 0, 1.0, 0.0)
    mask_sent[...] = (
        dot_nn(picker_rows, mask_full.astype(low)).astype(low).reshape(mask_sent.shape)
    )

    for k, other in far_places:
        router_line(k, other).wait_recv()
    for j, other in others:
        router_plane(j, other).start()

    def mask_copy(j, other):
        return remote(
            mask_sent.at[other], masks_hbm.at[member], m_send.at[j], m_recv.at[j], (place, other)
        )

    for j, other in others:
        mask_copy(j, other).start()
    masks_own = pltpu.make_async_copy(mask_sent.at[member], masks_hbm.at[member], local_sems.at[0])
    masks_own.start()

    for step in range(2, count - 1):
        line_gather_step(step, *hidden_line)

    def grad_line(c):
        return (count, place, member, grad_full.at[c], dy_send.at[c], dy_recv.at[c])

    def grad_copy(c, j, other):
        return remote(
            grad_sent.at[c, other], grad_hbm.at[c, member], d_send.at[c, j], d_recv.at[c, j], (place, other)
        )

    def grad_own(c):
        return pltpu.make_async_copy(
            grad_sent.at[c, member], grad_hbm.at[c, member], local_sems.at[16 + c]
        )

    def grad_tick(tick):
        for c in range(chunks):
            step = tick - c
            if 0 <= step < count:
                line_gather_step(step, *grad_line(c))
            if step == count - 1:
                picked = dot_nn(
                    picker_ref[...].reshape(rows, length), grad_full[c].reshape(length, wide)
                ).astype(low)
                grad_sent[c] = picked.reshape(planes, slots, wide)
                for j, other in others:
                    grad_copy(c, j, other).start()
                grad_own(c).start()

    ticks = list(range(chunks + count - 1))
    grad_tick(ticks.pop(0))
    line_gather_step(count - 1, *hidden_line)

    for j, other in others:
        gain_plane(j, other).wait_recv()
    per_row = HEAD_SIZE // shard
    small_total = jnp.sum(gains_all[...].astype(jnp.float32), axis=(0, 1))
    gain_rows = []
    for row in range(2):
        parts = []
        for group in range(MODEL_WIDTH // HEAD_SIZE):
            part = jnp.zeros((1, HEAD_SIZE), jnp.float32)
            for index in range(group * per_row, (group + 1) * per_row):
                part += gains_all[index // planes, index % planes, row : row + 1, :].astype(jnp.float32)
            parts.append(part)
        gain_rows.append(jnp.concatenate(parts, axis=1))
    gains_ref[0:1, :] = gain_rows[0]
    gains_ref[1:2, :] = gain_rows[1]
    gain_query = small_total[2:3, :]
    gain_key = small_total[3:4, :]
    gains_ref[2:3, :HEAD_SIZE] = gain_query
    gains_ref[3:4, :HEAD_SIZE] = gain_key

    def normalize(values, gain):
        return (
            values
            * lax.rsqrt(jnp.mean(values * values, axis=-1, keepdims=True) + EPSILON)
            * gain
        )

    for block in range(count):
        values = hidden_full[block].astype(jnp.float32)
        normed[block * tokens : (block + 1) * tokens, :] = normalize(values, gain_rows[0]).astype(low)
    stores = [pltpu.make_async_copy(normed, normed_hbm, local_sems.at[1])]
    stores[-1].start()

    for k, other in far_chips:
        block_copy(k, other).wait_recv()
    for k, other in far_chips:
        block_pair(k, lax.rem(chip + chips - k, chips)).start()
    for k, other in far_chips:
        out_copy(k, other).wait_recv()
    for k, other in far_chips:
        out_pair(k, lax.rem(chip + chips - k, chips)).start()
    block_pair(0, chip).wait_recv()
    for k, other in far_chips:
        block_pair(k, lax.rem(chip + chips - k, chips)).wait_recv()
    weights = own_cols[...].reshape(MODEL_WIDTH, query_columns + 2 * HEAD_SIZE)
    stores.append(pltpu.make_async_copy(own_cols, own_cols_hbm, local_sems.at[2]))
    stores[-1].start()

    def prepare(values, gain):
        turned = normalize(values, gain)
        return turned * turn_cos_ref[...] + pltpu.roll(turned, HEAD_SIZE // 2, 1) * turn_sin_ref[...]

    paired = dot_nn(normed[...], weights[:, query_columns:])
    proj[heads] = paired[:, :HEAD_SIZE]
    proj[heads + 1] = paired[:, HEAD_SIZE:]
    pair[0] = prepare(paired[:, :HEAD_SIZE], gain_key).astype(low)
    pair[1] = paired[:, HEAD_SIZE:].astype(low)
    projected = dot_nn(normed[...], weights[:, :query_columns])
    for head in range(heads):
        proj[head] = projected[:, head * HEAD_SIZE : (head + 1) * HEAD_SIZE]
    value_turned = jnp.transpose(paired[:, HEAD_SIZE:]).astype(low)
    stores.append(pltpu.make_async_copy(proj, proj_hbm, local_sems.at[3]))
    stores[-1].start()
    stores.append(pltpu.make_async_copy(pair, pair_hbm, local_sems.at[4]))
    stores[-1].start()
    together = min(max(1, 2048 // length), heads)

    def some_heads(index, carry):
        first = index * together
        some = pl.ds(first, together)
        for k in range(together):
            queries[first + k] = prepare(proj[first + k], gain_query).astype(low)
        for block in range(count):
            begin, end = block * tokens, (block + 1) * tokens
            query = queries[some, begin:end, :].reshape(together * tokens, HEAD_SIZE)
            scores = dot_nt(pair[0, :end, :], query) * scale
            shape = (end, together * tokens)
            key_ids = lax.broadcasted_iota(jnp.int32, shape, 0) - begin
            query_ids = lax.rem(lax.broadcasted_iota(jnp.int32, shape, 1), tokens)
            scores = jnp.where(key_ids <= query_ids, scores, FILLER)
            top = jnp.max(scores, axis=0, keepdims=True)
            powers = jnp.exp(scores - top)
            total = jnp.sum(powers, axis=0, keepdims=True)
            lse = top + jnp.log(total)
            for k in range(together):
                lse_ref[first + k, :, begin:end] = lse[:, k * tokens : (k + 1) * tokens]
            probs = (powers * (1.0 / total)).astype(low)
            mixed = dot_nn(value_turned[:, :end], probs)
            heads_low[some, begin:end, :] = (
                jnp.transpose(mixed).astype(low).reshape(together, tokens, HEAD_SIZE)
            )
        return carry

    for part in range(heads // together):
        some_heads(part, 0)
        for _ in range(4 * together // heads):
            if ticks:
                grad_tick(ticks.pop(0))
    stores.append(pltpu.make_async_copy(queries, query_hbm, local_sems.at[5]))
    stores[-1].start()
    stores.append(pltpu.make_async_copy(heads_low, heads_hbm, local_sems.at[6]))
    stores[-1].start()

    out_pair(0, chip).wait_recv()
    for k, other in far_chips:
        out_pair(k, lax.rem(chip + chips - k, chips)).wait_recv()
    out_all = out_rows[...].reshape(query_columns, MODEL_WIDTH)
    stores.append(pltpu.make_async_copy(out_rows, out_rows_hbm, local_sems.at[7]))
    stores[-1].start()

    def project(block, carry):
        at = pl.ds(pl.multiple_of(block * tokens, tokens), tokens)
        mixed = jnp.concatenate([heads_low[head, at, :] for head in range(heads)], axis=1)
        branch[block] = dot_nn(mixed, out_all).astype(low)
        return carry

    lax.fori_loop(0, count, project, 0)
    line = (count, place, member, branch, sums, rs_send, rs_recv)
    for step in range(count - 1):
        line_sum_step(step, *line)
        for _ in range(-(-len(ticks) // (count - 1 - step))):
            grad_tick(ticks.pop(0))
    line_sum_end(*line, hidden1_ref)
    hidden1 = hidden_ref[...].astype(jnp.float32) + hidden1_ref[...]
    hidden1_ref[...] = hidden1
    mixed_ref[...] = normalize(hidden1, gain_rows[1]).astype(low)

    for j, other in others:
        router_plane(j, other).wait_recv()
    router_out[...] = router_all[...].reshape(router_out.shape)
    for j, other in others:
        mask_copy(j, other).wait_recv()
        for c in range(chunks):
            grad_copy(c, j, other).wait_recv()
    for k, other in far_places:
        gain_line(k, other).wait_send()
        column_copy(k, other).wait_send()
        places_line(k, other).wait_send()
        router_line(k, other).wait_send()
    for k, other in far_chips:
        out_copy(k, other).wait_send()
        block_copy(k, other).wait_send()
        out_pair(k, other).wait_send()
        block_pair(k, other).wait_send()
    out_pair(0, chip).wait_send()
    block_pair(0, chip).wait_send()
    for j, other in others:
        gain_plane(j, other).wait_send()
        router_plane(j, other).wait_send()
        mask_copy(j, other).wait_send()
        for c in range(chunks):
            grad_copy(c, j, other).wait_send()
    for c in range(chunks):
        grad_own(c).wait()
        line_gather_end(*grad_line(c))
    line_gather_end(*hidden_line)
    masks_own.wait()
    for store in stores:
        store.wait()


def attention_forward(
    count, planes, heads, shard, capacity, slots, chunks,
    hidden, routes, gain_one, gain_two, query_gain, key_gain, router, qkv, out_weight, cotangent,
    turn_cos, turn_sin,
):
    tokens = hidden.shape[0]
    length = count * tokens
    width = (heads + 2) * HEAD_SIZE
    chips = planes // 2
    wide = MODEL_WIDTH // chunks
    experts = -(-router.shape[-1] // 128) * 128
    small_rows = 16
    out_block = out_weight.shape[0]
    low, full = jnp.bfloat16, jnp.float32
    vmem = pl.BlockSpec(memory_space=pltpu.VMEM)
    anywhere = pl.BlockSpec(memory_space=pl.ANY)
    dma = pltpu.SemaphoreType.DMA
    shape = jax.ShapeDtypeStruct
    return pl.pallas_call(
        functools.partial(forward_kernel, count, planes, tokens, heads, shard, capacity, chunks),
        out_shape=(
            shape((tokens, MODEL_WIDTH), full),
            shape((tokens, MODEL_WIDTH), low),
            shape((heads, 1, length), full),
            shape((8, MODEL_WIDTH), full),
            shape((planes, slots, length), low),
            shape((MODEL_WIDTH, experts), low),
            shape((count, planes, shard, width), low),
            shape((planes, out_block, MODEL_WIDTH), low),
            shape((length, MODEL_WIDTH), low),
            shape((heads, length, HEAD_SIZE), low),
            shape((heads, length, HEAD_SIZE), low),
            shape((2, length, HEAD_SIZE), low),
            shape((heads + 2, length, HEAD_SIZE), full),
            shape((chunks, planes, slots, wide), low),
            shape((planes, slots, experts), low),
        ),
        in_specs=[vmem] * 12,
        out_specs=(vmem,) * 6 + (anywhere,) * 9,
        scratch_shapes=[
            pltpu.VMEM((count, shard, width), low),
            pltpu.VMEM((count, planes, shard, width), low),
            dma((3, max(count, chips))),
            dma((3, max(count, chips))),
            pltpu.VMEM((planes, out_block, MODEL_WIDTH), low),
            dma((2, chips)),
            dma((2, chips)),
            pltpu.VMEM((count, tokens, MODEL_WIDTH), low),
            dma((2, count, 2)),
            dma((2, count, 2)),
            pltpu.VMEM((count, planes, small_rows, HEAD_SIZE), low),
            dma((count,)),
            dma((count,)),
            dma((planes,)),
            dma((planes,)),
            pltpu.VMEM((count, planes, shard, experts), low),
            dma((count,)),
            dma((count,)),
            dma((planes,)),
            dma((planes,)),
            pltpu.VMEM((count, tokens, experts), low),
            dma((count,)),
            dma((count,)),
            pltpu.VMEM((length, MODEL_WIDTH), low),
            pltpu.VMEM((heads + 2, length, HEAD_SIZE), full),
            pltpu.VMEM((heads, length, HEAD_SIZE), low),
            pltpu.VMEM((2, length, HEAD_SIZE), low),
            pltpu.VMEM((heads, length, HEAD_SIZE), low),
            pltpu.VMEM((chunks, count, tokens, wide), low),
            dma((chunks, 2, count, 1)),
            dma((chunks, 2, count, 1)),
            pltpu.VMEM((chunks, planes, slots, wide), low),
            dma((chunks, planes)),
            dma((chunks, planes)),
            pltpu.VMEM((planes, slots, experts), low),
            dma((planes,)),
            dma((planes,)),
            pltpu.VMEM((count, tokens, MODEL_WIDTH), low),
            pltpu.VMEM((count + 1, tokens, MODEL_WIDTH), low),
            dma((2, count, 2)),
            dma((2, count, 2)),
            dma((16 + chunks,)),
        ],
        compiler_params=pltpu.CompilerParams(
            collective_id=1, has_side_effects=True, vmem_limit_bytes=VMEM_BYTES
        ),
        name="attention_forward",
    )(
        hidden, routes, gain_one, gain_two, query_gain, key_gain, router, qkv, out_weight, cotangent,
        turn_cos, turn_sin,
    )


def segments(slots):
    step = max(16, slots // 4 // 16 * 16)
    starts = [step * k for k in range(slots // step)]
    return list(zip(starts, starts[1:] + [slots]))


def ranked_block(rank, place, count):
    short = jnp.minimum(place, count - 1 - place)
    near = (rank + 1) // 2
    side = -1 if rank % 2 else 1
    far = rank - short
    far_side = jnp.where(place < count - 1 - place, 1, -1)
    return jnp.where(rank <= 2 * short, place + side * near, place + far_side * far)


def block_rank(block, place, count):
    short = jnp.minimum(place, count - 1 - place)
    away = jnp.abs(block - place)
    near = 2 * away - jnp.where(block < place, 1, 0)
    return jnp.where(away <= short, near, short + away)


def expert_kernel(
    count, planes, tokens, capacity, chunks,
    mixed_ref, hidden1_ref, cotangent_ref, gains_ref, routes_ref, masks_ref,
    picker_hbm, grad_hbm, router_hbm, in_hbm, back_hbm,
    grad_hidden_ref, branch_ref, router_ref, grad_in_hbm, grad_back_hbm, combined_hbm,
    picker, grad_rows, router, weight_in, weight_back, local_sems,
    full, ag_send, ag_recv,
    sent, arrived, x_send, x_recv,
    gate_up, act, grad_gate_up, gate_rows,
    back_arrived, b_send, b_recv,
    gate_sent, gate_arrived, gate_own, gate_sums, gate_total, g_send, g_recv, gs_send, gs_recv,
    sums, rs_send, rs_recv, in_tiles, back_tile, tile_sems,
):
    place = lax.axis_index("seq")
    member = lax.axis_index("dp")
    slots = sent.shape[1]
    rows = planes * slots
    length = count * tokens
    wide = MODEL_WIDTH // chunks
    own_expert = place * planes + member
    experts = count * planes
    lanes = router.shape[-1]
    extra = gate_sent.shape[-1]
    low = jnp.bfloat16
    pieces = segments(slots)
    others = [(j, lax.rem(member + j, planes)) for j in range(1, planes)]

    loads = [
        pltpu.make_async_copy(picker_hbm, picker, local_sems.at[0]),
        pltpu.make_async_copy(in_hbm, weight_in, local_sems.at[1]),
        pltpu.make_async_copy(router_hbm, router, local_sems.at[2]),
        pltpu.make_async_copy(back_hbm, weight_back, local_sems.at[3]),
    ] + [
        pltpu.make_async_copy(
            grad_hbm.at[c], grad_rows.at[:, :, pl.ds(c * wide, wide)], local_sems.at[4 + c]
        )
        for c in range(chunks)
    ]
    for load in loads:
        load.start()
    full[place] = mixed_ref[...]
    greet([(place, other) for _, other in others] + [(lax.rem(place + k, count), member) for k in range(1, count)])

    line = (count, place, member, full, ag_send, ag_recv)

    def row_copy(i, j, other):
        low_row, high_row = pieces[i]
        part = pl.ds(low_row, high_row - low_row)
        return remote(
            sent.at[other, part], arrived.at[member, part], x_send.at[i, j], x_recv.at[i, j], (place, other)
        )

    def back_copy(i, j, other):
        low_row, high_row = pieces[i]
        part = pl.ds(low_row, high_row - low_row)
        return remote(
            sent.at[other, part], back_arrived.at[member, part], b_send.at[i, j], b_recv.at[i, j],
            (place, other),
        )

    def lanes_of(block):
        return pl.ds(pl.multiple_of(block * tokens, tokens), tokens)

    line_gather_step(0, *line)
    loads[0].wait()
    done = 0
    for i, (begin, end) in enumerate(pieces):
        needed = count - 1 if i == len(pieces) - 1 else min((end - 1) // capacity, count - 1)
        while done < needed:
            done += 1
            line_gather_step(done, *line)
        height = planes * (end - begin)
        picked = jnp.zeros((height, MODEL_WIDTH), jnp.float32)
        for rank in range(begin // capacity, min((end - 1) // capacity, count - 1) + 1):
            block = ranked_block(rank, place, count)
            choice = picker[:, begin:end, lanes_of(block)].reshape(height, tokens)
            picked += dot_nn(choice, full[block])
        sent[:, begin:end, :] = picked.astype(low).reshape(planes, end - begin, MODEL_WIDTH)
        for j, other in others:
            row_copy(i, j, other).start()
        arrived[member, begin:end, :] = sent[member, begin:end, :]
    for load in loads[1:]:
        load.wait()

    own_lanes = lax.broadcasted_iota(jnp.int32, (tokens, lanes), 1)
    named = jnp.zeros((tokens, lanes), jnp.float32)
    chosen = jnp.transpose(routes_ref[...].astype(jnp.float32))
    for k in range(TOP):
        named += jnp.where(chosen[:, k : k + 1] == own_lanes.astype(jnp.float32), 1.0, 0.0)

    def masked_gates(scores, mask):
        shifted = jnp.where(mask > 0, scores, FILLER)
        powers = jnp.where(mask > 0, jnp.exp(shifted - jnp.max(shifted, axis=-1, keepdims=True)), 0.0)
        total = jnp.sum(powers, axis=-1, keepdims=True)
        return powers / jnp.where(total > 0, total, 1.0)

    own_gates = masked_gates(dot_nn(mixed_ref[...], router[...]), named)

    def work(i):
        begin, end = pieces[i]
        height = planes * (end - begin)
        x = arrived[:, begin:end, :].reshape(height, MODEL_WIDTH)
        gate_up[:height, :] = dot_nn(x, weight_in[...])
        mask = masks_ref[:, begin:end, :].reshape(height, lanes).astype(jnp.float32)
        gates = masked_gates(dot_nn(x, router[...]), mask)
        lane_ids = lax.broadcasted_iota(jnp.int32, (height, lanes), 1)
        gate = jnp.sum(jnp.where(lane_ids == own_expert, gates, 0.0), axis=-1, keepdims=True)
        gate_rows[:, begin:end, :] = jnp.broadcast_to(gate, (height, HEAD_SIZE)).reshape(
            planes, end - begin, HEAD_SIZE
        )
        grads = grad_rows[:, begin:end, :].reshape(height, MODEL_WIDTH).astype(jnp.float32)
        grad_act = dot_nt((grads * gate).astype(low), weight_back[...])
        gate_part = gate_up[:height, :FF]
        up_part = gate_up[:height, FF:]
        chance = jax.nn.sigmoid(gate_part)
        silu = gate_part * chance
        act[:, begin:end, :] = (silu * up_part).astype(low).reshape(planes, end - begin, FF)
        slope = chance + silu * (1.0 - chance)
        grad_gate = (grad_act * up_part * slope).astype(low)
        grad_up = (grad_act * silu).astype(low)
        grad_gate_up[:, begin:end, :FF] = grad_gate.reshape(planes, end - begin, FF)
        grad_gate_up[:, begin:end, FF:] = grad_up.reshape(planes, end - begin, FF)
        for j, other in others:
            row_copy(i, j, other).wait_send()
        back = jnp.concatenate([grad_gate, grad_up], axis=1)
        for c in range(chunks):
            columns = slice(c * wide, (c + 1) * wide)
            sent[:, begin:end, columns] = (
                dot_nt(back, weight_in[columns, :]).astype(low).reshape(planes, end - begin, wide)
            )
        back_arrived[member, begin:end, :] = sent[member, begin:end, :]

    def send_back(i):
        for j, other in others:
            back_copy(i, j, other).start()

    last = len(pieces) - 1
    for i in range(last):
        for j, other in others:
            row_copy(i, j, other).wait_recv()
        work(i)
    for j, other in others:
        row_copy(last, j, other).wait_recv()
    send_back(last - 1)
    work(last)
    send_back(last)
    line_gather_end(*line)

    tile = in_tiles.shape[1]

    def in_copy(slot, index):
        return pltpu.make_async_copy(
            in_tiles.at[slot],
            grad_in_hbm.at[pl.ds(pl.multiple_of(index * tile, tile), tile), pl.ds(slot * FF, FF)],
            tile_sems.at[slot],
        )

    def in_gradient(index, carry):
        x = arrived[:, :, pl.ds(pl.multiple_of(index * tile, tile), tile)].reshape(rows, tile)
        for slot in range(2):

            @pl.when(index > 0)
            def _():
                in_copy(slot, index).wait()

            grads = grad_gate_up[:, :, slot * FF : (slot + 1) * FF].reshape(rows, FF)
            in_tiles[slot] = dot_tn(x, grads).astype(low)
            in_copy(slot, index).start()
        return carry

    def outputs(c, grad_gate):
        columns = pl.ds(pl.multiple_of(c * wide, wide), wide)
        result = dot_nn(act[...].reshape(rows, FF), weight_back[:, columns])
        result = result.astype(low).astype(jnp.float32)
        grads = grad_rows[:, :, columns].reshape(rows, wide).astype(jnp.float32)
        scale = gate_rows[...].reshape(rows, HEAD_SIZE)[:, 0:1]
        grad_rows[:, :, columns] = (grads * scale).astype(low).reshape(planes, slots, wide)
        arrived[:, :, columns] = (result * scale).astype(low).reshape(planes, slots, wide)
        return grad_gate + jnp.sum(result * grads, axis=-1, keepdims=True)

    def gate_copy(j, other):
        return remote(
            gate_sent.at[other], gate_arrived.at[member], g_send.at[j], g_recv.at[j], (place, other)
        )

    def back_tile_copy(index):
        return pltpu.make_async_copy(
            back_tile,
            grad_back_hbm.at[:, pl.ds(pl.multiple_of(index * tile, tile), tile)],
            tile_sems.at[2],
        )

    def back_gradient(index, carry):
        grads = grad_rows[:, :, pl.ds(pl.multiple_of(index * tile, tile), tile)].reshape(rows, tile)
        result = dot_tn(act[...].reshape(rows, FF), grads)

        @pl.when(index > 0)
        def _():
            back_tile_copy(index).wait()

        back_tile[...] = result.astype(low)
        back_tile_copy(index).start()
        return carry

    tiles = MODEL_WIDTH // tile
    lax.fori_loop(0, tiles, in_gradient, 0)
    grad_gate = lax.fori_loop(0, chunks, outputs, jnp.zeros((rows, 1), jnp.float32))
    combined = pltpu.make_async_copy(arrived, combined_hbm, tile_sems.at[3])
    combined.start()
    high = grad_gate.astype(low).astype(jnp.float32)
    rest = grad_gate - high
    wide_lanes = lax.broadcasted_iota(jnp.int32, (rows, extra), 1)
    columns = jnp.where(
        wide_lanes == own_expert, high, jnp.where(wide_lanes == own_expert + experts, rest, 0.0)
    )
    gate_sent[...] = columns.astype(low).reshape(gate_sent.shape)
    for j, other in others:
        gate_copy(j, other).start()
    gate_arrived[member] = gate_sent[member]
    for i in range(last - 2, -1, -1):
        send_back(i)
    lax.fori_loop(0, tiles, back_gradient, 0)

    for j, other in others:
        gate_copy(j, other).wait_recv()
    gate_own[...] = (
        dot_tn(picker[...].reshape(rows, length), gate_arrived[...].reshape(rows, extra))
        .astype(low)
        .reshape(count, tokens, extra)
    )
    gate_line = (count, place, member, gate_own, gate_sums, gs_send, gs_recv)
    sums_line = (count, place, member, full, sums, rs_send, rs_recv)
    come = set()
    for step in range(count):
        rank = count - 1 - step
        first = rank * capacity // 16 * 16
        final = min(-(-(rank + 1) * capacity // 16) * 16, slots)
        for i in range(last, -1, -1):
            begin, end = pieces[i]
            if i not in come and begin < final and end > first:
                come.add(i)
                for j, other in others:
                    back_copy(i, j, other).wait_recv()
        block = ranked_block(rank, place, count)
        height = planes * (final - first)
        choice = picker[:, first:final, lanes_of(block)].reshape(height, tokens)
        full[block] = dot_tn(
            choice, back_arrived[:, first:final, :].reshape(height, MODEL_WIDTH)
        ).astype(low)
        if step < count - 1:
            line_sum_step(step, *gate_line)
            line_sum_step(step, *sums_line)
    for i in range(len(pieces)):
        if i not in come:
            for j, other in others:
                back_copy(i, j, other).wait_recv()
    line_sum_end(*gate_line, gate_total)
    line_sum_end(*sums_line, grad_hidden_ref)

    if experts % 128 == 0:
        grad_gates = gate_total[:, :experts] + gate_total[:, experts:]
    else:
        grad_gates = gate_total[...] + pltpu.roll(gate_total[...], extra - experts, 1)
    middle = jnp.sum(own_gates * grad_gates, axis=-1, keepdims=True)
    grad_logits = (own_gates * (grad_gates - middle)).astype(low)
    grad_mixed = grad_hidden_ref[...] + dot_nt(grad_logits, router[...])
    router_ref[:experts, :] = dot_tn(grad_logits, mixed_ref[...])[:experts]
    hidden = hidden1_ref[...]
    inverse = lax.rsqrt(jnp.mean(hidden * hidden, axis=-1, keepdims=True) + EPSILON)
    unit = hidden * inverse
    router_ref[experts:, :] = jnp.broadcast_to(
        jnp.sum(grad_mixed * unit, axis=0, keepdims=True), (8, MODEL_WIDTH)
    )
    turned = grad_mixed * gains_ref[1:2, :]
    grad_norm = inverse * (turned - unit * jnp.mean(turned * unit, axis=-1, keepdims=True))
    grad_hidden = cotangent_ref[...].astype(jnp.float32) + grad_norm
    grad_hidden_ref[...] = grad_hidden
    branch_ref[...] = grad_hidden.astype(low)

    for j, other in others:
        for i in range(len(pieces)):
            back_copy(i, j, other).wait_send()
        gate_copy(j, other).wait_send()
    in_copy(0, 0).wait()
    in_copy(1, 0).wait()
    back_tile_copy(0).wait()
    combined.wait()


def expert_layer(
    count, planes, capacity, mixed, hidden1, cotangent, gains, routes, masks, picker, grad_rows,
    router, weight_in, weight_back,
):
    tokens = mixed.shape[0]
    chunks, _, slots, wide = grad_rows.shape
    rows = planes * slots
    extra = -(-2 * count * planes // 128) * 128
    lanes = router.shape[-1]
    height = planes * max(end - begin for begin, end in segments(slots))
    tile = 256 if rows < 1280 else 128
    pieces = len(segments(slots))
    low, kind = jnp.bfloat16, jnp.float32
    vmem = pl.BlockSpec(memory_space=pltpu.VMEM)
    anywhere = pl.BlockSpec(memory_space=pl.ANY)
    dma = pltpu.SemaphoreType.DMA
    shape = jax.ShapeDtypeStruct
    blocks = (planes, slots, MODEL_WIDTH)
    return pl.pallas_call(
        functools.partial(expert_kernel, count, planes, tokens, capacity, chunks),
        out_shape=(
            shape((tokens, MODEL_WIDTH), kind),
            shape((tokens, MODEL_WIDTH), low),
            shape((count * planes + 8, MODEL_WIDTH), kind),
            shape(weight_in.shape, low),
            shape(weight_back.shape, low),
            shape(blocks, low),
        ),
        in_specs=[vmem] * 6 + [anywhere] * 5,
        out_specs=(vmem,) * 3 + (anywhere,) * 3,
        scratch_shapes=[
            pltpu.VMEM(picker.shape, low),
            pltpu.VMEM(blocks, low),
            pltpu.VMEM(router.shape, low),
            pltpu.VMEM(weight_in.shape, low),
            pltpu.VMEM(weight_back.shape, low),
            dma((4 + chunks,)),
            pltpu.VMEM((count, tokens, MODEL_WIDTH), low),
            dma((2, count, 2)),
            dma((2, count, 2)),
            pltpu.VMEM(blocks, low),
            pltpu.VMEM(blocks, low),
            dma((pieces, planes)),
            dma((pieces, planes)),
            pltpu.VMEM((height, 2 * FF), kind),
            pltpu.VMEM((planes, slots, FF), low),
            pltpu.VMEM((planes, slots, 2 * FF), low),
            pltpu.VMEM((planes, slots, HEAD_SIZE), kind),
            pltpu.VMEM(blocks, low),
            dma((pieces, planes)),
            dma((pieces, planes)),
            pltpu.VMEM((planes, slots, extra), low),
            pltpu.VMEM((planes, slots, extra), low),
            pltpu.VMEM((count, tokens, extra), low),
            pltpu.VMEM((count + 1, tokens, extra), low),
            pltpu.VMEM((tokens, extra), kind),
            dma((planes,)),
            dma((planes,)),
            dma((2, count, 1)),
            dma((2, count, 1)),
            pltpu.VMEM((count + 1, tokens, MODEL_WIDTH), low),
            dma((2, count, 2)),
            dma((2, count, 2)),
            pltpu.VMEM((2, tile, FF), low),
            pltpu.VMEM((FF, tile), low),
            dma((4,)),
        ],
        compiler_params=pltpu.CompilerParams(
            collective_id=2, has_side_effects=True, vmem_limit_bytes=VMEM_BYTES
        ),
        name="expert_layer",
    )(
        mixed, hidden1, cotangent, gains, routes, masks, picker, grad_rows, router, weight_in,
        weight_back,
    )


def finish_kernel(
    in_ref, back_ref, hidden_ref, mixed_ref, input_ref, out_ref, qkv_ref,
    in_full, back_full, output, input_full, out_full, qkv_full,
):
    in_full[...] = in_ref[...].astype(jnp.float32)
    back_full[...] = back_ref[...].astype(jnp.float32)
    output[...] = (hidden_ref[...] + mixed_ref[...]).astype(jnp.bfloat16)
    input_full[...] = input_ref[...]
    out_full[...] = out_ref[...]
    qkv_full[...] = qkv_ref[...]


def finish(grad_in, grad_back, hidden1, mixed, grad_input, shard_out, shard_qkv):
    steps = 8
    arrays = (grad_in, grad_back, hidden1, mixed, grad_input, shard_out, shard_qkv)

    def by_rows(array):
        return pl.BlockSpec((array.shape[0] // steps, array.shape[1]), lambda i: (i, 0))

    def by_columns(array):
        return pl.BlockSpec((array.shape[0], array.shape[1] // steps), lambda i: (0, i))

    specs = [by_rows(array) for array in arrays[:5]] + [by_columns(array) for array in arrays[5:]]
    results = (grad_in, grad_back, hidden1, grad_input, shard_out, shard_qkv)
    kinds = (jnp.float32, jnp.float32, jnp.bfloat16) + (jnp.float32,) * 3
    return pl.pallas_call(
        finish_kernel,
        grid=(steps,),
        out_shape=tuple(jax.ShapeDtypeStruct(a.shape, k) for a, k in zip(results, kinds)),
        in_specs=specs,
        out_specs=tuple([specs[0], specs[1], specs[2], specs[4], specs[5], specs[6]]),
        compiler_params=pltpu.CompilerParams(vmem_limit_bytes=VMEM_BYTES),
        name="finish",
    )(*arrays)


def turn_tables(length):
    half = HEAD_SIZE // 2
    freqs = np.float32(ROPE_BASE) ** (-(np.arange(half, dtype=np.float32) * np.float32(2 / HEAD_SIZE)))
    angles = np.arange(length, dtype=np.float32)[:, None] * freqs[None, :]
    cosine, sine = np.cos(angles), np.sin(angles)
    return (
        jnp.asarray(np.concatenate([cosine, cosine], axis=1), jnp.float32),
        jnp.asarray(np.concatenate([-sine, sine], axis=1), jnp.float32),
    )


def body(
    hidden_in,
    routes,
    norm1_gain,
    query_gain,
    key_gain,
    qkv_weight,
    out_weight,
    norm2_gain,
    router,
    gate_up_weight,
    down_weight,
    cotangent,
):
    tokens = hidden_in.shape[1]
    sequence_number = lax.axis_size("seq")
    planes = lax.axis_size("dp")
    devices = sequence_number * planes
    group = lax.axis_index("seq")
    member = lax.axis_index("dp")
    index = group * planes + member
    heads = QUERY_HEADS // sequence_number
    query_columns = heads * HEAD_SIZE
    head_replicas = sequence_number // KEY_VALUE_HEADS
    capacity = (tokens * TOP * 9 + 8 * devices - 1) // (8 * devices)
    slots = -(-sequence_number * capacity // 16) * 16
    chunks = 4
    sequence_length = sequence_number * tokens
    shard = norm1_gain.shape[0]
    small_shard = query_gain.shape[0]

    turn_cos, turn_sin = turn_tables(sequence_length)
    (
        hidden1, mixed_low, lse, gains, picker, full_router, own_cols, out_rows, normed_full,
        heads_low, queries, pair, projected, grad_rows, masks,
    ) = attention_forward(
        sequence_number,
        planes,
        heads,
        shard,
        capacity,
        slots,
        chunks,
        hidden_in[0],
        routes[0].T,
        norm1_gain[None],
        norm2_gain[None],
        query_gain[None],
        key_gain[None],
        router,
        qkv_weight,
        out_weight,
        cotangent[0],
        turn_cos,
        turn_sin,
    )
    (
        grad_hidden1, grad_branch, grad_router, grad_weight_in, grad_weight_back, combined_rows,
    ) = expert_layer(
        sequence_number,
        planes,
        capacity,
        mixed_low,
        hidden1,
        cotangent[0],
        gains,
        routes[0].T,
        masks,
        picker,
        grad_rows,
        full_router,
        gate_up_weight[0],
        down_weight[0],
    )
    (
        grad_input, shard_out, shard_qkv, mixed_total, router_total, gain_total, _,
    ) = attention_backward(
        sequence_number,
        planes,
        heads,
        shard,
        capacity,
        grad_branch,
        grad_hidden1,
        hidden_in[0],
        gains,
        grad_router,
        out_rows,
        own_cols,
        normed_full,
        heads_low,
        queries,
        pair,
        projected,
        picker,
        combined_rows,
        lse,
        turn_cos,
        turn_sin,
    )
    grad_weight_in, grad_weight_back, output, grad_input, shard_out, shard_qkv = finish(
        grad_weight_in, grad_weight_back, hidden1, mixed_total, grad_input, shard_out, shard_qkv
    )
    index = group * planes + member
    router_own = lax.dynamic_slice_in_dim(router_total, member * shard, shard, 1)
    gain_own = lax.dynamic_slice_in_dim(
        gain_total[: MODEL_WIDTH // HEAD_SIZE].reshape(1, MODEL_WIDTH), index * shard, shard, 1
    )
    head_gains = lax.dynamic_slice_in_dim(
        gain_total[MODEL_WIDTH // HEAD_SIZE :][:2], index * small_shard, small_shard, 1
    )
    return (
        output[None],
        grad_input[None],
        gain_own[0],
        head_gains[0],
        head_gains[1],
        shard_qkv,
        shard_out,
        router_own[devices],
        router_own[:devices].T,
        grad_weight_in[None],
        grad_weight_back[None],
    )


def solution(mesh):
    in_specs = (
        P("dp", "seq", None),
        P("dp", "seq", None),
        P(("seq", "dp")),
        P(("seq", "dp")),
        P(("seq", "dp")),
        P(("seq", "dp"), None),
        P(("seq", "dp"), None),
        P(("seq", "dp")),
        P(("seq", "dp"), None),
        P(("seq", "dp"), None, None),
        P(("seq", "dp"), None, None),
        P("dp", "seq", None),
    )
    out_specs = (
        P("dp", "seq", None),
        P("dp", "seq", None),
        P(("seq", "dp")),
        P(("seq", "dp")),
        P(("seq", "dp")),
        P(("seq", "dp"), None),
        P(("seq", "dp"), None),
        P(("seq", "dp")),
        P(("seq", "dp"), None),
        P(("seq", "dp"), None, None),
        P(("seq", "dp"), None, None),
    )
    return jax.shard_map(body, mesh=mesh, in_specs=in_specs, out_specs=out_specs, check_vma=False)
```

```python
import functools
import jax
import jax.numpy as jnp
import numpy as np
from jax import lax
from jax.experimental import pallas as pl
from jax.experimental.pallas import tpu as pltpu
from jax.sharding import PartitionSpec as P


MODEL_WIDTH = 2048
QUERY_HEADS = 32
KEY_VALUE_HEADS = 4
HEAD_SIZE = 128
FF = 768
TOP = 8


EPSILON = 1e-06
ROPE_BASE = 1000000.0
FILLER = -1e30
QUERY_BLOCK = 512


MESH = pl.DeviceIdType.MESH
VMEM_BYTES = 63 * 1024 * 1024


def dot_nn(left, right):
    return jnp.dot(left, right, preferred_element_type=jnp.float32)


def dot_nt(left, right):
    return lax.dot_general(
        left, right, (((1,), (1,)), ((), ())), preferred_element_type=jnp.float32
    )


def dot_tn(left, right):
    return lax.dot_general(
        left, right, (((0,), (0,)), ((), ())), preferred_element_type=jnp.float32
    )


def greet(peers, between=None):
    barrier = pltpu.get_barrier_semaphore()
    for peer in peers:
        pl.semaphore_signal(barrier, inc=1, device_id=peer, device_id_type=MESH)
    if between is not None:
        between()
    pl.semaphore_wait(barrier, len(peers))


def remote(source, target, send_sem, recv_sem, device):
    return pltpu.make_async_remote_copy(
        src_ref=source,
        dst_ref=target,
        send_sem=send_sem,
        recv_sem=recv_sem,
        device_id=device,
        device_id_type=MESH,
    )


def line_gather_step(step, count, place, column, blocks, send_sems, recv_sems):
    parts = send_sems.shape[-1]
    height = blocks.shape[1] // parts
    for part in range(parts):
        rows = pl.ds(part * height, height)
        for side, away in ((0, 1), (1, -1)):
            origin = place - away * step
            there = (origin >= 0) & (origin < count)
            target = place + away

            def copy(come, device):
                block = blocks.at[origin, rows]
                return remote(
                    block, block, send_sems.at[side, step, part], recv_sems.at[side, come, part],
                    (device, column),
                )

            if step > 0:

                @pl.when(there)
                def _():
                    copy(step, place).wait_recv()

            if step < count - 1:

                @pl.when(there & (target >= 0) & (target < count))
                def _():
                    copy(step + 1, target).start()


def line_gather_end(count, place, column, blocks, send_sems, recv_sems):
    parts = send_sems.shape[-1]
    height = blocks.shape[1] // parts
    for step in range(count - 1):
        for part in range(parts):
            rows = pl.ds(part * height, height)
            for side, away in ((0, 1), (1, -1)):
                origin = place - away * step
                target = place + away

                @pl.when((origin >= 0) & (origin < count) & (target >= 0) & (target < count))
                def _():
                    block = blocks.at[origin, rows]
                    remote(
                        block, block, send_sems.at[side, step, part], recv_sems.at[side, step, part],
                        (place, column),
                    ).wait_send()


def line_sum_step(step, count, place, column, own, sums, send_sems, recv_sems):
    parts = send_sems.shape[-1]
    height = own.shape[1] // parts
    for part in range(parts):
        rows = pl.ds(part * height, height)
        for side in range(2):
            if side == 0:
                turn = step - place
                index = count - 1 - turn
                active = (turn >= 0) & (index > place)
                target, slot = place + 1, index
            else:
                index = step - (count - 1 - place)
                active = (index >= 0) & (index < place)
                target, slot = place - 1, jnp.where(index == place - 1, count, index)
            fresh = place == (0 if side == 0 else count - 1)

            @pl.when(active)
            def _():
                block = sums.at[index, rows]

                def copy(goal, device):
                    return remote(
                        block, sums.at[goal, rows], send_sems.at[side, index, part],
                        recv_sems.at[side, index, part], (device, column),
                    )

                @pl.when(jnp.logical_not(fresh))
                def _():
                    copy(index, place).wait_recv()
                    sums[index, rows] = (
                        sums[index, rows].astype(jnp.float32) + own[index, rows].astype(jnp.float32)
                    ).astype(jnp.bfloat16)

                @pl.when(fresh)
                def _():
                    sums[index, rows] = own[index, rows]

                copy(slot, target).start()


def line_sum_end(count, place, column, own, sums, send_sems, recv_sems, total):
    parts = send_sems.shape[-1]
    height = own.shape[1] // parts
    for part in range(parts):
        rows = pl.ds(part * height, height)
        total[rows, :] = own[place, rows].astype(jnp.float32)
        for side, come in ((0, place > 0), (1, place < count - 1)):
            slot = place if side == 0 else count

            @pl.when(come)
            def _():
                block = sums.at[slot, rows]
                remote(
                    block, block, send_sems.at[side, place, part], recv_sems.at[side, place, part],
                    (place, column),
                ).wait_recv()
                total[rows, :] += sums[slot, rows].astype(jnp.float32)

    for step in range(count - 1):
        last = count - 1 - step
        for part in range(parts):
            rows = pl.ds(part * height, height)
            for side, index, sent in ((0, last, last > place), (1, step, step < place)):

                @pl.when(sent)
                def _():
                    block = sums.at[index, rows]
                    remote(
                        block, block, send_sems.at[side, index, part], recv_sems.at[side, index, part],
                        (place, column),
                    ).wait_send()


def backward_kernel(
    count, planes, tokens, heads, shard, capacity,
    branch_ref, grad_hidden_ref, hidden_ref, gains_ref, router_ref,
    out_rows_hbm, own_cols_hbm, normed_hbm, heads_hbm, query_hbm, pair_hbm,
    proj_hbm, picker_hbm, combined_hbm, lse_ref, turn_cos_ref, turn_sin_ref,
    grad_input_ref, out_total, qkv_total, mixed_total, router_total, gain_total, mixed_arrived,
    out_rows, own_cols, normed, heads_low, queries, pair, proj, picker, local_sems,
    branch_full, ag_send, ag_recv,
    grad_heads, grad_proj, grad_pair, gain_parts,
    grad_out, out_pair, out_far, out_sems,
    grad_cols, col_pair, col_far, col_sums, columns_out, col_sems,
    normed_room, normed_sums, rs_send, rs_recv, z_sems,
    mixed_rows, mixed_part, mixed_sums, mix_send, mix_recv, mix_local, ms_send, ms_recv,
    router_line, router_sum, router_chip, router_pair, router_sems,
    gain_own, gain_line, gain_chip, gain_pair, gain_sems,
):
    place = lax.axis_index("seq")
    member = lax.axis_index("dp")
    core = lax.rem(member, 2)
    chip = member // 2
    chips = planes // 2
    partner = member + 1 - 2 * core
    length = count * tokens
    query_columns = heads * HEAD_SIZE
    width = query_columns + 2 * HEAD_SIZE
    out_block = query_columns // planes
    scale = HEAD_SIZE ** (-0.5)
    chunks = mixed_part.shape[0]
    wide = MODEL_WIDTH // chunks
    shared = normed_room.shape[0] == 1
    normed_part = branch_full if shared else normed_room
    slots = mixed_rows.shape[1]
    low = jnp.bfloat16

    loads = [
        pltpu.make_async_copy(source, target, local_sems.at[index])
        for index, (source, target) in enumerate(
            [
                (out_rows_hbm, out_rows),
                (query_hbm, queries),
                (pair_hbm, pair),
                (heads_hbm, heads_low),
                (proj_hbm, proj),
                (own_cols_hbm, own_cols),
                (normed_hbm, normed),
                (picker_hbm, picker),
            ]
        )
    ]
    for load in loads:
        load.start()
    branch_full[place] = branch_ref[...]

    far_chips = [(k, lax.rem(chip + k, chips)) for k in range(1, chips)]
    far_places = [(k, lax.rem(place + k, count)) for k in range(1, count)]
    others = [(j, lax.rem(member + j, planes)) for j in range(1, planes)]
    greet([(place, other) for _, other in others] + [(other, member) for _, other in far_places])

    line = (count, place, member, branch_full, ag_send, ag_recv)
    line_gather_step(0, *line)

    def mixed_copy(c, j, other):
        part = pl.ds(c * wide, wide)
        return remote(
            combined_hbm.at[other, :, part], mixed_arrived.at[member, :, part],
            mix_send.at[c, j], mix_recv.at[c, j], (place, other),
        )

    def mixed_send(c):
        for j, other in others:
            mixed_copy(c, j, other).start()

    mixed_send(0)
    mixed_own = pltpu.make_async_copy(
        combined_hbm.at[member], mixed_arrived.at[member], mix_local.at[0]
    )
    mixed_own.start()
    for load in loads:
        load.wait()

    gain_query = gains_ref[2:3, :HEAD_SIZE]
    gain_key = gains_ref[3:4, :HEAD_SIZE]
    grad_pair[...] = jnp.zeros_like(grad_pair)
    gain_parts[...] = jnp.zeros_like(gain_parts)
    key_turned = jnp.transpose(pair[0].astype(jnp.float32)).astype(low)

    def unprepare(grad, raw, gain, cosine, sine):
        turned = grad * cosine - pltpu.roll(grad, HEAD_SIZE // 2, 1) * sine
        inverse = lax.rsqrt(jnp.mean(raw * raw, axis=-1, keepdims=True) + EPSILON)
        unit = raw * inverse
        gain_part = jnp.sum(turned * unit, axis=0, keepdims=True)
        turned = turned * gain
        middle = jnp.mean(turned * unit, axis=-1, keepdims=True)
        return inverse * (turned - unit * middle), gain_part

    together = min(max(1, 2048 // length), heads)

    def process(block):
        at = pl.ds(pl.multiple_of(block * tokens, tokens), tokens)
        partial_heads = dot_nt(
            branch_full[block], out_rows[...].reshape(query_columns, MODEL_WIDTH)
        ).astype(low)
        for head in range(heads):
            grad_heads[head] = partial_heads[:, head * HEAD_SIZE : (head + 1) * HEAD_SIZE]

        cosine, sine = turn_cos_ref[at, :], turn_sin_ref[at, :]

        def some_heads(index, carry):
            first = index * together
            some = pl.ds(first, together)
            query = queries[some, at, :].reshape(together * tokens, HEAD_SIZE)
            grad = grad_heads[some].reshape(together * tokens, HEAD_SIZE)
            scores = dot_nt(pair[0], query) * scale
            shape = (length, together * tokens)
            key_ids = lax.broadcasted_iota(jnp.int32, shape, 0) - block * tokens
            query_ids = lax.rem(lax.broadcasted_iota(jnp.int32, shape, 1), tokens)
            scores = jnp.where(key_ids <= query_ids, scores, FILLER)
            lse = jnp.concatenate([lse_ref[first + k, :, at] for k in range(together)], axis=1)
            probs = jnp.exp(scores - lse)
            grad_probs = dot_nt(pair[1], grad)
            delta = jnp.sum(probs * grad_probs, axis=0, keepdims=True)
            grad_scores = (probs * (grad_probs - delta)).astype(low)
            grad_pair[0] += dot_nn(grad_scores, query) * scale
            grad_pair[1] += dot_nn(probs.astype(low), grad)
            grad_query = jnp.transpose(dot_nn(key_turned, grad_scores)) * scale
            for k in range(together):
                grad_raw, gain_part = unprepare(
                    grad_query[k * tokens : (k + 1) * tokens],
                    proj[first + k, at, :],
                    gain_query,
                    cosine,
                    sine,
                )
                gain_parts[0:1, :] += gain_part
                columns = pl.ds(pl.multiple_of((first + k) * HEAD_SIZE, HEAD_SIZE), HEAD_SIZE)
                grad_proj[at, columns] = grad_raw.astype(low)
            return carry

        lax.fori_loop(0, heads // together, some_heads, 0)

    def gather(step):
        line_gather_step(step, *line)

        def side(index, carry):
            block = place - step + 2 * step * index

            @pl.when((block >= 0) & (block < count))
            def _():
                process(block)

            return carry

        lax.fori_loop(0, 2, side, 0)

    def mixed_line(c):
        return (count, place, member, mixed_part.at[c], mixed_sums.at[c], ms_send.at[c], ms_recv.at[c])

    def mixed_chunk(c):
        for j, other in others:
            mixed_copy(c, j, other).wait_recv()
        if c == 0:
            mixed_own.wait()
        load = pltpu.make_async_copy(
            mixed_arrived.at[:, :, pl.ds(c * wide, wide)], mixed_rows, mix_local.at[1]
        )
        load.start()
        load.wait()
        for rank in range(count):
            block = ranked_block(rank, place, count)
            first = rank * capacity // 16 * 16
            final = min(-(-(rank + 1) * capacity // 16) * 16, slots)
            height = planes * (final - first)
            at = pl.ds(pl.multiple_of(block * tokens, tokens), tokens)
            choice = picker[:, first:final, at].reshape(height, tokens)
            mixed_part[c, block] = dot_tn(
                choice, mixed_rows[:, first:final, :].reshape(height, wide)
            ).astype(low)

    waves = list(range(chunks + count - 2))

    def mixed_wave():
        wave = waves.pop(0)
        for c in range(chunks):
            if 0 <= wave - c < count - 1:
                line_sum_step(wave - c, *mixed_line(c))

    process(place)
    mixed_send(1)
    for step in range(1, count):
        gather(step)
        if step < count - 1 and step <= chunks - 2:
            mixed_send(step + 1)
            mixed_chunk(step - 1)
            mixed_wave()
    mixed_done = min(chunks - 2, count - 2)
    for c in range(mixed_done + 2, chunks):
        mixed_send(c)
    line_gather_end(*line)

    per_head = HEAD_SIZE // out_block

    def out_gradient(head):
        all_branch = branch_full[...].reshape(length, MODEL_WIDTH)
        part = dot_tn(heads_low[head], all_branch).astype(low)
        if per_head == 1:
            grad_out[head] = part
        else:
            grad_out[head * per_head : (head + 1) * per_head] = part.reshape(
                per_head, out_block, MODEL_WIDTH
            )

    def out_copy(k):
        return remote(
            grad_out.at[2 * k + 1 - core], out_pair.at[k], out_sems.at[0, k], out_sems.at[1, k],
            (place, partner),
        )

    def out_far_copy(k, other):
        return remote(
            out_pair.at[other], out_far.at[k - 1], out_sems.at[2, k], out_sems.at[3, k],
            (place, 2 * other + core),
        )

    def out_gradients():
        if per_head == 1:
            for k in range(chips):
                out_gradient(2 * k + 1 - core)
                out_copy(k).start()

            def rest(k, carry):
                out_gradient(2 * k + core)
                return carry

            lax.fori_loop(0, chips, rest, 0)
        else:
            for head in range(heads):
                out_gradient(head)
            for k in range(chips):
                out_copy(k).start()

    def out_pairs():
        for k in range(chips):
            out_copy(k).wait_recv()
            out_pair[k] = (
                out_pair[k].astype(jnp.float32) + grad_out[2 * k + core].astype(jnp.float32)
            ).astype(low)
        for k, other in far_chips:
            out_far_copy(k, other).start()

    lane_part = MODEL_WIDTH // count

    def router_far(k, other):
        return remote(
            router_ref.at[:, pl.ds(pl.multiple_of(other * lane_part, lane_part), lane_part)],
            router_line.at[k - 1], router_sems.at[0, k], router_sems.at[1, k], (other, member),
        )

    def router_near(k, other):
        return remote(
            router_sum.at[0], router_chip.at[k - 1], router_sems.at[2, k], router_sems.at[3, k],
            (place, 2 * other + core),
        )

    def router_last():
        return remote(
            router_sum.at[1], router_pair, router_sems.at[2, 0], router_sems.at[3, 0], (place, partner)
        )

    groups = [(0, heads + 2)]

    def columns_of(group):
        return pl.ds(groups[group][0] * HEAD_SIZE, (groups[group][1] - groups[group][0]) * HEAD_SIZE)

    def col_copy(group, k):
        part = columns_of(group)
        return remote(
            grad_cols.at[:, 2 * k + 1 - core, :, part], col_pair.at[k, :, :, part],
            col_sems.at[group, 0, k], col_sems.at[group, 1, k], (place, partner),
        )

    def col_far_copy(group, k, other):
        part = columns_of(group)
        return remote(
            col_pair.at[other, :, :, part], col_far.at[k - 1, :, :, part],
            col_sems.at[group, 2, k], col_sems.at[group, 3, k], (place, 2 * other + core),
        )

    def z_copy(group, k, other):
        part = columns_of(group)
        return remote(
            col_sums.at[other, :, part], columns_out.at[place, :, part],
            z_sems.at[group, 0, k], z_sems.at[group, 1, k], (other, member),
        )

    def col_gradient(group):
        first, final = groups[group]
        grads = grad_proj[:, first * HEAD_SIZE : final * HEAD_SIZE]
        block_width = planes * shard
        for block in range(count):
            part = dot_tn(normed[:, block * block_width : (block + 1) * block_width], grads)
            grad_cols[block, :, :, first * HEAD_SIZE : final * HEAD_SIZE] = part.astype(low).reshape(
                planes, shard, (final - first) * HEAD_SIZE
            )
        for k in range(chips):
            col_copy(group, k).start()

    def col_pairs(group):
        first, final = groups[group]
        columns = slice(first * HEAD_SIZE, final * HEAD_SIZE)
        for k in range(chips):
            col_copy(group, k).wait_recv()
            col_pair[k, :, :, columns] = (
                col_pair[k, :, :, columns].astype(jnp.float32)
                + grad_cols[:, 2 * k + core, :, columns].astype(jnp.float32)
            ).astype(low)
        for k, other in far_chips:
            col_far_copy(group, k, other).start()

    def col_totals(group):
        first, final = groups[group]
        columns = slice(first * HEAD_SIZE, final * HEAD_SIZE)
        total = col_pair[chip, :, :, columns].astype(jnp.float32)
        for k, other in far_chips:
            col_far_copy(group, k, other).wait_recv()
            total += col_far[k - 1, :, :, columns].astype(jnp.float32)
        col_sums[:, :, columns] = total.astype(low)
        for k, other in far_places:
            z_copy(group, k, other).start()
        columns_out[place, :, columns] = col_sums[place, :, columns]

    grad_raw, gain_part = unprepare(
        grad_pair[0], proj[heads], gain_key, turn_cos_ref[...], turn_sin_ref[...]
    )
    gain_parts[1:2, :] += gain_part
    grad_proj[:, query_columns : query_columns + HEAD_SIZE] = grad_raw.astype(low)
    grad_proj[:, query_columns + HEAD_SIZE :] = grad_pair[1].astype(low)

    def gain_far(k, other):
        return remote(
            gain_own.at[0], gain_line.at[k - 1], gain_sems.at[0, k], gain_sems.at[1, k], (other, member)
        )

    def gain_near(k, other):
        return remote(
            gain_own.at[1], gain_chip.at[k - 1], gain_sems.at[2, k], gain_sems.at[3, k],
            (place, 2 * other + core),
        )

    def gain_last():
        return remote(
            gain_own.at[2], gain_pair, gain_sems.at[2, 0], gain_sems.at[3, 0], (place, partner)
        )

    sums = (count, place, member, normed_part, normed_sums, rs_send, rs_recv)

    def normed_step(step):
        block = ranked_block(count - 1 - step, place, count)
        at = pl.ds(pl.multiple_of(block * tokens, tokens), tokens)
        part = dot_nt(grad_proj[at, :], own_cols[...].reshape(MODEL_WIDTH, width))
        normed_part[block] = part.astype(low)
        if step < count - 1:
            line_sum_step(step, *sums)
        return jnp.sum(part * normed[at, :].astype(jnp.float32), axis=0, keepdims=True)

    if shared:
        out_gradients()
    gain_row = normed_step(0)
    col_gradient(0)
    col_pairs(0)
    for c in range(mixed_done, chunks):
        mixed_chunk(c)
        mixed_wave()
    gain_row += normed_step(1)
    if not shared:
        out_gradients()
    out_pairs()
    for k, other in far_places:
        router_far(k, other).start()
    if waves:
        mixed_wave()
    for step in range(2, count):
        gain_row += normed_step(step)
    gain_row = gain_row / gains_ref[0:1, :]
    for k in range(MODEL_WIDTH // HEAD_SIZE):
        gain_own[0, k : k + 1, :] = gain_row[:, k * HEAD_SIZE : (k + 1) * HEAD_SIZE]
    gain_own[0, MODEL_WIDTH // HEAD_SIZE :, :] = gain_parts[...]
    for k, other in far_places:
        gain_far(k, other).start()
    while waves:
        mixed_wave()
    own_lanes = pl.ds(pl.multiple_of(place * lane_part, lane_part), lane_part)
    total = router_ref[:, own_lanes]
    for k, other in far_places:
        router_far(k, other).wait_recv()
        total += router_line[k - 1]
    router_sum[0] = total
    for k, other in far_chips:
        router_near(k, other).start()
    total = gain_own[0]
    for k, other in far_places:
        gain_far(k, other).wait_recv()
        total += gain_line[k - 1]
    gain_own[1] = total
    for k, other in far_chips:
        gain_near(k, other).start()
    col_totals(0)
    for c in range(chunks):
        line_sum_end(*mixed_line(c), mixed_total.at[:, c * wide : (c + 1) * wide])
    line_sum_end(*sums, grad_input_ref)
    total = out_pair[chip].astype(jnp.float32)
    for k, other in far_chips:
        out_far_copy(k, other).wait_recv()
        total += out_far[k - 1].astype(jnp.float32)
    out_total[...] = total
    total = router_sum[0]
    for k, other in far_chips:
        router_near(k, other).wait_recv()
        total += router_chip[k - 1]
    router_sum[1] = total
    router_last().start()
    total = gain_own[1]
    for k, other in far_chips:
        gain_near(k, other).wait_recv()
        total += gain_chip[k - 1]
    gain_own[2] = total
    gain_last().start()
    gain_last().wait_recv()
    gain_total[...] = gain_own[2] + gain_pair[...]
    router_last().wait_recv()
    router_total[...] = router_sum[1] + router_pair[...]

    hidden = hidden_ref[...].astype(jnp.float32)
    inverse = lax.rsqrt(jnp.mean(hidden * hidden, axis=-1, keepdims=True) + EPSILON)
    unit = hidden * inverse
    grad_normed = grad_input_ref[...]
    turned = grad_normed * gains_ref[0:1, :]
    grad_input_ref[...] = grad_hidden_ref[...] + inverse * (
        turned - unit * jnp.mean(turned * unit, axis=-1, keepdims=True)
    )
    for group in range(len(groups)):
        for k, other in far_places:
            z_copy(group, k, other).wait_recv()
            z_copy(group, k, other).wait_send()
        for part in range(count):
            qkv_total[:, part * query_columns : (part + 1) * query_columns] = columns_out[
                part, :, :query_columns
            ].astype(jnp.float32)
        replicas = count // KEY_VALUE_HEADS
        for head in range(2 * KEY_VALUE_HEADS):
            kind, pair_head = head // KEY_VALUE_HEADS, head % KEY_VALUE_HEADS
            begin = query_columns + kind * HEAD_SIZE
            total = jnp.zeros((shard, HEAD_SIZE), jnp.float32)
            for part in range(pair_head * replicas, (pair_head + 1) * replicas):
                total += columns_out[part, :, begin : begin + HEAD_SIZE].astype(jnp.float32)
            begin = (QUERY_HEADS + head) * HEAD_SIZE
            qkv_total[:, begin : begin + HEAD_SIZE] = total
        for k in range(chips):
            col_copy(group, k).wait_send()
        for k, other in far_chips:
            col_far_copy(group, k, other).wait_send()
    for k in range(chips):
        out_copy(k).wait_send()
    for k, other in far_chips:
        out_far_copy(k, other).wait_send()
        router_near(k, other).wait_send()
        gain_near(k, other).wait_send()
    for k, other in far_places:
        router_far(k, other).wait_send()
        gain_far(k, other).wait_send()
    router_last().wait_send()
    gain_last().wait_send()
    for c in range(chunks):
        for j, other in others:
            mixed_copy(c, j, other).wait_send()


def attention_backward(
    count, planes, heads, shard, capacity, branch, grad_hidden, hidden, gains, router, out_rows, own_cols, normed,
    heads_low, queries, pair, proj, picker, combined, lse, turn_cos, turn_sin,
):
    tokens = branch.shape[0]
    length = count * tokens
    width = (heads + 2) * HEAD_SIZE
    chips = planes // 2
    out_block = heads * HEAD_SIZE // planes
    chunks = 4
    wide = MODEL_WIDTH // chunks
    gain_rows = MODEL_WIDTH // HEAD_SIZE + 8
    router_part = (router.shape[0], MODEL_WIDTH // count)
    low, kind = jnp.bfloat16, jnp.float32
    vmem = pl.BlockSpec(memory_space=pltpu.VMEM)
    anywhere = pl.BlockSpec(memory_space=pl.ANY)
    dma = pltpu.SemaphoreType.DMA
    shape = jax.ShapeDtypeStruct
    most = max(count, chips)
    return pl.pallas_call(
        functools.partial(backward_kernel, count, planes, tokens, heads, shard, capacity),
        out_shape=(
            shape((tokens, MODEL_WIDTH), kind),
            shape((out_block, MODEL_WIDTH), kind),
            shape((shard, (QUERY_HEADS + 2 * KEY_VALUE_HEADS) * HEAD_SIZE), kind),
            shape((tokens, MODEL_WIDTH), kind),
            shape(router_part, kind),
            shape((gain_rows, HEAD_SIZE), kind),
            shape(combined.shape, low),
        ),
        in_specs=[vmem] * 5 + [anywhere] * 9 + [vmem] * 3,
        out_specs=(vmem,) * 6 + (anywhere,),
        scratch_shapes=[
            pltpu.VMEM(out_rows.shape, low),
            pltpu.VMEM(own_cols.shape, low),
            pltpu.VMEM(normed.shape, low),
            pltpu.VMEM(heads_low.shape, low),
            pltpu.VMEM(queries.shape, low),
            pltpu.VMEM(pair.shape, low),
            pltpu.VMEM(proj.shape, kind),
            pltpu.VMEM(picker.shape, low),
            dma((8,)),
            pltpu.VMEM((count, tokens, MODEL_WIDTH), low),
            dma((2, count, 2)),
            dma((2, count, 2)),
            pltpu.VMEM((heads, tokens, HEAD_SIZE), low),
            pltpu.VMEM((length, width), low),
            pltpu.VMEM((2, length, HEAD_SIZE), kind),
            pltpu.VMEM((8, HEAD_SIZE), kind),
            pltpu.VMEM((planes, out_block, MODEL_WIDTH), low),
            pltpu.VMEM((chips, out_block, MODEL_WIDTH), low),
            pltpu.VMEM((chips - 1, out_block, MODEL_WIDTH), low),
            dma((4, chips)),
            pltpu.VMEM((count, planes, shard, width), low),
            pltpu.VMEM((chips, count, shard, width), low),
            pltpu.VMEM((chips - 1, count, shard, width), low),
            pltpu.VMEM((count, shard, width), low),
            pltpu.VMEM((count, shard, width), low),
            dma((2, 4, chips)),
            pltpu.VMEM((count if count <= 4 else 1, tokens, MODEL_WIDTH), low),
            pltpu.VMEM((count + 1, tokens, MODEL_WIDTH), low),
            dma((2, count, 2)),
            dma((2, count, 2)),
            dma((2, 2, count)),
            pltpu.VMEM(combined.shape[:2] + (wide,), low),
            pltpu.VMEM((chunks, count, tokens, wide), low),
            pltpu.VMEM((chunks, count + 1, tokens, wide), low),
            dma((chunks, planes)),
            dma((chunks, planes)),
            dma((2,)),
            dma((chunks, 2, count, 1)),
            dma((chunks, 2, count, 1)),
            pltpu.VMEM((count - 1,) + router_part, kind),
            pltpu.VMEM((2,) + router_part, kind),
            pltpu.VMEM((chips - 1,) + router_part, kind),
            pltpu.VMEM(router_part, kind),
            dma((4, most)),
            pltpu.VMEM((3, gain_rows, HEAD_SIZE), kind),
            pltpu.VMEM((count - 1, gain_rows, HEAD_SIZE), kind),
            pltpu.VMEM((chips - 1, gain_rows, HEAD_SIZE), kind),
            pltpu.VMEM((gain_rows, HEAD_SIZE), kind),
            dma((4, most)),
        ],
        compiler_params=pltpu.CompilerParams(
            collective_id=3, has_side_effects=True, vmem_limit_bytes=VMEM_BYTES
        ),
        name="attention_backward",
    )(
        branch, grad_hidden, hidden, gains, router, out_rows, own_cols, normed, heads_low, queries,
        pair, proj, picker, combined, lse, turn_cos, turn_sin,
    )


def forward_kernel(
    count, planes, tokens, heads, shard, capacity, chunks,
    hidden_ref, routes_ref, gain1_ref, gain2_ref, query_gain_ref, key_gain_ref, router_ref, qkv_ref,
    out_ref, cotangent_ref, turn_cos_ref, turn_sin_ref,
    hidden1_ref, mixed_ref, lse_ref, gains_ref, picker_ref,
    router_out, own_cols_hbm, out_rows_hbm, normed_hbm, heads_hbm, query_hbm, pair_hbm, proj_hbm,
    grad_hbm, masks_hbm,
    column_send, own_cols, c_send, c_recv,
    out_rows, o_send, o_recv,
    hidden_full, h_send, h_recv,
    gains_all, gz_send, gz_recv, gd_send, gd_recv,
    router_all, rz_send, rz_recv, rd_send, rd_recv,
    places_all, p_send, p_recv,
    normed, proj, queries, pair, heads_low,
    grad_full, dy_send, dy_recv,
    grad_sent, d_send, d_recv, mask_sent, m_send, m_recv,
    branch, sums, rs_send, rs_recv, local_sems,
):
    place = lax.axis_index("seq")
    member = lax.axis_index("dp")
    core = lax.rem(member, 2)
    chip = member // 2
    chips = planes // 2
    partner = member + 1 - 2 * core
    length = count * tokens
    query_columns = heads * HEAD_SIZE
    replicas = count // KEY_VALUE_HEADS
    wide = MODEL_WIDTH // chunks
    slots = grad_sent.shape[2]
    rows = planes * slots
    low = jnp.bfloat16
    scale = HEAD_SIZE ** (-0.5)
    far_places = [(k, lax.rem(place + k, count)) for k in range(1, count)]
    far_chips = [(k, lax.rem(chip + k, chips)) for k in range(1, chips)]
    others = [(j, lax.rem(member + j, planes)) for j in range(1, planes)]

    def column_parts():
        for part in range(count):
            head = part // replicas
            keys = QUERY_HEADS * HEAD_SIZE + head * HEAD_SIZE
            values = keys + KEY_VALUE_HEADS * HEAD_SIZE
            column_send[part, :, :query_columns] = qkv_ref[
                :, part * query_columns : (part + 1) * query_columns
            ]
            column_send[part, :, query_columns : query_columns + HEAD_SIZE] = qkv_ref[
                :, keys : keys + HEAD_SIZE
            ]
            column_send[part, :, query_columns + HEAD_SIZE :] = qkv_ref[
                :, values : values + HEAD_SIZE
            ]

    greet(
        [(place, other) for _, other in others] + [(other, member) for _, other in far_places],
        column_parts,
    )

    def column_copy(k, other):
        return remote(
            column_send.at[other], own_cols.at[place, member], c_send.at[0, k], c_recv.at[0, k],
            (other, member),
        )

    def gain_line(k, other):
        mine = gains_all.at[place, member]
        return remote(mine, mine, gz_send.at[k], gz_recv.at[k], (other, member))

    def router_line(k, other):
        mine = router_all.at[place, member]
        return remote(mine, mine, rz_send.at[k], rz_recv.at[k], (other, member))

    def places_line(k, other):
        mine = places_all.at[place]
        return remote(mine, mine, p_send.at[k], p_recv.at[k], (other, member))

    def out_copy(k, other):
        return remote(
            out_ref, out_rows.at[member], o_send.at[0, k], o_recv.at[0, k], (place, 2 * other + core)
        )

    def out_pair(k, other):
        source = out_ref if k == 0 else out_rows.at[2 * other + core]
        return remote(
            source, out_rows.at[2 * other + core], o_send.at[1, k], o_recv.at[1, k], (place, partner)
        )

    def block_copy(k, other):
        mine = own_cols.at[:, member]
        return remote(mine, mine, c_send.at[1, k], c_recv.at[1, k], (place, 2 * other + core))

    def block_pair(k, other):
        block = own_cols.at[:, 2 * other + core]
        return remote(block, block, c_send.at[2, k], c_recv.at[2, k], (place, partner))

    for k, other in far_places:
        column_copy(k, other).start()
    for k, other in far_chips:
        out_copy(k, other).start()
    out_pair(0, chip).start()

    hidden_line = (count, place, member, hidden_full, h_send, h_recv)
    index = place * planes + member
    row_lanes = lax.broadcasted_iota(jnp.int32, (1, HEAD_SIZE), 1)
    pieces = []
    for ref in (gain1_ref, gain2_ref, query_gain_ref, key_gain_ref):
        gain_width = ref.shape[1]
        values = ref[...].astype(jnp.float32)
        begin = lax.rem(index, HEAD_SIZE // gain_width) * gain_width
        piece = jnp.zeros((1, HEAD_SIZE), jnp.float32)
        for k in range(gain_width):
            piece += jnp.where(row_lanes == begin + k, values[:, k : k + 1], 0.0)
        pieces.append(piece)
    pieces.append(jnp.zeros((gains_all.shape[2] - 4, HEAD_SIZE), jnp.float32))
    gains_all[place, member] = jnp.concatenate(pieces, axis=0).astype(low)
    for k, other in far_places:
        gain_line(k, other).start()
    hidden_full[place] = hidden_ref[...]
    line_gather_step(0, *hidden_line)
    router_all[place, member] = jnp.zeros(router_all.shape[2:], low)
    router_all[place, member, :, : router_ref.shape[0]] = jnp.transpose(
        router_ref[...].astype(jnp.float32)
    ).astype(low)
    lanes = lax.broadcasted_iota(jnp.int32, (tokens, places_all.shape[-1]), 1)
    named = jnp.zeros(lanes.shape, jnp.float32)
    chosen = jnp.transpose(routes_ref[...].astype(jnp.float32))
    for k in range(TOP):
        named += jnp.where(chosen[:, k : k + 1] == lanes.astype(jnp.float32), 1.0, 0.0)
    row_ids = lax.broadcasted_iota(jnp.int32, (tokens, tokens), 0)
    col_ids = lax.broadcasted_iota(jnp.int32, (tokens, tokens), 1)
    before = jnp.where(row_ids > col_ids, 1.0, 0.0).astype(low)
    earlier = dot_nn(before, named.astype(low))
    places_all[place] = jnp.where(named > 0, earlier, -512.0).astype(low)
    for c in range(chunks):
        grad_full[c, place] = cotangent_ref[:, c * wide : (c + 1) * wide]
    for k, other in far_places:
        places_line(k, other).start()
        router_line(k, other).start()
    own_cols[place, member] = column_send[place]
    out_rows[member] = out_ref[...]

    def gain_plane(j, other):
        mine = gains_all.at[:, member]
        return remote(mine, mine, gd_send.at[j], gd_recv.at[j], (place, other))

    def router_plane(j, other):
        mine = router_all.at[:, member]
        return remote(mine, mine, rd_send.at[j], rd_recv.at[j], (place, other))

    for k, other in far_places:
        gain_line(k, other).wait_recv()
    for j, other in others:
        gain_plane(j, other).start()
    for k, other in far_places:
        column_copy(k, other).wait_recv()
    for k, other in far_chips:
        block_copy(k, other).start()
    block_pair(0, chip).start()
    line_gather_step(1, *hidden_line)

    for k, other in far_places:
        places_line(k, other).wait_recv()
    experts = places_all.shape[-1]
    pick_rows = lax.broadcasted_iota(jnp.int32, (rows, experts), 0)
    pick_experts = lax.broadcasted_iota(jnp.int32, (rows, experts), 1) - place * planes
    slot_ids = lax.broadcasted_iota(jnp.int32, (rows, length), 0)
    token_ids = lax.broadcasted_iota(jnp.int32, (rows, length), 1)
    offsets = jnp.zeros((rows, length), jnp.int32)
    choose = jnp.zeros((rows, experts), jnp.float32)
    for other in range(planes):
        inside = (pick_rows >= other * slots) & (pick_rows < (other + 1) * slots)
        choose += jnp.where(inside & (pick_experts == other), 1.0, 0.0)
        offsets = jnp.where(slot_ids >= other * slots, other * slots, offsets)
    before_block = jnp.zeros((rows, length), jnp.int32)
    for block in range(count):
        before_block = jnp.where(
            token_ids >= block * tokens, block_rank(block, place, count) * capacity, before_block
        )
    wanted = dot_nt(choose.astype(low), places_all[...].reshape(length, experts))
    picker_rows = jnp.where(
        wanted == (slot_ids - offsets - before_block).astype(jnp.float32), 1.0, 0.0
    ).astype(low)
    picker_ref[...] = picker_rows.reshape(planes, slots, length)
    mask_full = jnp.where(places_all[...].reshape(length, experts).astype(jnp.float32) >= 0, 1.0, 0.0)
    mask_sent[...] = (
        dot_nn(picker_rows, mask_full.astype(low)).astype(low).reshape(mask_sent.shape)
    )

    for k, other in far_places:
        router_line(k, other).wait_recv()
    for j, other in others:
        router_plane(j, other).start()

    def mask_copy(j, other):
        return remote(
            mask_sent.at[other], masks_hbm.at[member], m_send.at[j], m_recv.at[j], (place, other)
        )

    for j, other in others:
        mask_copy(j, other).start()
    masks_own = pltpu.make_async_copy(mask_sent.at[member], masks_hbm.at[member], local_sems.at[0])
    masks_own.start()

    for step in range(2, count - 1):
        line_gather_step(step, *hidden_line)

    def grad_line(c):
        return (count, place, member, grad_full.at[c], dy_send.at[c], dy_recv.at[c])

    def grad_copy(c, j, other):
        return remote(
            grad_sent.at[c, other], grad_hbm.at[c, member], d_send.at[c, j], d_recv.at[c, j], (place, other)
        )

    def grad_own(c):
        return pltpu.make_async_copy(
            grad_sent.at[c, member], grad_hbm.at[c, member], local_sems.at[16 + c]
        )

    def grad_tick(tick):
        for c in range(chunks):
            step = tick - c
            if 0 <= step < count:
                line_gather_step(step, *grad_line(c))
            if step == count - 1:
                picked = dot_nn(
                    picker_ref[...].reshape(rows, length), grad_full[c].reshape(length, wide)
                ).astype(low)
                grad_sent[c] = picked.reshape(planes, slots, wide)
                for j, other in others:
                    grad_copy(c, j, other).start()
                grad_own(c).start()

    ticks = list(range(chunks + count - 1))
    grad_tick(ticks.pop(0))
    line_gather_step(count - 1, *hidden_line)

    for j, other in others:
        gain_plane(j, other).wait_recv()
    per_row = HEAD_SIZE // shard
    small_total = jnp.sum(gains_all[...].astype(jnp.float32), axis=(0, 1))
    gain_rows = []
    for row in range(2):
        parts = []
        for group in range(MODEL_WIDTH // HEAD_SIZE):
            part = jnp.zeros((1, HEAD_SIZE), jnp.float32)
            for index in range(group * per_row, (group + 1) * per_row):
                part += gains_all[index // planes, index % planes, row : row + 1, :].astype(jnp.float32)
            parts.append(part)
        gain_rows.append(jnp.concatenate(parts, axis=1))
    gains_ref[0:1, :] = gain_rows[0]
    gains_ref[1:2, :] = gain_rows[1]
    gain_query = small_total[2:3, :]
    gain_key = small_total[3:4, :]
    gains_ref[2:3, :HEAD_SIZE] = gain_query
    gains_ref[3:4, :HEAD_SIZE] = gain_key

    def normalize(values, gain):
        return (
            values
            * lax.rsqrt(jnp.mean(values * values, axis=-1, keepdims=True) + EPSILON)
            * gain
        )

    for block in range(count):
        values = hidden_full[block].astype(jnp.float32)
        normed[block * tokens : (block + 1) * tokens, :] = normalize(values, gain_rows[0]).astype(low)
    stores = [pltpu.make_async_copy(normed, normed_hbm, local_sems.at[1])]
    stores[-1].start()

    for k, other in far_chips:
        block_copy(k, other).wait_recv()
    for k, other in far_chips:
        block_pair(k, lax.rem(chip + chips - k, chips)).start()
    for k, other in far_chips:
        out_copy(k, other).wait_recv()
    for k, other in far_chips:
        out_pair(k, lax.rem(chip + chips - k, chips)).start()
    block_pair(0, chip).wait_recv()
    for k, other in far_chips:
        block_pair(k, lax.rem(chip + chips - k, chips)).wait_recv()
    weights = own_cols[...].reshape(MODEL_WIDTH, query_columns + 2 * HEAD_SIZE)
    stores.append(pltpu.make_async_copy(own_cols, own_cols_hbm, local_sems.at[2]))
    stores[-1].start()

    def prepare(values, gain):
        turned = normalize(values, gain)
        return turned * turn_cos_ref[...] + pltpu.roll(turned, HEAD_SIZE // 2, 1) * turn_sin_ref[...]

    paired = dot_nn(normed[...], weights[:, query_columns:])
    proj[heads] = paired[:, :HEAD_SIZE]
    proj[heads + 1] = paired[:, HEAD_SIZE:]
    pair[0] = prepare(paired[:, :HEAD_SIZE], gain_key).astype(low)
    pair[1] = paired[:, HEAD_SIZE:].astype(low)
    projected = dot_nn(normed[...], weights[:, :query_columns])
    for head in range(heads):
        proj[head] = projected[:, head * HEAD_SIZE : (head + 1) * HEAD_SIZE]
    value_turned = jnp.transpose(paired[:, HEAD_SIZE:]).astype(low)
    stores.append(pltpu.make_async_copy(proj, proj_hbm, local_sems.at[3]))
    stores[-1].start()
    stores.append(pltpu.make_async_copy(pair, pair_hbm, local_sems.at[4]))
    stores[-1].start()
    together = min(max(1, 2048 // length), heads)

    def some_heads(index, carry):
        first = index * together
        some = pl.ds(first, together)
        for k in range(together):
            queries[first + k] = prepare(proj[first + k], gain_query).astype(low)
        for block in range(count):
            begin, end = block * tokens, (block + 1) * tokens
            query = queries[some, begin:end, :].reshape(together * tokens, HEAD_SIZE)
            scores = dot_nt(pair[0, :end, :], query) * scale
            shape = (end, together * tokens)
            key_ids = lax.broadcasted_iota(jnp.int32, shape, 0) - begin
            query_ids = lax.rem(lax.broadcasted_iota(jnp.int32, shape, 1), tokens)
            scores = jnp.where(key_ids <= query_ids, scores, FILLER)
            top = jnp.max(scores, axis=0, keepdims=True)
            powers = jnp.exp(scores - top)
            total = jnp.sum(powers, axis=0, keepdims=True)
            lse = top + jnp.log(total)
            for k in range(together):
                lse_ref[first + k, :, begin:end] = lse[:, k * tokens : (k + 1) * tokens]
            probs = (powers * (1.0 / total)).astype(low)
            mixed = dot_nn(value_turned[:, :end], probs)
            heads_low[some, begin:end, :] = (
                jnp.transpose(mixed).astype(low).reshape(together, tokens, HEAD_SIZE)
            )
        return carry

    for part in range(heads // together):
        some_heads(part, 0)
        for _ in range(4 * together // heads):
            if ticks:
                grad_tick(ticks.pop(0))
    stores.append(pltpu.make_async_copy(queries, query_hbm, local_sems.at[5]))
    stores[-1].start()
    stores.append(pltpu.make_async_copy(heads_low, heads_hbm, local_sems.at[6]))
    stores[-1].start()

    out_pair(0, chip).wait_recv()
    for k, other in far_chips:
        out_pair(k, lax.rem(chip + chips - k, chips)).wait_recv()
    out_all = out_rows[...].reshape(query_columns, MODEL_WIDTH)
    stores.append(pltpu.make_async_copy(out_rows, out_rows_hbm, local_sems.at[7]))
    stores[-1].start()

    def project(block, carry):
        at = pl.ds(pl.multiple_of(block * tokens, tokens), tokens)
        mixed = jnp.concatenate([heads_low[head, at, :] for head in range(heads)], axis=1)
        branch[block] = dot_nn(mixed, out_all).astype(low)
        return carry

    lax.fori_loop(0, count, project, 0)
    line = (count, place, member, branch, sums, rs_send, rs_recv)
    for step in range(count - 1):
        line_sum_step(step, *line)
        for _ in range(-(-len(ticks) // (count - 1 - step))):
            grad_tick(ticks.pop(0))
    line_sum_end(*line, hidden1_ref)
    hidden1 = hidden_ref[...].astype(jnp.float32) + hidden1_ref[...]
    hidden1_ref[...] = hidden1
    mixed_ref[...] = normalize(hidden1, gain_rows[1]).astype(low)

    for j, other in others:
        router_plane(j, other).wait_recv()
    router_out[...] = router_all[...].reshape(router_out.shape)
    for j, other in others:
        mask_copy(j, other).wait_recv()
        for c in range(chunks):
            grad_copy(c, j, other).wait_recv()
    for k, other in far_places:
        gain_line(k, other).wait_send()
        column_copy(k, other).wait_send()
        places_line(k, other).wait_send()
        router_line(k, other).wait_send()
    for k, other in far_chips:
        out_copy(k, other).wait_send()
        block_copy(k, other).wait_send()
        out_pair(k, other).wait_send()
        block_pair(k, other).wait_send()
    out_pair(0, chip).wait_send()
    block_pair(0, chip).wait_send()
    for j, other in others:
        gain_plane(j, other).wait_send()
        router_plane(j, other).wait_send()
        mask_copy(j, other).wait_send()
        for c in range(chunks):
            grad_copy(c, j, other).wait_send()
    for c in range(chunks):
        grad_own(c).wait()
        line_gather_end(*grad_line(c))
    line_gather_end(*hidden_line)
    masks_own.wait()
    for store in stores:
        store.wait()


def attention_forward(
    count, planes, heads, shard, capacity, slots, chunks,
    hidden, routes, gain_one, gain_two, query_gain, key_gain, router, qkv, out_weight, cotangent,
    turn_cos, turn_sin,
):
    tokens = hidden.shape[0]
    length = count * tokens
    width = (heads + 2) * HEAD_SIZE
    chips = planes // 2
    wide = MODEL_WIDTH // chunks
    experts = -(-router.shape[0] // 128) * 128
    small_rows = 16
    out_block = out_weight.shape[0]
    low, full = jnp.bfloat16, jnp.float32
    vmem = pl.BlockSpec(memory_space=pltpu.VMEM)
    anywhere = pl.BlockSpec(memory_space=pl.ANY)
    dma = pltpu.SemaphoreType.DMA
    shape = jax.ShapeDtypeStruct
    return pl.pallas_call(
        functools.partial(forward_kernel, count, planes, tokens, heads, shard, capacity, chunks),
        out_shape=(
            shape((tokens, MODEL_WIDTH), full),
            shape((tokens, MODEL_WIDTH), low),
            shape((heads, 1, length), full),
            shape((8, MODEL_WIDTH), full),
            shape((planes, slots, length), low),
            shape((MODEL_WIDTH, experts), low),
            shape((count, planes, shard, width), low),
            shape((planes, out_block, MODEL_WIDTH), low),
            shape((length, MODEL_WIDTH), low),
            shape((heads, length, HEAD_SIZE), low),
            shape((heads, length, HEAD_SIZE), low),
            shape((2, length, HEAD_SIZE), low),
            shape((heads + 2, length, HEAD_SIZE), full),
            shape((chunks, planes, slots, wide), low),
            shape((planes, slots, experts), low),
        ),
        in_specs=[vmem] * 12,
        out_specs=(vmem,) * 6 + (anywhere,) * 9,
        scratch_shapes=[
            pltpu.VMEM((count, shard, width), low),
            pltpu.VMEM((count, planes, shard, width), low),
            dma((3, max(count, chips))),
            dma((3, max(count, chips))),
            pltpu.VMEM((planes, out_block, MODEL_WIDTH), low),
            dma((2, chips)),
            dma((2, chips)),
            pltpu.VMEM((count, tokens, MODEL_WIDTH), low),
            dma((2, count, 2)),
            dma((2, count, 2)),
            pltpu.VMEM((count, planes, small_rows, HEAD_SIZE), low),
            dma((count,)),
            dma((count,)),
            dma((planes,)),
            dma((planes,)),
            pltpu.VMEM((count, planes, shard, experts), low),
            dma((count,)),
            dma((count,)),
            dma((planes,)),
            dma((planes,)),
            pltpu.VMEM((count, tokens, experts), low),
            dma((count,)),
            dma((count,)),
            pltpu.VMEM((length, MODEL_WIDTH), low),
            pltpu.VMEM((heads + 2, length, HEAD_SIZE), full),
            pltpu.VMEM((heads, length, HEAD_SIZE), low),
            pltpu.VMEM((2, length, HEAD_SIZE), low),
            pltpu.VMEM((heads, length, HEAD_SIZE), low),
            pltpu.VMEM((chunks, count, tokens, wide), low),
            dma((chunks, 2, count, 1)),
            dma((chunks, 2, count, 1)),
            pltpu.VMEM((chunks, planes, slots, wide), low),
            dma((chunks, planes)),
            dma((chunks, planes)),
            pltpu.VMEM((planes, slots, experts), low),
            dma((planes,)),
            dma((planes,)),
            pltpu.VMEM((count, tokens, MODEL_WIDTH), low),
            pltpu.VMEM((count + 1, tokens, MODEL_WIDTH), low),
            dma((2, count, 2)),
            dma((2, count, 2)),
            dma((16 + chunks,)),
        ],
        compiler_params=pltpu.CompilerParams(
            collective_id=1, has_side_effects=True, vmem_limit_bytes=VMEM_BYTES
        ),
        name="attention_forward",
    )(
        hidden, routes, gain_one, gain_two, query_gain, key_gain, router, qkv, out_weight, cotangent,
        turn_cos, turn_sin,
    )


def segments(slots):
    step = max(16, slots // 4 // 16 * 16)
    starts = [step * k for k in range(slots // step)]
    return list(zip(starts, starts[1:] + [slots]))


def ranked_block(rank, place, count):
    short = jnp.minimum(place, count - 1 - place)
    near = (rank + 1) // 2
    side = -1 if rank % 2 else 1
    far = rank - short
    far_side = jnp.where(place < count - 1 - place, 1, -1)
    return jnp.where(rank <= 2 * short, place + side * near, place + far_side * far)


def block_rank(block, place, count):
    short = jnp.minimum(place, count - 1 - place)
    away = jnp.abs(block - place)
    near = 2 * away - jnp.where(block < place, 1, 0)
    return jnp.where(away <= short, near, short + away)


def expert_kernel(
    count, planes, tokens, capacity, chunks,
    mixed_ref, hidden1_ref, cotangent_ref, gains_ref, routes_ref, masks_ref,
    picker_hbm, grad_hbm, router_hbm, in_hbm, back_hbm,
    grad_hidden_ref, branch_ref, router_ref, grad_in_hbm, grad_back_hbm, combined_hbm,
    picker, grad_rows, router, weight_in, weight_back, local_sems,
    full, ag_send, ag_recv,
    sent, arrived, x_send, x_recv,
    gate_up, act, grad_gate_up, gate_rows,
    back_arrived, b_send, b_recv,
    gate_sent, gate_arrived, gate_own, gate_sums, gate_total, g_send, g_recv, gs_send, gs_recv,
    sums, rs_send, rs_recv, in_tiles, back_tile, tile_sems,
):
    place = lax.axis_index("seq")
    member = lax.axis_index("dp")
    slots = sent.shape[1]
    rows = planes * slots
    length = count * tokens
    wide = MODEL_WIDTH // chunks
    own_expert = place * planes + member
    experts = count * planes
    lanes = router.shape[-1]
    extra = gate_sent.shape[-1]
    low = jnp.bfloat16
    pieces = segments(slots)
    others = [(j, lax.rem(member + j, planes)) for j in range(1, planes)]

    loads = [
        pltpu.make_async_copy(picker_hbm, picker, local_sems.at[0]),
        pltpu.make_async_copy(in_hbm, weight_in, local_sems.at[1]),
        pltpu.make_async_copy(router_hbm, router, local_sems.at[2]),
        pltpu.make_async_copy(back_hbm, weight_back, local_sems.at[3]),
    ] + [
        pltpu.make_async_copy(
            grad_hbm.at[c], grad_rows.at[:, :, pl.ds(c * wide, wide)], local_sems.at[4 + c]
        )
        for c in range(chunks)
    ]
    for load in loads:
        load.start()
    full[place] = mixed_ref[...]
    greet([(place, other) for _, other in others] + [(lax.rem(place + k, count), member) for k in range(1, count)])

    line = (count, place, member, full, ag_send, ag_recv)

    def row_copy(i, j, other):
        low_row, high_row = pieces[i]
        part = pl.ds(low_row, high_row - low_row)
        return remote(
            sent.at[other, part], arrived.at[member, part], x_send.at[i, j], x_recv.at[i, j], (place, other)
        )

    def back_copy(i, j, other):
        low_row, high_row = pieces[i]
        part = pl.ds(low_row, high_row - low_row)
        return remote(
            sent.at[other, part], back_arrived.at[member, part], b_send.at[i, j], b_recv.at[i, j],
            (place, other),
        )

    def lanes_of(block):
        return pl.ds(pl.multiple_of(block * tokens, tokens), tokens)

    line_gather_step(0, *line)
    loads[0].wait()
    done = 0
    for i, (begin, end) in enumerate(pieces):
        needed = count - 1 if i == len(pieces) - 1 else min((end - 1) // capacity, count - 1)
        while done < needed:
            done += 1
            line_gather_step(done, *line)
        height = planes * (end - begin)
        picked = jnp.zeros((height, MODEL_WIDTH), jnp.float32)
        for rank in range(begin // capacity, min((end - 1) // capacity, count - 1) + 1):
            block = ranked_block(rank, place, count)
            choice = picker[:, begin:end, lanes_of(block)].reshape(height, tokens)
            picked += dot_nn(choice, full[block])
        sent[:, begin:end, :] = picked.astype(low).reshape(planes, end - begin, MODEL_WIDTH)
        for j, other in others:
            row_copy(i, j, other).start()
        arrived[member, begin:end, :] = sent[member, begin:end, :]
    for load in loads[1:]:
        load.wait()

    own_lanes = lax.broadcasted_iota(jnp.int32, (tokens, lanes), 1)
    named = jnp.zeros((tokens, lanes), jnp.float32)
    chosen = jnp.transpose(routes_ref[...].astype(jnp.float32))
    for k in range(TOP):
        named += jnp.where(chosen[:, k : k + 1] == own_lanes.astype(jnp.float32), 1.0, 0.0)

    def masked_gates(scores, mask):
        shifted = jnp.where(mask > 0, scores, FILLER)
        powers = jnp.where(mask > 0, jnp.exp(shifted - jnp.max(shifted, axis=-1, keepdims=True)), 0.0)
        total = jnp.sum(powers, axis=-1, keepdims=True)
        return powers / jnp.where(total > 0, total, 1.0)

    own_gates = masked_gates(dot_nn(mixed_ref[...], router[...]), named)

    def work(i):
        begin, end = pieces[i]
        height = planes * (end - begin)
        x = arrived[:, begin:end, :].reshape(height, MODEL_WIDTH)
        gate_up[:height, :] = dot_nn(x, weight_in[...])
        mask = masks_ref[:, begin:end, :].reshape(height, lanes).astype(jnp.float32)
        gates = masked_gates(dot_nn(x, router[...]), mask)
        lane_ids = lax.broadcasted_iota(jnp.int32, (height, lanes), 1)
        gate = jnp.sum(jnp.where(lane_ids == own_expert, gates, 0.0), axis=-1, keepdims=True)
        gate_rows[:, begin:end, :] = jnp.broadcast_to(gate, (height, HEAD_SIZE)).reshape(
            planes, end - begin, HEAD_SIZE
        )
        grads = grad_rows[:, begin:end, :].reshape(height, MODEL_WIDTH).astype(jnp.float32)
        grad_act = dot_nt((grads * gate).astype(low), weight_back[...])
        gate_part = gate_up[:height, :FF]
        up_part = gate_up[:height, FF:]
        chance = jax.nn.sigmoid(gate_part)
        silu = gate_part * chance
        act[:, begin:end, :] = (silu * up_part).astype(low).reshape(planes, end - begin, FF)
        slope = chance + silu * (1.0 - chance)
        grad_gate = (grad_act * up_part * slope).astype(low)
        grad_up = (grad_act * silu).astype(low)
        grad_gate_up[:, begin:end, :FF] = grad_gate.reshape(planes, end - begin, FF)
        grad_gate_up[:, begin:end, FF:] = grad_up.reshape(planes, end - begin, FF)
        for j, other in others:
            row_copy(i, j, other).wait_send()
        back = jnp.concatenate([grad_gate, grad_up], axis=1)
        for c in range(chunks):
            columns = slice(c * wide, (c + 1) * wide)
            sent[:, begin:end, columns] = (
                dot_nt(back, weight_in[columns, :]).astype(low).reshape(planes, end - begin, wide)
            )
        back_arrived[member, begin:end, :] = sent[member, begin:end, :]

    def send_back(i):
        for j, other in others:
            back_copy(i, j, other).start()

    last = len(pieces) - 1
    for i in range(last):
        for j, other in others:
            row_copy(i, j, other).wait_recv()
        work(i)
    for j, other in others:
        row_copy(last, j, other).wait_recv()
    send_back(last - 1)
    work(last)
    send_back(last)
    line_gather_end(*line)

    tile = in_tiles.shape[1]

    def in_copy(slot, index):
        return pltpu.make_async_copy(
            in_tiles.at[slot],
            grad_in_hbm.at[pl.ds(pl.multiple_of(index * tile, tile), tile), pl.ds(slot * FF, FF)],
            tile_sems.at[slot],
        )

    def in_gradient(index, carry):
        x = arrived[:, :, pl.ds(pl.multiple_of(index * tile, tile), tile)].reshape(rows, tile)
        for slot in range(2):

            @pl.when(index > 0)
            def _():
                in_copy(slot, index).wait()

            grads = grad_gate_up[:, :, slot * FF : (slot + 1) * FF].reshape(rows, FF)
            in_tiles[slot] = dot_tn(x, grads).astype(low)
            in_copy(slot, index).start()
        return carry

    def outputs(c, grad_gate):
        columns = pl.ds(pl.multiple_of(c * wide, wide), wide)
        result = dot_nn(act[...].reshape(rows, FF), weight_back[:, columns])
        result = result.astype(low).astype(jnp.float32)
        grads = grad_rows[:, :, columns].reshape(rows, wide).astype(jnp.float32)
        scale = gate_rows[...].reshape(rows, HEAD_SIZE)[:, 0:1]
        grad_rows[:, :, columns] = (grads * scale).astype(low).reshape(planes, slots, wide)
        arrived[:, :, columns] = (result * scale).astype(low).reshape(planes, slots, wide)
        return grad_gate + jnp.sum(result * grads, axis=-1, keepdims=True)

    def gate_copy(j, other):
        return remote(
            gate_sent.at[other], gate_arrived.at[member], g_send.at[j], g_recv.at[j], (place, other)
        )

    def back_tile_copy(index):
        return pltpu.make_async_copy(
            back_tile,
            grad_back_hbm.at[:, pl.ds(pl.multiple_of(index * tile, tile), tile)],
            tile_sems.at[2],
        )

    def back_gradient(index, carry):
        grads = grad_rows[:, :, pl.ds(pl.multiple_of(index * tile, tile), tile)].reshape(rows, tile)
        result = dot_tn(act[...].reshape(rows, FF), grads)

        @pl.when(index > 0)
        def _():
            back_tile_copy(index).wait()

        back_tile[...] = result.astype(low)
        back_tile_copy(index).start()
        return carry

    tiles = MODEL_WIDTH // tile
    lax.fori_loop(0, tiles, in_gradient, 0)
    grad_gate = lax.fori_loop(0, chunks, outputs, jnp.zeros((rows, 1), jnp.float32))
    combined = pltpu.make_async_copy(arrived, combined_hbm, tile_sems.at[3])
    combined.start()
    high = grad_gate.astype(low).astype(jnp.float32)
    rest = grad_gate - high
    wide_lanes = lax.broadcasted_iota(jnp.int32, (rows, extra), 1)
    columns = jnp.where(
        wide_lanes == own_expert, high, jnp.where(wide_lanes == own_expert + experts, rest, 0.0)
    )
    gate_sent[...] = columns.astype(low).reshape(gate_sent.shape)
    for j, other in others:
        gate_copy(j, other).start()
    gate_arrived[member] = gate_sent[member]
    for i in range(last - 2, -1, -1):
        send_back(i)
    lax.fori_loop(0, tiles, back_gradient, 0)

    for j, other in others:
        gate_copy(j, other).wait_recv()
    gate_own[...] = (
        dot_tn(picker[...].reshape(rows, length), gate_arrived[...].reshape(rows, extra))
        .astype(low)
        .reshape(count, tokens, extra)
    )
    gate_line = (count, place, member, gate_own, gate_sums, gs_send, gs_recv)
    sums_line = (count, place, member, full, sums, rs_send, rs_recv)
    come = set()
    for step in range(count):
        rank = count - 1 - step
        first = rank * capacity // 16 * 16
        final = min(-(-(rank + 1) * capacity // 16) * 16, slots)
        for i in range(last, -1, -1):
            begin, end = pieces[i]
            if i not in come and begin < final and end > first:
                come.add(i)
                for j, other in others:
                    back_copy(i, j, other).wait_recv()
        block = ranked_block(rank, place, count)
        height = planes * (final - first)
        choice = picker[:, first:final, lanes_of(block)].reshape(height, tokens)
        full[block] = dot_tn(
            choice, back_arrived[:, first:final, :].reshape(height, MODEL_WIDTH)
        ).astype(low)
        if step < count - 1:
            line_sum_step(step, *gate_line)
            line_sum_step(step, *sums_line)
    for i in range(len(pieces)):
        if i not in come:
            for j, other in others:
                back_copy(i, j, other).wait_recv()
    line_sum_end(*gate_line, gate_total)
    line_sum_end(*sums_line, grad_hidden_ref)

    if experts % 128 == 0:
        grad_gates = gate_total[:, :experts] + gate_total[:, experts:]
    else:
        grad_gates = gate_total[...] + pltpu.roll(gate_total[...], extra - experts, 1)
    middle = jnp.sum(own_gates * grad_gates, axis=-1, keepdims=True)
    grad_logits = (own_gates * (grad_gates - middle)).astype(low)
    grad_mixed = grad_hidden_ref[...] + dot_nt(grad_logits, router[...])
    router_ref[:experts, :] = dot_tn(grad_logits, mixed_ref[...])[:experts]
    hidden = hidden1_ref[...]
    inverse = lax.rsqrt(jnp.mean(hidden * hidden, axis=-1, keepdims=True) + EPSILON)
    unit = hidden * inverse
    router_ref[experts:, :] = jnp.broadcast_to(
        jnp.sum(grad_mixed * unit, axis=0, keepdims=True), (8, MODEL_WIDTH)
    )
    turned = grad_mixed * gains_ref[1:2, :]
    grad_norm = inverse * (turned - unit * jnp.mean(turned * unit, axis=-1, keepdims=True))
    grad_hidden = cotangent_ref[...].astype(jnp.float32) + grad_norm
    grad_hidden_ref[...] = grad_hidden
    branch_ref[...] = grad_hidden.astype(low)

    for j, other in others:
        for i in range(len(pieces)):
            back_copy(i, j, other).wait_send()
        gate_copy(j, other).wait_send()
    in_copy(0, 0).wait()
    in_copy(1, 0).wait()
    back_tile_copy(0).wait()
    combined.wait()


def expert_layer(
    count, planes, capacity, mixed, hidden1, cotangent, gains, routes, masks, picker, grad_rows,
    router, weight_in, weight_back,
):
    tokens = mixed.shape[0]
    chunks, _, slots, wide = grad_rows.shape
    rows = planes * slots
    extra = -(-2 * count * planes // 128) * 128
    lanes = router.shape[-1]
    height = planes * max(end - begin for begin, end in segments(slots))
    tile = 256 if rows < 1280 else 128
    pieces = len(segments(slots))
    low, kind = jnp.bfloat16, jnp.float32
    vmem = pl.BlockSpec(memory_space=pltpu.VMEM)
    anywhere = pl.BlockSpec(memory_space=pl.ANY)
    dma = pltpu.SemaphoreType.DMA
    shape = jax.ShapeDtypeStruct
    blocks = (planes, slots, MODEL_WIDTH)
    return pl.pallas_call(
        functools.partial(expert_kernel, count, planes, tokens, capacity, chunks),
        out_shape=(
            shape((tokens, MODEL_WIDTH), kind),
            shape((tokens, MODEL_WIDTH), low),
            shape((count * planes + 8, MODEL_WIDTH), kind),
            shape(weight_in.shape, low),
            shape(weight_back.shape, low),
            shape(blocks, low),
        ),
        in_specs=[vmem] * 6 + [anywhere] * 5,
        out_specs=(vmem,) * 3 + (anywhere,) * 3,
        scratch_shapes=[
            pltpu.VMEM(picker.shape, low),
            pltpu.VMEM(blocks, low),
            pltpu.VMEM(router.shape, low),
            pltpu.VMEM(weight_in.shape, low),
            pltpu.VMEM(weight_back.shape, low),
            dma((4 + chunks,)),
            pltpu.VMEM((count, tokens, MODEL_WIDTH), low),
            dma((2, count, 2)),
            dma((2, count, 2)),
            pltpu.VMEM(blocks, low),
            pltpu.VMEM(blocks, low),
            dma((pieces, planes)),
            dma((pieces, planes)),
            pltpu.VMEM((height, 2 * FF), kind),
            pltpu.VMEM((planes, slots, FF), low),
            pltpu.VMEM((planes, slots, 2 * FF), low),
            pltpu.VMEM((planes, slots, HEAD_SIZE), kind),
            pltpu.VMEM(blocks, low),
            dma((pieces, planes)),
            dma((pieces, planes)),
            pltpu.VMEM((planes, slots, extra), low),
            pltpu.VMEM((planes, slots, extra), low),
            pltpu.VMEM((count, tokens, extra), low),
            pltpu.VMEM((count + 1, tokens, extra), low),
            pltpu.VMEM((tokens, extra), kind),
            dma((planes,)),
            dma((planes,)),
            dma((2, count, 1)),
            dma((2, count, 1)),
            pltpu.VMEM((count + 1, tokens, MODEL_WIDTH), low),
            dma((2, count, 2)),
            dma((2, count, 2)),
            pltpu.VMEM((2, tile, FF), low),
            pltpu.VMEM((FF, tile), low),
            dma((4,)),
        ],
        compiler_params=pltpu.CompilerParams(
            collective_id=2, has_side_effects=True, vmem_limit_bytes=VMEM_BYTES
        ),
        name="expert_layer",
    )(
        mixed, hidden1, cotangent, gains, routes, masks, picker, grad_rows, router, weight_in,
        weight_back,
    )


def finish_kernel(
    in_ref, back_ref, hidden_ref, mixed_ref, input_ref, out_ref, qkv_ref,
    in_full, back_full, output, input_full, out_full, qkv_full,
):
    in_full[...] = in_ref[...].astype(jnp.float32)
    back_full[...] = back_ref[...].astype(jnp.float32)
    output[...] = (hidden_ref[...] + mixed_ref[...]).astype(jnp.bfloat16)
    input_full[...] = input_ref[...]
    out_full[...] = out_ref[...]
    qkv_full[...] = qkv_ref[...]


def finish(grad_in, grad_back, hidden1, mixed, grad_input, shard_out, shard_qkv):
    steps = 8
    arrays = (grad_in, grad_back, hidden1, mixed, grad_input, shard_out, shard_qkv)

    def by_rows(array):
        return pl.BlockSpec((array.shape[0] // steps, array.shape[1]), lambda i: (i, 0))

    def by_columns(array):
        return pl.BlockSpec((array.shape[0], array.shape[1] // steps), lambda i: (0, i))

    specs = [by_rows(array) for array in arrays[:5]] + [by_columns(array) for array in arrays[5:]]
    results = (grad_in, grad_back, hidden1, grad_input, shard_out, shard_qkv)
    kinds = (jnp.float32, jnp.float32, jnp.bfloat16) + (jnp.float32,) * 3
    return pl.pallas_call(
        finish_kernel,
        grid=(steps,),
        out_shape=tuple(jax.ShapeDtypeStruct(a.shape, k) for a, k in zip(results, kinds)),
        in_specs=specs,
        out_specs=tuple([specs[0], specs[1], specs[2], specs[4], specs[5], specs[6]]),
        compiler_params=pltpu.CompilerParams(vmem_limit_bytes=VMEM_BYTES),
        name="finish",
    )(*arrays)


def turn_tables(length):
    half = HEAD_SIZE // 2
    freqs = np.float32(ROPE_BASE) ** (-(np.arange(half, dtype=np.float32) * np.float32(2 / HEAD_SIZE)))
    angles = np.arange(length, dtype=np.float32)[:, None] * freqs[None, :]
    cosine, sine = np.cos(angles), np.sin(angles)
    return (
        jnp.asarray(np.concatenate([cosine, cosine], axis=1), jnp.float32),
        jnp.asarray(np.concatenate([-sine, sine], axis=1), jnp.float32),
    )


def body(
    hidden_in,
    routes,
    norm1_gain,
    query_gain,
    key_gain,
    qkv_weight,
    out_weight,
    norm2_gain,
    router,
    gate_up_weight,
    down_weight,
    cotangent,
):
    tokens = hidden_in.shape[1]
    sequence_number = lax.axis_size("seq")
    planes = lax.axis_size("dp")
    devices = sequence_number * planes
    group = lax.axis_index("seq")
    member = lax.axis_index("dp")
    index = group * planes + member
    heads = QUERY_HEADS // sequence_number
    query_columns = heads * HEAD_SIZE
    head_replicas = sequence_number // KEY_VALUE_HEADS
    capacity = (tokens * TOP * 9 + 8 * devices - 1) // (8 * devices)
    slots = -(-sequence_number * capacity // 16) * 16
    chunks = 4
    sequence_length = sequence_number * tokens
    shard = norm1_gain.shape[0]
    small_shard = query_gain.shape[0]

    turn_cos, turn_sin = turn_tables(sequence_length)
    (
        hidden1, mixed_low, lse, gains, picker, full_router, own_cols, out_rows, normed_full,
        heads_low, queries, pair, projected, grad_rows, masks,
    ) = attention_forward(
        sequence_number,
        planes,
        heads,
        shard,
        capacity,
        slots,
        chunks,
        hidden_in[0],
        routes[0].T,
        norm1_gain[None],
        norm2_gain[None],
        query_gain[None],
        key_gain[None],
        router.T,
        qkv_weight,
        out_weight,
        cotangent[0],
        turn_cos,
        turn_sin,
    )
    (
        grad_hidden1, grad_branch, grad_router, grad_weight_in, grad_weight_back, combined_rows,
    ) = expert_layer(
        sequence_number,
        planes,
        capacity,
        mixed_low,
        hidden1,
        cotangent[0],
        gains,
        routes[0].T,
        masks,
        picker,
        grad_rows,
        full_router,
        gate_up_weight[0],
        down_weight[0],
    )
    (
        grad_input, shard_out, shard_qkv, mixed_total, router_total, gain_total, _,
    ) = attention_backward(
        sequence_number,
        planes,
        heads,
        shard,
        capacity,
        grad_branch,
        grad_hidden1,
        hidden_in[0],
        gains,
        grad_router,
        out_rows,
        own_cols,
        normed_full,
        heads_low,
        queries,
        pair,
        projected,
        picker,
        combined_rows,
        lse,
        turn_cos,
        turn_sin,
    )
    grad_weight_in, grad_weight_back, output, grad_input, shard_out, shard_qkv = finish(
        grad_weight_in, grad_weight_back, hidden1, mixed_total, grad_input, shard_out, shard_qkv
    )
    index = group * planes + member
    router_own = lax.dynamic_slice_in_dim(router_total, member * shard, shard, 1)
    gain_own = lax.dynamic_slice_in_dim(
        gain_total[: MODEL_WIDTH // HEAD_SIZE].reshape(1, MODEL_WIDTH), index * shard, shard, 1
    )
    head_gains = lax.dynamic_slice_in_dim(
        gain_total[MODEL_WIDTH // HEAD_SIZE :][:2], index * small_shard, small_shard, 1
    )
    return (
        output[None],
        grad_input[None],
        gain_own[0],
        head_gains[0],
        head_gains[1],
        shard_qkv,
        shard_out,
        router_own[devices],
        router_own[:devices].T,
        grad_weight_in[None],
        grad_weight_back[None],
    )


def solution(mesh):
    in_specs = (
        P("dp", "seq", None),
        P("dp", "seq", None),
        P(("seq", "dp")),
        P(("seq", "dp")),
        P(("seq", "dp")),
        P(("seq", "dp"), None),
        P(("seq", "dp"), None),
        P(("seq", "dp")),
        P(("seq", "dp"), None),
        P(("seq", "dp"), None, None),
        P(("seq", "dp"), None, None),
        P("dp", "seq", None),
    )
    out_specs = (
        P("dp", "seq", None),
        P("dp", "seq", None),
        P(("seq", "dp")),
        P(("seq", "dp")),
        P(("seq", "dp")),
        P(("seq", "dp"), None),
        P(("seq", "dp"), None),
        P(("seq", "dp")),
        P(("seq", "dp"), None),
        P(("seq", "dp"), None, None),
        P(("seq", "dp"), None, None),
    )
    return jax.shard_map(body, mesh=mesh, in_specs=in_specs, out_specs=out_specs, check_vma=False)
```
